32 devices in a mesh: groups: 2 (over y), tensor: 4 (over z), batch: 4 (over x, core).
Axes of the slice: x: 2, y: 2, z: 4, core: 2. Of those that a mesh axis runs over, the one named last changes fastest.
Arguments:
- queries: bfloat16 [256, 32, 128], P(('groups', 'batch'), 'tensor'), parts along dimension 0
- key_cache: bfloat16 [256, 4, 96, 128], P(('groups', 'batch')), parts along dimension 0
- value_cache: bfloat16 [256, 4, 96, 128], P(('groups', 'batch')), parts along dimension 0, may hold values from -6 to 6
- new_key: bfloat16 [256, 4, 128], P(('groups', 'batch')), parts along dimension 0, may hold values from -6 to 6
- new_value: bfloat16 [256, 4, 128], P(('groups', 'batch')), parts along dimension 0, may hold values from -6 to 6
- lengths: int32 [256], P(('groups', 'batch')), parts along dimension 0, may hold values from 1 to 96
- out_weight: bfloat16 [4096, 8192], P('tensor'), may hold values from -0.09375 to 0.09375
- shrink_weight: bfloat16 [16, 4096, 64], P('batch', 'tensor'), may hold values from -0.09375 to 0.09375
- expand_weight: bfloat16 [16, 64, 8192], P('batch', None, 'tensor'), may hold values from -0.75 to 0.75
- adapter_rank: int32 [16], P('batch'), may hold values from 8 to 64
- adapter_list: int32 [64], P(('groups', 'batch')), parts along dimension 0, may hold values from 0 to 15, as said below
- row_adapter: int32 [256], P(('groups', 'batch')), parts along dimension 0, may hold values from 0 to 7
Outputs:
- mixed: bfloat16 [256, 8192], P(('groups', 'batch'), 'tensor'), parts along dimension 0
The draws below stay inside these ranges and needn't reach their ends.
There are 2 independent parts, one for each index of `groups`. The reference program is written for one: setup_inputs(seed, part) draws one part's arguments, and reference() takes and returns one part's arrays. A program takes and returns all parts, laid end to end along the dimension named above; an argument that names none is the same for every part. Nothing has to cross between parts.
Inputs may be any that keep to these rules, and one draw needn't show every extreme that they name: `adapter_list`: the 8 ids of one batch group are distinct; at most 2 of them lie among the ids b * 4 to (b + 1) * 4 - 1 of any one batch index b, and in every group exactly 2 lie on some index.
All inputs are finite; a program needn't handle non-finite values.
Results may differ from the reference program's by a relative error of at most 0.0075.
Values may be sent and summed in bfloat16 or wider, within the bound.
No kernel may reach another device: no remote copies, remote signals or barrier semaphores. Data moves between devices by JAX's collectives and lax.ppermute only.
A program may use at most 128 MiB of HBM per device.

```python
import jax
import jax.numpy as jnp
from jax import lax

D = 8192
HQ = 32
KVH = 4
HD = 128
R = 64
ROWS_DEV = 32
CTX = 96
POOL_DEV = 4
NEED = 8
CAP = 2
QPK = 8
QD = 4096
ROWS = 128
NPOOL = 16
N_BATCH = 4


def shared_keys(key):
    return jax.random.normal(key, (ROWS, KVH, CTX, HD), jnp.float32)


def draw_key_cache(key, part):
    base_keys = shared_keys(key)
    return base_keys.astype(jnp.bfloat16)


def draw_queries(key, part):
    key = jax.random.fold_in(key, 5)
    drawn = jax.random.normal(key, (ROWS, HQ, HD), jnp.float32)
    return drawn.astype(jnp.bfloat16)


def draw_adapter_list(key, part):
    key = jax.random.fold_in(key, 11)

    def one_group(group_index):
        group_key = jax.random.fold_in(key, group_index)
        forced_owner = jax.random.randint(jax.random.fold_in(group_key, 1), (), 0, N_BATCH)
        candidates = jax.random.permutation(jax.random.fold_in(group_key, 2), N_BATCH * CAP)
        elsewhere = jnp.where(candidates // CAP != forced_owner, 0, 1)
        ordered = candidates[jnp.argsort(elsewhere, stable=True)]
        forced = forced_owner * CAP + jnp.arange(CAP)
        chosen = jnp.concatenate([forced, ordered[:NEED - CAP]])
        owner_of = chosen // CAP
        slot_of = chosen % CAP

        def owner_table(owner_index):
            return jax.random.permutation(jax.random.fold_in(group_key, 100 + owner_index), POOL_DEV)
        tables = jax.vmap(owner_table)(jnp.arange(N_BATCH))
        local_ids = tables[owner_of, slot_of]
        return owner_of * POOL_DEV + local_ids
    return jax.vmap(one_group)(jnp.arange(N_BATCH)).reshape(-1).astype(jnp.int32)


def plant(array, key, smallest, high):
    longest = array.shape.index(max(array.shape))
    spots = []
    for shift in (0, 1):
        where = [jax.random.randint(jax.random.fold_in(key, axis), (), 0, length) for axis, length in enumerate(array.shape)]
        where[longest] = (where[longest] + shift) % array.shape[longest]
        spots.append(tuple(where))
    return array.at[spots[0]].set(smallest).at[spots[1]].set(high)


def block_levels(key, shape, shards, low, top_value):
    gain, own = 1.0, jax.random.fold_in(key, 6)
    for axis_at, shards_of in shards:
        heights = jnp.exp(jax.random.uniform(jax.random.fold_in(own, axis_at), (shards_of,), jnp.float32, low / len(shards), top_value / len(shards)))
        gain = gain * jnp.repeat(heights, shape[axis_at] // shards_of).reshape([-1 if axis == axis_at else 1 for axis in range(len(shape))])
    return gain


def bell_draw(rng, shape, spread, reach, pieces=(), dtype=jnp.bfloat16):
    result = jax.random.normal(rng, shape, jnp.float32) * spread
    if len(pieces) > 0:
        result = block_levels(rng, shape, pieces, -0.22, 0.18) * result
    return jnp.clip(result, min=-reach, max=reach).astype(dtype)


def setup_inputs(seed: int = 0, part: int = 0) -> dict:
    streams_of = jax.random.split(jax.random.key(seed), 13)
    own_keys = jax.random.split(jax.random.fold_in(streams_of[12], part), 13)
    queries = draw_queries(jax.random.fold_in(jax.random.fold_in(streams_of[12], part), 71), part)
    key_cache = draw_key_cache(jax.random.fold_in(jax.random.fold_in(streams_of[12], part), 71), part)
    value_cache = bell_draw(own_keys[2], (ROWS, KVH, CTX, HD), 1.0, 6.0, ((0, 4),))
    new_key = bell_draw(own_keys[3], (ROWS, KVH, HD), 1.0, 6.0, ((0, 4),))
    new_value = bell_draw(own_keys[4], (ROWS, KVH, HD), 1.0, 6.0, ((0, 4),))
    lengths = plant(jax.random.randint(own_keys[5], (ROWS,), 1, CTX + 1), jax.random.fold_in(own_keys[5], 1), 1, CTX).astype(jnp.int32)
    out_weight = bell_draw(streams_of[6], (QD, D), QD ** -0.5, 0.09375, ((0, 4),))
    shrink_weight = bell_draw(streams_of[7], (NPOOL, QD, R), QD ** -0.5, 0.09375, ((0, 4), (1, 4)))
    expand_weight = bell_draw(streams_of[8], (NPOOL, R, D), R ** -0.5, 0.75, ((0, 4), (2, 4)))
    adapter_rank = plant(jax.random.randint(streams_of[9], (NPOOL,), R // 8, R + 1), jax.random.fold_in(streams_of[9], 1), R // 8, R).astype(jnp.int32)
    adapter_list = draw_adapter_list(jax.random.fold_in(jax.random.fold_in(streams_of[12], part), 71), part)
    row_adapter = plant(jax.random.randint(own_keys[11], (ROWS,), 0, NEED), jax.random.fold_in(own_keys[11], 1), 0, NEED - 1).astype(jnp.int32)
    return {"queries": queries, "key_cache": key_cache, "value_cache": value_cache, "new_key": new_key, "new_value": new_value, "lengths": lengths, "out_weight": out_weight, "shrink_weight": shrink_weight, "expand_weight": expand_weight, "adapter_rank": adapter_rank, "adapter_list": adapter_list, "row_adapter": row_adapter}


def reference(queries, key_cache, value_cache, new_key, new_value, lengths, out_weight, shrink_weight, expand_weight, adapter_rank, adapter_list, row_adapter):
    row_count = queries.shape[0]
    score_scale = HD ** -0.5
    query_full = queries.astype(jnp.float32).reshape(row_count, KVH, QPK, HD)
    scores = jnp.einsum('rgqd,rgpd->rgqp', query_full, key_cache.astype(jnp.float32)) * score_scale
    fresh = jnp.einsum('rgqd,rgd->rgq', query_full, new_key.astype(jnp.float32)) * score_scale
    valid = jnp.arange(CTX)[None, :] < lengths[:, None]
    masked = jnp.where(valid[:, None, None, :], scores, jnp.float32(-1e30))
    highest = jnp.maximum(jnp.max(masked, axis=-1), fresh)
    cached_exp = jnp.where(valid[:, None, None, :], jnp.exp(masked - highest[..., None]), jnp.float32(0.0))
    fresh_exp = jnp.exp(fresh - highest)
    totals = jnp.sum(cached_exp, axis=-1) + fresh_exp
    cached_w = (cached_exp / totals[..., None]).astype(jnp.bfloat16)
    fresh_w = (fresh_exp / totals).astype(jnp.bfloat16)
    attended = jnp.einsum('rgqp,rgpd->rgqd', cached_w.astype(jnp.float32), value_cache.astype(jnp.float32))
    attended = attended + fresh_w.astype(jnp.float32)[..., None] * new_value.astype(jnp.float32)[:, :, None, :]
    attended = attended.astype(jnp.bfloat16).reshape(row_count, QD)
    base = jnp.dot(attended, out_weight, preferred_element_type=jnp.float32)
    group_index = (jnp.arange(row_count) // ROWS_DEV).astype(jnp.int32)
    adapter = jnp.take(adapter_list, group_index * NEED + row_adapter).astype(jnp.int32)
    keep_cols = (jnp.arange(R)[None, :] < jnp.take(adapter_rank, adapter)[:, None]).astype(jnp.float32)

    def shrink_row(item):
        row_vec, ident = item
        factor = lax.dynamic_index_in_dim(shrink_weight, ident, 0, keepdims=False)
        return jnp.dot(row_vec, factor, preferred_element_type=jnp.float32)

    shrink = (lax.map(shrink_row, (attended, adapter)) * keep_cols).astype(jnp.bfloat16)

    def expand_row(item):
        row_vec, ident = item
        factor = lax.dynamic_index_in_dim(expand_weight, ident, 0, keepdims=False)
        return jnp.dot(row_vec, factor, preferred_element_type=jnp.float32)

    delta = lax.map(expand_row, (shrink, adapter))
    return (base + delta).astype(jnp.bfloat16)
```

```python
import jax
import jax.numpy as jnp
from jax import lax
from jax.sharding import PartitionSpec as P

HQ = 32
KVH = 4


def attend(queries, key_cache, value_cache, new_key, new_value, lengths):
    row_count, head_count, head_width = queries.shape
    per_group = HQ // KVH
    kv_local = max(1, head_count // per_group)
    first_group = lax.axis_index("tensor") * head_count // per_group
    key_local = lax.dynamic_slice_in_dim(key_cache, first_group, kv_local, 1)
    value_local = lax.dynamic_slice_in_dim(value_cache, first_group, kv_local, 1)
    newkey_local = lax.dynamic_slice_in_dim(new_key, first_group, kv_local, 1)
    newvalue_local = lax.dynamic_slice_in_dim(new_value, first_group, kv_local, 1)
    positions = key_cache.shape[2]
    score_scale = head_width ** (-0.5)
    grouped = queries.reshape(row_count, kv_local, head_count // kv_local, head_width)
    scores = (
        jnp.einsum("rgqd,rgpd->rgqp", grouped, key_local, preferred_element_type=jnp.float32)
        * score_scale
    )
    fresh = (
        jnp.einsum("rgqd,rgd->rgq", grouped, newkey_local, preferred_element_type=jnp.float32)
        * score_scale
    )
    valid = jnp.arange(positions)[None, :] < lengths[:, None]
    masked = jnp.where(valid[:, None, None, :], scores, jnp.float32(-1e30))
    highest = jnp.maximum(jnp.max(masked, axis=-1), fresh)
    cached_exp = jnp.where(
        valid[:, None, None, :], jnp.exp(masked - highest[..., None]), jnp.float32(0.0)
    )
    fresh_exp = jnp.exp(fresh - highest)
    totals = jnp.sum(cached_exp, axis=-1) + fresh_exp
    cached_w = (cached_exp / totals[..., None]).astype(jnp.bfloat16)
    fresh_w = (fresh_exp / totals).astype(jnp.bfloat16)
    attended = jnp.einsum(
        "rgqp,rgpd->rgqd", cached_w, value_local, preferred_element_type=jnp.float32
    )
    attended = (
        attended
        + fresh_w.astype(jnp.float32)[..., None] * newvalue_local.astype(jnp.float32)[:, :, None, :]
    )
    return attended.astype(jnp.bfloat16).reshape(row_count, head_count * head_width)


def shifted(array, axis, size, shift):
    return lax.ppermute(array, axis, [(i, (i + shift) % size) for i in range(size)])


def local(
    tensor_size,
    batch_size,
    queries,
    key_cache,
    value_cache,
    new_key,
    new_value,
    lengths,
    out_weight,
    shrink_weight,
    expand_weight,
    adapter_rank,
    adapter_list,
    row_adapter,
):
    f32, bf16 = jnp.float32, jnp.bfloat16
    tensor_at = lax.axis_index("tensor")
    batch_at = lax.axis_index("batch")
    pool, _, rank_width = shrink_weight.shape
    block = expand_weight.shape[2]
    adapter = jnp.take(adapter_list, row_adapter)
    attended = attend(queries, key_cache, value_cache, new_key, new_value, lengths)
    rows, width = attended.shape

    tagged = jnp.concatenate(
        [attended, jnp.broadcast_to(adapter.astype(bf16)[:, None], (rows, 128))], axis=1
    )
    visitors = [tagged] + [
        shifted(tagged, "batch", batch_size, shift) for shift in range(1, batch_size)
    ]
    everyone = jnp.concatenate(visitors, axis=0)

    def base_block(shift):
        start = ((tensor_at + shift) % tensor_size) * block
        weight = lax.dynamic_slice_in_dim(out_weight, start, block, 1)
        return jnp.dot(attended, weight, preferred_element_type=f32)

    base_in = [
        shifted(base_block(shift).astype(bf16), "tensor", tensor_size, shift)
        for shift in range(1, tensor_size)
    ]
    base = base_block(0)

    all_rows = rows * batch_size
    slot = everyone[:, width].astype(jnp.int32) - batch_at * pool
    terms = jnp.einsum(
        "rq,nqk->rnk", everyone[:, :width], shrink_weight, preferred_element_type=f32
    )
    hot = slot[:, None] == jnp.arange(pool)[None, :]
    keep = jnp.arange(rank_width)[None, :] < adapter_rank[:, None]
    part = jnp.sum(jnp.where(hot[:, :, None] & keep[None], terms, f32(0.0)), axis=1)
    total = part
    for shift in range(1, tensor_size):
        total = total + shifted(part, "tensor", tensor_size, shift)
    shrink = total.astype(bf16)
    spread = (hot.astype(bf16)[:, :, None] * shrink[:, None, :]).reshape(
        all_rows, pool * rank_width
    )
    delta = jnp.dot(
        spread, expand_weight.reshape(pool * rank_width, block), preferred_element_type=f32
    )
    result = base + delta[:rows]
    for shift in range(1, batch_size):
        home = delta[shift * rows : (shift + 1) * rows].astype(bf16)
        result = result + shifted(home, "batch", batch_size, -shift).astype(f32)
    for arrived in base_in:
        result = result + arrived.astype(f32)
    return result.astype(bf16)


def solution(mesh):
    placed = (
        P(("groups", "batch"), "tensor", None),
        P(("groups", "batch"), None, None, None),
        P(("groups", "batch"), None, None, None),
        P(("groups", "batch"), None, None),
        P(("groups", "batch"), None, None),
        P(("groups", "batch")),
        P("tensor", None),
        P("batch", "tensor", None),
        P("batch", None, "tensor"),
        P("batch"),
        P(("groups", "batch")),
        P(("groups", "batch")),
    )

    def placed_local(*arrays):
        return local(mesh.shape["tensor"], mesh.shape["batch"], *arrays)

    return jax.shard_map(
        placed_local,
        mesh=mesh,
        in_specs=placed,
        out_specs=P(("groups", "batch"), "tensor"),
        check_vma=False,
    )
```

```python
import functools

import jax
import jax.numpy as jnp
from jax import lax
from jax.experimental import pallas as pl
from jax.experimental.pallas import tpu as pltpu
from jax.sharding import PartitionSpec as P

HQ = 32
KVH = 4
LANES = 128
VMEM = pltpu.VMEM
F32, BF16 = jnp.float32, jnp.bfloat16


def shifted(array, axis, size, shift):
    return lax.ppermute(array, axis, [(i, (i + shift) % size) for i in range(size)])


def lane_of(shape):
    return lax.broadcasted_iota(jnp.int32, shape, len(shape) - 1)


def attend_kernel(
    parts,
    lengths,
    row_adapter,
    adapter_list,
    group_at,
    queries,
    key_cache,
    value_cache,
    new_key,
    new_value,
    tagged,
    keys,
    values,
    spread_out,
    key_sems,
    value_sems,
):
    rows, heads, width = queries.shape
    positions = key_cache.shape[2]
    group = group_at[0]
    some = rows // parts

    def copies(part):
        at = pl.ds(part * some, some)
        return (
            pltpu.make_async_copy(key_cache.at[at, group], keys.at[at], key_sems.at[part]),
            pltpu.make_async_copy(value_cache.at[at, group], values.at[at], value_sems.at[part]),
        )

    for part in range(parts):
        for copy in copies(part):
            copy.start()
    at_row = lax.broadcasted_iota(jnp.int32, (rows, LANES), 0)
    tag = jnp.zeros((rows, LANES), jnp.int32)
    for row in range(rows):
        tag = jnp.where(at_row == row, adapter_list[row_adapter[row]], tag)
    tagged[:, heads * width :] = tag.astype(F32).astype(BF16)

    group_row = lax.broadcasted_iota(jnp.int32, new_key.shape, 1) == group
    fresh_key = jnp.sum(
        jnp.where(group_row, new_key[...].astype(F32), F32(0.0)), axis=1, keepdims=True
    )
    fresh_value = jnp.sum(
        jnp.where(group_row, new_value[...].astype(F32), F32(0.0)), axis=1, keepdims=True
    )
    score_scale = width ** (-0.5)
    fresh = jnp.sum(queries[...].astype(F32) * fresh_key, axis=-1, keepdims=True) * score_scale
    for part in range(parts):
        at = slice(part * some, (part + 1) * some)
        key_copy, value_copy = copies(part)
        key_copy.wait()
        scores = (
            lax.dot_general(
                queries[at], keys[at], (((2,), (2,)), ((0,), (0,))), preferred_element_type=F32
            )
            * score_scale
        )
        length = jnp.stack(
            [
                jnp.full((heads, positions), lengths[row], jnp.int32)
                for row in range(part * some, (part + 1) * some)
            ]
        )
        valid = lane_of(scores.shape) < length
        masked = jnp.where(valid, scores, F32(-1e30))
        highest = jnp.maximum(jnp.max(masked, axis=-1, keepdims=True), fresh[at])
        cached_exp = jnp.where(valid, jnp.exp(masked - highest), F32(0.0))
        fresh_exp = jnp.exp(fresh[at] - highest)
        totals = jnp.sum(cached_exp, axis=-1, keepdims=True) + fresh_exp
        cached_w = (cached_exp / totals).astype(BF16)
        fresh_w = (fresh_exp / totals).astype(BF16).astype(F32)
        value_copy.wait()
        attended = lax.dot_general(
            cached_w, values[at], (((2,), (1,)), ((0,), (0,))), preferred_element_type=F32
        )
        attended = attended + fresh_w * fresh_value[at]
        spread_out[pl.ds(part * some * heads, some * heads)] = attended.reshape(
            some * heads, width
        )
    for head in range(heads):
        tagged[:, head * width : (head + 1) * width] = spread_out[
            pl.ds(head, rows, stride=heads)
        ].astype(BF16)


def attend(queries, key_cache, value_cache, new_key, new_value, lengths, adapter_list, row_adapter):
    rows, heads, width = queries.shape
    positions = key_cache.shape[2]
    per_group = HQ // KVH
    group_at = (lax.axis_index("tensor") * heads // per_group).reshape(1).astype(jnp.int32)
    full = -(-heads // 8) * 8
    if full != heads:
        queries = jnp.pad(queries, ((0, 0), (0, full - heads), (0, 0)))
    parts = 2
    smem = pl.BlockSpec(memory_space=pltpu.SMEM)
    whole = pl.BlockSpec(memory_space=VMEM)
    away = pl.BlockSpec(memory_space=pl.ANY)
    tagged = pl.pallas_call(
        functools.partial(attend_kernel, parts),
        out_shape=jax.ShapeDtypeStruct((rows, full * width + LANES), BF16),
        in_specs=[smem] * 4 + [whole, away, away, whole, whole],
        out_specs=whole,
        scratch_shapes=[
            VMEM((rows, positions, width), BF16),
            VMEM((rows, positions, width), BF16),
            VMEM((rows * full, width), F32),
            pltpu.SemaphoreType.DMA((parts,)),
            pltpu.SemaphoreType.DMA((parts,)),
        ],
        compiler_params=pltpu.CompilerParams(vmem_limit_bytes=8 << 20),
        cost_estimate=pl.CostEstimate(
            flops=4 * rows * heads * positions * width,
            bytes_accessed=4 * rows * positions * width,
            transcendentals=rows * heads * positions,
        ),
        name="attention",
    )(lengths, row_adapter, adapter_list, group_at, queries, key_cache, value_cache, new_key, new_value)
    if full != heads:
        tagged = jnp.concatenate([tagged[:, : heads * width], tagged[:, full * width :]], axis=1)
    return tagged


def base_kernel(shifts, tensor_size, block, piece, column_at, tagged, out_weight, *rest):
    outs, (held, sems) = rest[: len(shifts)], rest[len(shifts) :]
    width = out_weight.shape[0]
    pieces = block // piece

    def copy(which, part):
        start = column_at[which] * block + part * piece
        at = which * pieces + part
        return pltpu.make_async_copy(
            out_weight.at[:, pl.ds(pl.multiple_of(start, piece), piece)],
            held.at[at],
            sems.at[at],
        )

    for which in range(len(shifts)):
        for part in range(pieces):
            copy(which, part).start()
    for which, out in enumerate(outs):
        for part in range(pieces):
            copy(which, part).wait()
            out[:, part * piece : (part + 1) * piece] = jnp.dot(
                tagged[:, :width], held[which * pieces + part], preferred_element_type=F32
            ).astype(out.dtype)


def base_blocks(tagged, out_weight, tensor_size, block, shifts):
    rows = tagged.shape[0]
    width = out_weight.shape[0]
    piece = min(block, 512)
    here = lax.axis_index("tensor")
    column_at = jnp.stack([(here + shift) % tensor_size for shift in shifts]).astype(jnp.int32)
    whole = pl.BlockSpec(memory_space=VMEM)
    held = len(shifts) * block // piece
    return pl.pallas_call(
        functools.partial(base_kernel, shifts, tensor_size, block, piece),
        out_shape=[
            jax.ShapeDtypeStruct((rows, block), BF16 if shift else F32) for shift in shifts
        ],
        in_specs=[pl.BlockSpec(memory_space=pltpu.SMEM), whole, pl.BlockSpec(memory_space=pl.ANY)],
        out_specs=[whole] * len(shifts),
        scratch_shapes=[VMEM((held, width, piece), BF16), pltpu.SemaphoreType.DMA((held,))],
        compiler_params=pltpu.CompilerParams(
            vmem_limit_bytes=(2 * held * width * piece) + (8 << 20)
        ),
        cost_estimate=pl.CostEstimate(
            flops=2 * rows * width * block * len(shifts),
            bytes_accessed=2 * width * block * len(shifts),
            transcendentals=0,
        ),
        name="base_" + "_".join(str(shift) for shift in shifts),
    )(column_at, tagged, out_weight)


def slots_of(tags, first):
    return tags.astype(F32).astype(jnp.int32) - first


def shrink_kernel(count, first_at, rank, *refs):
    blocks, (factors, out) = refs[:count], refs[count:]
    pool, rank_width, width = factors.shape
    rows = jnp.concatenate([block[:, :width] for block in blocks], axis=0)
    slot = slots_of(jnp.concatenate([block[:, width:] for block in blocks], axis=0), first_at[0])
    terms = lax.dot_general(
        rows,
        factors[...].reshape(pool * rank_width, width),
        (((1,), (1,)), ((), ())),
        preferred_element_type=F32,
    )
    lane = lane_of(slot.shape)
    per = LANES // rank_width
    kept = jnp.zeros(slot.shape, F32)
    for tile in range(pool // per):
        mine, limit = tile * per + lane // rank_width, jnp.zeros_like(lane)
        for n in range(tile * per, (tile + 1) * per):
            limit = jnp.where(mine == n, rank[n], limit)
        keep = (slot == mine) & (lane % rank_width < limit)
        kept = kept + jnp.where(keep, terms[:, tile * LANES : (tile + 1) * LANES], F32(0.0))
    both = kept + pltpu.roll(kept, rank_width, 1)
    half = both.shape[0] // 2
    out[...] = jnp.where(lane[:half] < rank_width, both[:half], both[half:]).astype(out.dtype)


def shrink_part(blocks, shrink_weight, adapter_rank, first_at):
    pool, width, rank_width = shrink_weight.shape
    rows = blocks[0].shape[0] * len(blocks)
    smem = pl.BlockSpec(memory_space=pltpu.SMEM)
    whole = pl.BlockSpec(memory_space=VMEM)
    return pl.pallas_call(
        functools.partial(shrink_kernel, len(blocks)),
        out_shape=jax.ShapeDtypeStruct((rows // 2, LANES), BF16),
        in_specs=[smem, smem] + [whole] * (len(blocks) + 1),
        out_specs=whole,
        compiler_params=pltpu.CompilerParams(vmem_limit_bytes=8 << 20),
        cost_estimate=pl.CostEstimate(
            flops=2 * rows * width * pool * rank_width,
            bytes_accessed=2 * width * (rows + pool * rank_width),
            transcendentals=0,
        ),
        name="shrink",
    )(first_at, adapter_rank, *blocks, jnp.swapaxes(shrink_weight, 1, 2))


def expand_kernel(count, sums, rank_width, first_at, *refs):
    tags, refs = refs[:count], refs[count:]
    parts, (factors, base), outs = refs[:sums], refs[sums : sums + 2], refs[sums + 2 :]
    slot = slots_of(jnp.concatenate([tag[...] for tag in tags], axis=0), first_at[0])
    total = parts[0][...].astype(F32)
    for part in parts[1:]:
        total = total + part[...].astype(F32)
    total = total.astype(BF16).astype(F32)
    other = pltpu.roll(total, rank_width, 1)
    low = lane_of(total.shape) < rank_width
    shrink = jnp.concatenate(
        [jnp.where(low, total, other), jnp.where(low, other, total)], axis=0
    )
    lane = lane_of(slot.shape)
    per = LANES // rank_width
    spread = jnp.concatenate(
        [
            jnp.where(slot == tile * per + lane // rank_width, shrink, F32(0.0)).astype(BF16)
            for tile in range(factors.shape[0] // LANES)
        ],
        axis=1,
    )
    rows, block = base.shape
    piece = min(block, 512)
    for at in range(0, block, piece):
        delta = jnp.dot(spread, factors[:, at : at + piece], preferred_element_type=F32)
        outs[0][:, at : at + piece] = base[:, at : at + piece] + delta[:rows]
        for which in range(1, count):
            outs[which][:, at : at + piece] = delta[which * rows : (which + 1) * rows].astype(BF16)


def expand(blocks, parts, expand_weight, base, first_at):
    pool, rank_width, block = expand_weight.shape
    rows, tagged_width = blocks[0].shape
    count = len(blocks)
    whole = pl.BlockSpec(memory_space=VMEM)
    tag = pl.BlockSpec((rows, LANES), lambda i: (0, tagged_width // LANES - 1))
    full = pl.BlockSpec((pool * rank_width, block), lambda i: (0, 0))
    part = pl.BlockSpec(parts[0].shape, lambda i: (0, 0))
    one = pl.BlockSpec((rows, block), lambda i: (0, 0))
    return pl.pallas_call(
        functools.partial(expand_kernel, count, len(parts), rank_width),
        grid=(1,),
        out_shape=[
            jax.ShapeDtypeStruct((rows, block), BF16 if which else F32) for which in range(count)
        ],
        in_specs=[pl.BlockSpec(memory_space=pltpu.SMEM)]
        + [tag] * count
        + [part] * len(parts)
        + [full, one],
        out_specs=[one] * count,
        compiler_params=pltpu.CompilerParams(vmem_limit_bytes=16 << 20),
        cost_estimate=pl.CostEstimate(
            flops=2 * rows * count * pool * rank_width * block,
            bytes_accessed=2 * pool * rank_width * block,
            transcendentals=0,
        ),
        name="expand",
    )(first_at, *blocks, *parts, expand_weight.reshape(pool * rank_width, block), base)


def local(
    tensor_size,
    batch_size,
    queries,
    key_cache,
    value_cache,
    new_key,
    new_value,
    lengths,
    out_weight,
    shrink_weight,
    expand_weight,
    adapter_rank,
    adapter_list,
    row_adapter,
):
    pool = shrink_weight.shape[0]
    block = expand_weight.shape[2]
    first_at = (lax.axis_index("batch") * pool).reshape(1).astype(jnp.int32)
    tagged = attend(
        queries, key_cache, value_cache, new_key, new_value, lengths, adapter_list, row_adapter
    )
    visitors = [tagged] + [
        shifted(tagged, "batch", batch_size, shift) for shift in range(1, batch_size)
    ]
    order = sorted(range(1, tensor_size), key=lambda s: -min(s, tensor_size - s)) + [0]
    half = tensor_size // 2
    terms = dict(zip(order[:half], base_blocks(tagged, out_weight, tensor_size, block, order[:half])))
    terms.update(
        zip(order[half:], base_blocks(tagged, out_weight, tensor_size, block, order[half:]))
    )
    base_in = [shifted(terms[shift], "tensor", tensor_size, shift) for shift in order[:-1]]

    part = shrink_part(visitors, shrink_weight, adapter_rank, first_at)
    parts = [part] + [
        shifted(part, "tensor", tensor_size, shift) for shift in range(1, tensor_size)
    ]
    homes = expand(visitors, parts, expand_weight, terms[0], first_at)
    result = homes[0]
    for arrived in base_in:
        result = result + arrived.astype(F32)
    for shift in range(1, batch_size):
        result = result + shifted(homes[shift], "batch", batch_size, -shift).astype(F32)
    return result.astype(BF16)


def solution(mesh):
    placed = (
        P(("groups", "batch"), "tensor", None),
        P(("groups", "batch"), None, None, None),
        P(("groups", "batch"), None, None, None),
        P(("groups", "batch"), None, None),
        P(("groups", "batch"), None, None),
        P(("groups", "batch")),
        P("tensor", None),
        P("batch", "tensor", None),
        P("batch", None, "tensor"),
        P("batch"),
        P(("groups", "batch")),
        P(("groups", "batch")),
    )

    def placed_local(*arrays):
        return local(mesh.shape["tensor"], mesh.shape["batch"], *arrays)

    return jax.shard_map(
        placed_local,
        mesh=mesh,
        in_specs=placed,
        out_specs=P(("groups", "batch"), "tensor"),
        check_vma=False,
    )
```

```python
import functools

import jax
import jax.numpy as jnp
from jax import lax
from jax.experimental import pallas as pl
from jax.experimental.pallas import tpu as pltpu
from jax.sharding import PartitionSpec as P

HQ = 32
KVH = 4
LANES = 128
VMEM = pltpu.VMEM
GRANT = 56 << 20
F32, BF16 = jnp.float32, jnp.bfloat16


def shifted(array, axis, size, shift):
    return lax.ppermute(array, axis, [(i, (i + shift) % size) for i in range(size)])


def lane_of(shape):
    return lax.broadcasted_iota(jnp.int32, shape, len(shape) - 1)


def attend_kernel(
    parts,
    lengths,
    row_adapter,
    adapter_list,
    group_at,
    queries,
    key_cache,
    value_cache,
    new_key,
    new_value,
    tagged,
    keys,
    values,
    spread_out,
    key_sems,
    value_sems,
):
    rows, heads, width = queries.shape
    positions = key_cache.shape[2]
    group = group_at[0]
    some = rows // parts

    def copies(part):
        at = pl.ds(part * some, some)
        return (
            pltpu.make_async_copy(key_cache.at[at, group], keys.at[at], key_sems.at[part]),
            pltpu.make_async_copy(value_cache.at[at, group], values.at[at], value_sems.at[part]),
        )

    for part in range(parts):
        for copy in copies(part):
            copy.start()
    at_row = lax.broadcasted_iota(jnp.int32, (rows, LANES), 0)
    tag = jnp.zeros((rows, LANES), jnp.int32)
    for row in range(rows):
        tag = jnp.where(at_row == row, adapter_list[row_adapter[row]], tag)
    tagged[:, heads * width :] = tag.astype(F32).astype(BF16)

    group_row = lax.broadcasted_iota(jnp.int32, new_key.shape, 1) == group
    fresh_key = jnp.sum(
        jnp.where(group_row, new_key[...].astype(F32), F32(0.0)), axis=1, keepdims=True
    )
    fresh_value = jnp.sum(
        jnp.where(group_row, new_value[...].astype(F32), F32(0.0)), axis=1, keepdims=True
    )
    score_scale = width ** (-0.5)
    fresh = jnp.sum(queries[...].astype(F32) * fresh_key, axis=-1, keepdims=True) * score_scale
    for part in range(parts):
        at = slice(part * some, (part + 1) * some)
        key_copy, value_copy = copies(part)
        key_copy.wait()
        scores = (
            lax.dot_general(
                queries[at], keys[at], (((2,), (2,)), ((0,), (0,))), preferred_element_type=F32
            )
            * score_scale
        )
        length = jnp.stack(
            [
                jnp.full((heads, positions), lengths[row], jnp.int32)
                for row in range(part * some, (part + 1) * some)
            ]
        )
        valid = lane_of(scores.shape) < length
        masked = jnp.where(valid, scores, F32(-1e30))
        highest = jnp.maximum(jnp.max(masked, axis=-1, keepdims=True), fresh[at])
        cached_exp = jnp.where(valid, jnp.exp(masked - highest), F32(0.0))
        fresh_exp = jnp.exp(fresh[at] - highest)
        totals = jnp.sum(cached_exp, axis=-1, keepdims=True) + fresh_exp
        cached_w = (cached_exp / totals).astype(BF16)
        fresh_w = (fresh_exp / totals).astype(BF16).astype(F32)
        value_copy.wait()
        attended = lax.dot_general(
            cached_w, values[at], (((2,), (1,)), ((0,), (0,))), preferred_element_type=F32
        )
        attended = attended + fresh_w * fresh_value[at]
        spread_out[pl.ds(part * some * heads, some * heads)] = attended.reshape(
            some * heads, width
        )
    for head in range(heads):
        tagged[:, head * width : (head + 1) * width] = spread_out[
            pl.ds(head, rows, stride=heads)
        ].astype(BF16)


def attend(queries, key_cache, value_cache, new_key, new_value, lengths, adapter_list, row_adapter):
    rows, heads, width = queries.shape
    positions = key_cache.shape[2]
    per_group = HQ // KVH
    group_at = (lax.axis_index("tensor") * heads // per_group).reshape(1).astype(jnp.int32)
    full = -(-heads // 8) * 8
    if full != heads:
        queries = jnp.pad(queries, ((0, 0), (0, full - heads), (0, 0)))
    parts = 2
    smem = pl.BlockSpec(memory_space=pltpu.SMEM)
    whole = pl.BlockSpec(memory_space=VMEM)
    away = pl.BlockSpec(memory_space=pl.ANY)
    tagged = pl.pallas_call(
        functools.partial(attend_kernel, parts),
        out_shape=jax.ShapeDtypeStruct((rows, full * width + LANES), BF16),
        in_specs=[smem] * 4 + [whole, away, away, whole, whole],
        out_specs=whole,
        scratch_shapes=[
            VMEM((rows, positions, width), BF16),
            VMEM((rows, positions, width), BF16),
            VMEM((rows * full, width), F32),
            pltpu.SemaphoreType.DMA((parts,)),
            pltpu.SemaphoreType.DMA((parts,)),
        ],
        compiler_params=pltpu.CompilerParams(vmem_limit_bytes=GRANT),
        cost_estimate=pl.CostEstimate(
            flops=4 * rows * heads * positions * width,
            bytes_accessed=4 * rows * positions * width,
            transcendentals=rows * heads * positions,
        ),
        name="attention",
    )(lengths, row_adapter, adapter_list, group_at, queries, key_cache, value_cache, new_key, new_value)
    if full != heads:
        tagged = jnp.concatenate([tagged[:, : heads * width], tagged[:, full * width :]], axis=1)
    return tagged


def base_kernel(shifts, tensor_size, block, piece, column_at, tagged, out_weight, *rest):
    outs, (held, sems) = rest[: len(shifts)], rest[len(shifts) :]
    width = out_weight.shape[0]
    pieces = block // piece

    def copy(which, part):
        start = column_at[which] * block + part * piece
        at = which * pieces + part
        return pltpu.make_async_copy(
            out_weight.at[:, pl.ds(pl.multiple_of(start, piece), piece)],
            held.at[at],
            sems.at[at],
        )

    for which in range(len(shifts)):
        for part in range(pieces):
            copy(which, part).start()
    for which, out in enumerate(outs):
        for part in range(pieces):
            copy(which, part).wait()
            out[:, part * piece : (part + 1) * piece] = jnp.dot(
                tagged[:, :width], held[which * pieces + part], preferred_element_type=F32
            ).astype(out.dtype)


def base_blocks(tagged, out_weight, tensor_size, block, shifts):
    rows = tagged.shape[0]
    width = out_weight.shape[0]
    piece = min(block, 512)
    here = lax.axis_index("tensor")
    column_at = jnp.stack([(here + shift) % tensor_size for shift in shifts]).astype(jnp.int32)
    whole = pl.BlockSpec(memory_space=VMEM)
    held = len(shifts) * block // piece
    return pl.pallas_call(
        functools.partial(base_kernel, shifts, tensor_size, block, piece),
        out_shape=[
            jax.ShapeDtypeStruct((rows, block), BF16 if shift else F32) for shift in shifts
        ],
        in_specs=[pl.BlockSpec(memory_space=pltpu.SMEM), whole, pl.BlockSpec(memory_space=pl.ANY)],
        out_specs=[whole] * len(shifts),
        scratch_shapes=[VMEM((held, width, piece), BF16), pltpu.SemaphoreType.DMA((held,))],
        compiler_params=pltpu.CompilerParams(vmem_limit_bytes=GRANT),
        cost_estimate=pl.CostEstimate(
            flops=2 * rows * width * block * len(shifts),
            bytes_accessed=2 * width * block * len(shifts),
            transcendentals=0,
        ),
        name="base_" + "_".join(str(shift) for shift in shifts),
    )(column_at, tagged, out_weight)


def slots_of(tags, first):
    return tags.astype(F32).astype(jnp.int32) - first


def shrink_kernel(count, first_at, rank, *refs):
    blocks, (factors, out) = refs[:count], refs[count:]
    pool, rank_width, width = factors.shape
    rows = jnp.concatenate([block[:, :width] for block in blocks], axis=0)
    slot = slots_of(jnp.concatenate([block[:, width:] for block in blocks], axis=0), first_at[0])
    terms = lax.dot_general(
        rows,
        factors[...].reshape(pool * rank_width, width),
        (((1,), (1,)), ((), ())),
        preferred_element_type=F32,
    )
    lane = lane_of(slot.shape)
    per = LANES // rank_width
    kept = jnp.zeros(slot.shape, F32)
    for tile in range(pool // per):
        mine, limit = tile * per + lane // rank_width, jnp.zeros_like(lane)
        for n in range(tile * per, (tile + 1) * per):
            limit = jnp.where(mine == n, rank[n], limit)
        keep = (slot == mine) & (lane % rank_width < limit)
        kept = kept + jnp.where(keep, terms[:, tile * LANES : (tile + 1) * LANES], F32(0.0))
    both = kept + pltpu.roll(kept, rank_width, 1)
    half = both.shape[0] // 2
    out[...] = jnp.where(lane[:half] < rank_width, both[:half], both[half:]).astype(out.dtype)


def shrink_part(blocks, shrink_weight, adapter_rank, first_at):
    pool, width, rank_width = shrink_weight.shape
    rows = blocks[0].shape[0] * len(blocks)
    smem = pl.BlockSpec(memory_space=pltpu.SMEM)
    whole = pl.BlockSpec(memory_space=VMEM)
    return pl.pallas_call(
        functools.partial(shrink_kernel, len(blocks)),
        out_shape=jax.ShapeDtypeStruct((rows // 2, LANES), BF16),
        in_specs=[smem, smem] + [whole] * (len(blocks) + 1),
        out_specs=whole,
        compiler_params=pltpu.CompilerParams(vmem_limit_bytes=8 << 20),
        cost_estimate=pl.CostEstimate(
            flops=2 * rows * width * pool * rank_width,
            bytes_accessed=2 * width * (rows + pool * rank_width),
            transcendentals=0,
        ),
        name="shrink",
    )(first_at, adapter_rank, *blocks, jnp.swapaxes(shrink_weight, 1, 2))


def expand_kernel(count, sums, rank_width, first_at, *refs):
    tags, refs = refs[:count], refs[count:]
    parts, (factors, base), outs = refs[:sums], refs[sums : sums + 2], refs[sums + 2 :]
    slot = slots_of(jnp.concatenate([tag[...] for tag in tags], axis=0), first_at[0])
    total = parts[0][...].astype(F32)
    for part in parts[1:]:
        total = total + part[...].astype(F32)
    total = total.astype(BF16).astype(F32)
    other = pltpu.roll(total, rank_width, 1)
    low = lane_of(total.shape) < rank_width
    shrink = jnp.concatenate(
        [jnp.where(low, total, other), jnp.where(low, other, total)], axis=0
    )
    lane = lane_of(slot.shape)
    per = LANES // rank_width
    spread = jnp.concatenate(
        [
            jnp.where(slot == tile * per + lane // rank_width, shrink, F32(0.0)).astype(BF16)
            for tile in range(factors.shape[0] // LANES)
        ],
        axis=1,
    )
    rows, block = base.shape
    piece = min(block, 512)
    for at in range(0, block, piece):
        delta = jnp.dot(spread, factors[:, at : at + piece], preferred_element_type=F32)
        outs[0][:, at : at + piece] = base[:, at : at + piece] + delta[:rows]
        for which in range(1, count):
            outs[which][:, at : at + piece] = delta[which * rows : (which + 1) * rows].astype(BF16)


def expand(blocks, parts, expand_weight, base, first_at):
    pool, rank_width, block = expand_weight.shape
    rows, tagged_width = blocks[0].shape
    count = len(blocks)
    whole = pl.BlockSpec(memory_space=VMEM)
    tag = pl.BlockSpec((rows, LANES), lambda i: (0, tagged_width // LANES - 1))
    full = pl.BlockSpec((pool * rank_width, block), lambda i: (0, 0))
    part = pl.BlockSpec(parts[0].shape, lambda i: (0, 0))
    one = pl.BlockSpec((rows, block), lambda i: (0, 0))
    return pl.pallas_call(
        functools.partial(expand_kernel, count, len(parts), rank_width),
        grid=(1,),
        out_shape=[
            jax.ShapeDtypeStruct((rows, block), BF16 if which else F32) for which in range(count)
        ],
        in_specs=[pl.BlockSpec(memory_space=pltpu.SMEM)]
        + [tag] * count
        + [part] * len(parts)
        + [full, one],
        out_specs=[one] * count,
        compiler_params=pltpu.CompilerParams(vmem_limit_bytes=16 << 20),
        cost_estimate=pl.CostEstimate(
            flops=2 * rows * count * pool * rank_width * block,
            bytes_accessed=2 * pool * rank_width * block,
            transcendentals=0,
        ),
        name="expand",
    )(first_at, *blocks, *parts, expand_weight.reshape(pool * rank_width, block), base)


def local(
    tensor_size,
    batch_size,
    queries,
    key_cache,
    value_cache,
    new_key,
    new_value,
    lengths,
    out_weight,
    shrink_weight,
    expand_weight,
    adapter_rank,
    adapter_list,
    row_adapter,
):
    pool = shrink_weight.shape[0]
    block = expand_weight.shape[2]
    first_at = (lax.axis_index("batch") * pool).reshape(1).astype(jnp.int32)
    tagged = attend(
        queries, key_cache, value_cache, new_key, new_value, lengths, adapter_list, row_adapter
    )
    visitors = [tagged] + [
        shifted(tagged, "batch", batch_size, shift) for shift in range(1, batch_size)
    ]
    order = sorted(range(1, tensor_size), key=lambda s: -min(s, tensor_size - s)) + [0]
    half = tensor_size // 2
    terms = dict(zip(order[:half], base_blocks(tagged, out_weight, tensor_size, block, order[:half])))
    terms.update(
        zip(order[half:], base_blocks(tagged, out_weight, tensor_size, block, order[half:]))
    )
    base_in = [shifted(terms[shift], "tensor", tensor_size, shift) for shift in order[:-1]]

    part = shrink_part(visitors, shrink_weight, adapter_rank, first_at)
    parts = [part] + [
        shifted(part, "tensor", tensor_size, shift) for shift in range(1, tensor_size)
    ]
    homes = expand(visitors, parts, expand_weight, terms[0], first_at)
    result = homes[0]
    for arrived in base_in:
        result = result + arrived.astype(F32)
    for shift in range(1, batch_size):
        result = result + shifted(homes[shift], "batch", batch_size, -shift).astype(F32)
    return result.astype(BF16)


def solution(mesh):
    placed = (
        P(("groups", "batch"), "tensor", None),
        P(("groups", "batch"), None, None, None),
        P(("groups", "batch"), None, None, None),
        P(("groups", "batch"), None, None),
        P(("groups", "batch"), None, None),
        P(("groups", "batch")),
        P("tensor", None),
        P("batch", "tensor", None),
        P("batch", None, "tensor"),
        P("batch"),
        P(("groups", "batch")),
        P(("groups", "batch")),
    )

    def placed_local(*arrays):
        return local(mesh.shape["tensor"], mesh.shape["batch"], *arrays)

    return jax.shard_map(
        placed_local,
        mesh=mesh,
        in_specs=placed,
        out_specs=P(("groups", "batch"), "tensor"),
        check_vma=False,
    )
```

```python
import functools

import jax
import jax.numpy as jnp
from jax import lax
from jax.experimental import pallas as pl
from jax.experimental.pallas import tpu as pltpu
from jax.sharding import PartitionSpec as P

HQ = 32
KVH = 4
LANES = 128
VMEM = pltpu.VMEM
GRANT = 56 << 20
F32, BF16 = jnp.float32, jnp.bfloat16


def exchanged(blocks, axis):
    return lax.all_to_all(blocks, axis, 0, 0, tiled=True)


def lane_of(shape):
    return lax.broadcasted_iota(jnp.int32, shape, len(shape) - 1)


def attend_kernel(parts, copies_out, group_at, *refs):
    given, (tagged, *scratch) = refs[:8], refs[8:]
    held, (spread_out, small_sems, key_sems, value_sems) = scratch[:8], scratch[8:]
    key_cache, value_cache = given[:2]
    keys, values, queries, new_key, new_value, lengths, row_adapter, adapter_list = held
    rows, heads, width = queries.shape
    positions = key_cache.shape[2]
    group = group_at[0]
    some = rows // parts

    def cache_copies(part):
        at = pl.ds(part * some, some)
        return (
            pltpu.make_async_copy(key_cache.at[at, group], keys.at[at], key_sems.at[part]),
            pltpu.make_async_copy(value_cache.at[at, group], values.at[at], value_sems.at[part]),
        )

    small = [
        pltpu.make_async_copy(given[i], held[i], small_sems.at[i - 2]) for i in range(2, 8)
    ]
    for copy in small:
        copy.start()
    for part in range(parts):
        for copy in cache_copies(part):
            copy.start()
    for copy in small:
        copy.wait()
    at_row = lax.broadcasted_iota(jnp.int32, (rows, LANES), 0)
    tag = jnp.zeros((rows, LANES), jnp.int32)
    for row in range(rows):
        tag = jnp.where(at_row == row, adapter_list[row_adapter[row]], tag)
    tag = tag.astype(F32).astype(BF16)

    group_row = lax.broadcasted_iota(jnp.int32, new_key.shape, 1) == group
    fresh_key = jnp.sum(
        jnp.where(group_row, new_key[...].astype(F32), F32(0.0)), axis=1, keepdims=True
    )
    fresh_value = jnp.sum(
        jnp.where(group_row, new_value[...].astype(F32), F32(0.0)), axis=1, keepdims=True
    )
    score_scale = width ** (-0.5)
    fresh = jnp.sum(queries[...].astype(F32) * fresh_key, axis=-1, keepdims=True) * score_scale
    for part in range(parts):
        at = slice(part * some, (part + 1) * some)
        key_copy, value_copy = cache_copies(part)
        key_copy.wait()
        scores = (
            lax.dot_general(
                queries[at], keys[at], (((2,), (2,)), ((0,), (0,))), preferred_element_type=F32
            )
            * score_scale
        )
        length = jnp.stack(
            [
                jnp.full((heads, positions), lengths[row], jnp.int32)
                for row in range(part * some, (part + 1) * some)
            ]
        )
        valid = lane_of(scores.shape) < length
        masked = jnp.where(valid, scores, F32(-1e30))
        highest = jnp.maximum(jnp.max(masked, axis=-1, keepdims=True), fresh[at])
        cached_exp = jnp.where(valid, jnp.exp(masked - highest), F32(0.0))
        fresh_exp = jnp.exp(fresh[at] - highest)
        totals = jnp.sum(cached_exp, axis=-1, keepdims=True) + fresh_exp
        cached_w = (cached_exp / totals).astype(BF16)
        fresh_w = (fresh_exp / totals).astype(BF16).astype(F32)
        value_copy.wait()
        attended = lax.dot_general(
            cached_w, values[at], (((2,), (1,)), ((0,), (0,))), preferred_element_type=F32
        )
        attended = attended + fresh_w * fresh_value[at]
        spread_out[pl.ds(part * some * heads, some * heads)] = attended.reshape(
            some * heads, width
        )
    for copy in range(copies_out):
        tagged[copy * rows : (copy + 1) * rows, heads * width :] = tag
    for head in range(heads):
        block = spread_out[pl.ds(head, rows, stride=heads)].astype(BF16)
        for copy in range(copies_out):
            tagged[copy * rows : (copy + 1) * rows, head * width : (head + 1) * width] = block


def attend(
    copies_out,
    queries,
    key_cache,
    value_cache,
    new_key,
    new_value,
    lengths,
    adapter_list,
    row_adapter,
):
    rows, heads, width = queries.shape
    positions = key_cache.shape[2]
    per_group = HQ // KVH
    group_at = (lax.axis_index("tensor") * heads // per_group).reshape(1).astype(jnp.int32)
    full = -(-heads // 8) * 8
    if full != heads:
        queries = jnp.pad(queries, ((0, 0), (0, full - heads), (0, 0)))
    parts = 2
    smem = pl.BlockSpec(memory_space=pltpu.SMEM)
    away = pl.BlockSpec(memory_space=pl.ANY)
    tagged = pl.pallas_call(
        functools.partial(attend_kernel, parts, copies_out),
        out_shape=jax.ShapeDtypeStruct((copies_out * rows, full * width + LANES), BF16),
        in_specs=[smem] + [away] * 8,
        out_specs=pl.BlockSpec(memory_space=VMEM),
        scratch_shapes=[
            VMEM((rows, positions, width), BF16),
            VMEM((rows, positions, width), BF16),
            VMEM(queries.shape, BF16),
            VMEM(new_key.shape, BF16),
            VMEM(new_value.shape, BF16),
            pltpu.SMEM(lengths.shape, jnp.int32),
            pltpu.SMEM(row_adapter.shape, jnp.int32),
            pltpu.SMEM(adapter_list.shape, jnp.int32),
            VMEM((rows * full, width), F32),
            pltpu.SemaphoreType.DMA((6,)),
            pltpu.SemaphoreType.DMA((parts,)),
            pltpu.SemaphoreType.DMA((parts,)),
        ],
        compiler_params=pltpu.CompilerParams(vmem_limit_bytes=GRANT),
        cost_estimate=pl.CostEstimate(
            flops=4 * rows * heads * positions * width,
            bytes_accessed=4 * rows * positions * width,
            transcendentals=rows * heads * positions,
        ),
        name="attention",
    )(
        group_at,
        key_cache,
        value_cache,
        queries,
        new_key,
        new_value,
        lengths,
        row_adapter,
        adapter_list,
    )
    if full != heads:
        tagged = jnp.concatenate([tagged[:, : heads * width], tagged[:, full * width :]], axis=1)
    return tagged


def base_kernel(starts, rows, piece, deep, tagged, out_weight, out, held, sems):
    width = out_weight.shape[0]
    count = len(starts)

    def copy(at):
        return pltpu.make_async_copy(
            out_weight.at[:, pl.ds(starts[at], piece)], held.at[at % deep], sems.at[at % deep]
        )

    for at in range(min(deep, count)):
        copy(at).start()
    per = out.shape[1] // piece
    for at in range(count):
        copy(at).wait()
        term = jnp.dot(tagged[:rows, :width], held[at % deep], preferred_element_type=F32)
        to, column = at // per * rows, at % per * piece
        out[to : to + rows, column : column + piece] = term.astype(out.dtype)
        if at + deep < count:
            copy(at + deep).start()


def base_blocks(tagged, out_weight, rows, tensor_size, block, first, last):
    width = out_weight.shape[0]
    piece = min(last - first, 256)
    starts = [
        to * block + column for to in range(tensor_size) for column in range(first, last, piece)
    ]
    deep = 6
    whole = pl.BlockSpec(memory_space=VMEM)
    return pl.pallas_call(
        functools.partial(base_kernel, starts, rows, piece, deep),
        out_shape=jax.ShapeDtypeStruct((tensor_size * rows, last - first), BF16),
        in_specs=[whole, pl.BlockSpec(memory_space=pl.ANY)],
        out_specs=whole,
        scratch_shapes=[VMEM((deep, width, piece), BF16), pltpu.SemaphoreType.DMA((deep,))],
        compiler_params=pltpu.CompilerParams(vmem_limit_bytes=GRANT),
        cost_estimate=pl.CostEstimate(
            flops=2 * rows * width * (last - first) * tensor_size,
            bytes_accessed=2 * width * (last - first) * tensor_size,
            transcendentals=0,
        ),
        name="base_terms",
    )(tagged, out_weight)


def slots_of(tags, first):
    return tags.astype(F32).astype(jnp.int32) - first


def shrink_kernel(copies_out, first_at, rank, everyone, factors, out):
    pool, rank_width, width = factors.shape
    slot = slots_of(everyone[:, width:], first_at[0])
    terms = lax.dot_general(
        everyone[:, :width],
        factors[...].reshape(pool * rank_width, width),
        (((1,), (1,)), ((), ())),
        preferred_element_type=F32,
    )
    lane = lane_of(slot.shape)
    per = LANES // rank_width
    kept = jnp.zeros(slot.shape, F32)
    for tile in range(pool // per):
        mine, limit = tile * per + lane // rank_width, jnp.zeros_like(lane)
        for n in range(tile * per, (tile + 1) * per):
            limit = jnp.where(mine == n, rank[n], limit)
        keep = (slot == mine) & (lane % rank_width < limit)
        kept = kept + jnp.where(keep, terms[:, tile * LANES : (tile + 1) * LANES], F32(0.0))
    both = kept + pltpu.roll(kept, rank_width, 1)
    half = both.shape[0] // 2
    packed = jnp.where(lane[:half] < rank_width, both[:half], both[half:]).astype(out.dtype)
    for copy in range(copies_out):
        out[copy * half : (copy + 1) * half] = packed


def shrink_part(copies_out, everyone, shrink_weight, adapter_rank, first_at):
    pool, width, rank_width = shrink_weight.shape
    rows = everyone.shape[0]
    smem = pl.BlockSpec(memory_space=pltpu.SMEM)
    whole = pl.BlockSpec(memory_space=VMEM)
    return pl.pallas_call(
        functools.partial(shrink_kernel, copies_out),
        out_shape=jax.ShapeDtypeStruct((copies_out * rows // 2, LANES), BF16),
        in_specs=[smem, smem, whole, whole],
        out_specs=whole,
        compiler_params=pltpu.CompilerParams(vmem_limit_bytes=8 << 20),
        cost_estimate=pl.CostEstimate(
            flops=2 * rows * width * pool * rank_width,
            bytes_accessed=2 * width * (rows + pool * rank_width),
            transcendentals=0,
        ),
        name="shrink",
    )(first_at, adapter_rank, everyone, jnp.swapaxes(shrink_weight, 1, 2))


def expand_kernel(sums, rank_width, first_at, everyone, parts, factors, out):
    slot = slots_of(everyone[...], first_at[0])
    half = parts.shape[0] // sums
    total = parts[:half].astype(F32)
    for at in range(1, sums):
        total = total + parts[at * half : (at + 1) * half].astype(F32)
    total = total.astype(BF16).astype(F32)
    other = pltpu.roll(total, rank_width, 1)
    low = lane_of(total.shape) < rank_width
    shrink = jnp.concatenate(
        [jnp.where(low, total, other), jnp.where(low, other, total)], axis=0
    )
    lane = lane_of(slot.shape)
    per = LANES // rank_width
    spread = jnp.concatenate(
        [
            jnp.where(slot == tile * per + lane // rank_width, shrink, F32(0.0)).astype(BF16)
            for tile in range(factors.shape[0] // LANES)
        ],
        axis=1,
    )
    block = out.shape[1]
    piece = min(block, 512)
    for at in range(0, block, piece):
        out[:, at : at + piece] = jnp.dot(
            spread, factors[:, at : at + piece], preferred_element_type=F32
        ).astype(BF16)


def expand(sums, everyone, parts, expand_weight, first_at):
    pool, rank_width, block = expand_weight.shape
    rows, tagged_width = everyone.shape
    tag = pl.BlockSpec((rows, LANES), lambda i: (0, tagged_width // LANES - 1))
    full = pl.BlockSpec((pool * rank_width, block), lambda i: (0, 0))
    return pl.pallas_call(
        functools.partial(expand_kernel, sums, rank_width),
        grid=(1,),
        out_shape=jax.ShapeDtypeStruct((rows, block), BF16),
        in_specs=[
            pl.BlockSpec(memory_space=pltpu.SMEM),
            tag,
            pl.BlockSpec(parts.shape, lambda i: (0, 0)),
            full,
        ],
        out_specs=pl.BlockSpec((rows, block), lambda i: (0, 0)),
        compiler_params=pltpu.CompilerParams(vmem_limit_bytes=16 << 20),
        cost_estimate=pl.CostEstimate(
            flops=2 * rows * pool * rank_width * block,
            bytes_accessed=2 * pool * rank_width * block,
            transcendentals=0,
        ),
        name="expand",
    )(first_at, everyone, parts, expand_weight.reshape(pool * rank_width, block))


def local(
    tensor_size,
    batch_size,
    queries,
    key_cache,
    value_cache,
    new_key,
    new_value,
    lengths,
    out_weight,
    shrink_weight,
    expand_weight,
    adapter_rank,
    adapter_list,
    row_adapter,
):
    rows = queries.shape[0]
    pool = shrink_weight.shape[0]
    block = expand_weight.shape[2]
    first_at = (lax.axis_index("batch") * pool).reshape(1).astype(jnp.int32)
    tagged = attend(
        batch_size,
        queries,
        key_cache,
        value_cache,
        new_key,
        new_value,
        lengths,
        adapter_list,
        row_adapter,
    )
    everyone = exchanged(tagged, "batch")
    base_in = [
        exchanged(
            base_blocks(tagged, out_weight, rows, tensor_size, block, at, at + block // 2),
            "tensor",
        )
        for at in (0, block // 2)
    ]
    part = shrink_part(tensor_size, everyone, shrink_weight, adapter_rank, first_at)
    parts = exchanged(part, "tensor")
    homes = exchanged(expand(tensor_size, everyone, parts, expand_weight, first_at), "batch")

    def total(arrived, count):
        return jnp.sum(arrived.reshape(count, rows, -1).astype(F32), axis=0)

    base = jnp.concatenate([total(half, tensor_size) for half in base_in], axis=1)
    return (base + total(homes, batch_size)).astype(BF16)


def solution(mesh):
    placed = (
        P(("groups", "batch"), "tensor", None),
        P(("groups", "batch"), None, None, None),
        P(("groups", "batch"), None, None, None),
        P(("groups", "batch"), None, None),
        P(("groups", "batch"), None, None),
        P(("groups", "batch")),
        P("tensor", None),
        P("batch", "tensor", None),
        P("batch", None, "tensor"),
        P("batch"),
        P(("groups", "batch")),
        P(("groups", "batch")),
    )

    def placed_local(*arrays):
        return local(mesh.shape["tensor"], mesh.shape["batch"], *arrays)

    return jax.shard_map(
        placed_local,
        mesh=mesh,
        in_specs=placed,
        out_specs=P(("groups", "batch"), "tensor"),
        check_vma=False,
    )
```

```python
import functools

import jax
import jax.numpy as jnp
from jax import lax
from jax.experimental import pallas as pl
from jax.experimental.pallas import tpu as pltpu
from jax.sharding import PartitionSpec as P

HQ = 32
KVH = 4
LANES = 128
VMEM = pltpu.VMEM
GRANT = 56 << 20
F32, BF16 = jnp.float32, jnp.bfloat16


def permuted(array, axis, size, partner):
    return lax.ppermute(array, axis, [(i, partner(i)) for i in range(size)])


def in_hbm(*arrays):
    return [pltpu.with_memory_space_constraint(array, pltpu.HBM) for array in arrays]


def lane_of(shape):
    return lax.broadcasted_iota(jnp.int32, shape, len(shape) - 1)


def attend_kernel(parts, group_at, *refs):
    given, (tagged, *scratch) = refs[:8], refs[8:]
    held, (spread_out, small_sems, key_sems, value_sems) = scratch[:8], scratch[8:]
    key_cache, value_cache = given[:2]
    keys, values, queries, new_key, new_value, lengths, row_adapter, adapter_list = held
    rows, heads, width = queries.shape
    positions = key_cache.shape[2]
    group = group_at[0]
    some = rows // parts

    def cache_copies(part):
        at = pl.ds(part * some, some)
        return (
            pltpu.make_async_copy(key_cache.at[at, group], keys.at[at], key_sems.at[part]),
            pltpu.make_async_copy(value_cache.at[at, group], values.at[at], value_sems.at[part]),
        )

    small = [
        pltpu.make_async_copy(given[i], held[i], small_sems.at[i - 2]) for i in range(2, 8)
    ]
    for copy in small:
        copy.start()
    for part in range(parts):
        for copy in cache_copies(part):
            copy.start()
    for copy in small:
        copy.wait()
    at_row = lax.broadcasted_iota(jnp.int32, (rows, LANES), 0)
    tag = jnp.zeros((rows, LANES), jnp.int32)
    for row in range(rows):
        tag = jnp.where(at_row == row, adapter_list[row_adapter[row]], tag)
    tag = tag.astype(F32).astype(BF16)

    group_row = lax.broadcasted_iota(jnp.int32, new_key.shape, 1) == group
    fresh_key = jnp.sum(
        jnp.where(group_row, new_key[...].astype(F32), F32(0.0)), axis=1, keepdims=True
    )
    fresh_value = jnp.sum(
        jnp.where(group_row, new_value[...].astype(F32), F32(0.0)), axis=1, keepdims=True
    )
    score_scale = width ** (-0.5)
    fresh = jnp.sum(queries[...].astype(F32) * fresh_key, axis=-1, keepdims=True) * score_scale
    for part in range(parts):
        at = slice(part * some, (part + 1) * some)
        key_copy, value_copy = cache_copies(part)
        key_copy.wait()
        scores = (
            lax.dot_general(
                queries[at], keys[at], (((2,), (2,)), ((0,), (0,))), preferred_element_type=F32
            )
            * score_scale
        )
        length = jnp.stack(
            [
                jnp.full((heads, positions), lengths[row], jnp.int32)
                for row in range(part * some, (part + 1) * some)
            ]
        )
        valid = lane_of(scores.shape) < length
        masked = jnp.where(valid, scores, F32(-1e30))
        highest = jnp.maximum(jnp.max(masked, axis=-1, keepdims=True), fresh[at])
        cached_exp = jnp.where(valid, jnp.exp(masked - highest), F32(0.0))
        fresh_exp = jnp.exp(fresh[at] - highest)
        totals = jnp.sum(cached_exp, axis=-1, keepdims=True) + fresh_exp
        cached_w = (cached_exp / totals).astype(BF16)
        fresh_w = (fresh_exp / totals).astype(BF16).astype(F32)
        value_copy.wait()
        attended = lax.dot_general(
            cached_w, values[at], (((2,), (1,)), ((0,), (0,))), preferred_element_type=F32
        )
        attended = attended + fresh_w * fresh_value[at]
        spread_out[pl.ds(part * some * heads, some * heads)] = attended.reshape(
            some * heads, width
        )
    tagged[:, heads * width :] = tag
    for head in range(heads):
        tagged[:, head * width : (head + 1) * width] = spread_out[
            pl.ds(head, rows, stride=heads)
        ].astype(BF16)


def attend(
    queries,
    key_cache,
    value_cache,
    new_key,
    new_value,
    lengths,
    adapter_list,
    row_adapter,
):
    rows, heads, width = queries.shape
    positions = key_cache.shape[2]
    per_group = HQ // KVH
    group_at = (lax.axis_index("tensor") * heads // per_group).reshape(1).astype(jnp.int32)
    full = -(-heads // 8) * 8
    if full != heads:
        queries = jnp.pad(queries, ((0, 0), (0, full - heads), (0, 0)))
    parts = 2
    smem = pl.BlockSpec(memory_space=pltpu.SMEM)
    away = pl.BlockSpec(memory_space=pl.ANY)
    tagged = pl.pallas_call(
        functools.partial(attend_kernel, parts),
        out_shape=jax.ShapeDtypeStruct((rows, full * width + LANES), BF16),
        in_specs=[smem] + [away] * 8,
        out_specs=pl.BlockSpec(memory_space=VMEM),
        scratch_shapes=[
            VMEM((rows, positions, width), BF16),
            VMEM((rows, positions, width), BF16),
            VMEM(queries.shape, BF16),
            VMEM(new_key.shape, BF16),
            VMEM(new_value.shape, BF16),
            pltpu.SMEM(lengths.shape, jnp.int32),
            pltpu.SMEM(row_adapter.shape, jnp.int32),
            pltpu.SMEM(adapter_list.shape, jnp.int32),
            VMEM((rows * full, width), F32),
            pltpu.SemaphoreType.DMA((6,)),
            pltpu.SemaphoreType.DMA((parts,)),
            pltpu.SemaphoreType.DMA((parts,)),
        ],
        compiler_params=pltpu.CompilerParams(vmem_limit_bytes=8 << 20),
        cost_estimate=pl.CostEstimate(
            flops=4 * rows * heads * positions * width,
            bytes_accessed=4 * rows * positions * width,
            transcendentals=rows * heads * positions,
        ),
        name="attention",
    )(
        group_at,
        *in_hbm(
            key_cache,
            value_cache,
            queries,
            new_key,
            new_value,
            lengths,
            row_adapter,
            adapter_list,
        ),
    )
    if full != heads:
        tagged = jnp.concatenate([tagged[:, : heads * width], tagged[:, full * width :]], axis=1)
    return tagged


def base_kernel(ahead, deep, tensor_at, tagged, out_weight, *refs):
    before, (out, held, sums, sems) = refs[:-4], refs[-4:]
    _, deep_rows, block = held.shape
    rows, width = tagged.shape[0], out_weight.shape[0]
    count = width // deep_rows
    column = pl.ds(pl.multiple_of((tensor_at[0] ^ ahead) * block, block), block)

    def copy(at):
        return pltpu.make_async_copy(
            out_weight.at[pl.ds(at * deep_rows, deep_rows), column],
            held.at[at % deep],
            sems.at[at % deep],
        )

    for at in range(min(deep, count)):
        copy(at).start()
    if before:
        out[: before[0].shape[0]] = before[0][...]
    first = out.shape[0] - rows
    piece = min(block, 512)
    for at in range(count):
        copy(at).wait()
        inputs = slice(at * deep_rows, (at + 1) * deep_rows)
        for start in range(0, block, piece):
            columns = slice(start, start + piece)
            term = jnp.dot(
                tagged[:, inputs], held[at % deep, :, columns], preferred_element_type=F32
            )
            if at:
                term = term + sums[:, columns]
            if at < count - 1:
                sums[:, columns] = term
            else:
                out[first:, columns] = term.astype(out.dtype)
        if at + deep < count:
            copy(at + deep).start()


def base_block(tensor_at, tagged, out_weight, block, ahead, dtype, *before):
    rows = tagged.shape[0]
    width = out_weight.shape[0]
    deep, deep_rows = 4, min(width, 256)
    whole = pl.BlockSpec(memory_space=VMEM)
    out_rows = rows + sum(each.shape[0] for each in before)
    return pl.pallas_call(
        functools.partial(base_kernel, ahead, deep),
        out_shape=jax.ShapeDtypeStruct((out_rows, block), dtype),
        in_specs=[pl.BlockSpec(memory_space=pltpu.SMEM), whole, pl.BlockSpec(memory_space=pl.ANY)]
        + [whole] * len(before),
        out_specs=whole,
        scratch_shapes=[
            VMEM((deep, deep_rows, block), BF16),
            VMEM((rows, block), F32),
            pltpu.SemaphoreType.DMA((deep,)),
        ],
        compiler_params=pltpu.CompilerParams(vmem_limit_bytes=12 << 20),
        cost_estimate=pl.CostEstimate(
            flops=2 * rows * width * block,
            bytes_accessed=2 * width * block,
            transcendentals=0,
        ),
        name="base_terms",
    )(tensor_at, tagged, *in_hbm(out_weight), *before)


def slots_of(tags, first):
    return tags.astype(F32).astype(jnp.int32) - first


def shrink_kernel(first_at, rank, *refs):
    blocks, (factors, out) = refs[:-2], refs[-2:]
    pool, rank_width, width = factors.shape
    everyone = jnp.concatenate([block[...] for block in blocks], axis=0)
    slot = slots_of(everyone[:, width:], first_at[0])
    terms = lax.dot_general(
        everyone[:, :width],
        factors[...].reshape(pool * rank_width, width),
        (((1,), (1,)), ((), ())),
        preferred_element_type=F32,
    )
    lane = lane_of(slot.shape)
    per = LANES // rank_width
    kept = jnp.zeros(slot.shape, F32)
    for tile in range(pool // per):
        mine, limit = tile * per + lane // rank_width, jnp.zeros_like(lane)
        for n in range(tile * per, (tile + 1) * per):
            limit = jnp.where(mine == n, rank[n], limit)
        keep = (slot == mine) & (lane % rank_width < limit)
        kept = kept + jnp.where(keep, terms[:, tile * LANES : (tile + 1) * LANES], F32(0.0))
    both = kept + pltpu.roll(kept, rank_width, 1)
    half = both.shape[0] // 2
    out[...] = jnp.where(lane[:half] < rank_width, both[:half], both[half:]).astype(out.dtype)


def shrink_part(blocks, shrink_weight, adapter_rank, first_at):
    pool, width, rank_width = shrink_weight.shape
    rows = len(blocks) * blocks[0].shape[0]
    smem = pl.BlockSpec(memory_space=pltpu.SMEM)
    whole = pl.BlockSpec(memory_space=VMEM)
    return pl.pallas_call(
        shrink_kernel,
        out_shape=jax.ShapeDtypeStruct((rows // 2, LANES), BF16),
        in_specs=[smem, smem] + [whole] * (len(blocks) + 1),
        out_specs=whole,
        compiler_params=pltpu.CompilerParams(vmem_limit_bytes=8 << 20),
        cost_estimate=pl.CostEstimate(
            flops=2 * rows * width * pool * rank_width,
            bytes_accessed=2 * width * (rows + pool * rank_width),
            transcendentals=0,
        ),
        name="shrink",
    )(first_at, adapter_rank, *blocks, jnp.swapaxes(shrink_weight, 1, 2))


def expand_kernel(count, sums, rank_width, first_at, *refs):
    tags, parts, (factors, kept, given) = refs[:count], refs[count : count + sums], refs[-3:]
    slot = slots_of(jnp.concatenate([tag[...] for tag in tags], axis=0), first_at[0])
    total = parts[0][...].astype(F32)
    for part in parts[1:]:
        total = total + part[...].astype(F32)
    total = total.astype(BF16).astype(F32)
    other = pltpu.roll(total, rank_width, 1)
    low = lane_of(total.shape) < rank_width
    shrink = jnp.concatenate(
        [jnp.where(low, total, other), jnp.where(low, other, total)], axis=0
    )
    lane = lane_of(slot.shape)
    per = LANES // rank_width
    spread = jnp.concatenate(
        [
            jnp.where(slot == tile * per + lane // rank_width, shrink, F32(0.0)).astype(BF16)
            for tile in range(factors.shape[0] // LANES)
        ],
        axis=1,
    )
    half, block = kept.shape
    piece = min(block, 512)
    for at in range(0, block, piece):
        delta = jnp.dot(spread, factors[:, at : at + piece], preferred_element_type=F32)
        kept[:, at : at + piece] = delta[:half].astype(kept.dtype)
        given[:, at : at + piece] = delta[half:].astype(given.dtype)


def expand(blocks, parts, expand_weight, first_at):
    pool, rank_width, block = expand_weight.shape
    rows, tagged_width = blocks[0].shape
    count = len(blocks)
    half = rows * count // 2
    tag = pl.BlockSpec((rows, LANES), lambda i: (0, tagged_width // LANES - 1))
    full = pl.BlockSpec((pool * rank_width, block), lambda i: (0, 0))
    part = pl.BlockSpec(parts[0].shape, lambda i: (0, 0))
    out = pl.BlockSpec((half, block), lambda i: (0, 0))
    return pl.pallas_call(
        functools.partial(expand_kernel, count, len(parts), rank_width),
        grid=(1,),
        out_shape=[jax.ShapeDtypeStruct((half, block), BF16)] * 2,
        in_specs=[pl.BlockSpec(memory_space=pltpu.SMEM)]
        + [tag] * count
        + [part] * len(parts)
        + [full],
        out_specs=[out, out],
        compiler_params=pltpu.CompilerParams(vmem_limit_bytes=16 << 20),
        cost_estimate=pl.CostEstimate(
            flops=2 * rows * count * pool * rank_width * block,
            bytes_accessed=2 * pool * rank_width * block,
            transcendentals=0,
        ),
        name="expand",
    )(first_at, *blocks, *parts, expand_weight.reshape(pool * rank_width, block))


def local(
    tensor_size,
    batch_size,
    queries,
    key_cache,
    value_cache,
    new_key,
    new_value,
    lengths,
    out_weight,
    shrink_weight,
    expand_weight,
    adapter_rank,
    adapter_list,
    row_adapter,
):
    rows = queries.shape[0]
    pool = shrink_weight.shape[0]
    block = expand_weight.shape[2]
    chips = batch_size // 2
    first_at = (lax.axis_index("batch") * pool).reshape(1).astype(jnp.int32)
    tensor_at = lax.axis_index("tensor").reshape(1).astype(jnp.int32)

    def to_sibling(array):
        return permuted(array, "batch", batch_size, lambda i: i ^ 1)

    def to_chip(array, shift):
        return permuted(array, "batch", batch_size, lambda i: (i + 2 * shift) % batch_size)

    def across(array, bit):
        return permuted(array, "tensor", tensor_size, lambda i: i ^ bit)

    def wide(array):
        return array.astype(F32)

    def terms(ahead, dtype, *before):
        return base_block(tensor_at, tagged, out_weight, block, ahead, dtype, *before)

    tagged = attend(
        queries, key_cache, value_cache, new_key, new_value, lengths, adapter_list, row_adapter
    )
    beside = to_sibling(tagged)
    visiting = [to_chip(tagged, shift) for shift in range(1, chips)]
    odd = terms(1, BF16)
    visiting, odd = lax.optimization_barrier((visiting, odd))
    mine = [tagged] + visiting
    blocks = mine + [beside] + [to_sibling(each) for each in visiting]
    for ahead in range(3, tensor_size, 2):
        odd = terms(ahead, BF16, odd)
    blocks, odd = lax.optimization_barrier((blocks, odd))

    part = shrink_part(blocks, shrink_weight, adapter_rank, first_at)
    parts = [part, across(part, 1)]
    arrived = across(odd, 1)
    base = {ahead: terms(ahead, BF16 if ahead else F32) for ahead in range(2, tensor_size, 2)}
    bit = 2
    while bit < tensor_size:
        part = (wide(parts[0]) + wide(parts[1])).astype(BF16)
        parts = [part, across(part, bit)]
        bit *= 2
    base[0] = terms(0, F32)
    kept, given = expand(blocks, parts, expand_weight, first_at)
    given = to_sibling(given)

    bit, sent = 1, range(1, tensor_size, 2)
    while True:
        for place, ahead in enumerate(sent):
            base[ahead ^ bit] = wide(base[ahead ^ bit]) + wide(
                arrived[place * rows : (place + 1) * rows]
            )
        bit *= 2
        if bit >= tensor_size:
            break
        sent = [ahead for ahead in sorted(base) if ahead & bit]
        message = [base.pop(ahead).astype(BF16) for ahead in sent]
        arrived = across(jnp.concatenate(message, axis=0), bit)

    result = base[0] + wide(kept[:rows]) + wide(given[:rows])
    for shift in range(1, chips):
        at = slice(shift * rows, (shift + 1) * rows)
        home = (wide(kept[at]) + wide(given[at])).astype(BF16)
        result = result + wide(to_chip(home, -shift))
    return result.astype(BF16)


def solution(mesh):
    placed = (
        P(("groups", "batch"), "tensor", None),
        P(("groups", "batch"), None, None, None),
        P(("groups", "batch"), None, None, None),
        P(("groups", "batch"), None, None),
        P(("groups", "batch"), None, None),
        P(("groups", "batch")),
        P("tensor", None),
        P("batch", "tensor", None),
        P("batch", None, "tensor"),
        P("batch"),
        P(("groups", "batch")),
        P(("groups", "batch")),
    )

    def placed_local(*arrays):
        return local(mesh.shape["tensor"], mesh.shape["batch"], *arrays)

    return jax.shard_map(
        placed_local,
        mesh=mesh,
        in_specs=placed,
        out_specs=P(("groups", "batch"), "tensor"),
        check_vma=False,
    )
```

```python
import functools

import jax
import jax.numpy as jnp
from jax import lax
from jax.experimental import pallas as pl
from jax.experimental.pallas import tpu as pltpu
from jax.sharding import PartitionSpec as P

HQ = 32
KVH = 4
LANES = 128
VMEM = pltpu.VMEM
GRANT = 56 << 20
F32, BF16 = jnp.float32, jnp.bfloat16


def permuted(array, axis, size, partner):
    return lax.ppermute(array, axis, [(i, partner(i)) for i in range(size)])


def in_hbm(*arrays):
    return [pltpu.with_memory_space_constraint(array, pltpu.HBM) for array in arrays]


def lane_of(shape):
    return lax.broadcasted_iota(jnp.int32, shape, len(shape) - 1)


def attend_kernel(parts, group_at, early_at, *refs):
    given, (out_weight, tagged, early, *scratch) = refs[:8], refs[8:]
    held, (spread_out, small_sems, key_sems, value_sems, early_sem) = scratch[:8], scratch[8:]
    key_cache, value_cache = given[:2]
    keys, values, queries, new_key, new_value, lengths, row_adapter, adapter_list = held
    rows, heads, width = queries.shape
    positions = key_cache.shape[2]
    group = group_at[0]
    some = rows // parts

    def cache_copies(part):
        at = pl.ds(part * some, some)
        return (
            pltpu.make_async_copy(key_cache.at[at, group], keys.at[at], key_sems.at[part]),
            pltpu.make_async_copy(value_cache.at[at, group], values.at[at], value_sems.at[part]),
        )

    small = [
        pltpu.make_async_copy(given[i], held[i], small_sems.at[i - 2]) for i in range(2, 8)
    ]
    for copy in small:
        copy.start()
    for part in range(parts):
        for copy in cache_copies(part):
            copy.start()
    block = early.shape[1]
    start = pl.multiple_of(early_at[0] * block, block)
    early_copy = pltpu.make_async_copy(out_weight.at[:, pl.ds(start, block)], early, early_sem)
    early_copy.start()
    for copy in small:
        copy.wait()
    at_row = lax.broadcasted_iota(jnp.int32, (rows, LANES), 0)
    tag = jnp.zeros((rows, LANES), jnp.int32)
    for row in range(rows):
        tag = jnp.where(at_row == row, adapter_list[row_adapter[row]], tag)
    tag = tag.astype(F32).astype(BF16)

    group_row = lax.broadcasted_iota(jnp.int32, new_key.shape, 1) == group
    fresh_key = jnp.sum(
        jnp.where(group_row, new_key[...].astype(F32), F32(0.0)), axis=1, keepdims=True
    )
    fresh_value = jnp.sum(
        jnp.where(group_row, new_value[...].astype(F32), F32(0.0)), axis=1, keepdims=True
    )
    score_scale = width ** (-0.5)
    fresh = jnp.sum(queries[...].astype(F32) * fresh_key, axis=-1, keepdims=True) * score_scale
    for part in range(parts):
        at = slice(part * some, (part + 1) * some)
        key_copy, value_copy = cache_copies(part)
        key_copy.wait()
        scores = (
            lax.dot_general(
                queries[at], keys[at], (((2,), (2,)), ((0,), (0,))), preferred_element_type=F32
            )
            * score_scale
        )
        length = jnp.stack(
            [
                jnp.full((heads, positions), lengths[row], jnp.int32)
                for row in range(part * some, (part + 1) * some)
            ]
        )
        valid = lane_of(scores.shape) < length
        masked = jnp.where(valid, scores, F32(-1e30))
        highest = jnp.maximum(jnp.max(masked, axis=-1, keepdims=True), fresh[at])
        cached_exp = jnp.where(valid, jnp.exp(masked - highest), F32(0.0))
        fresh_exp = jnp.exp(fresh[at] - highest)
        totals = jnp.sum(cached_exp, axis=-1, keepdims=True) + fresh_exp
        cached_w = (cached_exp / totals).astype(BF16)
        fresh_w = (fresh_exp / totals).astype(BF16).astype(F32)
        value_copy.wait()
        attended = lax.dot_general(
            cached_w, values[at], (((2,), (1,)), ((0,), (0,))), preferred_element_type=F32
        )
        attended = attended + fresh_w * fresh_value[at]
        spread_out[pl.ds(part * some * heads, some * heads)] = attended.reshape(
            some * heads, width
        )
    tagged[:, heads * width :] = tag
    for head in range(heads):
        tagged[:, head * width : (head + 1) * width] = spread_out[
            pl.ds(head, rows, stride=heads)
        ].astype(BF16)
    early_copy.wait()


def attend(
    early_at,
    block,
    out_weight,
    queries,
    key_cache,
    value_cache,
    new_key,
    new_value,
    lengths,
    adapter_list,
    row_adapter,
):
    rows, heads, width = queries.shape
    positions = key_cache.shape[2]
    per_group = HQ // KVH
    group_at = (lax.axis_index("tensor") * heads // per_group).reshape(1).astype(jnp.int32)
    full = -(-heads // 8) * 8
    if full != heads:
        queries = jnp.pad(queries, ((0, 0), (0, full - heads), (0, 0)))
    parts = 2
    smem = pl.BlockSpec(memory_space=pltpu.SMEM)
    away = pl.BlockSpec(memory_space=pl.ANY)
    tagged, early = pl.pallas_call(
        functools.partial(attend_kernel, parts),
        out_shape=[
            jax.ShapeDtypeStruct((rows, full * width + LANES), BF16),
            VMEM((out_weight.shape[0], block), BF16),
        ],
        in_specs=[smem, smem] + [away] * 9,
        out_specs=[pl.BlockSpec(memory_space=VMEM)] * 2,
        scratch_shapes=[
            VMEM((rows, positions, width), BF16),
            VMEM((rows, positions, width), BF16),
            VMEM(queries.shape, BF16),
            VMEM(new_key.shape, BF16),
            VMEM(new_value.shape, BF16),
            pltpu.SMEM(lengths.shape, jnp.int32),
            pltpu.SMEM(row_adapter.shape, jnp.int32),
            pltpu.SMEM(adapter_list.shape, jnp.int32),
            VMEM((rows * full, width), F32),
            pltpu.SemaphoreType.DMA((6,)),
            pltpu.SemaphoreType.DMA((parts,)),
            pltpu.SemaphoreType.DMA((parts,)),
            pltpu.SemaphoreType.DMA,
        ],
        compiler_params=pltpu.CompilerParams(vmem_limit_bytes=8 << 20),
        cost_estimate=pl.CostEstimate(
            flops=4 * rows * heads * positions * width,
            bytes_accessed=4 * rows * positions * width,
            transcendentals=rows * heads * positions,
        ),
        name="attention",
    )(
        group_at,
        early_at,
        *in_hbm(
            key_cache,
            value_cache,
            queries,
            new_key,
            new_value,
            lengths,
            row_adapter,
            adapter_list,
            out_weight,
        ),
    )
    if full != heads:
        tagged = jnp.concatenate([tagged[:, : heads * width], tagged[:, full * width :]], axis=1)
    return tagged, early


def put_stacked(out, start, term, first=0):
    rows = term.shape[0]
    for column in range(0, term.shape[1], LANES):
        at = first + (start + column) // LANES * rows
        out[at : at + rows] = term[:, column : column + LANES].astype(out.dtype)


def base_kernel(ahead, deep, tensor_at, tagged, out_weight, *refs):
    *near, out, held, sums, sems = refs
    _, deep_rows, block = held.shape
    width = out_weight.shape[0]
    count = width // deep_rows
    column = pl.ds(pl.multiple_of((tensor_at[0] ^ ahead) * block, block), block)

    def copy(at):
        return pltpu.make_async_copy(
            out_weight.at[pl.ds(at * deep_rows, deep_rows), column],
            held.at[at % deep],
            sems.at[at % deep],
        )

    for at in range(min(deep, count)):
        copy(at).start()
    piece = min(block, 512)
    if near:
        early, early_out = near
        for start in range(0, block, piece):
            columns = slice(start, start + piece)
            term = jnp.dot(tagged[:, :width], early[:, columns], preferred_element_type=F32)
            put_stacked(early_out, start, term)
    for at in range(count):
        copy(at).wait()
        inputs = slice(at * deep_rows, (at + 1) * deep_rows)
        for start in range(0, block, piece):
            columns = slice(start, start + piece)
            term = jnp.dot(
                tagged[:, inputs], held[at % deep, :, columns], preferred_element_type=F32
            )
            if at:
                term = term + sums[:, columns]
            if at < count - 1:
                sums[:, columns] = term
            else:
                put_stacked(out, start, term)
        if at + deep < count:
            copy(at + deep).start()


def base_block(tensor_at, tagged, out_weight, block, ahead, *early):
    rows = tagged.shape[0]
    width = out_weight.shape[0]
    deep, deep_rows = 4, min(width, 256)
    whole = pl.BlockSpec(memory_space=VMEM)
    count = 1 + len(early)
    return pl.pallas_call(
        functools.partial(base_kernel, ahead, deep),
        out_shape=[jax.ShapeDtypeStruct((block // LANES * rows, LANES), BF16)] * count,
        in_specs=[pl.BlockSpec(memory_space=pltpu.SMEM), whole, pl.BlockSpec(memory_space=pl.ANY)]
        + [whole] * len(early),
        out_specs=[whole] * count,
        scratch_shapes=[
            VMEM((deep, deep_rows, block), BF16),
            VMEM((rows, block), F32),
            pltpu.SemaphoreType.DMA((deep,)),
        ],
        compiler_params=pltpu.CompilerParams(vmem_limit_bytes=12 << 20),
        cost_estimate=pl.CostEstimate(
            flops=2 * rows * width * block * count,
            bytes_accessed=2 * width * block * count,
            transcendentals=0,
        ),
        name="base_terms",
    )(tensor_at, tagged, *in_hbm(out_weight), *early)


def slots_of(tags, first):
    return tags.astype(F32).astype(jnp.int32) - first


def shrink_kernel(first_at, rank, *refs):
    blocks, (factors, terms_ahead, out) = refs[:-3], refs[-3:]
    above = terms_ahead.shape[0]
    out[:above] = terms_ahead[...]
    pool, rank_width, width = factors.shape
    everyone = jnp.concatenate([block[...] for block in blocks], axis=0)
    slot = slots_of(everyone[:, width:], first_at[0])
    terms = lax.dot_general(
        everyone[:, :width],
        factors[...].reshape(pool * rank_width, width),
        (((1,), (1,)), ((), ())),
        preferred_element_type=F32,
    )
    lane = lane_of(slot.shape)
    per = LANES // rank_width
    kept = jnp.zeros(slot.shape, F32)
    for tile in range(pool // per):
        mine, limit = tile * per + lane // rank_width, jnp.zeros_like(lane)
        for n in range(tile * per, (tile + 1) * per):
            limit = jnp.where(mine == n, rank[n], limit)
        keep = (slot == mine) & (lane % rank_width < limit)
        kept = kept + jnp.where(keep, terms[:, tile * LANES : (tile + 1) * LANES], F32(0.0))
    both = kept + pltpu.roll(kept, rank_width, 1)
    half = both.shape[0] // 2
    packed = jnp.where(lane[:half] < rank_width, both[:half], both[half:])
    out[above:] = packed.astype(out.dtype)


def shrink_part(blocks, shrink_weight, adapter_rank, first_at, terms_ahead):
    pool, width, rank_width = shrink_weight.shape
    rows = len(blocks) * blocks[0].shape[0]
    smem = pl.BlockSpec(memory_space=pltpu.SMEM)
    whole = pl.BlockSpec(memory_space=VMEM)
    return pl.pallas_call(
        shrink_kernel,
        out_shape=jax.ShapeDtypeStruct((terms_ahead.shape[0] + rows // 2, LANES), BF16),
        in_specs=[smem, smem] + [whole] * (len(blocks) + 2),
        out_specs=whole,
        compiler_params=pltpu.CompilerParams(vmem_limit_bytes=8 << 20),
        cost_estimate=pl.CostEstimate(
            flops=2 * rows * width * pool * rank_width,
            bytes_accessed=2 * width * (rows + pool * rank_width),
            transcendentals=0,
        ),
        name="shrink",
    )(first_at, adapter_rank, *blocks, jnp.swapaxes(shrink_weight, 1, 2), terms_ahead)


def expand_kernel(count, sums, rank_width, first_at, *refs):
    tags, parts, (factors, kept, given) = refs[:count], refs[count : count + sums], refs[-3:]
    slot = slots_of(jnp.concatenate([tag[...] for tag in tags], axis=0), first_at[0])
    total = parts[0][...].astype(F32)
    for part in parts[1:]:
        total = total + part[...].astype(F32)
    total = total.astype(BF16).astype(F32)
    other = pltpu.roll(total, rank_width, 1)
    low = lane_of(total.shape) < rank_width
    shrink = jnp.concatenate(
        [jnp.where(low, total, other), jnp.where(low, other, total)], axis=0
    )
    lane = lane_of(slot.shape)
    per = LANES // rank_width
    spread = jnp.concatenate(
        [
            jnp.where(slot == tile * per + lane // rank_width, shrink, F32(0.0)).astype(BF16)
            for tile in range(factors.shape[0] // LANES)
        ],
        axis=1,
    )
    block = factors.shape[1]
    rows = tags[0].shape[0]
    piece = min(block, 512)
    stack = block // LANES * rows
    for at in range(0, block, piece):
        delta = jnp.dot(spread, factors[:, at : at + piece], preferred_element_type=F32)
        for which in range(count):
            out = kept if which < count // 2 else given
            put_stacked(
                out, at, delta[which * rows : (which + 1) * rows], which % (count // 2) * stack
            )


def expand(blocks, parts, expand_weight, first_at):
    pool, rank_width, block = expand_weight.shape
    rows, tagged_width = blocks[0].shape
    count = len(blocks)
    half = rows * count // 2 * block // LANES
    tag = pl.BlockSpec((rows, LANES), lambda i: (0, tagged_width // LANES - 1))
    full = pl.BlockSpec((pool * rank_width, block), lambda i: (0, 0))
    part = pl.BlockSpec(parts[0].shape, lambda i: (0, 0))
    out = pl.BlockSpec((half, LANES), lambda i: (0, 0))
    return pl.pallas_call(
        functools.partial(expand_kernel, count, len(parts), rank_width),
        grid=(1,),
        out_shape=[jax.ShapeDtypeStruct((half, LANES), BF16)] * 2,
        in_specs=[pl.BlockSpec(memory_space=pltpu.SMEM)]
        + [tag] * count
        + [part] * len(parts)
        + [full],
        out_specs=[out, out],
        compiler_params=pltpu.CompilerParams(vmem_limit_bytes=16 << 20),
        cost_estimate=pl.CostEstimate(
            flops=2 * rows * count * pool * rank_width * block,
            bytes_accessed=2 * pool * rank_width * block,
            transcendentals=0,
        ),
        name="expand",
    )(first_at, *blocks, *parts, expand_weight.reshape(pool * rank_width, block))


def total_kernel(kept, given, *refs):
    terms, out = refs[:-1], refs[-1]
    rows = out.shape[0]
    for column in range(0, out.shape[1], LANES):
        at = slice(column // LANES * rows, (column // LANES + 1) * rows)
        total = kept[at].astype(F32) + given[at].astype(F32)
        for term in terms:
            total = total + term[at].astype(F32)
        out[:, column : column + LANES] = total.astype(out.dtype)


def total(rows, block, kept, given, terms):
    whole = pl.BlockSpec(memory_space=VMEM)
    return pl.pallas_call(
        total_kernel,
        out_shape=jax.ShapeDtypeStruct((rows, block), BF16),
        in_specs=[whole] * (2 + len(terms)),
        out_specs=whole,
        compiler_params=pltpu.CompilerParams(vmem_limit_bytes=8 << 20),
        cost_estimate=pl.CostEstimate(
            flops=rows * block * (2 + len(terms)),
            bytes_accessed=2 * rows * block * (3 + len(terms)),
            transcendentals=0,
        ),
        name="total",
    )(kept, given, *terms)


def local(
    tensor_size,
    batch_size,
    queries,
    key_cache,
    value_cache,
    new_key,
    new_value,
    lengths,
    out_weight,
    shrink_weight,
    expand_weight,
    adapter_rank,
    adapter_list,
    row_adapter,
):
    rows = queries.shape[0]
    pool = shrink_weight.shape[0]
    block = expand_weight.shape[2]
    chips = batch_size // 2
    first_at = (lax.axis_index("batch") * pool).reshape(1).astype(jnp.int32)
    tensor_at = lax.axis_index("tensor").reshape(1).astype(jnp.int32)

    def to_sibling(array):
        return permuted(array, "batch", batch_size, lambda i: i ^ 1)

    def to_chip(array, shift):
        return permuted(array, "batch", batch_size, lambda i: (i + 2 * shift) % batch_size)

    def across(array, bit):
        return permuted(array, "tensor", tensor_size, lambda i: i ^ bit)

    def wide(array):
        return array.astype(F32)

    stack = block // LANES * rows
    tagged, early = attend(
        tensor_at ^ 3,
        block,
        out_weight,
        queries,
        key_cache,
        value_cache,
        new_key,
        new_value,
        lengths,
        adapter_list,
        row_adapter,
    )
    visiting = [to_chip(tagged, shift) for shift in range(1, chips)]
    beside = to_sibling(tagged)
    third, next_door = base_block(tensor_at, tagged, out_weight, block, 1, early)
    visiting, third, next_door = lax.optimization_barrier((visiting, third, next_door))
    blocks = [tagged] + visiting + [beside] + [to_sibling(each) for each in visiting]

    message = shrink_part(blocks, shrink_weight, adapter_rank, first_at, third)
    arrived = across(message, 1)
    (second,) = base_block(tensor_at, tagged, out_weight, block, 2)
    arrived, second = lax.optimization_barrier((arrived, second))
    part = (wide(message[stack:]) + wide(arrived[stack:])).astype(BF16)
    parts, bit = [part], 2
    while bit < tensor_size:
        if len(parts) > 1:
            part = (wide(parts[0]) + wide(parts[1])).astype(BF16)
        parts = [part, across(part, bit)]
        bit *= 2
    terms = [across((wide(second) + wide(arrived[:stack])).astype(BF16), 2)]
    for ahead in range(4, tensor_size, 2):
        (near,) = base_block(tensor_at, tagged, out_weight, block, ahead)
        (far,) = base_block(tensor_at, tagged, out_weight, block, ahead + 1)
        terms.append(across((wide(near) + wide(across(far, 1))).astype(BF16), ahead))

    kept, given = expand(blocks, parts, expand_weight, first_at)
    given = to_sibling(given)
    homes = [
        (wide(kept[at : at + stack]) + wide(given[at : at + stack])).astype(BF16)
        for at in range(stack, chips * stack, stack)
    ]
    homes, next_door, late_tagged = lax.optimization_barrier((homes, next_door, tagged))
    terms += [to_chip(home, -shift) for shift, home in enumerate(homes, 1)]
    terms.append(across(next_door, 1))
    terms += base_block(tensor_at, late_tagged, out_weight, block, 0)
    return total(rows, block, kept, given, terms)


def solution(mesh):
    placed = (
        P(("groups", "batch"), "tensor", None),
        P(("groups", "batch"), None, None, None),
        P(("groups", "batch"), None, None, None),
        P(("groups", "batch"), None, None),
        P(("groups", "batch"), None, None),
        P(("groups", "batch")),
        P("tensor", None),
        P("batch", "tensor", None),
        P("batch", None, "tensor"),
        P("batch"),
        P(("groups", "batch")),
        P(("groups", "batch")),
    )

    def placed_local(*arrays):
        return local(mesh.shape["tensor"], mesh.shape["batch"], *arrays)

    return jax.shard_map(
        placed_local,
        mesh=mesh,
        in_specs=placed,
        out_specs=P(("groups", "batch"), "tensor"),
        check_vma=False,
    )
```

```python
import functools

import jax
import jax.numpy as jnp
from jax import lax
from jax.experimental import pallas as pl
from jax.experimental.pallas import tpu as pltpu
from jax.sharding import PartitionSpec as P

HQ = 32
KVH = 4
LANES = 128
VMEM = pltpu.VMEM
GRANT = 56 << 20
F32, BF16 = jnp.float32, jnp.bfloat16


def permuted(array, axis, size, partner):
    return lax.ppermute(array, axis, [(i, partner(i)) for i in range(size)])


def in_hbm(*arrays):
    return [pltpu.with_memory_space_constraint(array, pltpu.HBM) for array in arrays]


def lane_of(shape):
    return lax.broadcasted_iota(jnp.int32, shape, len(shape) - 1)


def attend_kernel(parts, group_at, early_at, *refs):
    given, (out_weight, tagged, early, *scratch) = refs[:8], refs[8:]
    held, (spread_out, small_sems, key_sems, value_sems, early_sem) = scratch[:8], scratch[8:]
    key_cache, value_cache = given[:2]
    keys, values, queries, new_key, new_value, lengths, row_adapter, adapter_list = held
    rows, heads, width = queries.shape
    positions = key_cache.shape[2]
    group = group_at[0]
    some = rows // parts

    def cache_copies(part):
        at = pl.ds(part * some, some)
        return (
            pltpu.make_async_copy(key_cache.at[at, group], keys.at[at], key_sems.at[part]),
            pltpu.make_async_copy(value_cache.at[at, group], values.at[at], value_sems.at[part]),
        )

    small = [
        pltpu.make_async_copy(given[i], held[i], small_sems.at[i - 2]) for i in range(2, 8)
    ]
    for copy in small:
        copy.start()
    for part in range(parts):
        for copy in cache_copies(part):
            copy.start()
    block = early.shape[1]
    start = pl.multiple_of(early_at[0] * block, block)
    early_copy = pltpu.make_async_copy(out_weight.at[:, pl.ds(start, block)], early, early_sem)
    early_copy.start()
    for copy in small:
        copy.wait()
    at_row = lax.broadcasted_iota(jnp.int32, (rows, LANES), 0)
    tag = jnp.zeros((rows, LANES), jnp.int32)
    for row in range(rows):
        tag = jnp.where(at_row == row, adapter_list[row_adapter[row]], tag)
    tag = tag.astype(F32).astype(BF16)

    group_row = lax.broadcasted_iota(jnp.int32, new_key.shape, 1) == group
    fresh_key = jnp.sum(
        jnp.where(group_row, new_key[...].astype(F32), F32(0.0)), axis=1, keepdims=True
    )
    fresh_value = jnp.sum(
        jnp.where(group_row, new_value[...].astype(F32), F32(0.0)), axis=1, keepdims=True
    )
    score_scale = width ** (-0.5)
    fresh = jnp.sum(queries[...].astype(F32) * fresh_key, axis=-1, keepdims=True) * score_scale
    for part in range(parts):
        at = slice(part * some, (part + 1) * some)
        key_copy, value_copy = cache_copies(part)
        key_copy.wait()
        scores = (
            lax.dot_general(
                queries[at], keys[at], (((2,), (2,)), ((0,), (0,))), preferred_element_type=F32
            )
            * score_scale
        )
        length = jnp.stack(
            [
                jnp.full((heads, positions), lengths[row], jnp.int32)
                for row in range(part * some, (part + 1) * some)
            ]
        )
        valid = lane_of(scores.shape) < length
        masked = jnp.where(valid, scores, F32(-1e30))
        highest = jnp.maximum(jnp.max(masked, axis=-1, keepdims=True), fresh[at])
        cached_exp = jnp.where(valid, jnp.exp(masked - highest), F32(0.0))
        fresh_exp = jnp.exp(fresh[at] - highest)
        totals = jnp.sum(cached_exp, axis=-1, keepdims=True) + fresh_exp
        cached_w = (cached_exp / totals).astype(BF16)
        fresh_w = (fresh_exp / totals).astype(BF16).astype(F32)
        value_copy.wait()
        attended = lax.dot_general(
            cached_w, values[at], (((2,), (1,)), ((0,), (0,))), preferred_element_type=F32
        )
        attended = attended + fresh_w * fresh_value[at]
        spread_out[pl.ds(part * some * heads, some * heads)] = attended.reshape(
            some * heads, width
        )
    tagged[:, heads * width :] = tag
    for head in range(heads):
        tagged[:, head * width : (head + 1) * width] = spread_out[
            pl.ds(head, rows, stride=heads)
        ].astype(BF16)
    early_copy.wait()


def attend(
    early_at,
    block,
    out_weight,
    queries,
    key_cache,
    value_cache,
    new_key,
    new_value,
    lengths,
    adapter_list,
    row_adapter,
):
    rows, heads, width = queries.shape
    positions = key_cache.shape[2]
    per_group = HQ // KVH
    group_at = (lax.axis_index("tensor") * heads // per_group).reshape(1).astype(jnp.int32)
    full = -(-heads // 8) * 8
    if full != heads:
        queries = jnp.pad(queries, ((0, 0), (0, full - heads), (0, 0)))
    parts = 2
    smem = pl.BlockSpec(memory_space=pltpu.SMEM)
    away = pl.BlockSpec(memory_space=pl.ANY)
    tagged, early = pl.pallas_call(
        functools.partial(attend_kernel, parts),
        out_shape=[
            jax.ShapeDtypeStruct((rows, full * width + LANES), BF16),
            VMEM((out_weight.shape[0], block), BF16),
        ],
        in_specs=[smem, smem] + [away] * 9,
        out_specs=[pl.BlockSpec(memory_space=VMEM)] * 2,
        scratch_shapes=[
            VMEM((rows, positions, width), BF16),
            VMEM((rows, positions, width), BF16),
            VMEM(queries.shape, BF16),
            VMEM(new_key.shape, BF16),
            VMEM(new_value.shape, BF16),
            pltpu.SMEM(lengths.shape, jnp.int32),
            pltpu.SMEM(row_adapter.shape, jnp.int32),
            pltpu.SMEM(adapter_list.shape, jnp.int32),
            VMEM((rows * full, width), F32),
            pltpu.SemaphoreType.DMA((6,)),
            pltpu.SemaphoreType.DMA((parts,)),
            pltpu.SemaphoreType.DMA((parts,)),
            pltpu.SemaphoreType.DMA,
        ],
        compiler_params=pltpu.CompilerParams(vmem_limit_bytes=8 << 20),
        cost_estimate=pl.CostEstimate(
            flops=4 * rows * heads * positions * width,
            bytes_accessed=4 * rows * positions * width,
            transcendentals=rows * heads * positions,
        ),
        name="attention",
    )(
        group_at,
        early_at,
        *in_hbm(
            key_cache,
            value_cache,
            queries,
            new_key,
            new_value,
            lengths,
            row_adapter,
            adapter_list,
            out_weight,
        ),
    )
    if full != heads:
        tagged = jnp.concatenate([tagged[:, : heads * width], tagged[:, full * width :]], axis=1)
    return tagged, early


def put_stacked(out, start, term, first=0, others=()):
    rows = term.shape[0]
    for column in range(0, term.shape[1], LANES):
        at = first + (start + column) // LANES * rows
        part = term[:, column : column + LANES]
        for other in others:
            part = part + other[at : at + rows].astype(F32)
        out[at : at + rows] = part.astype(out.dtype)


def base_kernel(ahead, deep, arriving, tensor_at, tagged, out_weight, *refs):
    arrived, (*near, out, held, sums, sems) = refs[:arriving], refs[arriving:]
    _, deep_rows, block = held.shape
    width = out_weight.shape[0]
    count = width // deep_rows
    column = pl.ds(pl.multiple_of((tensor_at[0] ^ ahead) * block, block), block)

    def copy(at):
        return pltpu.make_async_copy(
            out_weight.at[pl.ds(at * deep_rows, deep_rows), column],
            held.at[at % deep],
            sems.at[at % deep],
        )

    for at in range(min(deep, count)):
        copy(at).start()
    piece = min(block, 512)
    if near:
        early, early_out = near
        for start in range(0, block, piece):
            columns = slice(start, start + piece)
            term = jnp.dot(tagged[:, :width], early[:, columns], preferred_element_type=F32)
            put_stacked(early_out, start, term)
    for at in range(count):
        copy(at).wait()
        inputs = slice(at * deep_rows, (at + 1) * deep_rows)
        for start in range(0, block, piece):
            columns = slice(start, start + piece)
            term = jnp.dot(
                tagged[:, inputs], held[at % deep, :, columns], preferred_element_type=F32
            )
            if at:
                term = term + sums[:, columns]
            if at < count - 1:
                sums[:, columns] = term
            else:
                put_stacked(out, start, term, 0, arrived)
        if at + deep < count:
            copy(at + deep).start()


def base_block(tensor_at, tagged, out_weight, block, ahead, early=(), arrived=()):
    rows = tagged.shape[0]
    width = out_weight.shape[0]
    deep, deep_rows = 4, min(width, 256)
    whole = pl.BlockSpec(memory_space=VMEM)
    count = 1 + len(early)
    return pl.pallas_call(
        functools.partial(base_kernel, ahead, deep, len(arrived)),
        out_shape=[jax.ShapeDtypeStruct((block // LANES * rows, LANES), BF16 if ahead else F32)]
        * count,
        in_specs=[pl.BlockSpec(memory_space=pltpu.SMEM), whole, pl.BlockSpec(memory_space=pl.ANY)]
        + [whole] * (len(arrived) + len(early)),
        out_specs=[whole] * count,
        scratch_shapes=[
            VMEM((deep, deep_rows, block), BF16),
            VMEM((rows, block), F32),
            pltpu.SemaphoreType.DMA((deep,)),
        ],
        compiler_params=pltpu.CompilerParams(vmem_limit_bytes=12 << 20),
        cost_estimate=pl.CostEstimate(
            flops=2 * rows * width * block * count,
            bytes_accessed=2 * width * block * (2 if arrived else count),
            transcendentals=0,
        ),
        name="base_terms",
    )(tensor_at, tagged, *in_hbm(out_weight), *arrived, *early)


def slots_of(tags, batch_at, pool, tile, per):
    lane = lane_of(tags.shape)
    ids = tags.astype(F32).astype(jnp.int32)
    mine = tile * per + lane // (LANES // per)
    held = tile * per // pool
    return ids - (batch_at[0] ^ held) * pool + held * pool, mine


def shrink_kernel(batch_at, *refs):
    blocks, factors, out = refs[:-3], refs[-3:-1], refs[-1]
    pool, rank_width, width = factors[0].shape
    everyone = jnp.concatenate([block[...] for block in blocks], axis=0)
    per = LANES // rank_width
    lane = lane_of((everyone.shape[0], LANES))
    kept = jnp.zeros(lane.shape, F32)
    for held, weights in enumerate(factors):
        terms = lax.dot_general(
            everyone[:, :width],
            weights[...].reshape(pool * rank_width, width),
            (((1,), (1,)), ((), ())),
            preferred_element_type=F32,
        )
        for tile in range(pool // per):
            slot, mine = slots_of(everyone[:, width:], batch_at, pool, held * pool // per + tile, per)
            kept = kept + jnp.where(
                slot == mine, terms[:, tile * LANES : (tile + 1) * LANES], F32(0.0)
            )
    both = kept + pltpu.roll(kept, rank_width, 1)
    half = both.shape[0] // 2
    packed = jnp.where(lane[:half] < rank_width, both[:half], both[half:])
    out[...] = packed.astype(out.dtype)


def shrink_part(blocks, factors, batch_at):
    pool, rank_width, width = factors[0].shape
    rows = len(blocks) * blocks[0].shape[0]
    smem = pl.BlockSpec(memory_space=pltpu.SMEM)
    whole = pl.BlockSpec(memory_space=VMEM)
    return pl.pallas_call(
        shrink_kernel,
        out_shape=jax.ShapeDtypeStruct((rows // 2, LANES), BF16),
        in_specs=[smem] + [whole] * (len(blocks) + 2),
        out_specs=whole,
        compiler_params=pltpu.CompilerParams(vmem_limit_bytes=8 << 20),
        cost_estimate=pl.CostEstimate(
            flops=4 * rows * width * pool * rank_width,
            bytes_accessed=2 * width * (rows + 2 * pool * rank_width),
            transcendentals=0,
        ),
        name="shrink",
    )(batch_at, *blocks, *factors)


def expand_kernel(count, sums, rank_width, batch_at, rank, sibling_rank, *refs):
    tags, parts = refs[:count], refs[count : count + sums]
    factors, outs = refs[count + sums : count + sums + 2], refs[count + sums + 2 :]
    tags = jnp.concatenate([tag[...] for tag in tags], axis=0)
    total = parts[0][...].astype(F32)
    for part in parts[1:]:
        total = total + part[...].astype(F32)
    total = total.astype(BF16).astype(F32)
    other = pltpu.roll(total, rank_width, 1)
    low = lane_of(total.shape) < rank_width
    shrink = jnp.concatenate(
        [jnp.where(low, total, other), jnp.where(low, other, total)], axis=0
    )
    per = LANES // rank_width
    inputs, block = factors[0].shape
    pool = inputs // rank_width
    tiles = []
    for tile in range(2 * pool // per):
        slot, mine = slots_of(tags, batch_at, pool, tile, per)
        lane, limit = lane_of(tags.shape) % rank_width, jnp.zeros_like(mine)
        for n in range(tile * per, (tile + 1) * per):
            limit = jnp.where(mine == n, (rank, sibling_rank)[n // pool][n % pool], limit)
        tiles.append(jnp.where((slot == mine) & (lane < limit), shrink, F32(0.0)).astype(BF16))
    half = len(tiles) // 2
    spreads = [jnp.concatenate(tiles[:half], axis=1), jnp.concatenate(tiles[half:], axis=1)]
    rows = tags.shape[0] // count
    piece = min(block, 512)
    for at in range(0, block, piece):
        delta = sum(
            jnp.dot(spread, each[:, at : at + piece], preferred_element_type=F32)
            for spread, each in zip(spreads, factors)
        )
        for which, out in enumerate(outs):
            put_stacked(out, at, delta[which * rows : (which + 1) * rows])


def expand(blocks, parts, factors, ranks, batch_at):
    pool, rank_width, block = factors[0].shape
    rows, tagged_width = blocks[0].shape
    count = len(blocks)
    stack = rows * block // LANES
    tag = pl.BlockSpec((rows, LANES), lambda i: (0, tagged_width // LANES - 1))
    full = pl.BlockSpec((pool * rank_width, block), lambda i: (0, 0))
    part = pl.BlockSpec(parts[0].shape, lambda i: (0, 0))
    return pl.pallas_call(
        functools.partial(expand_kernel, count, len(parts), rank_width),
        grid=(1,),
        out_shape=[jax.ShapeDtypeStruct((stack, LANES), BF16) for _ in blocks],
        in_specs=[pl.BlockSpec(memory_space=pltpu.SMEM)] * 3
        + [tag] * count
        + [part] * len(parts)
        + [full] * 2,
        out_specs=[pl.BlockSpec((stack, LANES), lambda i: (0, 0)) for _ in blocks],
        compiler_params=pltpu.CompilerParams(vmem_limit_bytes=16 << 20),
        cost_estimate=pl.CostEstimate(
            flops=4 * rows * count * pool * rank_width * block,
            bytes_accessed=2 * pool * rank_width * block,
            transcendentals=0,
        ),
        name="expand",
    )(batch_at, *ranks, *blocks, *parts, *[each.reshape(pool * rank_width, block) for each in factors])


def total_kernel(*refs):
    terms, out = refs[:-1], refs[-1]
    rows = out.shape[0]
    for column in range(0, out.shape[1], LANES):
        at = slice(column // LANES * rows, (column // LANES + 1) * rows)
        total = terms[0][at].astype(F32)
        for term in terms[1:]:
            total = total + term[at].astype(F32)
        out[:, column : column + LANES] = total.astype(out.dtype)


def total(rows, block, terms):
    whole = pl.BlockSpec(memory_space=VMEM)
    return pl.pallas_call(
        total_kernel,
        out_shape=jax.ShapeDtypeStruct((rows, block), BF16),
        in_specs=[whole] * len(terms),
        out_specs=whole,
        compiler_params=pltpu.CompilerParams(vmem_limit_bytes=8 << 20),
        cost_estimate=pl.CostEstimate(
            flops=rows * block * len(terms),
            bytes_accessed=2 * rows * block * (1 + len(terms)),
            transcendentals=0,
        ),
        name="total",
    )(*terms)


def partial_kernel(*refs):
    terms, out = refs[:-1], refs[-1]
    total = terms[0][...].astype(F32)
    for term in terms[1:]:
        total = total + term[...].astype(F32)
    out[...] = total


def partial_total(terms):
    whole = pl.BlockSpec(memory_space=VMEM)
    return pl.pallas_call(
        partial_kernel,
        out_shape=jax.ShapeDtypeStruct(terms[0].shape, F32),
        in_specs=[whole] * len(terms),
        out_specs=whole,
        compiler_params=pltpu.CompilerParams(vmem_limit_bytes=8 << 20),
        cost_estimate=pl.CostEstimate(
            flops=terms[0].size * len(terms),
            bytes_accessed=8 << 20,
            transcendentals=0,
        ),
        name="partial_total",
    )(*terms)


def local(
    tensor_size,
    batch_size,
    queries,
    key_cache,
    value_cache,
    new_key,
    new_value,
    lengths,
    out_weight,
    shrink_weight,
    expand_weight,
    adapter_rank,
    adapter_list,
    row_adapter,
):
    rows = queries.shape[0]
    block = expand_weight.shape[2]
    chips = batch_size // 2
    batch_at = lax.axis_index("batch").reshape(1).astype(jnp.int32)
    tensor_at = lax.axis_index("tensor").reshape(1).astype(jnp.int32)

    def to_sibling(array):
        return permuted(array, "batch", batch_size, lambda i: i ^ 1)

    def to_chip(array, shift):
        return permuted(array, "batch", batch_size, lambda i: (i + 2 * shift) % batch_size)

    def across(array, bit):
        return permuted(array, "tensor", tensor_size, lambda i: i ^ bit)

    def wide(array):
        return array.astype(F32)

    stack = block // LANES * rows
    tagged, early = attend(
        tensor_at ^ 3,
        block,
        out_weight,
        queries,
        key_cache,
        value_cache,
        new_key,
        new_value,
        lengths,
        adapter_list,
        row_adapter,
    )
    ranks = [adapter_rank, to_sibling(adapter_rank)]
    shrink_weight = jnp.swapaxes(shrink_weight, 1, 2)
    shrink_factors = [shrink_weight, to_sibling(shrink_weight)]
    expand_factors = [expand_weight, to_sibling(expand_weight)]
    visiting = [to_chip(tagged, shift) for shift in range(1, chips)]
    third, next_door = base_block(tensor_at, tagged, out_weight, block, 1, [early])
    visiting, third, next_door = lax.optimization_barrier((visiting, third, next_door))
    blocks = [tagged] + visiting
    third = across(third, 1)

    part = shrink_part(blocks, shrink_factors, batch_at)
    parts = [part, across(part, 1)]
    part, later_tagged = lax.optimization_barrier((part, tagged))
    (second,) = base_block(tensor_at, later_tagged, out_weight, block, 2)
    second = (wide(second) + wide(third)).astype(BF16)
    parts, second = lax.optimization_barrier((parts, second))
    bit = 2
    while bit < tensor_size:
        part = (wide(parts[0]) + wide(parts[1])).astype(BF16)
        parts = [part, across(part, bit)]
        bit *= 2
    arrived = [across(second, 2), across(next_door, 1)]
    for ahead in range(4, tensor_size, 2):
        (near,) = base_block(tensor_at, tagged, out_weight, block, ahead)
        (far,) = base_block(tensor_at, tagged, out_weight, block, ahead + 1)
        arrived.append(across((wide(near) + wide(across(far, 1))).astype(BF16), ahead))

    deltas = expand(blocks, parts, expand_factors, ranks, batch_at)
    deltas, late_tagged = lax.optimization_barrier((deltas, tagged))
    (own,) = base_block(tensor_at, late_tagged, out_weight, block, 0)
    terms = [partial_total([own, deltas[0], *arrived])]
    terms += [to_chip(home, -shift) for shift, home in enumerate(deltas[1:], 1)]
    return total(rows, block, terms)


def solution(mesh):
    placed = (
        P(("groups", "batch"), "tensor", None),
        P(("groups", "batch"), None, None, None),
        P(("groups", "batch"), None, None, None),
        P(("groups", "batch"), None, None),
        P(("groups", "batch"), None, None),
        P(("groups", "batch")),
        P("tensor", None),
        P("batch", "tensor", None),
        P("batch", None, "tensor"),
        P("batch"),
        P(("groups", "batch")),
        P(("groups", "batch")),
    )

    def placed_local(*arrays):
        return local(mesh.shape["tensor"], mesh.shape["batch"], *arrays)

    return jax.shard_map(
        placed_local,
        mesh=mesh,
        in_specs=placed,
        out_specs=P(("groups", "batch"), "tensor"),
        check_vma=False,
    )
```

```python
import functools

import jax
import jax.numpy as jnp
from jax import lax
from jax.experimental import pallas as pl
from jax.experimental.pallas import tpu as pltpu
from jax.sharding import PartitionSpec as P

HQ = 32
KVH = 4
LANES = 128
VMEM = pltpu.VMEM
GRANT = 56 << 20
F32, BF16 = jnp.float32, jnp.bfloat16


def permuted(array, axis, size, partner):
    return lax.ppermute(array, axis, [(i, partner(i)) for i in range(size)])


def in_hbm(*arrays):
    return [pltpu.with_memory_space_constraint(array, pltpu.HBM) for array in arrays]


def lane_of(shape):
    return lax.broadcasted_iota(jnp.int32, shape, len(shape) - 1)


def attend_kernel(parts, rank_width, group_at, early_at, *refs):
    given, (out_weight, tagged, early, limits, *scratch) = refs[:9], refs[9:]
    held, (spread_out, small_sems, key_sems, value_sems, early_sem) = scratch[:9], scratch[9:]
    key_cache, value_cache = given[:2]
    keys, values, queries, new_key, new_value, lengths, row_adapter, adapter_list, ranks = held
    rows, heads, width = queries.shape
    positions = key_cache.shape[2]
    group = group_at[0]
    some = rows // parts

    def cache_copies(part):
        at = pl.ds(part * some, some)
        return (
            pltpu.make_async_copy(key_cache.at[at, group], keys.at[at], key_sems.at[part]),
            pltpu.make_async_copy(value_cache.at[at, group], values.at[at], value_sems.at[part]),
        )

    small = [
        pltpu.make_async_copy(given[i], held[i], small_sems.at[i - 2]) for i in range(2, 9)
    ]
    for copy in small:
        copy.start()
    for part in range(parts):
        for copy in cache_copies(part):
            copy.start()
    block = early.shape[1]
    start = pl.multiple_of(early_at[0] * block, block)
    early_copy = pltpu.make_async_copy(out_weight.at[:, pl.ds(start, block)], early, early_sem)
    early_copy.start()
    for copy in small:
        copy.wait()
    at_row = lax.broadcasted_iota(jnp.int32, (rows, LANES), 0)
    tag = jnp.zeros((rows, LANES), jnp.int32)
    for row in range(rows):
        tag = jnp.where(at_row == row, adapter_list[row_adapter[row]], tag)
    tag = tag.astype(F32).astype(BF16)
    slot = lax.broadcasted_iota(jnp.int32, limits.shape, 0) * (LANES // rank_width)
    slot = slot + lane_of(limits.shape) // rank_width
    limit = jnp.zeros(limits.shape, jnp.int32)
    for held_at in range(ranks.shape[0]):
        limit = jnp.where(slot == held_at, ranks[held_at], limit)
    limits[...] = limit

    group_row = lax.broadcasted_iota(jnp.int32, new_key.shape, 1) == group
    fresh_key = jnp.sum(
        jnp.where(group_row, new_key[...].astype(F32), F32(0.0)), axis=1, keepdims=True
    )
    fresh_value = jnp.sum(
        jnp.where(group_row, new_value[...].astype(F32), F32(0.0)), axis=1, keepdims=True
    )
    score_scale = width ** (-0.5)
    fresh = jnp.sum(queries[...].astype(F32) * fresh_key, axis=-1, keepdims=True) * score_scale
    for part in range(parts):
        at = slice(part * some, (part + 1) * some)
        key_copy, value_copy = cache_copies(part)
        key_copy.wait()
        scores = (
            lax.dot_general(
                queries[at], keys[at], (((2,), (2,)), ((0,), (0,))), preferred_element_type=F32
            )
            * score_scale
        )
        length = jnp.stack(
            [
                jnp.full((heads, positions), lengths[row], jnp.int32)
                for row in range(part * some, (part + 1) * some)
            ]
        )
        valid = lane_of(scores.shape) < length
        masked = jnp.where(valid, scores, F32(-1e30))
        highest = jnp.maximum(jnp.max(masked, axis=-1, keepdims=True), fresh[at])
        cached_exp = jnp.where(valid, jnp.exp(masked - highest), F32(0.0))
        fresh_exp = jnp.exp(fresh[at] - highest)
        totals = jnp.sum(cached_exp, axis=-1, keepdims=True) + fresh_exp
        cached_w = (cached_exp / totals).astype(BF16)
        fresh_w = (fresh_exp / totals).astype(BF16).astype(F32)
        value_copy.wait()
        attended = lax.dot_general(
            cached_w, values[at], (((2,), (1,)), ((0,), (0,))), preferred_element_type=F32
        )
        attended = attended + fresh_w * fresh_value[at]
        spread_out[pl.ds(part * some * heads, some * heads)] = attended.reshape(
            some * heads, width
        )
    tagged[:, heads * width :] = tag
    for head in range(heads):
        tagged[:, head * width : (head + 1) * width] = spread_out[
            pl.ds(head, rows, stride=heads)
        ].astype(BF16)
    early_copy.wait()


def attend(
    early_at,
    block,
    out_weight,
    queries,
    key_cache,
    value_cache,
    new_key,
    new_value,
    lengths,
    adapter_list,
    row_adapter,
    adapter_rank,
    rank_width,
):
    rows, heads, width = queries.shape
    positions = key_cache.shape[2]
    per_group = HQ // KVH
    group_at = (lax.axis_index("tensor") * heads // per_group).reshape(1).astype(jnp.int32)
    full = -(-heads // 8) * 8
    if full != heads:
        queries = jnp.pad(queries, ((0, 0), (0, full - heads), (0, 0)))
    parts = 2
    smem = pl.BlockSpec(memory_space=pltpu.SMEM)
    away = pl.BlockSpec(memory_space=pl.ANY)
    tagged, early, limits = pl.pallas_call(
        functools.partial(attend_kernel, parts, rank_width),
        out_shape=[
            jax.ShapeDtypeStruct((rows, full * width + LANES), BF16),
            VMEM((out_weight.shape[0], block), BF16),
            jax.ShapeDtypeStruct((8, LANES), jnp.int32),
        ],
        in_specs=[smem, smem] + [away] * 10,
        out_specs=[pl.BlockSpec(memory_space=VMEM)] * 3,
        scratch_shapes=[
            VMEM((rows, positions, width), BF16),
            VMEM((rows, positions, width), BF16),
            VMEM(queries.shape, BF16),
            VMEM(new_key.shape, BF16),
            VMEM(new_value.shape, BF16),
            pltpu.SMEM(lengths.shape, jnp.int32),
            pltpu.SMEM(row_adapter.shape, jnp.int32),
            pltpu.SMEM(adapter_list.shape, jnp.int32),
            pltpu.SMEM(adapter_rank.shape, jnp.int32),
            VMEM((rows * full, width), F32),
            pltpu.SemaphoreType.DMA((7,)),
            pltpu.SemaphoreType.DMA((parts,)),
            pltpu.SemaphoreType.DMA((parts,)),
            pltpu.SemaphoreType.DMA,
        ],
        compiler_params=pltpu.CompilerParams(vmem_limit_bytes=8 << 20),
        cost_estimate=pl.CostEstimate(
            flops=4 * rows * heads * positions * width,
            bytes_accessed=4 * rows * positions * width,
            transcendentals=rows * heads * positions,
        ),
        name="attention",
    )(
        group_at,
        early_at,
        *in_hbm(
            key_cache,
            value_cache,
            queries,
            new_key,
            new_value,
            lengths,
            row_adapter,
            adapter_list,
            adapter_rank,
            out_weight,
        ),
    )
    if full != heads:
        tagged = jnp.concatenate([tagged[:, : heads * width], tagged[:, full * width :]], axis=1)
    return tagged, early, limits


def put_stacked(out, start, term, first=0, others=()):
    rows = term.shape[0]
    for column in range(0, term.shape[1], LANES):
        at = first + (start + column) // LANES * rows
        part = term[:, column : column + LANES]
        for other in others:
            part = part + other[at : at + rows].astype(F32)
        out[at : at + rows] = part.astype(out.dtype)


def base_kernel(ahead, deep, arriving, tensor_at, tagged, out_weight, *refs):
    arrived, (*near, out, held, sums, sems) = refs[:arriving], refs[arriving:]
    _, deep_rows, block = held.shape
    width = out_weight.shape[0]
    count = width // deep_rows
    column = pl.ds(pl.multiple_of((tensor_at[0] ^ ahead) * block, block), block)

    def copy(at):
        return pltpu.make_async_copy(
            out_weight.at[pl.ds(at * deep_rows, deep_rows), column],
            held.at[at % deep],
            sems.at[at % deep],
        )

    for at in range(min(deep, count)):
        copy(at).start()
    piece = min(block, 512)
    if near:
        early, early_out = near
        for start in range(0, block, piece):
            columns = slice(start, start + piece)
            term = jnp.dot(tagged[:, :width], early[:, columns], preferred_element_type=F32)
            put_stacked(early_out, start, term)
    for at in range(count):
        copy(at).wait()
        inputs = slice(at * deep_rows, (at + 1) * deep_rows)
        for start in range(0, block, piece):
            columns = slice(start, start + piece)
            term = jnp.dot(
                tagged[:, inputs], held[at % deep, :, columns], preferred_element_type=F32
            )
            if at:
                term = term + sums[:, columns]
            if at < count - 1:
                sums[:, columns] = term
            else:
                put_stacked(out, start, term, 0, arrived)
        if at + deep < count:
            copy(at + deep).start()


def base_block(tensor_at, tagged, out_weight, block, ahead, early=(), arrived=()):
    rows = tagged.shape[0]
    width = out_weight.shape[0]
    deep, deep_rows = 4, min(width, 256)
    whole = pl.BlockSpec(memory_space=VMEM)
    count = 1 + len(early)
    return pl.pallas_call(
        functools.partial(base_kernel, ahead, deep, len(arrived)),
        out_shape=[jax.ShapeDtypeStruct((block // LANES * rows, LANES), BF16 if ahead else F32)]
        * count,
        in_specs=[pl.BlockSpec(memory_space=pltpu.SMEM), whole, pl.BlockSpec(memory_space=pl.ANY)]
        + [whole] * (len(arrived) + len(early)),
        out_specs=[whole] * count,
        scratch_shapes=[
            VMEM((deep, deep_rows, block), BF16),
            VMEM((rows, block), F32),
            pltpu.SemaphoreType.DMA((deep,)),
        ],
        compiler_params=pltpu.CompilerParams(vmem_limit_bytes=12 << 20),
        cost_estimate=pl.CostEstimate(
            flops=2 * rows * width * block * count,
            bytes_accessed=2 * width * block * (2 if arrived else count),
            transcendentals=0,
        ),
        name="base_terms",
    )(tensor_at, tagged, *in_hbm(out_weight), *arrived, *early)


def slots_of(tags, batch_at, pool, tile, per):
    lane = lane_of(tags.shape)
    ids = tags.astype(F32).astype(jnp.int32)
    mine = tile * per + lane // (LANES // per)
    held = tile * per // pool
    return ids - (batch_at[0] ^ held) * pool + held * pool, mine


def shrink_kernel(batch_at, *refs):
    blocks, factors, out = refs[:-3], refs[-3:-1], refs[-1]
    pool, rank_width, width = factors[0].shape
    everyone = jnp.concatenate([block[...] for block in blocks], axis=0)
    per = LANES // rank_width
    lane = lane_of((everyone.shape[0], LANES))
    kept = jnp.zeros(lane.shape, F32)
    for held, weights in enumerate(factors):
        terms = lax.dot_general(
            everyone[:, :width],
            weights[...].reshape(pool * rank_width, width),
            (((1,), (1,)), ((), ())),
            preferred_element_type=F32,
        )
        for tile in range(pool // per):
            slot, mine = slots_of(everyone[:, width:], batch_at, pool, held * pool // per + tile, per)
            kept = kept + jnp.where(
                slot == mine, terms[:, tile * LANES : (tile + 1) * LANES], F32(0.0)
            )
    both = kept + pltpu.roll(kept, rank_width, 1)
    half = both.shape[0] // 2
    packed = jnp.where(lane[:half] < rank_width, both[:half], both[half:])
    out[...] = packed.astype(out.dtype)


def shrink_part(blocks, factors, batch_at):
    pool, rank_width, width = factors[0].shape
    rows = len(blocks) * blocks[0].shape[0]
    smem = pl.BlockSpec(memory_space=pltpu.SMEM)
    whole = pl.BlockSpec(memory_space=VMEM)
    return pl.pallas_call(
        shrink_kernel,
        out_shape=jax.ShapeDtypeStruct((rows // 2, LANES), BF16),
        in_specs=[smem] + [whole] * (len(blocks) + 2),
        out_specs=whole,
        compiler_params=pltpu.CompilerParams(vmem_limit_bytes=8 << 20),
        cost_estimate=pl.CostEstimate(
            flops=4 * rows * width * pool * rank_width,
            bytes_accessed=2 * width * (rows + 2 * pool * rank_width),
            transcendentals=0,
        ),
        name="shrink",
    )(batch_at, *blocks, *factors)


def expand_kernel(count, sums, rank_width, batch_at, *refs):
    limits, refs = refs[:2], refs[2:]
    tags, parts = refs[:count], refs[count : count + sums]
    factors, outs = refs[count + sums : count + sums + 2], refs[count + sums + 2 :]
    tags = jnp.concatenate([tag[...] for tag in tags], axis=0)
    total = parts[0][...].astype(F32)
    for part in parts[1:]:
        total = total + part[...].astype(F32)
    total = total.astype(BF16).astype(F32)
    other = pltpu.roll(total, rank_width, 1)
    low = lane_of(total.shape) < rank_width
    shrink = jnp.concatenate(
        [jnp.where(low, total, other), jnp.where(low, other, total)], axis=0
    )
    per = LANES // rank_width
    inputs, block = factors[0].shape
    pool = inputs // rank_width
    tiles = []
    for tile in range(2 * pool // per):
        slot, mine = slots_of(tags, batch_at, pool, tile, per)
        held, at = divmod(tile * per, pool)
        limit = limits[held][at // per : at // per + 1]
        keep = (slot == mine) & (lane_of(tags.shape) % rank_width < limit)
        tiles.append(jnp.where(keep, shrink, F32(0.0)).astype(BF16))
    half = len(tiles) // 2
    spreads = [jnp.concatenate(tiles[:half], axis=1), jnp.concatenate(tiles[half:], axis=1)]
    rows = tags.shape[0] // count
    piece = min(block, 512)
    for at in range(0, block, piece):
        delta = sum(
            jnp.dot(spread, each[:, at : at + piece], preferred_element_type=F32)
            for spread, each in zip(spreads, factors)
        )
        for which, out in enumerate(outs):
            put_stacked(out, at, delta[which * rows : (which + 1) * rows])


def expand(blocks, parts, factors, limits, batch_at):
    pool, rank_width, block = factors[0].shape
    rows, tagged_width = blocks[0].shape
    count = len(blocks)
    stack = rows * block // LANES
    tag = pl.BlockSpec((rows, LANES), lambda i: (0, tagged_width // LANES - 1))
    full = pl.BlockSpec((pool * rank_width, block), lambda i: (0, 0))
    part = pl.BlockSpec(parts[0].shape, lambda i: (0, 0))
    return pl.pallas_call(
        functools.partial(expand_kernel, count, len(parts), rank_width),
        grid=(1,),
        out_shape=[jax.ShapeDtypeStruct((stack, LANES), BF16) for _ in blocks],
        in_specs=[pl.BlockSpec(memory_space=pltpu.SMEM)]
        + [pl.BlockSpec(each.shape, lambda i: (0, 0)) for each in limits]
        + [tag] * count
        + [part] * len(parts)
        + [full] * 2,
        out_specs=[pl.BlockSpec((stack, LANES), lambda i: (0, 0)) for _ in blocks],
        compiler_params=pltpu.CompilerParams(vmem_limit_bytes=16 << 20),
        cost_estimate=pl.CostEstimate(
            flops=4 * rows * count * pool * rank_width * block,
            bytes_accessed=2 * pool * rank_width * block,
            transcendentals=0,
        ),
        name="expand",
    )(batch_at, *limits, *blocks, *parts, *[each.reshape(pool * rank_width, block) for each in factors])


def total_kernel(*refs):
    terms, out = refs[:-1], refs[-1]
    rows = out.shape[0]
    for column in range(0, out.shape[1], LANES):
        at = slice(column // LANES * rows, (column // LANES + 1) * rows)
        total = terms[0][at].astype(F32)
        for term in terms[1:]:
            total = total + term[at].astype(F32)
        out[:, column : column + LANES] = total.astype(out.dtype)


def total(rows, block, terms):
    whole = pl.BlockSpec(memory_space=VMEM)
    return pl.pallas_call(
        total_kernel,
        out_shape=jax.ShapeDtypeStruct((rows, block), BF16),
        in_specs=[whole] * len(terms),
        out_specs=whole,
        compiler_params=pltpu.CompilerParams(vmem_limit_bytes=8 << 20),
        cost_estimate=pl.CostEstimate(
            flops=rows * block * len(terms),
            bytes_accessed=2 * rows * block * (1 + len(terms)),
            transcendentals=0,
        ),
        name="total",
    )(*terms)


def partial_kernel(*refs):
    terms, out = refs[:-1], refs[-1]
    total = terms[0][...].astype(F32)
    for term in terms[1:]:
        total = total + term[...].astype(F32)
    out[...] = total


def partial_total(terms, weight):
    whole = pl.BlockSpec(memory_space=VMEM)
    return pl.pallas_call(
        partial_kernel,
        out_shape=jax.ShapeDtypeStruct(terms[0].shape, F32),
        in_specs=[whole] * len(terms),
        out_specs=whole,
        compiler_params=pltpu.CompilerParams(vmem_limit_bytes=8 << 20),
        cost_estimate=pl.CostEstimate(
            flops=terms[0].size * len(terms),
            bytes_accessed=4 * terms[0].size + weight,
            transcendentals=0,
        ),
        name="partial_total",
    )(*terms)


def local(
    tensor_size,
    batch_size,
    queries,
    key_cache,
    value_cache,
    new_key,
    new_value,
    lengths,
    out_weight,
    shrink_weight,
    expand_weight,
    adapter_rank,
    adapter_list,
    row_adapter,
):
    rows = queries.shape[0]
    block = expand_weight.shape[2]
    chips = batch_size // 2
    batch_at = lax.axis_index("batch").reshape(1).astype(jnp.int32)
    tensor_at = lax.axis_index("tensor").reshape(1).astype(jnp.int32)

    def to_sibling(array):
        return permuted(array, "batch", batch_size, lambda i: i ^ 1)

    def to_chip(array, shift):
        return permuted(array, "batch", batch_size, lambda i: (i + 2 * shift) % batch_size)

    def across(array, bit):
        return permuted(array, "tensor", tensor_size, lambda i: i ^ bit)

    def wide(array):
        return array.astype(F32)

    stack = block // LANES * rows
    tagged, early, limits = attend(
        tensor_at ^ 3,
        block,
        out_weight,
        queries,
        key_cache,
        value_cache,
        new_key,
        new_value,
        lengths,
        adapter_list,
        row_adapter,
        adapter_rank,
        shrink_weight.shape[2],
    )
    limits = [limits, to_sibling(limits)]
    shrink_weight = jnp.swapaxes(shrink_weight, 1, 2)
    shrink_factors = [shrink_weight, to_sibling(shrink_weight)]
    expand_factors = [expand_weight, to_sibling(expand_weight)]
    visiting = [to_chip(tagged, shift) for shift in range(1, chips)]
    third, next_door = base_block(tensor_at, tagged, out_weight, block, 1, [early])
    visiting, third, next_door, limits = lax.optimization_barrier(
        (visiting, third, next_door, limits)
    )
    blocks = [tagged] + visiting
    third = across(third, 1)

    part = shrink_part(blocks, shrink_factors, batch_at)
    parts = [part, across(part, 1)]
    part, later_tagged = lax.optimization_barrier((part, tagged))
    (second,) = base_block(tensor_at, later_tagged, out_weight, block, 2)
    second = (wide(second) + wide(third)).astype(BF16)
    parts, second = lax.optimization_barrier((parts, second))
    bit = 2
    while bit < tensor_size:
        part = (wide(parts[0]) + wide(parts[1])).astype(BF16)
        part, next_door = lax.optimization_barrier((part, next_door))
        parts = [part, across(part, bit)]
        bit *= 2
    arrived = [across(second, 2), across(next_door, 1)]
    for ahead in range(4, tensor_size, 2):
        (near,) = base_block(tensor_at, tagged, out_weight, block, ahead)
        (far,) = base_block(tensor_at, tagged, out_weight, block, ahead + 1)
        arrived.append(across((wide(near) + wide(across(far, 1))).astype(BF16), ahead))

    deltas = expand(blocks, parts, expand_factors, limits, batch_at)
    deltas, late_tagged = lax.optimization_barrier((deltas, tagged))
    (own,) = base_block(tensor_at, late_tagged, out_weight, block, 0)
    so_far = partial_total([own, deltas[0], arrived[0], *arrived[2:]], 0)
    terms = [partial_total([so_far, arrived[1]], 8 << 20)]
    terms += [to_chip(home, -shift) for shift, home in enumerate(deltas[1:], 1)]
    return total(rows, block, terms)


def solution(mesh):
    placed = (
        P(("groups", "batch"), "tensor", None),
        P(("groups", "batch"), None, None, None),
        P(("groups", "batch"), None, None, None),
        P(("groups", "batch"), None, None),
        P(("groups", "batch"), None, None),
        P(("groups", "batch")),
        P("tensor", None),
        P("batch", "tensor", None),
        P("batch", None, "tensor"),
        P("batch"),
        P(("groups", "batch")),
        P(("groups", "batch")),
    )

    def placed_local(*arrays):
        return local(mesh.shape["tensor"], mesh.shape["batch"], *arrays)

    return jax.shard_map(
        placed_local,
        mesh=mesh,
        in_specs=placed,
        out_specs=P(("groups", "batch"), "tensor"),
        check_vma=False,
    )
```

```python
import functools

import jax
import jax.numpy as jnp
from jax import lax
from jax.experimental import pallas as pl
from jax.experimental.pallas import tpu as pltpu
from jax.sharding import PartitionSpec as P

HQ = 32
KVH = 4
LANES = 128
VMEM = pltpu.VMEM
GRANT = 56 << 20
F32, BF16 = jnp.float32, jnp.bfloat16


def permuted(array, axis, size, partner):
    return lax.ppermute(array, axis, [(i, partner(i)) for i in range(size)])


def in_hbm(*arrays):
    return [pltpu.with_memory_space_constraint(array, pltpu.HBM) for array in arrays]


def lane_of(shape):
    return lax.broadcasted_iota(jnp.int32, shape, len(shape) - 1)


def attend_kernel(parts, group_at, early_at, *refs):
    given, (out_weight, tagged, early, kept_factors, *scratch) = refs[:10], refs[10:]
    held, (spread_out, small_sems, key_sems, value_sems, early_sem) = scratch[:10], scratch[10:]
    key_cache, value_cache = given[:2]
    keys, values, queries, new_key, new_value, lengths, row_adapter, adapter_list, ranks, factors = held
    rows, heads, width = queries.shape
    positions = key_cache.shape[2]
    group = group_at[0]
    some = rows // parts

    def cache_copies(part):
        at = pl.ds(part * some, some)
        return (
            pltpu.make_async_copy(key_cache.at[at, group], keys.at[at], key_sems.at[part]),
            pltpu.make_async_copy(value_cache.at[at, group], values.at[at], value_sems.at[part]),
        )

    small = [
        pltpu.make_async_copy(given[i], held[i], small_sems.at[i - 2]) for i in range(2, 10)
    ]
    factors_copy = small.pop()
    for copy in small:
        copy.start()
    for part in range(parts):
        for copy in cache_copies(part):
            copy.start()
    early_rows, block = early.shape
    start = pl.multiple_of(early_at[0] * block, block)
    early_copy = pltpu.make_async_copy(
        out_weight.at[pl.ds(0, early_rows), pl.ds(start, block)], early, early_sem
    )
    factors_copy.start()
    early_copy.start()
    for copy in small:
        copy.wait()
    at_row = lax.broadcasted_iota(jnp.int32, (rows, LANES), 0)
    tag = jnp.zeros((rows, LANES), jnp.int32)
    for row in range(rows):
        tag = jnp.where(at_row == row, adapter_list[row_adapter[row]], tag)
    tag = tag.astype(F32).astype(BF16)
    group_row = lax.broadcasted_iota(jnp.int32, new_key.shape, 1) == group
    fresh_key = jnp.sum(
        jnp.where(group_row, new_key[...].astype(F32), F32(0.0)), axis=1, keepdims=True
    )
    fresh_value = jnp.sum(
        jnp.where(group_row, new_value[...].astype(F32), F32(0.0)), axis=1, keepdims=True
    )
    score_scale = width ** (-0.5)
    fresh = jnp.sum(queries[...].astype(F32) * fresh_key, axis=-1, keepdims=True) * score_scale
    for part in range(parts):
        at = slice(part * some, (part + 1) * some)
        key_copy, value_copy = cache_copies(part)
        key_copy.wait()
        scores = (
            lax.dot_general(
                queries[at], keys[at], (((2,), (2,)), ((0,), (0,))), preferred_element_type=F32
            )
            * score_scale
        )
        length = jnp.stack(
            [
                jnp.full((heads, positions), lengths[row], jnp.int32)
                for row in range(part * some, (part + 1) * some)
            ]
        )
        valid = lane_of(scores.shape) < length
        masked = jnp.where(valid, scores, F32(-1e30))
        highest = jnp.maximum(jnp.max(masked, axis=-1, keepdims=True), fresh[at])
        cached_exp = jnp.where(valid, jnp.exp(masked - highest), F32(0.0))
        fresh_exp = jnp.exp(fresh[at] - highest)
        totals = jnp.sum(cached_exp, axis=-1, keepdims=True) + fresh_exp
        cached_w = (cached_exp / totals).astype(BF16)
        fresh_w = (fresh_exp / totals).astype(BF16).astype(F32)
        value_copy.wait()
        attended = lax.dot_general(
            cached_w, values[at], (((2,), (1,)), ((0,), (0,))), preferred_element_type=F32
        )
        attended = attended + fresh_w * fresh_value[at]
        spread_out[pl.ds(part * some * heads, some * heads)] = attended.reshape(
            some * heads, width
        )
    tagged[:, heads * width :] = tag
    for head in range(heads):
        tagged[:, head * width : (head + 1) * width] = spread_out[
            pl.ds(head, rows, stride=heads)
        ].astype(BF16)
    factors_copy.wait()
    for held_at in range(factors.shape[0]):
        factor = factors[held_at].astype(F32)
        column = lax.broadcasted_iota(jnp.int32, factor.shape, 0)
        kept = jnp.where(column < ranks[held_at], factor, F32(0.0))
        kept_factors[held_at] = kept.astype(kept_factors.dtype)
    early_copy.wait()


def attend(
    early_at,
    block,
    out_weight,
    queries,
    key_cache,
    value_cache,
    new_key,
    new_value,
    lengths,
    adapter_list,
    row_adapter,
    adapter_rank,
    factors,
):
    rows, heads, width = queries.shape
    positions = key_cache.shape[2]
    per_group = HQ // KVH
    group_at = (lax.axis_index("tensor") * heads // per_group).reshape(1).astype(jnp.int32)
    full = -(-heads // 8) * 8
    if full != heads:
        queries = jnp.pad(queries, ((0, 0), (0, full - heads), (0, 0)))
    parts = 4
    smem = pl.BlockSpec(memory_space=pltpu.SMEM)
    away = pl.BlockSpec(memory_space=pl.ANY)
    tagged, early, masked = pl.pallas_call(
        functools.partial(attend_kernel, parts),
        out_shape=[
            jax.ShapeDtypeStruct((rows, full * width + LANES), BF16),
            VMEM((out_weight.shape[0] // 2, block), BF16),
            VMEM(factors.shape, BF16),
        ],
        in_specs=[smem, smem] + [away] * 11,
        out_specs=[pl.BlockSpec(memory_space=VMEM)] * 3,
        scratch_shapes=[
            VMEM((rows, positions, width), BF16),
            VMEM((rows, positions, width), BF16),
            VMEM(queries.shape, BF16),
            VMEM(new_key.shape, BF16),
            VMEM(new_value.shape, BF16),
            pltpu.SMEM(lengths.shape, jnp.int32),
            pltpu.SMEM(row_adapter.shape, jnp.int32),
            pltpu.SMEM(adapter_list.shape, jnp.int32),
            pltpu.SMEM(adapter_rank.shape, jnp.int32),
            VMEM(factors.shape, BF16),
            VMEM((rows * full, width), F32),
            pltpu.SemaphoreType.DMA((8,)),
            pltpu.SemaphoreType.DMA((parts,)),
            pltpu.SemaphoreType.DMA((parts,)),
            pltpu.SemaphoreType.DMA,
        ],
        compiler_params=pltpu.CompilerParams(vmem_limit_bytes=12 << 20),
        cost_estimate=pl.CostEstimate(
            flops=4 * rows * heads * positions * width,
            bytes_accessed=4 * rows * positions * width,
            transcendentals=rows * heads * positions,
        ),
        name="attention",
    )(
        group_at,
        early_at,
        *in_hbm(
            key_cache,
            value_cache,
            queries,
            new_key,
            new_value,
            lengths,
            row_adapter,
            adapter_list,
            adapter_rank,
            factors,
            out_weight,
        ),
    )
    if full != heads:
        tagged = jnp.concatenate([tagged[:, : heads * width], tagged[:, full * width :]], axis=1)
    return tagged, early, masked


def put_stacked(out, start, term, first=0, others=()):
    rows = term.shape[0]
    for column in range(0, term.shape[1], LANES):
        at = first + (start + column) // LANES * rows
        part = term[:, column : column + LANES]
        for other in others:
            part = part + other[at : at + rows].astype(F32)
        out[at : at + rows] = part.astype(out.dtype)


def base_kernel(aheads, early_rows, deep, tensor_at, tagged, out_weight, *refs):
    early = refs[0] if early_rows else None
    outs, (held, sums, sems) = refs[bool(early_rows) : -3], refs[-3:]
    _, deep_rows, block = held.shape
    width = out_weight.shape[0]
    pieces = [
        (which, row)
        for which in range(len(aheads))
        for row in range(0 if which else early_rows, width, deep_rows)
    ]

    def copy(at):
        which, row = pieces[at]
        start = pl.multiple_of((tensor_at[0] ^ aheads[which]) * block, block)
        return pltpu.make_async_copy(
            out_weight.at[pl.ds(row, deep_rows), pl.ds(start, block)],
            held.at[at % deep],
            sems.at[at % deep],
        )

    for at in range(min(deep, len(pieces))):
        copy(at).start()
    piece = min(block, 512)
    if early_rows:
        for start in range(0, block, piece):
            columns = slice(start, start + piece)
            sums[:, columns] = jnp.dot(
                tagged[:, :early_rows], early[:, columns], preferred_element_type=F32
            )
    for at, (which, row) in enumerate(pieces):
        copy(at).wait()
        for start in range(0, block, piece):
            columns = slice(start, start + piece)
            term = jnp.dot(
                tagged[:, row : row + deep_rows],
                held[at % deep, :, columns],
                preferred_element_type=F32,
            )
            if row:
                term = term + sums[:, columns]
            if row + deep_rows < width:
                sums[:, columns] = term
            else:
                put_stacked(outs[which], start, term)
        if at + deep < len(pieces):
            copy(at + deep).start()


def base_terms(tensor_at, tagged, out_weight, block, aheads, early=None):
    rows = tagged.shape[0]
    width = out_weight.shape[0]
    deep, deep_rows = 4, min(width // 2, 256)
    early_rows = 0 if early is None else early.shape[0]
    whole = pl.BlockSpec(memory_space=VMEM)
    count = len(aheads)
    return pl.pallas_call(
        functools.partial(base_kernel, aheads, early_rows, deep),
        out_shape=[
            jax.ShapeDtypeStruct((block // LANES * rows, LANES), BF16 if ahead else F32)
            for ahead in aheads
        ],
        in_specs=[pl.BlockSpec(memory_space=pltpu.SMEM), whole, pl.BlockSpec(memory_space=pl.ANY)]
        + [whole] * bool(early_rows),
        out_specs=[whole] * count,
        scratch_shapes=[
            VMEM((deep, deep_rows, block), BF16),
            VMEM((rows, block), F32),
            pltpu.SemaphoreType.DMA((deep,)),
        ],
        compiler_params=pltpu.CompilerParams(vmem_limit_bytes=12 << 20),
        cost_estimate=pl.CostEstimate(
            flops=2 * rows * width * block * count,
            bytes_accessed=2 * width * block * count,
            transcendentals=0,
        ),
        name="base_terms",
    )(tensor_at, tagged, *in_hbm(out_weight), *([early] if early_rows else []))


def slots_of(tags, batch_at, pool, tile, per):
    lane = lane_of(tags.shape)
    ids = tags.astype(F32).astype(jnp.int32)
    mine = tile * per + lane // (LANES // per)
    held = tile * per // pool
    return ids - (batch_at[0] ^ held) * pool + held * pool, mine


def shrink_kernel(batch_at, *refs):
    blocks, factors, out = refs[:-3], refs[-3:-1], refs[-1]
    pool, rank_width, width = factors[0].shape
    everyone = jnp.concatenate([block[...] for block in blocks], axis=0)
    per = LANES // rank_width
    lane = lane_of((everyone.shape[0], LANES))
    kept = jnp.zeros(lane.shape, F32)
    for held, weights in enumerate(factors):
        terms = lax.dot_general(
            everyone[:, :width],
            weights[...].reshape(pool * rank_width, width),
            (((1,), (1,)), ((), ())),
            preferred_element_type=F32,
        )
        for tile in range(pool // per):
            slot, mine = slots_of(everyone[:, width:], batch_at, pool, held * pool // per + tile, per)
            kept = kept + jnp.where(
                slot == mine, terms[:, tile * LANES : (tile + 1) * LANES], F32(0.0)
            )
    both = kept + pltpu.roll(kept, rank_width, 1)
    half = both.shape[0] // 2
    packed = jnp.where(lane[:half] < rank_width, both[:half], both[half:])
    out[...] = packed.astype(out.dtype)


def shrink_part(blocks, factors, batch_at):
    pool, rank_width, width = factors[0].shape
    rows = len(blocks) * blocks[0].shape[0]
    smem = pl.BlockSpec(memory_space=pltpu.SMEM)
    whole = pl.BlockSpec(memory_space=VMEM)
    return pl.pallas_call(
        shrink_kernel,
        out_shape=jax.ShapeDtypeStruct((rows // 2, LANES), BF16),
        in_specs=[smem] + [whole] * (len(blocks) + 2),
        out_specs=whole,
        compiler_params=pltpu.CompilerParams(vmem_limit_bytes=8 << 20),
        cost_estimate=pl.CostEstimate(
            flops=4 * rows * width * pool * rank_width,
            bytes_accessed=2 * width * (rows + 2 * pool * rank_width),
            transcendentals=0,
        ),
        name="shrink",
    )(batch_at, *blocks, *factors)


def expand_kernel(count, sums, rank_width, batch_at, *refs):
    tags, parts = refs[:count], refs[count : count + sums]
    factors, outs = refs[count + sums : count + sums + 2], refs[count + sums + 2 :]
    tags = jnp.concatenate([tag[...] for tag in tags], axis=0)
    total = parts[0][...].astype(F32)
    for part in parts[1:]:
        total = total + part[...].astype(F32)
    total = total.astype(BF16).astype(F32)
    other = pltpu.roll(total, rank_width, 1)
    low = lane_of(total.shape) < rank_width
    shrink = jnp.concatenate(
        [jnp.where(low, total, other), jnp.where(low, other, total)], axis=0
    )
    per = LANES // rank_width
    inputs, block = factors[0].shape
    pool = inputs // rank_width
    tiles = []
    for tile in range(2 * pool // per):
        slot, mine = slots_of(tags, batch_at, pool, tile, per)
        tiles.append(jnp.where(slot == mine, shrink, F32(0.0)).astype(BF16))
    half = len(tiles) // 2
    spreads = [jnp.concatenate(tiles[:half], axis=1), jnp.concatenate(tiles[half:], axis=1)]
    rows = tags.shape[0] // count
    piece = min(block, 512)
    for at in range(0, block, piece):
        delta = sum(
            jnp.dot(spread, each[:, at : at + piece], preferred_element_type=F32)
            for spread, each in zip(spreads, factors)
        )
        for which, out in enumerate(outs):
            put_stacked(out, at, delta[which * rows : (which + 1) * rows])


def expand(blocks, parts, factors, batch_at):
    pool, rank_width, block = factors[0].shape
    rows, tagged_width = blocks[0].shape
    count = len(blocks)
    stack = rows * block // LANES
    tag = pl.BlockSpec((rows, LANES), lambda i: (0, tagged_width // LANES - 1))
    full = pl.BlockSpec((pool * rank_width, block), lambda i: (0, 0))
    part = pl.BlockSpec(parts[0].shape, lambda i: (0, 0))
    return pl.pallas_call(
        functools.partial(expand_kernel, count, len(parts), rank_width),
        grid=(1,),
        out_shape=[jax.ShapeDtypeStruct((stack, LANES), BF16) for _ in blocks],
        in_specs=[pl.BlockSpec(memory_space=pltpu.SMEM)]
        + [tag] * count
        + [part] * len(parts)
        + [full] * 2,
        out_specs=[pl.BlockSpec((stack, LANES), lambda i: (0, 0)) for _ in blocks],
        compiler_params=pltpu.CompilerParams(vmem_limit_bytes=16 << 20),
        cost_estimate=pl.CostEstimate(
            flops=4 * rows * count * pool * rank_width * block,
            bytes_accessed=2 * pool * rank_width * block,
            transcendentals=0,
        ),
        name="expand",
    )(batch_at, *blocks, *parts, *[each.reshape(pool * rank_width, block) for each in factors])


def total_kernel(*refs):
    terms, out = refs[:-1], refs[-1]
    rows = out.shape[0]
    for column in range(0, out.shape[1], LANES):
        at = slice(column // LANES * rows, (column // LANES + 1) * rows)
        total = terms[0][at].astype(F32)
        for term in terms[1:]:
            total = total + term[at].astype(F32)
        out[:, column : column + LANES] = total.astype(out.dtype)


def total(rows, block, terms):
    whole = pl.BlockSpec(memory_space=VMEM)
    return pl.pallas_call(
        total_kernel,
        out_shape=jax.ShapeDtypeStruct((rows, block), BF16),
        in_specs=[whole] * len(terms),
        out_specs=whole,
        compiler_params=pltpu.CompilerParams(vmem_limit_bytes=8 << 20),
        cost_estimate=pl.CostEstimate(
            flops=rows * block * len(terms),
            bytes_accessed=2 * rows * block * (1 + len(terms)),
            transcendentals=0,
        ),
        name="total",
    )(*terms)


def partial_kernel(*refs):
    terms, out = refs[:-1], refs[-1]
    total = terms[0][...].astype(F32)
    for term in terms[1:]:
        total = total + term[...].astype(F32)
    out[...] = total


def partial_total(terms, weight):
    whole = pl.BlockSpec(memory_space=VMEM)
    return pl.pallas_call(
        partial_kernel,
        out_shape=jax.ShapeDtypeStruct(terms[0].shape, F32),
        in_specs=[whole] * len(terms),
        out_specs=whole,
        compiler_params=pltpu.CompilerParams(vmem_limit_bytes=8 << 20),
        cost_estimate=pl.CostEstimate(
            flops=terms[0].size * len(terms),
            bytes_accessed=4 * terms[0].size + weight,
            transcendentals=0,
        ),
        name="partial_total",
    )(*terms)


def local(
    tensor_size,
    batch_size,
    queries,
    key_cache,
    value_cache,
    new_key,
    new_value,
    lengths,
    out_weight,
    shrink_weight,
    expand_weight,
    adapter_rank,
    adapter_list,
    row_adapter,
):
    rows = queries.shape[0]
    block = expand_weight.shape[2]
    chips = batch_size // 2
    batch_at = lax.axis_index("batch").reshape(1).astype(jnp.int32)
    tensor_at = lax.axis_index("tensor").reshape(1).astype(jnp.int32)

    def to_sibling(array):
        return permuted(array, "batch", batch_size, lambda i: i ^ 1)

    def to_chip(array, shift):
        return permuted(array, "batch", batch_size, lambda i: (i + 2 * shift) % batch_size)

    def across(array, bit):
        return permuted(array, "tensor", tensor_size, lambda i: i ^ bit)

    def wide(array):
        return array.astype(F32)

    stack = block // LANES * rows
    tagged, early, masked = attend(
        tensor_at ^ 3,
        block,
        out_weight,
        queries,
        key_cache,
        value_cache,
        new_key,
        new_value,
        lengths,
        adapter_list,
        row_adapter,
        adapter_rank,
        jnp.swapaxes(shrink_weight, 1, 2),
    )
    shrink_factors = [masked, to_sibling(masked)]
    expand_factors = [expand_weight, to_sibling(expand_weight)]
    visiting = [to_chip(tagged, shift) for shift in range(1, chips)]
    third, next_door = base_terms(tensor_at, tagged, out_weight, block, [3, 1], early)
    visiting, third, next_door = lax.optimization_barrier((visiting, third, next_door))
    blocks = [tagged] + visiting
    third = across(third, 1)

    part = shrink_part(blocks, shrink_factors, batch_at)
    parts = [part, across(part, 1)]
    part, later_tagged = lax.optimization_barrier((part, tagged))
    (second,) = base_terms(tensor_at, later_tagged, out_weight, block, [2])
    second = (wide(second) + wide(third)).astype(BF16)
    parts, second = lax.optimization_barrier((parts, second))
    bit = 2
    while bit < tensor_size:
        part = (wide(parts[0]) + wide(parts[1])).astype(BF16)
        part, next_door = lax.optimization_barrier((part, next_door))
        parts = [part, across(part, bit)]
        bit *= 2
    arrived = [across(second, 2), across(next_door, 1)]
    for ahead in range(4, tensor_size, 2):
        near, far = base_terms(tensor_at, tagged, out_weight, block, [ahead, ahead + 1])
        arrived.append(across((wide(near) + wide(across(far, 1))).astype(BF16), ahead))

    deltas = expand(blocks, parts, expand_factors, batch_at)
    deltas, late_tagged = lax.optimization_barrier((deltas, tagged))
    (own,) = base_terms(tensor_at, late_tagged, out_weight, block, [0])
    so_far = partial_total([own, deltas[0], arrived[0], *arrived[2:]], 0)
    terms = [partial_total([so_far, arrived[1]], 8 << 20)]
    terms += [to_chip(home, -shift) for shift, home in enumerate(deltas[1:], 1)]
    return total(rows, block, terms)


def solution(mesh):
    placed = (
        P(("groups", "batch"), "tensor", None),
        P(("groups", "batch"), None, None, None),
        P(("groups", "batch"), None, None, None),
        P(("groups", "batch"), None, None),
        P(("groups", "batch"), None, None),
        P(("groups", "batch")),
        P("tensor", None),
        P("batch", "tensor", None),
        P("batch", None, "tensor"),
        P("batch"),
        P(("groups", "batch")),
        P(("groups", "batch")),
    )

    def placed_local(*arrays):
        return local(mesh.shape["tensor"], mesh.shape["batch"], *arrays)

    return jax.shard_map(
        placed_local,
        mesh=mesh,
        in_specs=placed,
        out_specs=P(("groups", "batch"), "tensor"),
        check_vma=False,
    )
```

```python
import functools

import jax
import jax.numpy as jnp
from jax import lax
from jax.experimental import pallas as pl
from jax.experimental.pallas import tpu as pltpu
from jax.sharding import PartitionSpec as P

HQ = 32
KVH = 4
LANES = 128
VMEM = pltpu.VMEM
GRANT = 56 << 20
F32, BF16 = jnp.float32, jnp.bfloat16


def permuted(array, axis, size, partner):
    return lax.ppermute(array, axis, [(i, partner(i)) for i in range(size)])


def in_hbm(*arrays):
    return [pltpu.with_memory_space_constraint(array, pltpu.HBM) for array in arrays]


def lane_of(shape):
    return lax.broadcasted_iota(jnp.int32, shape, len(shape) - 1)


def attend_kernel(parts, rank_width, group_at, early_at, *refs):
    given, (out_weight, tagged, early, limits, *scratch) = refs[:9], refs[9:]
    held, (spread_out, small_sems, key_sems, value_sems, early_sem) = scratch[:9], scratch[9:]
    key_cache, value_cache = given[:2]
    keys, values, queries, new_key, new_value, lengths, row_adapter, adapter_list, ranks = held
    rows, heads, width = queries.shape
    positions = key_cache.shape[2]
    group = group_at[0]
    some = rows // parts

    def cache_copies(part):
        at = pl.ds(part * some, some)
        return (
            pltpu.make_async_copy(key_cache.at[at, group], keys.at[at], key_sems.at[part]),
            pltpu.make_async_copy(value_cache.at[at, group], values.at[at], value_sems.at[part]),
        )

    small = [
        pltpu.make_async_copy(given[i], held[i], small_sems.at[i - 2]) for i in range(2, 9)
    ]
    for copy in small:
        copy.start()
    for part in range(parts):
        for copy in cache_copies(part):
            copy.start()
    block = early.shape[1]
    start = pl.multiple_of(early_at[0] * block, block)
    early_copy = pltpu.make_async_copy(out_weight.at[:, pl.ds(start, block)], early, early_sem)
    early_copy.start()
    for copy in small:
        copy.wait()
    at_row = lax.broadcasted_iota(jnp.int32, (rows, LANES), 0)
    tag = jnp.zeros((rows, LANES), jnp.int32)
    for row in range(rows):
        tag = jnp.where(at_row == row, adapter_list[row_adapter[row]], tag)
    tag = tag.astype(F32).astype(BF16)
    slot = lax.broadcasted_iota(jnp.int32, limits.shape, 0) * (LANES // rank_width)
    slot = slot + lane_of(limits.shape) // rank_width
    limit = jnp.zeros(limits.shape, jnp.int32)
    for held_at in range(ranks.shape[0]):
        limit = jnp.where(slot == held_at, ranks[held_at], limit)
    limits[...] = limit

    group_row = lax.broadcasted_iota(jnp.int32, new_key.shape, 1) == group
    fresh_key = jnp.sum(
        jnp.where(group_row, new_key[...].astype(F32), F32(0.0)), axis=1, keepdims=True
    )
    fresh_value = jnp.sum(
        jnp.where(group_row, new_value[...].astype(F32), F32(0.0)), axis=1, keepdims=True
    )
    score_scale = width ** (-0.5)
    fresh = jnp.sum(queries[...].astype(F32) * fresh_key, axis=-1, keepdims=True) * score_scale
    for part in range(parts):
        at = slice(part * some, (part + 1) * some)
        key_copy, value_copy = cache_copies(part)
        key_copy.wait()
        scores = (
            lax.dot_general(
                queries[at], keys[at], (((2,), (2,)), ((0,), (0,))), preferred_element_type=F32
            )
            * score_scale
        )
        length = jnp.stack(
            [
                jnp.full((heads, positions), lengths[row], jnp.int32)
                for row in range(part * some, (part + 1) * some)
            ]
        )
        valid = lane_of(scores.shape) < length
        masked = jnp.where(valid, scores, F32(-1e30))
        highest = jnp.maximum(jnp.max(masked, axis=-1, keepdims=True), fresh[at])
        cached_exp = jnp.where(valid, jnp.exp(masked - highest), F32(0.0))
        fresh_exp = jnp.exp(fresh[at] - highest)
        totals = jnp.sum(cached_exp, axis=-1, keepdims=True) + fresh_exp
        cached_w = (cached_exp / totals).astype(BF16)
        fresh_w = (fresh_exp / totals).astype(BF16).astype(F32)
        value_copy.wait()
        attended = lax.dot_general(
            cached_w, values[at], (((2,), (1,)), ((0,), (0,))), preferred_element_type=F32
        )
        attended = attended + fresh_w * fresh_value[at]
        spread_out[pl.ds(part * some * heads, some * heads)] = attended.reshape(
            some * heads, width
        )
    tagged[:, heads * width :] = tag
    for head in range(heads):
        tagged[:, head * width : (head + 1) * width] = spread_out[
            pl.ds(head, rows, stride=heads)
        ].astype(BF16)
    early_copy.wait()


def attend(
    early_at,
    block,
    out_weight,
    queries,
    key_cache,
    value_cache,
    new_key,
    new_value,
    lengths,
    adapter_list,
    row_adapter,
    adapter_rank,
    rank_width,
):
    rows, heads, width = queries.shape
    positions = key_cache.shape[2]
    per_group = HQ // KVH
    group_at = (lax.axis_index("tensor") * heads // per_group).reshape(1).astype(jnp.int32)
    full = -(-heads // 8) * 8
    if full != heads:
        queries = jnp.pad(queries, ((0, 0), (0, full - heads), (0, 0)))
    parts = 1
    smem = pl.BlockSpec(memory_space=pltpu.SMEM)
    away = pl.BlockSpec(memory_space=pl.ANY)
    tagged, early, limits = pl.pallas_call(
        functools.partial(attend_kernel, parts, rank_width),
        out_shape=[
            jax.ShapeDtypeStruct((rows, full * width + LANES), BF16),
            VMEM((out_weight.shape[0], block), BF16),
            jax.ShapeDtypeStruct((8, LANES), jnp.int32),
        ],
        in_specs=[smem, smem] + [away] * 10,
        out_specs=[pl.BlockSpec(memory_space=VMEM)] * 3,
        scratch_shapes=[
            VMEM((rows, positions, width), BF16),
            VMEM((rows, positions, width), BF16),
            VMEM(queries.shape, BF16),
            VMEM(new_key.shape, BF16),
            VMEM(new_value.shape, BF16),
            pltpu.SMEM(lengths.shape, jnp.int32),
            pltpu.SMEM(row_adapter.shape, jnp.int32),
            pltpu.SMEM(adapter_list.shape, jnp.int32),
            pltpu.SMEM(adapter_rank.shape, jnp.int32),
            VMEM((rows * full, width), F32),
            pltpu.SemaphoreType.DMA((7,)),
            pltpu.SemaphoreType.DMA((parts,)),
            pltpu.SemaphoreType.DMA((parts,)),
            pltpu.SemaphoreType.DMA,
        ],
        compiler_params=pltpu.CompilerParams(vmem_limit_bytes=8 << 20),
        cost_estimate=pl.CostEstimate(
            flops=4 * rows * heads * positions * width,
            bytes_accessed=4 * rows * positions * width,
            transcendentals=rows * heads * positions,
        ),
        name="attention",
    )(
        group_at,
        early_at,
        *in_hbm(
            key_cache,
            value_cache,
            queries,
            new_key,
            new_value,
            lengths,
            row_adapter,
            adapter_list,
            adapter_rank,
            out_weight,
        ),
    )
    if full != heads:
        tagged = jnp.concatenate([tagged[:, : heads * width], tagged[:, full * width :]], axis=1)
    return tagged, early, limits


def put_stacked(out, start, term, first=0, others=()):
    rows = term.shape[0]
    for column in range(0, term.shape[1], LANES):
        at = first + (start + column) // LANES * rows
        part = term[:, column : column + LANES]
        for other in others:
            part = part + other[at : at + rows].astype(F32)
        out[at : at + rows] = part.astype(out.dtype)


def base_kernel(ahead, deep, arriving, tensor_at, tagged, out_weight, *refs):
    arrived, (*near, out, held, sums, sems) = refs[:arriving], refs[arriving:]
    _, deep_rows, block = held.shape
    width = out_weight.shape[0]
    count = width // deep_rows
    column = pl.ds(pl.multiple_of((tensor_at[0] ^ ahead) * block, block), block)

    def copy(at):
        return pltpu.make_async_copy(
            out_weight.at[pl.ds(at * deep_rows, deep_rows), column],
            held.at[at % deep],
            sems.at[at % deep],
        )

    for at in range(min(deep, count)):
        copy(at).start()
    piece = min(block, 512)
    if near:
        early, early_out = near
        for start in range(0, block, piece):
            columns = slice(start, start + piece)
            term = jnp.dot(tagged[:, :width], early[:, columns], preferred_element_type=F32)
            put_stacked(early_out, start, term)
    for at in range(count):
        copy(at).wait()
        inputs = slice(at * deep_rows, (at + 1) * deep_rows)
        for start in range(0, block, piece):
            columns = slice(start, start + piece)
            term = jnp.dot(
                tagged[:, inputs], held[at % deep, :, columns], preferred_element_type=F32
            )
            if at:
                term = term + sums[:, columns]
            if at < count - 1:
                sums[:, columns] = term
            else:
                put_stacked(out, start, term, 0, arrived)
        if at + deep < count:
            copy(at + deep).start()


def base_block(tensor_at, tagged, out_weight, block, ahead, early=(), arrived=()):
    rows = tagged.shape[0]
    width = out_weight.shape[0]
    deep, deep_rows = 4, min(width, 256)
    whole = pl.BlockSpec(memory_space=VMEM)
    count = 1 + len(early)
    return pl.pallas_call(
        functools.partial(base_kernel, ahead, deep, len(arrived)),
        out_shape=[jax.ShapeDtypeStruct((block // LANES * rows, LANES), BF16 if ahead else F32)]
        * count,
        in_specs=[pl.BlockSpec(memory_space=pltpu.SMEM), whole, pl.BlockSpec(memory_space=pl.ANY)]
        + [whole] * (len(arrived) + len(early)),
        out_specs=[whole] * count,
        scratch_shapes=[
            VMEM((deep, deep_rows, block), BF16),
            VMEM((rows, block), F32),
            pltpu.SemaphoreType.DMA((deep,)),
        ],
        compiler_params=pltpu.CompilerParams(vmem_limit_bytes=12 << 20),
        cost_estimate=pl.CostEstimate(
            flops=2 * rows * width * block * count,
            bytes_accessed=2 * width * block * (2 if arrived else count),
            transcendentals=0,
        ),
        name="base_terms",
    )(tensor_at, tagged, *in_hbm(out_weight), *arrived, *early)


def slots_of(tags, batch_at, pool, tile, per):
    lane = lane_of(tags.shape)
    ids = tags.astype(F32).astype(jnp.int32)
    mine = tile * per + lane // (LANES // per)
    held = tile * per // pool
    return ids - (batch_at[0] ^ held) * pool + held * pool, mine


def shrink_kernel(batch_at, *refs):
    blocks, factors, out = refs[:-3], refs[-3:-1], refs[-1]
    pool, rank_width, width = factors[0].shape
    everyone = jnp.concatenate([block[...] for block in blocks], axis=0)
    per = LANES // rank_width
    lane = lane_of((everyone.shape[0], LANES))
    kept = jnp.zeros(lane.shape, F32)
    for held, weights in enumerate(factors):
        terms = lax.dot_general(
            everyone[:, :width],
            weights[...].reshape(pool * rank_width, width),
            (((1,), (1,)), ((), ())),
            preferred_element_type=F32,
        )
        for tile in range(pool // per):
            slot, mine = slots_of(everyone[:, width:], batch_at, pool, held * pool // per + tile, per)
            kept = kept + jnp.where(
                slot == mine, terms[:, tile * LANES : (tile + 1) * LANES], F32(0.0)
            )
    both = kept + pltpu.roll(kept, rank_width, 1)
    half = both.shape[0] // 2
    packed = jnp.where(lane[:half] < rank_width, both[:half], both[half:])
    out[...] = packed.astype(out.dtype)


def shrink_part(blocks, factors, batch_at):
    pool, rank_width, width = factors[0].shape
    rows = len(blocks) * blocks[0].shape[0]
    smem = pl.BlockSpec(memory_space=pltpu.SMEM)
    whole = pl.BlockSpec(memory_space=VMEM)
    return pl.pallas_call(
        shrink_kernel,
        out_shape=jax.ShapeDtypeStruct((rows // 2, LANES), BF16),
        in_specs=[smem] + [whole] * (len(blocks) + 2),
        out_specs=whole,
        compiler_params=pltpu.CompilerParams(vmem_limit_bytes=8 << 20),
        cost_estimate=pl.CostEstimate(
            flops=4 * rows * width * pool * rank_width,
            bytes_accessed=2 * width * (rows + 2 * pool * rank_width),
            transcendentals=0,
        ),
        name="shrink",
    )(batch_at, *blocks, *factors)


def expand_kernel(count, sums, rank_width, batch_at, *refs):
    limits, refs = refs[:2], refs[2:]
    tags, parts = refs[:count], refs[count : count + sums]
    factors, outs = refs[count + sums : count + sums + 2], refs[count + sums + 2 :]
    tags = jnp.concatenate([tag[...] for tag in tags], axis=0)
    total = parts[0][...].astype(F32)
    for part in parts[1:]:
        total = total + part[...].astype(F32)
    total = total.astype(BF16).astype(F32)
    other = pltpu.roll(total, rank_width, 1)
    low = lane_of(total.shape) < rank_width
    shrink = jnp.concatenate(
        [jnp.where(low, total, other), jnp.where(low, other, total)], axis=0
    )
    per = LANES // rank_width
    inputs, block = factors[0].shape
    pool = inputs // rank_width
    tiles = []
    for tile in range(2 * pool // per):
        slot, mine = slots_of(tags, batch_at, pool, tile, per)
        held, at = divmod(tile * per, pool)
        limit = limits[held][at // per : at // per + 1]
        keep = (slot == mine) & (lane_of(tags.shape) % rank_width < limit)
        tiles.append(jnp.where(keep, shrink, F32(0.0)).astype(BF16))
    half = len(tiles) // 2
    spreads = [jnp.concatenate(tiles[:half], axis=1), jnp.concatenate(tiles[half:], axis=1)]
    rows = tags.shape[0] // count
    piece = min(block, 512)
    for at in range(0, block, piece):
        delta = sum(
            jnp.dot(spread, each[:, at : at + piece], preferred_element_type=F32)
            for spread, each in zip(spreads, factors)
        )
        for which, out in enumerate(outs):
            put_stacked(out, at, delta[which * rows : (which + 1) * rows])


def expand(blocks, parts, factors, limits, batch_at):
    pool, rank_width, block = factors[0].shape
    rows, tagged_width = blocks[0].shape
    count = len(blocks)
    stack = rows * block // LANES
    tag = pl.BlockSpec((rows, LANES), lambda i: (0, tagged_width // LANES - 1))
    full = pl.BlockSpec((pool * rank_width, block), lambda i: (0, 0))
    part = pl.BlockSpec(parts[0].shape, lambda i: (0, 0))
    return pl.pallas_call(
        functools.partial(expand_kernel, count, len(parts), rank_width),
        grid=(1,),
        out_shape=[jax.ShapeDtypeStruct((stack, LANES), BF16) for _ in blocks],
        in_specs=[pl.BlockSpec(memory_space=pltpu.SMEM)]
        + [pl.BlockSpec(each.shape, lambda i: (0, 0)) for each in limits]
        + [tag] * count
        + [part] * len(parts)
        + [full] * 2,
        out_specs=[pl.BlockSpec((stack, LANES), lambda i: (0, 0)) for _ in blocks],
        compiler_params=pltpu.CompilerParams(vmem_limit_bytes=16 << 20),
        cost_estimate=pl.CostEstimate(
            flops=4 * rows * count * pool * rank_width * block,
            bytes_accessed=2 * pool * rank_width * block,
            transcendentals=0,
        ),
        name="expand",
    )(batch_at, *limits, *blocks, *parts, *[each.reshape(pool * rank_width, block) for each in factors])


def total_kernel(*refs):
    terms, out = refs[:-1], refs[-1]
    rows = out.shape[0]
    for column in range(0, out.shape[1], LANES):
        at = slice(column // LANES * rows, (column // LANES + 1) * rows)
        total = terms[0][at].astype(F32)
        for term in terms[1:]:
            total = total + term[at].astype(F32)
        out[:, column : column + LANES] = total.astype(out.dtype)


def total(rows, block, terms):
    whole = pl.BlockSpec(memory_space=VMEM)
    return pl.pallas_call(
        total_kernel,
        out_shape=jax.ShapeDtypeStruct((rows, block), BF16),
        in_specs=[whole] * len(terms),
        out_specs=whole,
        compiler_params=pltpu.CompilerParams(vmem_limit_bytes=8 << 20),
        cost_estimate=pl.CostEstimate(
            flops=rows * block * len(terms),
            bytes_accessed=2 * rows * block * (1 + len(terms)),
            transcendentals=0,
        ),
        name="total",
    )(*terms)


def partial_kernel(*refs):
    terms, out = refs[:-1], refs[-1]
    total = terms[0][...].astype(F32)
    for term in terms[1:]:
        total = total + term[...].astype(F32)
    out[...] = total


def partial_total(terms, weight):
    whole = pl.BlockSpec(memory_space=VMEM)
    return pl.pallas_call(
        partial_kernel,
        out_shape=jax.ShapeDtypeStruct(terms[0].shape, F32),
        in_specs=[whole] * len(terms),
        out_specs=whole,
        compiler_params=pltpu.CompilerParams(vmem_limit_bytes=8 << 20),
        cost_estimate=pl.CostEstimate(
            flops=terms[0].size * len(terms),
            bytes_accessed=4 * terms[0].size + weight,
            transcendentals=0,
        ),
        name="partial_total",
    )(*terms)


def local(
    tensor_size,
    batch_size,
    queries,
    key_cache,
    value_cache,
    new_key,
    new_value,
    lengths,
    out_weight,
    shrink_weight,
    expand_weight,
    adapter_rank,
    adapter_list,
    row_adapter,
):
    rows = queries.shape[0]
    block = expand_weight.shape[2]
    chips = batch_size // 2
    batch_at = lax.axis_index("batch").reshape(1).astype(jnp.int32)
    tensor_at = lax.axis_index("tensor").reshape(1).astype(jnp.int32)

    def to_sibling(array):
        return permuted(array, "batch", batch_size, lambda i: i ^ 1)

    def to_chip(array, shift):
        return permuted(array, "batch", batch_size, lambda i: (i + 2 * shift) % batch_size)

    def across(array, bit):
        return permuted(array, "tensor", tensor_size, lambda i: i ^ bit)

    def wide(array):
        return array.astype(F32)

    stack = block // LANES * rows
    tagged, early, limits = attend(
        tensor_at ^ 3,
        block,
        out_weight,
        queries,
        key_cache,
        value_cache,
        new_key,
        new_value,
        lengths,
        adapter_list,
        row_adapter,
        adapter_rank,
        shrink_weight.shape[2],
    )
    limits = [limits, to_sibling(limits)]
    shrink_weight = jnp.swapaxes(shrink_weight, 1, 2)
    shrink_factors = [shrink_weight, to_sibling(shrink_weight)]
    visiting = [to_chip(tagged, shift) for shift in range(1, chips)]
    third, next_door = base_block(tensor_at, tagged, out_weight, block, 1, [early])
    visiting, third, next_door, limits = lax.optimization_barrier(
        (visiting, third, next_door, limits)
    )
    blocks = [tagged] + visiting
    third = across(third, 1)

    part = shrink_part(blocks, shrink_factors, batch_at)
    parts = [part, across(part, 1)]
    part, later_tagged, expand_weight = lax.optimization_barrier((part, tagged, expand_weight))
    expand_factors = [expand_weight, to_sibling(expand_weight)]
    (second,) = base_block(tensor_at, later_tagged, out_weight, block, 2)
    second = (wide(second) + wide(third)).astype(BF16)
    parts, second = lax.optimization_barrier((parts, second))
    bit = 2
    while bit < tensor_size:
        part = (wide(parts[0]) + wide(parts[1])).astype(BF16)
        part, next_door = lax.optimization_barrier((part, next_door))
        parts = [part, across(part, bit)]
        bit *= 2
    arrived = [across(second, 2), across(next_door, 1)]
    for ahead in range(4, tensor_size, 2):
        (near,) = base_block(tensor_at, tagged, out_weight, block, ahead)
        (far,) = base_block(tensor_at, tagged, out_weight, block, ahead + 1)
        arrived.append(across((wide(near) + wide(across(far, 1))).astype(BF16), ahead))

    deltas = expand(blocks, parts, expand_factors, limits, batch_at)
    deltas, late_tagged = lax.optimization_barrier((deltas, tagged))
    (own,) = base_block(tensor_at, late_tagged, out_weight, block, 0)
    so_far = partial_total([own, deltas[0], arrived[0], *arrived[2:]], 0)
    terms = [partial_total([so_far, arrived[1]], 8 << 20)]
    terms += [to_chip(home, -shift) for shift, home in enumerate(deltas[1:], 1)]
    return total(rows, block, terms)


def solution(mesh):
    placed = (
        P(("groups", "batch"), "tensor", None),
        P(("groups", "batch"), None, None, None),
        P(("groups", "batch"), None, None, None),
        P(("groups", "batch"), None, None),
        P(("groups", "batch"), None, None),
        P(("groups", "batch")),
        P("tensor", None),
        P("batch", "tensor", None),
        P("batch", None, "tensor"),
        P("batch"),
        P(("groups", "batch")),
        P(("groups", "batch")),
    )

    def placed_local(*arrays):
        return local(mesh.shape["tensor"], mesh.shape["batch"], *arrays)

    return jax.shard_map(
        placed_local,
        mesh=mesh,
        in_specs=placed,
        out_specs=P(("groups", "batch"), "tensor"),
        check_vma=False,
    )
```

```python
import functools

import jax
import jax.numpy as jnp
from jax import lax
from jax.experimental import pallas as pl
from jax.experimental.pallas import tpu as pltpu
from jax.sharding import PartitionSpec as P

HQ = 32
KVH = 4
LANES = 128
VMEM = pltpu.VMEM
GRANT = 56 << 20
F32, BF16 = jnp.float32, jnp.bfloat16


def permuted(array, axis, size, partner):
    return lax.ppermute(array, axis, [(i, partner(i)) for i in range(size)])


def in_hbm(*arrays):
    return [pltpu.with_memory_space_constraint(array, pltpu.HBM) for array in arrays]


def lane_of(shape):
    return lax.broadcasted_iota(jnp.int32, shape, len(shape) - 1)


def attend_kernel(parts, rank_width, group_at, early_at, *refs):
    given, (out_weight, tagged, early, limits, *scratch) = refs[:9], refs[9:]
    held, (spread_out, small_sems, key_sems, value_sems, early_sem) = scratch[:9], scratch[9:]
    key_cache, value_cache = given[:2]
    keys, values, queries, new_key, new_value, lengths, row_adapter, adapter_list, ranks = held
    rows, heads, width = queries.shape
    positions = key_cache.shape[2]
    group = group_at[0]
    some = rows // parts

    def cache_copies(part):
        at = pl.ds(part * some, some)
        return (
            pltpu.make_async_copy(key_cache.at[at, group], keys.at[at], key_sems.at[part]),
            pltpu.make_async_copy(value_cache.at[at, group], values.at[at], value_sems.at[part]),
        )

    small = [
        pltpu.make_async_copy(given[i], held[i], small_sems.at[i - 2]) for i in range(2, 9)
    ]
    for copy in small:
        copy.start()
    for part in range(parts):
        for copy in cache_copies(part):
            copy.start()
    block = early.shape[1]
    start = pl.multiple_of(early_at[0] * block, block)
    early_copy = pltpu.make_async_copy(out_weight.at[:, pl.ds(start, block)], early, early_sem)
    early_copy.start()
    for copy in small:
        copy.wait()
    at_row = lax.broadcasted_iota(jnp.int32, (rows, LANES), 0)
    tag = jnp.zeros((rows, LANES), jnp.int32)
    for row in range(rows):
        tag = jnp.where(at_row == row, adapter_list[row_adapter[row]], tag)
    tag = tag.astype(F32).astype(BF16)
    slot = lax.broadcasted_iota(jnp.int32, limits.shape, 0) * (LANES // rank_width)
    slot = slot + lane_of(limits.shape) // rank_width
    limit = jnp.zeros(limits.shape, jnp.int32)
    for held_at in range(ranks.shape[0]):
        limit = jnp.where(slot == held_at, ranks[held_at], limit)
    limits[...] = limit

    group_row = lax.broadcasted_iota(jnp.int32, new_key.shape, 1) == group
    fresh_key = jnp.sum(
        jnp.where(group_row, new_key[...].astype(F32), F32(0.0)), axis=1, keepdims=True
    )
    fresh_value = jnp.sum(
        jnp.where(group_row, new_value[...].astype(F32), F32(0.0)), axis=1, keepdims=True
    )
    score_scale = width ** (-0.5)
    fresh = jnp.sum(queries[...].astype(F32) * fresh_key, axis=-1, keepdims=True) * score_scale
    for part in range(parts):
        at = slice(part * some, (part + 1) * some)
        key_copy, value_copy = cache_copies(part)
        key_copy.wait()
        scores = (
            lax.dot_general(
                queries[at], keys[at], (((2,), (2,)), ((0,), (0,))), preferred_element_type=F32
            )
            * score_scale
        )
        length = jnp.stack(
            [
                jnp.full((heads, positions), lengths[row], jnp.int32)
                for row in range(part * some, (part + 1) * some)
            ]
        )
        valid = lane_of(scores.shape) < length
        masked = jnp.where(valid, scores, F32(-1e30))
        highest = jnp.maximum(jnp.max(masked, axis=-1, keepdims=True), fresh[at])
        cached_exp = jnp.where(valid, jnp.exp(masked - highest), F32(0.0))
        fresh_exp = jnp.exp(fresh[at] - highest)
        totals = jnp.sum(cached_exp, axis=-1, keepdims=True) + fresh_exp
        cached_w = (cached_exp / totals).astype(BF16)
        fresh_w = (fresh_exp / totals).astype(BF16).astype(F32)
        value_copy.wait()
        attended = lax.dot_general(
            cached_w, values[at], (((2,), (1,)), ((0,), (0,))), preferred_element_type=F32
        )
        attended = attended + fresh_w * fresh_value[at]
        spread_out[pl.ds(part * some * heads, some * heads)] = attended.reshape(
            some * heads, width
        )
    tagged[:, heads * width :] = tag
    for head in range(heads):
        tagged[:, head * width : (head + 1) * width] = spread_out[
            pl.ds(head, rows, stride=heads)
        ].astype(BF16)
    early_copy.wait()


def attend(
    early_at,
    block,
    out_weight,
    queries,
    key_cache,
    value_cache,
    new_key,
    new_value,
    lengths,
    adapter_list,
    row_adapter,
    adapter_rank,
    rank_width,
):
    rows, heads, width = queries.shape
    positions = key_cache.shape[2]
    per_group = HQ // KVH
    group_at = (lax.axis_index("tensor") * heads // per_group).reshape(1).astype(jnp.int32)
    full = -(-heads // 8) * 8
    if full != heads:
        queries = jnp.pad(queries, ((0, 0), (0, full - heads), (0, 0)))
    parts = 1
    smem = pl.BlockSpec(memory_space=pltpu.SMEM)
    away = pl.BlockSpec(memory_space=pl.ANY)
    tagged, early, limits = pl.pallas_call(
        functools.partial(attend_kernel, parts, rank_width),
        out_shape=[
            jax.ShapeDtypeStruct((rows, full * width + LANES), BF16),
            VMEM((out_weight.shape[0], block), BF16),
            jax.ShapeDtypeStruct((8, LANES), jnp.int32),
        ],
        in_specs=[smem, smem] + [away] * 10,
        out_specs=[pl.BlockSpec(memory_space=VMEM)] * 3,
        scratch_shapes=[
            VMEM((rows, positions, width), BF16),
            VMEM((rows, positions, width), BF16),
            VMEM(queries.shape, BF16),
            VMEM(new_key.shape, BF16),
            VMEM(new_value.shape, BF16),
            pltpu.SMEM(lengths.shape, jnp.int32),
            pltpu.SMEM(row_adapter.shape, jnp.int32),
            pltpu.SMEM(adapter_list.shape, jnp.int32),
            pltpu.SMEM(adapter_rank.shape, jnp.int32),
            VMEM((rows * full, width), F32),
            pltpu.SemaphoreType.DMA((7,)),
            pltpu.SemaphoreType.DMA((parts,)),
            pltpu.SemaphoreType.DMA((parts,)),
            pltpu.SemaphoreType.DMA,
        ],
        compiler_params=pltpu.CompilerParams(vmem_limit_bytes=8 << 20),
        cost_estimate=pl.CostEstimate(
            flops=4 * rows * heads * positions * width,
            bytes_accessed=4 * rows * positions * width,
            transcendentals=rows * heads * positions,
        ),
        name="attention",
    )(
        group_at,
        early_at,
        *in_hbm(
            key_cache,
            value_cache,
            queries,
            new_key,
            new_value,
            lengths,
            row_adapter,
            adapter_list,
            adapter_rank,
            out_weight,
        ),
    )
    if full != heads:
        tagged = jnp.concatenate([tagged[:, : heads * width], tagged[:, full * width :]], axis=1)
    return tagged, early, limits


def put_stacked(out, start, term, first=0, others=()):
    rows = term.shape[0]
    for column in range(0, term.shape[1], LANES):
        at = first + (start + column) // LANES * rows
        part = term[:, column : column + LANES]
        for other in others:
            part = part + other[at : at + rows].astype(F32)
        out[at : at + rows] = part.astype(out.dtype)


def base_kernel(ahead, deep, arriving, tensor_at, tagged, out_weight, *refs):
    arrived, (*near, out, held, sums, sems) = refs[:arriving], refs[arriving:]
    _, deep_rows, block = held.shape
    width = out_weight.shape[0]
    count = width // deep_rows
    column = pl.ds(pl.multiple_of((tensor_at[0] ^ ahead) * block, block), block)

    def copy(at):
        return pltpu.make_async_copy(
            out_weight.at[pl.ds(at * deep_rows, deep_rows), column],
            held.at[at % deep],
            sems.at[at % deep],
        )

    for at in range(min(deep, count)):
        copy(at).start()
    piece = min(block, 512)
    if near:
        early, early_out = near
        for start in range(0, block, piece):
            columns = slice(start, start + piece)
            term = jnp.dot(tagged[:, :width], early[:, columns], preferred_element_type=F32)
            put_stacked(early_out, start, term)
    for at in range(count):
        copy(at).wait()
        inputs = slice(at * deep_rows, (at + 1) * deep_rows)
        for start in range(0, block, piece):
            columns = slice(start, start + piece)
            term = jnp.dot(
                tagged[:, inputs], held[at % deep, :, columns], preferred_element_type=F32
            )
            if at:
                term = term + sums[:, columns]
            if at < count - 1:
                sums[:, columns] = term
            else:
                put_stacked(out, start, term, 0, arrived)
        if at + deep < count:
            copy(at + deep).start()


def base_block(tensor_at, tagged, out_weight, block, ahead, early=(), arrived=()):
    rows = tagged.shape[0]
    width = out_weight.shape[0]
    deep, deep_rows = 4, min(width, 256)
    whole = pl.BlockSpec(memory_space=VMEM)
    count = 1 + len(early)
    return pl.pallas_call(
        functools.partial(base_kernel, ahead, deep, len(arrived)),
        out_shape=[jax.ShapeDtypeStruct((block // LANES * rows, LANES), BF16 if ahead else F32)]
        * count,
        in_specs=[pl.BlockSpec(memory_space=pltpu.SMEM), whole, pl.BlockSpec(memory_space=pl.ANY)]
        + [whole] * (len(arrived) + len(early)),
        out_specs=[whole] * count,
        scratch_shapes=[
            VMEM((deep, deep_rows, block), BF16),
            VMEM((rows, block), F32),
            pltpu.SemaphoreType.DMA((deep,)),
        ],
        compiler_params=pltpu.CompilerParams(vmem_limit_bytes=12 << 20),
        cost_estimate=pl.CostEstimate(
            flops=2 * rows * width * block * count,
            bytes_accessed=2 * width * block * (2 if arrived else count),
            transcendentals=0,
        ),
        name="base_terms",
    )(tensor_at, tagged, *in_hbm(out_weight), *arrived, *early)


def slots_of(tags, batch_at, pool, tile, per):
    lane = lane_of(tags.shape)
    ids = tags.astype(F32).astype(jnp.int32)
    mine = tile * per + lane // (LANES // per)
    held = tile * per // pool
    return ids - (batch_at[0] ^ held) * pool + held * pool, mine


def shrink_kernel(batch_at, *refs):
    blocks, factors, out = refs[:-3], refs[-3:-1], refs[-1]
    pool, rank_width, width = factors[0].shape
    everyone = jnp.concatenate([block[...] for block in blocks], axis=0)
    per = LANES // rank_width
    lane = lane_of((everyone.shape[0], LANES))
    kept = jnp.zeros(lane.shape, F32)
    for held, weights in enumerate(factors):
        terms = lax.dot_general(
            everyone[:, :width],
            weights[...].reshape(pool * rank_width, width),
            (((1,), (1,)), ((), ())),
            preferred_element_type=F32,
        )
        for tile in range(pool // per):
            slot, mine = slots_of(everyone[:, width:], batch_at, pool, held * pool // per + tile, per)
            kept = kept + jnp.where(
                slot == mine, terms[:, tile * LANES : (tile + 1) * LANES], F32(0.0)
            )
    both = kept + pltpu.roll(kept, rank_width, 1)
    half = both.shape[0] // 2
    packed = jnp.where(lane[:half] < rank_width, both[:half], both[half:])
    out[...] = packed.astype(out.dtype)


def shrink_part(blocks, factors, batch_at):
    pool, rank_width, width = factors[0].shape
    rows = len(blocks) * blocks[0].shape[0]
    smem = pl.BlockSpec(memory_space=pltpu.SMEM)
    whole = pl.BlockSpec(memory_space=VMEM)
    return pl.pallas_call(
        shrink_kernel,
        out_shape=jax.ShapeDtypeStruct((rows // 2, LANES), BF16),
        in_specs=[smem] + [whole] * (len(blocks) + 2),
        out_specs=whole,
        compiler_params=pltpu.CompilerParams(vmem_limit_bytes=8 << 20),
        cost_estimate=pl.CostEstimate(
            flops=4 * rows * width * pool * rank_width,
            bytes_accessed=2 * width * (rows + 2 * pool * rank_width),
            transcendentals=0,
        ),
        name="shrink",
    )(batch_at, *blocks, *factors)


def expand_kernel(count, sums, rank_width, batch_at, *refs):
    limits, refs = refs[:2], refs[2:]
    tags, parts = refs[:count], refs[count : count + sums]
    factors, outs = refs[count + sums : count + sums + 2], refs[count + sums + 2 :]
    tags = jnp.concatenate([tag[...] for tag in tags], axis=0)
    total = parts[0][...].astype(F32)
    for part in parts[1:]:
        total = total + part[...].astype(F32)
    total = total.astype(BF16).astype(F32)
    other = pltpu.roll(total, rank_width, 1)
    low = lane_of(total.shape) < rank_width
    shrink = jnp.concatenate(
        [jnp.where(low, total, other), jnp.where(low, other, total)], axis=0
    )
    per = LANES // rank_width
    inputs, block = factors[0].shape
    pool = inputs // rank_width
    tiles = []
    for tile in range(2 * pool // per):
        slot, mine = slots_of(tags, batch_at, pool, tile, per)
        held, at = divmod(tile * per, pool)
        limit = limits[held][at // per : at // per + 1]
        keep = (slot == mine) & (lane_of(tags.shape) % rank_width < limit)
        tiles.append(jnp.where(keep, shrink, F32(0.0)).astype(BF16))
    half = len(tiles) // 2
    spreads = [jnp.concatenate(tiles[:half], axis=1), jnp.concatenate(tiles[half:], axis=1)]
    rows = tags.shape[0] // count
    piece = min(block, 512)
    for at in range(0, block, piece):
        delta = sum(
            jnp.dot(spread, each[:, at : at + piece], preferred_element_type=F32)
            for spread, each in zip(spreads, factors)
        )
        for which, out in enumerate(outs):
            put_stacked(out, at, delta[which * rows : (which + 1) * rows])


def expand(blocks, parts, factors, limits, batch_at):
    pool, rank_width, block = factors[0].shape
    rows, tagged_width = blocks[0].shape
    count = len(blocks)
    stack = rows * block // LANES
    tag = pl.BlockSpec((rows, LANES), lambda i: (0, tagged_width // LANES - 1))
    full = pl.BlockSpec((pool * rank_width, block), lambda i: (0, 0))
    part = pl.BlockSpec(parts[0].shape, lambda i: (0, 0))
    return pl.pallas_call(
        functools.partial(expand_kernel, count, len(parts), rank_width),
        grid=(1,),
        out_shape=[jax.ShapeDtypeStruct((stack, LANES), BF16) for _ in blocks],
        in_specs=[pl.BlockSpec(memory_space=pltpu.SMEM)]
        + [pl.BlockSpec(each.shape, lambda i: (0, 0)) for each in limits]
        + [tag] * count
        + [part] * len(parts)
        + [full] * 2,
        out_specs=[pl.BlockSpec((stack, LANES), lambda i: (0, 0)) for _ in blocks],
        compiler_params=pltpu.CompilerParams(vmem_limit_bytes=16 << 20),
        cost_estimate=pl.CostEstimate(
            flops=4 * rows * count * pool * rank_width * block,
            bytes_accessed=2 * pool * rank_width * block,
            transcendentals=0,
        ),
        name="expand",
    )(batch_at, *limits, *blocks, *parts, *[each.reshape(pool * rank_width, block) for each in factors])


def total_kernel(*refs):
    terms, out = refs[:-1], refs[-1]
    rows = out.shape[0]
    for column in range(0, out.shape[1], LANES):
        at = slice(column // LANES * rows, (column // LANES + 1) * rows)
        total = terms[0][at].astype(F32)
        for term in terms[1:]:
            total = total + term[at].astype(F32)
        out[:, column : column + LANES] = total.astype(out.dtype)


def total(rows, block, terms):
    whole = pl.BlockSpec(memory_space=VMEM)
    return pl.pallas_call(
        total_kernel,
        out_shape=jax.ShapeDtypeStruct((rows, block), BF16),
        in_specs=[whole] * len(terms),
        out_specs=whole,
        compiler_params=pltpu.CompilerParams(vmem_limit_bytes=8 << 20),
        cost_estimate=pl.CostEstimate(
            flops=rows * block * len(terms),
            bytes_accessed=2 * rows * block * (1 + len(terms)),
            transcendentals=0,
        ),
        name="total",
    )(*terms)


def partial_kernel(*refs):
    terms, out = refs[:-1], refs[-1]
    total = terms[0][...].astype(F32)
    for term in terms[1:]:
        total = total + term[...].astype(F32)
    out[...] = total


def partial_total(terms, weight):
    whole = pl.BlockSpec(memory_space=VMEM)
    return pl.pallas_call(
        partial_kernel,
        out_shape=jax.ShapeDtypeStruct(terms[0].shape, F32),
        in_specs=[whole] * len(terms),
        out_specs=whole,
        compiler_params=pltpu.CompilerParams(vmem_limit_bytes=8 << 20),
        cost_estimate=pl.CostEstimate(
            flops=terms[0].size * len(terms),
            bytes_accessed=4 * terms[0].size + weight,
            transcendentals=0,
        ),
        name="partial_total",
    )(*terms)


def local(
    tensor_size,
    batch_size,
    queries,
    key_cache,
    value_cache,
    new_key,
    new_value,
    lengths,
    out_weight,
    shrink_weight,
    expand_weight,
    adapter_rank,
    adapter_list,
    row_adapter,
):
    rows = queries.shape[0]
    block = expand_weight.shape[2]
    chips = batch_size // 2
    batch_at = lax.axis_index("batch").reshape(1).astype(jnp.int32)
    tensor_at = lax.axis_index("tensor").reshape(1).astype(jnp.int32)

    def to_sibling(array):
        return permuted(array, "batch", batch_size, lambda i: i ^ 1)

    def to_chip(array, shift):
        return permuted(array, "batch", batch_size, lambda i: (i + 2 * shift) % batch_size)

    def across(array, bit):
        return permuted(array, "tensor", tensor_size, lambda i: i ^ bit)

    def wide(array):
        return array.astype(F32)

    stack = block // LANES * rows
    tagged, early, limits = attend(
        tensor_at ^ 3,
        block,
        out_weight,
        queries,
        key_cache,
        value_cache,
        new_key,
        new_value,
        lengths,
        adapter_list,
        row_adapter,
        adapter_rank,
        shrink_weight.shape[2],
    )
    limits = [limits, to_sibling(limits)]
    shrink_weight = jnp.swapaxes(shrink_weight, 1, 2)
    shrink_factors = [shrink_weight, to_sibling(shrink_weight)]
    visiting = [to_chip(tagged, shift) for shift in range(1, chips)]
    third, next_door = base_block(tensor_at, tagged, out_weight, block, 1, [early])
    visiting, third, next_door, limits = lax.optimization_barrier(
        (visiting, third, next_door, limits)
    )
    blocks = [tagged] + visiting
    third = across(third, 1)

    part = shrink_part(blocks, shrink_factors, batch_at)
    parts = [part, across(part, 1)]
    part, later_tagged = lax.optimization_barrier((part, tagged))
    (second,) = base_block(tensor_at, later_tagged, out_weight, block, 2)
    second = (wide(second) + wide(third)).astype(BF16)
    parts, second, expand_weight = lax.optimization_barrier((parts, second, expand_weight))
    expand_factors = [expand_weight, to_sibling(expand_weight)]
    bit = 2
    while bit < tensor_size:
        part = (wide(parts[0]) + wide(parts[1])).astype(BF16)
        part, next_door = lax.optimization_barrier((part, next_door))
        parts = [part, across(part, bit)]
        bit *= 2
    arrived = [across(second, 2), across(next_door, 1)]
    for ahead in range(4, tensor_size, 2):
        (near,) = base_block(tensor_at, tagged, out_weight, block, ahead)
        (far,) = base_block(tensor_at, tagged, out_weight, block, ahead + 1)
        arrived.append(across((wide(near) + wide(across(far, 1))).astype(BF16), ahead))

    deltas = expand(blocks, parts, expand_factors, limits, batch_at)
    deltas, late_tagged = lax.optimization_barrier((deltas, tagged))
    (own,) = base_block(tensor_at, late_tagged, out_weight, block, 0)
    so_far = partial_total([own, deltas[0], arrived[0], *arrived[2:]], 0)
    terms = [partial_total([so_far, arrived[1]], 8 << 20)]
    terms += [to_chip(home, -shift) for shift, home in enumerate(deltas[1:], 1)]
    return total(rows, block, terms)


def solution(mesh):
    placed = (
        P(("groups", "batch"), "tensor", None),
        P(("groups", "batch"), None, None, None),
        P(("groups", "batch"), None, None, None),
        P(("groups", "batch"), None, None),
        P(("groups", "batch"), None, None),
        P(("groups", "batch")),
        P("tensor", None),
        P("batch", "tensor", None),
        P("batch", None, "tensor"),
        P("batch"),
        P(("groups", "batch")),
        P(("groups", "batch")),
    )

    def placed_local(*arrays):
        return local(mesh.shape["tensor"], mesh.shape["batch"], *arrays)

    return jax.shard_map(
        placed_local,
        mesh=mesh,
        in_specs=placed,
        out_specs=P(("groups", "batch"), "tensor"),
        check_vma=False,
    )
```

```python
import functools

import jax
import jax.numpy as jnp
from jax import lax
from jax.experimental import pallas as pl
from jax.experimental.pallas import tpu as pltpu
from jax.sharding import PartitionSpec as P

HQ = 32
KVH = 4
LANES = 128
VMEM = pltpu.VMEM
GRANT = 56 << 20
F32, BF16 = jnp.float32, jnp.bfloat16


def permuted(array, axis, size, partner):
    return lax.ppermute(array, axis, [(i, partner(i)) for i in range(size)])


def in_hbm(*arrays):
    return [pltpu.with_memory_space_constraint(array, pltpu.HBM) for array in arrays]


def lane_of(shape):
    return lax.broadcasted_iota(jnp.int32, shape, len(shape) - 1)


def attend_kernel(parts, rank_width, group_at, early_at, *refs):
    given, (out_weight, tagged, early, limits, *scratch) = refs[:9], refs[9:]
    held, (spread_out, small_sems, key_sems, value_sems, early_sem) = scratch[:9], scratch[9:]
    key_cache, value_cache = given[:2]
    keys, values, queries, new_key, new_value, lengths, row_adapter, adapter_list, ranks = held
    rows, heads, width = queries.shape
    positions = key_cache.shape[2]
    group = group_at[0]
    some = rows // parts

    def cache_copies(part):
        at = pl.ds(part * some, some)
        return (
            pltpu.make_async_copy(key_cache.at[at, group], keys.at[at], key_sems.at[part]),
            pltpu.make_async_copy(value_cache.at[at, group], values.at[at], value_sems.at[part]),
        )

    small = [
        pltpu.make_async_copy(given[i], held[i], small_sems.at[i - 2]) for i in range(2, 9)
    ]
    for copy in small:
        copy.start()
    for part in range(parts):
        for copy in cache_copies(part):
            copy.start()
    block = early.shape[1]
    start = pl.multiple_of(early_at[0] * block, block)
    early_copy = pltpu.make_async_copy(out_weight.at[:, pl.ds(start, block)], early, early_sem)
    early_copy.start()
    for copy in small:
        copy.wait()
    at_row = lax.broadcasted_iota(jnp.int32, (rows, LANES), 0)
    tag = jnp.zeros((rows, LANES), jnp.int32)
    for row in range(rows):
        tag = jnp.where(at_row == row, adapter_list[row_adapter[row]], tag)
    tag = tag.astype(F32).astype(BF16)
    slot = lax.broadcasted_iota(jnp.int32, limits.shape, 0) * (LANES // rank_width)
    slot = slot + lane_of(limits.shape) // rank_width
    limit = jnp.zeros(limits.shape, jnp.int32)
    for held_at in range(ranks.shape[0]):
        limit = jnp.where(slot == held_at, ranks[held_at], limit)
    limits[...] = limit

    group_row = lax.broadcasted_iota(jnp.int32, new_key.shape, 1) == group
    fresh_key = jnp.sum(
        jnp.where(group_row, new_key[...].astype(F32), F32(0.0)), axis=1, keepdims=True
    )
    fresh_value = jnp.sum(
        jnp.where(group_row, new_value[...].astype(F32), F32(0.0)), axis=1, keepdims=True
    )
    score_scale = width ** (-0.5)
    fresh = jnp.sum(queries[...].astype(F32) * fresh_key, axis=-1, keepdims=True) * score_scale
    for part in range(parts):
        at = slice(part * some, (part + 1) * some)
        key_copy, value_copy = cache_copies(part)
        key_copy.wait()
        scores = (
            lax.dot_general(
                queries[at], keys[at], (((2,), (2,)), ((0,), (0,))), preferred_element_type=F32
            )
            * score_scale
        )
        length = jnp.stack(
            [
                jnp.full((heads, positions), lengths[row], jnp.int32)
                for row in range(part * some, (part + 1) * some)
            ]
        )
        valid = lane_of(scores.shape) < length
        masked = jnp.where(valid, scores, F32(-1e30))
        highest = jnp.maximum(jnp.max(masked, axis=-1, keepdims=True), fresh[at])
        cached_exp = jnp.where(valid, jnp.exp(masked - highest), F32(0.0))
        fresh_exp = jnp.exp(fresh[at] - highest)
        totals = jnp.sum(cached_exp, axis=-1, keepdims=True) + fresh_exp
        cached_w = (cached_exp / totals).astype(BF16)
        fresh_w = (fresh_exp / totals).astype(BF16).astype(F32)
        value_copy.wait()
        attended = lax.dot_general(
            cached_w, values[at], (((2,), (1,)), ((0,), (0,))), preferred_element_type=F32
        )
        attended = attended + fresh_w * fresh_value[at]
        spread_out[pl.ds(part * some * heads, some * heads)] = attended.reshape(
            some * heads, width
        )
    tagged[:, heads * width :] = tag
    for head in range(heads):
        tagged[:, head * width : (head + 1) * width] = spread_out[
            pl.ds(head, rows, stride=heads)
        ].astype(BF16)
    early_copy.wait()


def attend(
    early_at,
    block,
    out_weight,
    queries,
    key_cache,
    value_cache,
    new_key,
    new_value,
    lengths,
    adapter_list,
    row_adapter,
    adapter_rank,
    rank_width,
):
    rows, heads, width = queries.shape
    positions = key_cache.shape[2]
    per_group = HQ // KVH
    group_at = (lax.axis_index("tensor") * heads // per_group).reshape(1).astype(jnp.int32)
    full = -(-heads // 8) * 8
    if full != heads:
        queries = jnp.pad(queries, ((0, 0), (0, full - heads), (0, 0)))
    parts = 2
    smem = pl.BlockSpec(memory_space=pltpu.SMEM)
    away = pl.BlockSpec(memory_space=pl.ANY)
    tagged, early, limits = pl.pallas_call(
        functools.partial(attend_kernel, parts, rank_width),
        out_shape=[
            jax.ShapeDtypeStruct((rows, full * width + LANES), BF16),
            VMEM((out_weight.shape[0], block), BF16),
            jax.ShapeDtypeStruct((8, LANES), jnp.int32),
        ],
        in_specs=[smem, smem] + [away] * 10,
        out_specs=[pl.BlockSpec(memory_space=VMEM)] * 3,
        scratch_shapes=[
            VMEM((rows, positions, width), BF16),
            VMEM((rows, positions, width), BF16),
            VMEM(queries.shape, BF16),
            VMEM(new_key.shape, BF16),
            VMEM(new_value.shape, BF16),
            pltpu.SMEM(lengths.shape, jnp.int32),
            pltpu.SMEM(row_adapter.shape, jnp.int32),
            pltpu.SMEM(adapter_list.shape, jnp.int32),
            pltpu.SMEM(adapter_rank.shape, jnp.int32),
            VMEM((rows * full, width), F32),
            pltpu.SemaphoreType.DMA((7,)),
            pltpu.SemaphoreType.DMA((parts,)),
            pltpu.SemaphoreType.DMA((parts,)),
            pltpu.SemaphoreType.DMA,
        ],
        compiler_params=pltpu.CompilerParams(vmem_limit_bytes=8 << 20),
        cost_estimate=pl.CostEstimate(
            flops=4 * rows * heads * positions * width,
            bytes_accessed=4 * rows * positions * width,
            transcendentals=rows * heads * positions,
        ),
        name="attention",
    )(
        group_at,
        early_at,
        *in_hbm(
            key_cache,
            value_cache,
            queries,
            new_key,
            new_value,
            lengths,
            row_adapter,
            adapter_list,
            adapter_rank,
            out_weight,
        ),
    )
    if full != heads:
        tagged = jnp.concatenate([tagged[:, : heads * width], tagged[:, full * width :]], axis=1)
    return tagged, early, limits


def put_stacked(out, start, term, first=0, others=()):
    rows = term.shape[0]
    for column in range(0, term.shape[1], LANES):
        at = first + (start + column) // LANES * rows
        part = term[:, column : column + LANES]
        for other in others:
            part = part + other[at : at + rows].astype(F32)
        out[at : at + rows] = part.astype(out.dtype)


def fetch_kernel(ahead, tensor_at, tagged, early, out_weight, out, fetched, sem):
    width, block = fetched.shape
    column = pl.ds(pl.multiple_of((tensor_at[0] ^ ahead) * block, block), block)
    copy = pltpu.make_async_copy(out_weight.at[:, column], fetched, sem)
    copy.start()
    piece = min(block, 512)
    for start in range(0, block, piece):
        columns = slice(start, start + piece)
        term = jnp.dot(tagged[:, :width], early[:, columns], preferred_element_type=F32)
        put_stacked(out, start, term)
    copy.wait()


def base_and_fetch(tensor_at, tagged, early, out_weight, ahead):
    rows = tagged.shape[0]
    width, block = early.shape
    whole = pl.BlockSpec(memory_space=VMEM)
    return pl.pallas_call(
        functools.partial(fetch_kernel, ahead),
        out_shape=[
            jax.ShapeDtypeStruct((block // LANES * rows, LANES), BF16),
            VMEM((width, block), BF16),
        ],
        in_specs=[
            pl.BlockSpec(memory_space=pltpu.SMEM),
            whole,
            whole,
            pl.BlockSpec(memory_space=pl.ANY),
        ],
        out_specs=[whole] * 2,
        scratch_shapes=[pltpu.SemaphoreType.DMA],
        compiler_params=pltpu.CompilerParams(vmem_limit_bytes=8 << 20),
        cost_estimate=pl.CostEstimate(
            flops=2 * rows * width * block,
            bytes_accessed=4 * width * block,
            transcendentals=0,
        ),
        name="base_and_fetch",
    )(tensor_at, tagged, early, *in_hbm(out_weight))


def base_kernel(ahead, deep, arriving, tensor_at, tagged, out_weight, *refs):
    arrived, (*near, out, held, sums, sems) = refs[:arriving], refs[arriving:]
    _, deep_rows, block = held.shape
    width = out_weight.shape[0]
    count = width // deep_rows
    column = pl.ds(pl.multiple_of((tensor_at[0] ^ ahead) * block, block), block)

    def copy(at):
        return pltpu.make_async_copy(
            out_weight.at[pl.ds(at * deep_rows, deep_rows), column],
            held.at[at % deep],
            sems.at[at % deep],
        )

    for at in range(min(deep, count)):
        copy(at).start()
    piece = min(block, 512)
    if near:
        early, early_out = near
        for start in range(0, block, piece):
            columns = slice(start, start + piece)
            term = jnp.dot(tagged[:, :width], early[:, columns], preferred_element_type=F32)
            put_stacked(early_out, start, term)
    for at in range(count):
        copy(at).wait()
        inputs = slice(at * deep_rows, (at + 1) * deep_rows)
        for start in range(0, block, piece):
            columns = slice(start, start + piece)
            term = jnp.dot(
                tagged[:, inputs], held[at % deep, :, columns], preferred_element_type=F32
            )
            if at:
                term = term + sums[:, columns]
            if at < count - 1:
                sums[:, columns] = term
            else:
                put_stacked(out, start, term, 0, arrived)
        if at + deep < count:
            copy(at + deep).start()


def base_block(tensor_at, tagged, out_weight, block, ahead, early=(), arrived=(), weight=1):
    rows = tagged.shape[0]
    width = out_weight.shape[0]
    deep, deep_rows = 4, min(width, 256)
    whole = pl.BlockSpec(memory_space=VMEM)
    count = 1 + len(early)
    return pl.pallas_call(
        functools.partial(base_kernel, ahead, deep, len(arrived)),
        out_shape=[jax.ShapeDtypeStruct((block // LANES * rows, LANES), BF16 if ahead else F32)]
        * count,
        in_specs=[pl.BlockSpec(memory_space=pltpu.SMEM), whole, pl.BlockSpec(memory_space=pl.ANY)]
        + [whole] * (len(arrived) + len(early)),
        out_specs=[whole] * count,
        scratch_shapes=[
            VMEM((deep, deep_rows, block), BF16),
            VMEM((rows, block), F32),
            pltpu.SemaphoreType.DMA((deep,)),
        ],
        compiler_params=pltpu.CompilerParams(vmem_limit_bytes=12 << 20),
        cost_estimate=pl.CostEstimate(
            flops=2 * rows * width * block * count * weight,
            bytes_accessed=2 * width * block * count,
            transcendentals=0,
        ),
        name="base_terms",
    )(tensor_at, tagged, *in_hbm(out_weight), *arrived, *early)


def slots_of(tags, batch_at, pool, tile, per):
    lane = lane_of(tags.shape)
    ids = tags.astype(F32).astype(jnp.int32)
    mine = tile * per + lane // (LANES // per)
    held = tile * per // pool
    return ids - (batch_at[0] ^ held) * pool + held * pool, mine


def shrink_kernel(batch_at, *refs):
    blocks, factors, out = refs[:-3], refs[-3:-1], refs[-1]
    pool, rank_width, width = factors[0].shape
    everyone = jnp.concatenate([block[...] for block in blocks], axis=0)
    per = LANES // rank_width
    lane = lane_of((everyone.shape[0], LANES))
    kept = jnp.zeros(lane.shape, F32)
    for held, weights in enumerate(factors):
        terms = lax.dot_general(
            everyone[:, :width],
            weights[...].reshape(pool * rank_width, width),
            (((1,), (1,)), ((), ())),
            preferred_element_type=F32,
        )
        for tile in range(pool // per):
            slot, mine = slots_of(everyone[:, width:], batch_at, pool, held * pool // per + tile, per)
            kept = kept + jnp.where(
                slot == mine, terms[:, tile * LANES : (tile + 1) * LANES], F32(0.0)
            )
    both = kept + pltpu.roll(kept, rank_width, 1)
    half = both.shape[0] // 2
    packed = jnp.where(lane[:half] < rank_width, both[:half], both[half:])
    out[...] = packed.astype(out.dtype)


def shrink_part(blocks, factors, batch_at):
    pool, rank_width, width = factors[0].shape
    rows = len(blocks) * blocks[0].shape[0]
    smem = pl.BlockSpec(memory_space=pltpu.SMEM)
    whole = pl.BlockSpec(memory_space=VMEM)
    return pl.pallas_call(
        shrink_kernel,
        out_shape=jax.ShapeDtypeStruct((rows // 2, LANES), BF16),
        in_specs=[smem] + [whole] * (len(blocks) + 2),
        out_specs=whole,
        compiler_params=pltpu.CompilerParams(vmem_limit_bytes=8 << 20),
        cost_estimate=pl.CostEstimate(
            flops=4 * rows * width * pool * rank_width,
            bytes_accessed=2 * width * (rows + 2 * pool * rank_width),
            transcendentals=0,
        ),
        name="shrink",
    )(batch_at, *blocks, *factors)


def expand_kernel(count, sums, rank_width, batch_at, *refs):
    limits, refs = refs[:2], refs[2:]
    tags, parts = refs[:count], refs[count : count + sums]
    factors, outs = refs[count + sums : count + sums + 2], refs[count + sums + 2 :]
    tags = jnp.concatenate([tag[...] for tag in tags], axis=0)
    total = parts[0][...].astype(F32)
    for part in parts[1:]:
        total = total + part[...].astype(F32)
    total = total.astype(BF16).astype(F32)
    other = pltpu.roll(total, rank_width, 1)
    low = lane_of(total.shape) < rank_width
    shrink = jnp.concatenate(
        [jnp.where(low, total, other), jnp.where(low, other, total)], axis=0
    )
    per = LANES // rank_width
    inputs, block = factors[0].shape
    pool = inputs // rank_width
    tiles = []
    for tile in range(2 * pool // per):
        slot, mine = slots_of(tags, batch_at, pool, tile, per)
        held, at = divmod(tile * per, pool)
        limit = limits[held][at // per : at // per + 1]
        keep = (slot == mine) & (lane_of(tags.shape) % rank_width < limit)
        tiles.append(jnp.where(keep, shrink, F32(0.0)).astype(BF16))
    half = len(tiles) // 2
    spreads = [jnp.concatenate(tiles[:half], axis=1), jnp.concatenate(tiles[half:], axis=1)]
    rows = tags.shape[0] // count
    piece = min(block, 512)
    for at in range(0, block, piece):
        delta = sum(
            jnp.dot(spread, each[:, at : at + piece], preferred_element_type=F32)
            for spread, each in zip(spreads, factors)
        )
        for which, out in enumerate(outs):
            put_stacked(out, at, delta[which * rows : (which + 1) * rows])


def expand(blocks, parts, factors, limits, batch_at):
    pool, rank_width, block = factors[0].shape
    rows, tagged_width = blocks[0].shape
    count = len(blocks)
    stack = rows * block // LANES
    tag = pl.BlockSpec((rows, LANES), lambda i: (0, tagged_width // LANES - 1))
    full = pl.BlockSpec((pool * rank_width, block), lambda i: (0, 0))
    part = pl.BlockSpec(parts[0].shape, lambda i: (0, 0))
    return pl.pallas_call(
        functools.partial(expand_kernel, count, len(parts), rank_width),
        grid=(1,),
        out_shape=[jax.ShapeDtypeStruct((stack, LANES), BF16) for _ in blocks],
        in_specs=[pl.BlockSpec(memory_space=pltpu.SMEM)]
        + [pl.BlockSpec(each.shape, lambda i: (0, 0)) for each in limits]
        + [tag] * count
        + [part] * len(parts)
        + [full] * 2,
        out_specs=[pl.BlockSpec((stack, LANES), lambda i: (0, 0)) for _ in blocks],
        compiler_params=pltpu.CompilerParams(vmem_limit_bytes=16 << 20),
        cost_estimate=pl.CostEstimate(
            flops=4 * rows * count * pool * rank_width * block,
            bytes_accessed=2 * pool * rank_width * block,
            transcendentals=0,
        ),
        name="expand",
    )(batch_at, *limits, *blocks, *parts, *[each.reshape(pool * rank_width, block) for each in factors])


def total_kernel(*refs):
    terms, out = refs[:-1], refs[-1]
    rows = out.shape[0]
    for column in range(0, out.shape[1], LANES):
        at = slice(column // LANES * rows, (column // LANES + 1) * rows)
        total = terms[0][at].astype(F32)
        for term in terms[1:]:
            total = total + term[at].astype(F32)
        out[:, column : column + LANES] = total.astype(out.dtype)


def total(rows, block, terms):
    whole = pl.BlockSpec(memory_space=VMEM)
    return pl.pallas_call(
        total_kernel,
        out_shape=jax.ShapeDtypeStruct((rows, block), BF16),
        in_specs=[whole] * len(terms),
        out_specs=whole,
        compiler_params=pltpu.CompilerParams(vmem_limit_bytes=8 << 20),
        cost_estimate=pl.CostEstimate(
            flops=rows * block * len(terms),
            bytes_accessed=2 * rows * block * (1 + len(terms)),
            transcendentals=0,
        ),
        name="total",
    )(*terms)


def partial_kernel(*refs):
    terms, out = refs[:-1], refs[-1]
    total = terms[0][...].astype(F32)
    for term in terms[1:]:
        total = total + term[...].astype(F32)
    out[...] = total


def partial_total(terms, weight):
    whole = pl.BlockSpec(memory_space=VMEM)
    return pl.pallas_call(
        partial_kernel,
        out_shape=jax.ShapeDtypeStruct(terms[0].shape, F32),
        in_specs=[whole] * len(terms),
        out_specs=whole,
        compiler_params=pltpu.CompilerParams(vmem_limit_bytes=8 << 20),
        cost_estimate=pl.CostEstimate(
            flops=terms[0].size * len(terms),
            bytes_accessed=4 * terms[0].size + weight,
            transcendentals=0,
        ),
        name="partial_total",
    )(*terms)


def local(
    tensor_size,
    batch_size,
    queries,
    key_cache,
    value_cache,
    new_key,
    new_value,
    lengths,
    out_weight,
    shrink_weight,
    expand_weight,
    adapter_rank,
    adapter_list,
    row_adapter,
):
    rows = queries.shape[0]
    block = expand_weight.shape[2]
    chips = batch_size // 2
    batch_at = lax.axis_index("batch").reshape(1).astype(jnp.int32)
    tensor_at = lax.axis_index("tensor").reshape(1).astype(jnp.int32)

    def to_sibling(array):
        return permuted(array, "batch", batch_size, lambda i: i ^ 1)

    def to_chip(array, shift):
        return permuted(array, "batch", batch_size, lambda i: (i + 2 * shift) % batch_size)

    def across(array, bit):
        return permuted(array, "tensor", tensor_size, lambda i: i ^ bit)

    def wide(array):
        return array.astype(F32)

    stack = block // LANES * rows
    tagged, early, limits = attend(
        tensor_at ^ 3,
        block,
        out_weight,
        queries,
        key_cache,
        value_cache,
        new_key,
        new_value,
        lengths,
        adapter_list,
        row_adapter,
        adapter_rank,
        shrink_weight.shape[2],
    )
    limits = [limits, to_sibling(limits)]
    shrink_weight = jnp.swapaxes(shrink_weight, 1, 2)
    shrink_factors = [shrink_weight, to_sibling(shrink_weight)]
    expand_factors = [expand_weight, to_sibling(expand_weight)]
    visiting = [to_chip(tagged, shift) for shift in range(1, chips)]
    third, fetched = base_and_fetch(tensor_at, tagged, early, out_weight, 2)
    visiting, fetched, limits = lax.optimization_barrier((visiting, fetched, limits))
    blocks = [tagged] + visiting
    third = across(third, 1)

    part = shrink_part(blocks, shrink_factors, batch_at)
    parts = [part, across(part, 1)]
    part, later_tagged = lax.optimization_barrier((part, tagged))
    second, next_door = base_block(
        tensor_at, later_tagged, out_weight, block, 1, [fetched], (), 12
    )
    second = (wide(second) + wide(third)).astype(BF16)
    parts, second = lax.optimization_barrier((parts, second))
    bit = 2
    while bit < tensor_size:
        part = (wide(parts[0]) + wide(parts[1])).astype(BF16)
        part, next_door = lax.optimization_barrier((part, next_door))
        parts = [part, across(part, bit)]
        bit *= 2
    arrived = [across(second, 2), across(next_door, 1)]
    for ahead in range(4, tensor_size, 2):
        (near,) = base_block(tensor_at, tagged, out_weight, block, ahead)
        (far,) = base_block(tensor_at, tagged, out_weight, block, ahead + 1)
        arrived.append(across((wide(near) + wide(across(far, 1))).astype(BF16), ahead))

    deltas = expand(blocks, parts, expand_factors, limits, batch_at)
    deltas, late_tagged = lax.optimization_barrier((deltas, tagged))
    (own,) = base_block(tensor_at, late_tagged, out_weight, block, 0)
    so_far = partial_total([own, deltas[0], arrived[0], *arrived[2:]], 0)
    terms = [partial_total([so_far, arrived[1]], 8 << 20)]
    terms += [to_chip(home, -shift) for shift, home in enumerate(deltas[1:], 1)]
    return total(rows, block, terms)


def solution(mesh):
    placed = (
        P(("groups", "batch"), "tensor", None),
        P(("groups", "batch"), None, None, None),
        P(("groups", "batch"), None, None, None),
        P(("groups", "batch"), None, None),
        P(("groups", "batch"), None, None),
        P(("groups", "batch")),
        P("tensor", None),
        P("batch", "tensor", None),
        P("batch", None, "tensor"),
        P("batch"),
        P(("groups", "batch")),
        P(("groups", "batch")),
    )

    def placed_local(*arrays):
        return local(mesh.shape["tensor"], mesh.shape["batch"], *arrays)

    return jax.shard_map(
        placed_local,
        mesh=mesh,
        in_specs=placed,
        out_specs=P(("groups", "batch"), "tensor"),
        check_vma=False,
    )
```

```python
import functools

import jax
import jax.numpy as jnp
from jax import lax
from jax.experimental import pallas as pl
from jax.experimental.pallas import tpu as pltpu
from jax.sharding import PartitionSpec as P

HQ = 32
KVH = 4
LANES = 128
VMEM = pltpu.VMEM
GRANT = 56 << 20
F32, BF16 = jnp.float32, jnp.bfloat16


def permuted(array, axis, size, partner):
    return lax.ppermute(array, axis, [(i, partner(i)) for i in range(size)])


def in_hbm(*arrays):
    return [pltpu.with_memory_space_constraint(array, pltpu.HBM) for array in arrays]


def lane_of(shape):
    return lax.broadcasted_iota(jnp.int32, shape, len(shape) - 1)


def attend_kernel(parts, rank_width, group_at, early_at, *refs):
    given, (out_weight, tagged, early, limits, *scratch) = refs[:9], refs[9:]
    held, (spread_out, small_sems, key_sems, value_sems, early_sem) = scratch[:9], scratch[9:]
    key_cache, value_cache = given[:2]
    keys, values, queries, new_key, new_value, lengths, row_adapter, adapter_list, ranks = held
    rows, heads, width = queries.shape
    positions = key_cache.shape[2]
    group = group_at[0]
    some = rows // parts

    def cache_copies(part):
        at = pl.ds(part * some, some)
        return (
            pltpu.make_async_copy(key_cache.at[at, group], keys.at[at], key_sems.at[part]),
            pltpu.make_async_copy(value_cache.at[at, group], values.at[at], value_sems.at[part]),
        )

    small = [
        pltpu.make_async_copy(given[i], held[i], small_sems.at[i - 2]) for i in range(2, 9)
    ]
    for copy in small:
        copy.start()
    for part in range(parts):
        for copy in cache_copies(part):
            copy.start()
    block = early.shape[1]
    start = pl.multiple_of(early_at[0] * block, block)
    early_copy = pltpu.make_async_copy(out_weight.at[:, pl.ds(start, block)], early, early_sem)
    early_copy.start()
    for copy in small:
        copy.wait()
    at_row = lax.broadcasted_iota(jnp.int32, (rows, LANES), 0)
    tag = jnp.zeros((rows, LANES), jnp.int32)
    for row in range(rows):
        tag = jnp.where(at_row == row, adapter_list[row_adapter[row]], tag)
    tag = tag.astype(F32).astype(BF16)
    slot = lax.broadcasted_iota(jnp.int32, limits.shape, 0) * (LANES // rank_width)
    slot = slot + lane_of(limits.shape) // rank_width
    limit = jnp.zeros(limits.shape, jnp.int32)
    for held_at in range(ranks.shape[0]):
        limit = jnp.where(slot == held_at, ranks[held_at], limit)
    limits[...] = limit

    group_row = lax.broadcasted_iota(jnp.int32, new_key.shape, 1) == group
    fresh_key = jnp.sum(
        jnp.where(group_row, new_key[...].astype(F32), F32(0.0)), axis=1, keepdims=True
    )
    fresh_value = jnp.sum(
        jnp.where(group_row, new_value[...].astype(F32), F32(0.0)), axis=1, keepdims=True
    )
    score_scale = width ** (-0.5)
    fresh = jnp.sum(queries[...].astype(F32) * fresh_key, axis=-1, keepdims=True) * score_scale
    for part in range(parts):
        at = slice(part * some, (part + 1) * some)
        key_copy, value_copy = cache_copies(part)
        key_copy.wait()
        scores = (
            lax.dot_general(
                queries[at], keys[at], (((2,), (2,)), ((0,), (0,))), preferred_element_type=F32
            )
            * score_scale
        )
        length = jnp.stack(
            [
                jnp.full((heads, positions), lengths[row], jnp.int32)
                for row in range(part * some, (part + 1) * some)
            ]
        )
        valid = lane_of(scores.shape) < length
        masked = jnp.where(valid, scores, F32(-1e30))
        highest = jnp.maximum(jnp.max(masked, axis=-1, keepdims=True), fresh[at])
        cached_exp = jnp.where(valid, jnp.exp(masked - highest), F32(0.0))
        fresh_exp = jnp.exp(fresh[at] - highest)
        totals = jnp.sum(cached_exp, axis=-1, keepdims=True) + fresh_exp
        cached_w = (cached_exp / totals).astype(BF16)
        fresh_w = (fresh_exp / totals).astype(BF16).astype(F32)
        value_copy.wait()
        attended = lax.dot_general(
            cached_w, values[at], (((2,), (1,)), ((0,), (0,))), preferred_element_type=F32
        )
        attended = attended + fresh_w * fresh_value[at]
        spread_out[pl.ds(part * some * heads, some * heads)] = attended.reshape(
            some * heads, width
        )
    tagged[:, heads * width :] = tag
    for head in range(heads):
        tagged[:, head * width : (head + 1) * width] = spread_out[
            pl.ds(head, rows, stride=heads)
        ].astype(BF16)
    early_copy.wait()


def attend(
    early_at,
    block,
    out_weight,
    queries,
    key_cache,
    value_cache,
    new_key,
    new_value,
    lengths,
    adapter_list,
    row_adapter,
    adapter_rank,
    rank_width,
):
    rows, heads, width = queries.shape
    positions = key_cache.shape[2]
    per_group = HQ // KVH
    group_at = (lax.axis_index("tensor") * heads // per_group).reshape(1).astype(jnp.int32)
    full = -(-heads // 8) * 8
    if full != heads:
        queries = jnp.pad(queries, ((0, 0), (0, full - heads), (0, 0)))
    parts = 2
    smem = pl.BlockSpec(memory_space=pltpu.SMEM)
    away = pl.BlockSpec(memory_space=pl.ANY)
    tagged, early, limits = pl.pallas_call(
        functools.partial(attend_kernel, parts, rank_width),
        out_shape=[
            jax.ShapeDtypeStruct((rows, full * width + LANES), BF16),
            VMEM((out_weight.shape[0], block), BF16),
            jax.ShapeDtypeStruct((8, LANES), jnp.int32),
        ],
        in_specs=[smem, smem] + [away] * 10,
        out_specs=[pl.BlockSpec(memory_space=VMEM)] * 3,
        scratch_shapes=[
            VMEM((rows, positions, width), BF16),
            VMEM((rows, positions, width), BF16),
            VMEM(queries.shape, BF16),
            VMEM(new_key.shape, BF16),
            VMEM(new_value.shape, BF16),
            pltpu.SMEM(lengths.shape, jnp.int32),
            pltpu.SMEM(row_adapter.shape, jnp.int32),
            pltpu.SMEM(adapter_list.shape, jnp.int32),
            pltpu.SMEM(adapter_rank.shape, jnp.int32),
            VMEM((rows * full, width), F32),
            pltpu.SemaphoreType.DMA((7,)),
            pltpu.SemaphoreType.DMA((parts,)),
            pltpu.SemaphoreType.DMA((parts,)),
            pltpu.SemaphoreType.DMA,
        ],
        compiler_params=pltpu.CompilerParams(vmem_limit_bytes=8 << 20),
        cost_estimate=pl.CostEstimate(
            flops=4 * rows * heads * positions * width,
            bytes_accessed=4 * rows * positions * width,
            transcendentals=rows * heads * positions,
        ),
        name="attention",
    )(
        group_at,
        early_at,
        *in_hbm(
            key_cache,
            value_cache,
            queries,
            new_key,
            new_value,
            lengths,
            row_adapter,
            adapter_list,
            adapter_rank,
            out_weight,
        ),
    )
    if full != heads:
        tagged = jnp.concatenate([tagged[:, : heads * width], tagged[:, full * width :]], axis=1)
    return tagged, early, limits


def put_stacked(out, start, term):
    rows = term.shape[0]
    for column in range(0, term.shape[1], LANES):
        at = (start + column) // LANES * rows
        out[at : at + rows] = term[:, column : column + LANES].astype(out.dtype)


def base_kernel(apart, piece, tensor_at, tagged, weight, *outs):
    width = weight.shape[0]
    for ahead, out in zip(apart, outs):
        block = out.shape[0] // tagged.shape[0] * LANES
        for at in range(0, block, piece):
            start = at
            if weight.shape[1] > block:
                start = pl.multiple_of((tensor_at[0] ^ ahead) * block + at, piece)
            term = jnp.dot(
                tagged[:, :width], weight[:, pl.ds(start, piece)], preferred_element_type=F32
            )
            put_stacked(out, at, term)


def base_terms(tensor_at, tagged, weight, block, apart, cost):
    rows = tagged.shape[0]
    width = weight.shape[0]
    whole = pl.BlockSpec(memory_space=VMEM)
    return pl.pallas_call(
        functools.partial(base_kernel, apart, min(block, 512)),
        out_shape=[
            jax.ShapeDtypeStruct((block // LANES * rows, LANES), BF16 if ahead else F32)
            for ahead in apart
        ],
        in_specs=[pl.BlockSpec(memory_space=pltpu.SMEM), whole, whole],
        out_specs=[whole] * len(apart),
        compiler_params=pltpu.CompilerParams(vmem_limit_bytes=6 << 20),
        cost_estimate=pl.CostEstimate(
            flops=cost * rows * width * block * len(apart),
            bytes_accessed=2 * width * block * len(apart),
            transcendentals=0,
        ),
        name="base_terms",
    )(tensor_at, tagged, weight)


def slots_of(tags, batch_at, pool, tile, per):
    lane = lane_of(tags.shape)
    ids = tags.astype(F32).astype(jnp.int32)
    mine = tile * per + lane // (LANES // per)
    held = tile * per // pool
    return ids - (batch_at[0] ^ held) * pool + held * pool, mine


def shrink_kernel(batch_at, *refs):
    blocks, factors, out = refs[:-3], refs[-3:-1], refs[-1]
    pool, rank_width, width = factors[0].shape
    everyone = jnp.concatenate([block[...] for block in blocks], axis=0)
    per = LANES // rank_width
    lane = lane_of((everyone.shape[0], LANES))
    kept = jnp.zeros(lane.shape, F32)
    for held, weights in enumerate(factors):
        terms = lax.dot_general(
            everyone[:, :width],
            weights[...].reshape(pool * rank_width, width),
            (((1,), (1,)), ((), ())),
            preferred_element_type=F32,
        )
        for tile in range(pool // per):
            slot, mine = slots_of(everyone[:, width:], batch_at, pool, held * pool // per + tile, per)
            kept = kept + jnp.where(
                slot == mine, terms[:, tile * LANES : (tile + 1) * LANES], F32(0.0)
            )
    both = kept + pltpu.roll(kept, rank_width, 1)
    half = both.shape[0] // 2
    packed = jnp.where(lane[:half] < rank_width, both[:half], both[half:])
    out[...] = packed.astype(out.dtype)


def shrink_part(blocks, factors, batch_at):
    pool, rank_width, width = factors[0].shape
    rows = len(blocks) * blocks[0].shape[0]
    smem = pl.BlockSpec(memory_space=pltpu.SMEM)
    whole = pl.BlockSpec(memory_space=VMEM)
    return pl.pallas_call(
        shrink_kernel,
        out_shape=jax.ShapeDtypeStruct((rows // 2, LANES), BF16),
        in_specs=[smem] + [whole] * (len(blocks) + 2),
        out_specs=whole,
        compiler_params=pltpu.CompilerParams(vmem_limit_bytes=8 << 20),
        cost_estimate=pl.CostEstimate(
            flops=4 * rows * width * pool * rank_width,
            bytes_accessed=2 * width * (rows + 2 * pool * rank_width),
            transcendentals=0,
        ),
        name="shrink",
    )(batch_at, *blocks, *factors)


def expand_kernel(count, sums, rank_width, batch_at, *refs):
    limits, refs = refs[:2], refs[2:]
    tags, parts = refs[:count], refs[count : count + sums]
    factors, outs = refs[count + sums : count + sums + 2], refs[count + sums + 2 :]
    tags = jnp.concatenate([tag[...] for tag in tags], axis=0)
    total = parts[0][...].astype(F32)
    for part in parts[1:]:
        total = total + part[...].astype(F32)
    total = total.astype(BF16).astype(F32)
    other = pltpu.roll(total, rank_width, 1)
    low = lane_of(total.shape) < rank_width
    shrink = jnp.concatenate(
        [jnp.where(low, total, other), jnp.where(low, other, total)], axis=0
    )
    per = LANES // rank_width
    inputs, block = factors[0].shape
    pool = inputs // rank_width
    tiles = []
    for tile in range(2 * pool // per):
        slot, mine = slots_of(tags, batch_at, pool, tile, per)
        held, at = divmod(tile * per, pool)
        limit = limits[held][at // per : at // per + 1]
        keep = (slot == mine) & (lane_of(tags.shape) % rank_width < limit)
        tiles.append(jnp.where(keep, shrink, F32(0.0)).astype(BF16))
    half = len(tiles) // 2
    spreads = [jnp.concatenate(tiles[:half], axis=1), jnp.concatenate(tiles[half:], axis=1)]
    rows = tags.shape[0] // count
    piece = min(block, 512)
    for at in range(0, block, piece):
        delta = sum(
            jnp.dot(spread, each[:, at : at + piece], preferred_element_type=F32)
            for spread, each in zip(spreads, factors)
        )
        for which, out in enumerate(outs):
            put_stacked(out, at, delta[which * rows : (which + 1) * rows])


def expand(blocks, parts, factors, limits, batch_at):
    pool, rank_width, block = factors[0].shape
    rows, tagged_width = blocks[0].shape
    count = len(blocks)
    stack = rows * block // LANES
    tag = pl.BlockSpec((rows, LANES), lambda i: (0, tagged_width // LANES - 1))
    full = pl.BlockSpec((pool * rank_width, block), lambda i: (0, 0))
    part = pl.BlockSpec(parts[0].shape, lambda i: (0, 0))
    return pl.pallas_call(
        functools.partial(expand_kernel, count, len(parts), rank_width),
        grid=(1,),
        out_shape=[jax.ShapeDtypeStruct((stack, LANES), BF16) for _ in blocks],
        in_specs=[pl.BlockSpec(memory_space=pltpu.SMEM)]
        + [pl.BlockSpec(each.shape, lambda i: (0, 0)) for each in limits]
        + [tag] * count
        + [part] * len(parts)
        + [full] * 2,
        out_specs=[pl.BlockSpec((stack, LANES), lambda i: (0, 0)) for _ in blocks],
        compiler_params=pltpu.CompilerParams(vmem_limit_bytes=16 << 20),
        cost_estimate=pl.CostEstimate(
            flops=4 * rows * count * pool * rank_width * block,
            bytes_accessed=2 * pool * rank_width * block,
            transcendentals=0,
        ),
        name="expand",
    )(batch_at, *limits, *blocks, *parts, *[each.reshape(pool * rank_width, block) for each in factors])


def total_kernel(*refs):
    terms, out = refs[:-1], refs[-1]
    rows = out.shape[0]
    for column in range(0, out.shape[1], LANES):
        at = slice(column // LANES * rows, (column // LANES + 1) * rows)
        total = terms[0][at].astype(F32)
        for term in terms[1:]:
            total = total + term[at].astype(F32)
        out[:, column : column + LANES] = total.astype(out.dtype)


def total(rows, block, terms):
    whole = pl.BlockSpec(memory_space=VMEM)
    return pl.pallas_call(
        total_kernel,
        out_shape=jax.ShapeDtypeStruct((rows, block), BF16),
        in_specs=[whole] * len(terms),
        out_specs=whole,
        compiler_params=pltpu.CompilerParams(vmem_limit_bytes=8 << 20),
        cost_estimate=pl.CostEstimate(
            flops=rows * block * len(terms),
            bytes_accessed=2 * rows * block * (1 + len(terms)),
            transcendentals=0,
        ),
        name="total",
    )(*terms)


def partial_kernel(*refs):
    terms, out = refs[:-1], refs[-1]
    total = terms[0][...].astype(F32)
    for term in terms[1:]:
        total = total + term[...].astype(F32)
    out[...] = total


def partial_total(terms, weight):
    whole = pl.BlockSpec(memory_space=VMEM)
    return pl.pallas_call(
        partial_kernel,
        out_shape=jax.ShapeDtypeStruct(terms[0].shape, F32),
        in_specs=[whole] * len(terms),
        out_specs=whole,
        compiler_params=pltpu.CompilerParams(vmem_limit_bytes=8 << 20),
        cost_estimate=pl.CostEstimate(
            flops=terms[0].size * len(terms),
            bytes_accessed=4 * terms[0].size + weight,
            transcendentals=0,
        ),
        name="partial_total",
    )(*terms)


def local(
    tensor_size,
    batch_size,
    queries,
    key_cache,
    value_cache,
    new_key,
    new_value,
    lengths,
    out_weight,
    shrink_weight,
    expand_weight,
    adapter_rank,
    adapter_list,
    row_adapter,
):
    rows = queries.shape[0]
    block = expand_weight.shape[2]
    chips = batch_size // 2
    batch_at = lax.axis_index("batch").reshape(1).astype(jnp.int32)
    tensor_at = lax.axis_index("tensor").reshape(1).astype(jnp.int32)

    def to_sibling(array):
        return permuted(array, "batch", batch_size, lambda i: i ^ 1)

    def to_chip(array, shift):
        return permuted(array, "batch", batch_size, lambda i: (i + 2 * shift) % batch_size)

    def across(array, bit):
        return permuted(array, "tensor", tensor_size, lambda i: i ^ bit)

    def wide(array):
        return array.astype(F32)

    stack = block // LANES * rows
    tagged, early, limits = attend(
        tensor_at ^ 3,
        block,
        out_weight,
        queries,
        key_cache,
        value_cache,
        new_key,
        new_value,
        lengths,
        adapter_list,
        row_adapter,
        adapter_rank,
        shrink_weight.shape[2],
    )
    limits = [limits, to_sibling(limits)]
    shrink_weight = jnp.swapaxes(shrink_weight, 1, 2)
    shrink_factors = [shrink_weight, to_sibling(shrink_weight)]
    expand_factors = [expand_weight, to_sibling(expand_weight)]
    visiting = [to_chip(tagged, shift) for shift in range(1, chips)]
    weight = pltpu.with_memory_space_constraint(out_weight, VMEM)
    (third,) = base_terms(tensor_at, tagged, early, block, [3], 120)
    visiting, limits = lax.optimization_barrier((visiting, limits))
    blocks = [tagged] + visiting
    third = across(third, 1)

    part = shrink_part(blocks, shrink_factors, batch_at)
    parts = [part, across(part, 1)]
    part, later_tagged = lax.optimization_barrier((part, tagged))
    second, next_door = base_terms(tensor_at, later_tagged, weight, block, [2, 1], 20)
    second = (wide(second) + wide(third)).astype(BF16)
    parts, second = lax.optimization_barrier((parts, second))
    bit = 2
    while bit < tensor_size:
        part = (wide(parts[0]) + wide(parts[1])).astype(BF16)
        part, next_door = lax.optimization_barrier((part, next_door))
        parts = [part, across(part, bit)]
        bit *= 2
    arrived = [across(second, 2), across(next_door, 1)]
    for ahead in range(4, tensor_size, 2):
        near, far = base_terms(tensor_at, tagged, weight, block, [ahead, ahead + 1], 20)
        arrived.append(across((wide(near) + wide(across(far, 1))).astype(BF16), ahead))

    deltas = expand(blocks, parts, expand_factors, limits, batch_at)
    deltas, late_tagged = lax.optimization_barrier((deltas, tagged))
    (own,) = base_terms(tensor_at, late_tagged, weight, block, [0], 20)
    so_far = partial_total([own, deltas[0], arrived[0], *arrived[2:]], 0)
    terms = [partial_total([so_far, arrived[1]], 8 << 20)]
    terms += [to_chip(home, -shift) for shift, home in enumerate(deltas[1:], 1)]
    return total(rows, block, terms)


def solution(mesh):
    placed = (
        P(("groups", "batch"), "tensor", None),
        P(("groups", "batch"), None, None, None),
        P(("groups", "batch"), None, None, None),
        P(("groups", "batch"), None, None),
        P(("groups", "batch"), None, None),
        P(("groups", "batch")),
        P("tensor", None),
        P("batch", "tensor", None),
        P("batch", None, "tensor"),
        P("batch"),
        P(("groups", "batch")),
        P(("groups", "batch")),
    )

    def placed_local(*arrays):
        return local(mesh.shape["tensor"], mesh.shape["batch"], *arrays)

    return jax.shard_map(
        placed_local,
        mesh=mesh,
        in_specs=placed,
        out_specs=P(("groups", "batch"), "tensor"),
        check_vma=False,
    )
```

```python
import functools

import jax
import jax.numpy as jnp
from jax import lax
from jax.experimental import pallas as pl
from jax.experimental.pallas import tpu as pltpu
from jax.sharding import PartitionSpec as P

HQ = 32
KVH = 4
LANES = 128
EARLY = (3, 2)
EARLY_CUTS = 4
VMEM = pltpu.VMEM
GRANT = 56 << 20
F32, BF16 = jnp.float32, jnp.bfloat16


def permuted(array, axis, size, partner):
    return lax.ppermute(array, axis, [(i, partner(i)) for i in range(size)])


def in_hbm(*arrays):
    return [pltpu.with_memory_space_constraint(array, pltpu.HBM) for array in arrays]


def lane_of(shape):
    return lax.broadcasted_iota(jnp.int32, shape, len(shape) - 1)


def attend_kernel(parts, rank_width, count, group_at, early_at, *refs):
    given, (out_weight, tagged, *early, limits) = refs[:9], refs[9 : 9 + 3 + count]
    scratch = refs[9 + 3 + count :]
    held, (spread_out, small_sems, key_sems, value_sems, early_sems) = scratch[:9], scratch[9:]
    key_cache, value_cache = given[:2]
    keys, values, queries, new_key, new_value, lengths, row_adapter, adapter_list, ranks = held
    rows, heads, width = queries.shape
    positions = key_cache.shape[2]
    group = group_at[0]
    some = rows // parts

    def cache_copies(part):
        at = pl.ds(part * some, some)
        return (
            pltpu.make_async_copy(key_cache.at[at, group], keys.at[at], key_sems.at[part]),
            pltpu.make_async_copy(value_cache.at[at, group], values.at[at], value_sems.at[part]),
        )

    small = [
        pltpu.make_async_copy(given[i], held[i], small_sems.at[i - 2]) for i in range(2, 9)
    ]
    for copy in small:
        copy.start()
    for part in range(parts):
        for copy in cache_copies(part):
            copy.start()
    early_copies = []
    for which, out in enumerate(early):
        rows_each, block = out.shape[0] // EARLY_CUTS, out.shape[1]
        start = pl.multiple_of((early_at[0] ^ EARLY[which]) * block, block)
        for cut in range(EARLY_CUTS):
            at = pl.ds(cut * rows_each, rows_each)
            early_copies.append(
                pltpu.make_async_copy(
                    out_weight.at[at, pl.ds(start, block)],
                    out.at[at],
                    early_sems.at[which * EARLY_CUTS + cut],
                )
            )
    for copy in early_copies:
        copy.start()
    for copy in small:
        copy.wait()
    at_row = lax.broadcasted_iota(jnp.int32, (rows, LANES), 0)
    tag = jnp.zeros((rows, LANES), jnp.int32)
    for row in range(rows):
        tag = jnp.where(at_row == row, adapter_list[row_adapter[row]], tag)
    tag = tag.astype(F32).astype(BF16)
    slot = lax.broadcasted_iota(jnp.int32, limits.shape, 0) * (LANES // rank_width)
    slot = slot + lane_of(limits.shape) // rank_width
    limit = jnp.zeros(limits.shape, jnp.int32)
    for held_at in range(ranks.shape[0]):
        limit = jnp.where(slot == held_at, ranks[held_at], limit)
    limits[...] = limit

    group_row = lax.broadcasted_iota(jnp.int32, new_key.shape, 1) == group
    fresh_key = jnp.sum(
        jnp.where(group_row, new_key[...].astype(F32), F32(0.0)), axis=1, keepdims=True
    )
    fresh_value = jnp.sum(
        jnp.where(group_row, new_value[...].astype(F32), F32(0.0)), axis=1, keepdims=True
    )
    score_scale = width ** (-0.5)
    fresh = jnp.sum(queries[...].astype(F32) * fresh_key, axis=-1, keepdims=True) * score_scale
    for part in range(parts):
        at = slice(part * some, (part + 1) * some)
        key_copy, value_copy = cache_copies(part)
        key_copy.wait()
        scores = (
            lax.dot_general(
                queries[at], keys[at], (((2,), (2,)), ((0,), (0,))), preferred_element_type=F32
            )
            * score_scale
        )
        length = jnp.stack(
            [
                jnp.full((heads, positions), lengths[row], jnp.int32)
                for row in range(part * some, (part + 1) * some)
            ]
        )
        valid = lane_of(scores.shape) < length
        masked = jnp.where(valid, scores, F32(-1e30))
        highest = jnp.maximum(jnp.max(masked, axis=-1, keepdims=True), fresh[at])
        cached_exp = jnp.where(valid, jnp.exp(masked - highest), F32(0.0))
        fresh_exp = jnp.exp(fresh[at] - highest)
        totals = jnp.sum(cached_exp, axis=-1, keepdims=True) + fresh_exp
        cached_w = (cached_exp / totals).astype(BF16)
        fresh_w = (fresh_exp / totals).astype(BF16).astype(F32)
        value_copy.wait()
        attended = lax.dot_general(
            cached_w, values[at], (((2,), (1,)), ((0,), (0,))), preferred_element_type=F32
        )
        attended = attended + fresh_w * fresh_value[at]
        spread_out[pl.ds(part * some * heads, some * heads)] = attended.reshape(
            some * heads, width
        )
    tagged[:, heads * width :] = tag
    for head in range(heads):
        tagged[:, head * width : (head + 1) * width] = spread_out[
            pl.ds(head, rows, stride=heads)
        ].astype(BF16)
    for copy in early_copies:
        copy.wait()


def attend(
    early_at,
    block,
    out_weight,
    queries,
    key_cache,
    value_cache,
    new_key,
    new_value,
    lengths,
    adapter_list,
    row_adapter,
    adapter_rank,
    rank_width,
):
    rows, heads, width = queries.shape
    positions = key_cache.shape[2]
    per_group = HQ // KVH
    group_at = (lax.axis_index("tensor") * heads // per_group).reshape(1).astype(jnp.int32)
    full = -(-heads // 8) * 8
    if full != heads:
        queries = jnp.pad(queries, ((0, 0), (0, full - heads), (0, 0)))
    parts = 2
    smem = pl.BlockSpec(memory_space=pltpu.SMEM)
    away = pl.BlockSpec(memory_space=pl.ANY)
    tagged, *early, limits = pl.pallas_call(
        functools.partial(attend_kernel, parts, rank_width, len(EARLY)),
        out_shape=[
            jax.ShapeDtypeStruct((rows, full * width + LANES), BF16),
            *[VMEM((out_weight.shape[0], block), BF16) for _ in EARLY],
            jax.ShapeDtypeStruct((8, LANES), jnp.int32),
        ],
        in_specs=[smem, smem] + [away] * 10,
        out_specs=[pl.BlockSpec(memory_space=VMEM)] * (2 + len(EARLY)),
        scratch_shapes=[
            VMEM((rows, positions, width), BF16),
            VMEM((rows, positions, width), BF16),
            VMEM(queries.shape, BF16),
            VMEM(new_key.shape, BF16),
            VMEM(new_value.shape, BF16),
            pltpu.SMEM(lengths.shape, jnp.int32),
            pltpu.SMEM(row_adapter.shape, jnp.int32),
            pltpu.SMEM(adapter_list.shape, jnp.int32),
            pltpu.SMEM(adapter_rank.shape, jnp.int32),
            VMEM((rows * full, width), F32),
            pltpu.SemaphoreType.DMA((7,)),
            pltpu.SemaphoreType.DMA((parts,)),
            pltpu.SemaphoreType.DMA((parts,)),
            pltpu.SemaphoreType.DMA((len(EARLY) * EARLY_CUTS,)),
        ],
        compiler_params=pltpu.CompilerParams(vmem_limit_bytes=8 << 20),
        cost_estimate=pl.CostEstimate(
            flops=4 * rows * heads * positions * width,
            bytes_accessed=4 * rows * positions * width,
            transcendentals=rows * heads * positions,
        ),
        name="attention",
    )(
        group_at,
        early_at,
        *in_hbm(
            key_cache,
            value_cache,
            queries,
            new_key,
            new_value,
            lengths,
            row_adapter,
            adapter_list,
            adapter_rank,
            out_weight,
        ),
    )
    if full != heads:
        tagged = jnp.concatenate([tagged[:, : heads * width], tagged[:, full * width :]], axis=1)
    return tagged, early, limits


def put_stacked(out, start, term):
    rows = term.shape[0]
    for column in range(0, term.shape[1], LANES):
        at = (start + column) // LANES * rows
        out[at : at + rows] = term[:, column : column + LANES].astype(out.dtype)


def base_kernel(apart, piece, tensor_at, tagged, weight, *outs):
    width = weight.shape[0]
    for ahead, out in zip(apart, outs):
        block = out.shape[0] // tagged.shape[0] * LANES
        for at in range(0, block, piece):
            start = at
            if weight.shape[1] > block:
                start = pl.multiple_of((tensor_at[0] ^ ahead) * block + at, piece)
            term = jnp.dot(
                tagged[:, :width], weight[:, pl.ds(start, piece)], preferred_element_type=F32
            )
            put_stacked(out, at, term)


def base_terms(tensor_at, tagged, weight, block, apart, cost):
    rows = tagged.shape[0]
    width = weight.shape[0]
    whole = pl.BlockSpec(memory_space=VMEM)
    return pl.pallas_call(
        functools.partial(base_kernel, apart, min(block, 512)),
        out_shape=[
            jax.ShapeDtypeStruct((block // LANES * rows, LANES), BF16 if ahead else F32)
            for ahead in apart
        ],
        in_specs=[pl.BlockSpec(memory_space=pltpu.SMEM), whole, whole],
        out_specs=[whole] * len(apart),
        compiler_params=pltpu.CompilerParams(vmem_limit_bytes=6 << 20),
        cost_estimate=pl.CostEstimate(
            flops=cost * rows * width * block * len(apart),
            bytes_accessed=2 * width * block * len(apart),
            transcendentals=0,
        ),
        name="base_terms",
    )(tensor_at, tagged, weight)


def stream_kernel(ahead, deep, tensor_at, tagged, out_weight, *refs):
    *near, out, held, sums, sems = refs
    _, deep_rows, block = held.shape
    width = out_weight.shape[0]
    count = width // deep_rows
    column = pl.ds(pl.multiple_of((tensor_at[0] ^ ahead) * block, block), block)

    def copy(at):
        return pltpu.make_async_copy(
            out_weight.at[pl.ds(at * deep_rows, deep_rows), column],
            held.at[at % deep],
            sems.at[at % deep],
        )

    for at in range(min(deep, count)):
        copy(at).start()
    piece = min(block, 512)
    if near:
        early, early_out = near
        for start in range(0, block, piece):
            columns = slice(start, start + piece)
            term = jnp.dot(tagged[:, :width], early[:, columns], preferred_element_type=F32)
            put_stacked(early_out, start, term)
    for at in range(count):
        copy(at).wait()
        inputs = slice(at * deep_rows, (at + 1) * deep_rows)
        for start in range(0, block, piece):
            columns = slice(start, start + piece)
            term = jnp.dot(
                tagged[:, inputs], held[at % deep, :, columns], preferred_element_type=F32
            )
            if at:
                term = term + sums[:, columns]
            if at < count - 1:
                sums[:, columns] = term
            else:
                put_stacked(out, start, term)
        if at + deep < count:
            copy(at + deep).start()


def stream_terms(tensor_at, tagged, out_weight, block, ahead, early=(), cost=2):
    rows = tagged.shape[0]
    width = out_weight.shape[0]
    deep, deep_rows = 4, min(width, 256)
    whole = pl.BlockSpec(memory_space=VMEM)
    count = 1 + len(early)
    return pl.pallas_call(
        functools.partial(stream_kernel, ahead, deep),
        out_shape=[jax.ShapeDtypeStruct((block // LANES * rows, LANES), BF16 if ahead else F32)]
        * count,
        in_specs=[pl.BlockSpec(memory_space=pltpu.SMEM), whole, pl.BlockSpec(memory_space=pl.ANY)]
        + [whole] * len(early),
        out_specs=[whole] * count,
        scratch_shapes=[
            VMEM((deep, deep_rows, block), BF16),
            VMEM((rows, block), F32),
            pltpu.SemaphoreType.DMA((deep,)),
        ],
        compiler_params=pltpu.CompilerParams(vmem_limit_bytes=12 << 20),
        cost_estimate=pl.CostEstimate(
            flops=cost * rows * width * block * count,
            bytes_accessed=2 * width * block * count,
            transcendentals=0,
        ),
        name="base_terms",
    )(tensor_at, tagged, *in_hbm(out_weight), *early)


def slots_of(tags, batch_at, pool, tile, per):
    lane = lane_of(tags.shape)
    ids = tags.astype(F32).astype(jnp.int32)
    mine = tile * per + lane // (LANES // per)
    held = tile * per // pool
    return ids - (batch_at[0] ^ held) * pool + held * pool, mine


def shrink_kernel(batch_at, *refs):
    blocks, factors, out = refs[:-3], refs[-3:-1], refs[-1]
    pool, rank_width, width = factors[0].shape
    everyone = jnp.concatenate([block[...] for block in blocks], axis=0)
    per = LANES // rank_width
    lane = lane_of((everyone.shape[0], LANES))
    kept = jnp.zeros(lane.shape, F32)
    for held, weights in enumerate(factors):
        terms = lax.dot_general(
            everyone[:, :width],
            weights[...].reshape(pool * rank_width, width),
            (((1,), (1,)), ((), ())),
            preferred_element_type=F32,
        )
        for tile in range(pool // per):
            slot, mine = slots_of(everyone[:, width:], batch_at, pool, held * pool // per + tile, per)
            kept = kept + jnp.where(
                slot == mine, terms[:, tile * LANES : (tile + 1) * LANES], F32(0.0)
            )
    both = kept + pltpu.roll(kept, rank_width, 1)
    half = both.shape[0] // 2
    packed = jnp.where(lane[:half] < rank_width, both[:half], both[half:])
    out[...] = packed.astype(out.dtype)


def shrink_part(blocks, factors, batch_at):
    pool, rank_width, width = factors[0].shape
    rows = len(blocks) * blocks[0].shape[0]
    smem = pl.BlockSpec(memory_space=pltpu.SMEM)
    whole = pl.BlockSpec(memory_space=VMEM)
    return pl.pallas_call(
        shrink_kernel,
        out_shape=jax.ShapeDtypeStruct((rows // 2, LANES), BF16),
        in_specs=[smem] + [whole] * (len(blocks) + 2),
        out_specs=whole,
        compiler_params=pltpu.CompilerParams(vmem_limit_bytes=8 << 20),
        cost_estimate=pl.CostEstimate(
            flops=4 * rows * width * pool * rank_width,
            bytes_accessed=2 * width * (rows + 2 * pool * rank_width),
            transcendentals=0,
        ),
        name="shrink",
    )(batch_at, *blocks, *factors)


def expand_kernel(count, sums, rank_width, batch_at, *refs):
    limits, refs = refs[:2], refs[2:]
    tags, parts = refs[:count], refs[count : count + sums]
    factors, outs = refs[count + sums : count + sums + 2], refs[count + sums + 2 :]
    tags = jnp.concatenate([tag[...] for tag in tags], axis=0)
    total = parts[0][...].astype(F32)
    for part in parts[1:]:
        total = total + part[...].astype(F32)
    total = total.astype(BF16).astype(F32)
    other = pltpu.roll(total, rank_width, 1)
    low = lane_of(total.shape) < rank_width
    shrink = jnp.concatenate(
        [jnp.where(low, total, other), jnp.where(low, other, total)], axis=0
    )
    per = LANES // rank_width
    inputs, block = factors[0].shape
    pool = inputs // rank_width
    tiles = []
    for tile in range(2 * pool // per):
        slot, mine = slots_of(tags, batch_at, pool, tile, per)
        held, at = divmod(tile * per, pool)
        limit = limits[held][at // per : at // per + 1]
        keep = (slot == mine) & (lane_of(tags.shape) % rank_width < limit)
        tiles.append(jnp.where(keep, shrink, F32(0.0)).astype(BF16))
    half = len(tiles) // 2
    spreads = [jnp.concatenate(tiles[:half], axis=1), jnp.concatenate(tiles[half:], axis=1)]
    rows = tags.shape[0] // count
    piece = min(block, 512)
    for at in range(0, block, piece):
        delta = sum(
            jnp.dot(spread, each[:, at : at + piece], preferred_element_type=F32)
            for spread, each in zip(spreads, factors)
        )
        for which, out in enumerate(outs):
            put_stacked(out, at, delta[which * rows : (which + 1) * rows])


def expand(blocks, parts, factors, limits, batch_at):
    pool, rank_width, block = factors[0].shape
    rows, tagged_width = blocks[0].shape
    count = len(blocks)
    stack = rows * block // LANES
    tag = pl.BlockSpec((rows, LANES), lambda i: (0, tagged_width // LANES - 1))
    full = pl.BlockSpec((pool * rank_width, block), lambda i: (0, 0))
    part = pl.BlockSpec(parts[0].shape, lambda i: (0, 0))
    return pl.pallas_call(
        functools.partial(expand_kernel, count, len(parts), rank_width),
        grid=(1,),
        out_shape=[jax.ShapeDtypeStruct((stack, LANES), BF16) for _ in blocks],
        in_specs=[pl.BlockSpec(memory_space=pltpu.SMEM)]
        + [pl.BlockSpec(each.shape, lambda i: (0, 0)) for each in limits]
        + [tag] * count
        + [part] * len(parts)
        + [full] * 2,
        out_specs=[pl.BlockSpec((stack, LANES), lambda i: (0, 0)) for _ in blocks],
        compiler_params=pltpu.CompilerParams(vmem_limit_bytes=16 << 20),
        cost_estimate=pl.CostEstimate(
            flops=4 * rows * count * pool * rank_width * block,
            bytes_accessed=2 * pool * rank_width * block,
            transcendentals=0,
        ),
        name="expand",
    )(batch_at, *limits, *blocks, *parts, *[each.reshape(pool * rank_width, block) for each in factors])


def total_kernel(*refs):
    terms, out = refs[:-1], refs[-1]
    rows = out.shape[0]
    for column in range(0, out.shape[1], LANES):
        at = slice(column // LANES * rows, (column // LANES + 1) * rows)
        total = terms[0][at].astype(F32)
        for term in terms[1:]:
            total = total + term[at].astype(F32)
        out[:, column : column + LANES] = total.astype(out.dtype)


def total(rows, block, terms):
    whole = pl.BlockSpec(memory_space=VMEM)
    return pl.pallas_call(
        total_kernel,
        out_shape=jax.ShapeDtypeStruct((rows, block), BF16),
        in_specs=[whole] * len(terms),
        out_specs=whole,
        compiler_params=pltpu.CompilerParams(vmem_limit_bytes=8 << 20),
        cost_estimate=pl.CostEstimate(
            flops=rows * block * len(terms),
            bytes_accessed=2 * rows * block * (1 + len(terms)),
            transcendentals=0,
        ),
        name="total",
    )(*terms)


def partial_kernel(*refs):
    terms, out = refs[:-1], refs[-1]
    total = terms[0][...].astype(F32)
    for term in terms[1:]:
        total = total + term[...].astype(F32)
    out[...] = total


def partial_total(terms, weight):
    whole = pl.BlockSpec(memory_space=VMEM)
    return pl.pallas_call(
        partial_kernel,
        out_shape=jax.ShapeDtypeStruct(terms[0].shape, F32),
        in_specs=[whole] * len(terms),
        out_specs=whole,
        compiler_params=pltpu.CompilerParams(vmem_limit_bytes=8 << 20),
        cost_estimate=pl.CostEstimate(
            flops=terms[0].size * len(terms),
            bytes_accessed=4 * terms[0].size + weight,
            transcendentals=0,
        ),
        name="partial_total",
    )(*terms)


def local(
    tensor_size,
    batch_size,
    queries,
    key_cache,
    value_cache,
    new_key,
    new_value,
    lengths,
    out_weight,
    shrink_weight,
    expand_weight,
    adapter_rank,
    adapter_list,
    row_adapter,
):
    rows = queries.shape[0]
    block = expand_weight.shape[2]
    chips = batch_size // 2
    batch_at = lax.axis_index("batch").reshape(1).astype(jnp.int32)
    tensor_at = lax.axis_index("tensor").reshape(1).astype(jnp.int32)

    def to_sibling(array):
        return permuted(array, "batch", batch_size, lambda i: i ^ 1)

    def to_chip(array, shift):
        return permuted(array, "batch", batch_size, lambda i: (i + 2 * shift) % batch_size)

    def across(array, bit):
        return permuted(array, "tensor", tensor_size, lambda i: i ^ bit)

    def wide(array):
        return array.astype(F32)

    stack = block // LANES * rows
    tagged, early, limits = attend(
        tensor_at,
        block,
        out_weight,
        queries,
        key_cache,
        value_cache,
        new_key,
        new_value,
        lengths,
        adapter_list,
        row_adapter,
        adapter_rank,
        shrink_weight.shape[2],
    )
    limits = [limits, to_sibling(limits)]
    shrink_weight = jnp.swapaxes(shrink_weight, 1, 2)
    shrink_factors = [shrink_weight, to_sibling(shrink_weight)]
    expand_factors = [expand_weight, to_sibling(expand_weight)]
    visiting = [to_chip(tagged, shift) for shift in range(1, chips)]
    (third,) = base_terms(tensor_at, tagged, early[0], block, [3], 60)
    visiting, limits = lax.optimization_barrier((visiting, limits))
    blocks = [tagged] + visiting
    third = across(third, 1)

    part = shrink_part(blocks, shrink_factors, batch_at)
    parts = [part, across(part, 1)]
    part, later_tagged = lax.optimization_barrier((part, tagged))
    second, next_door = stream_terms(
        tensor_at, later_tagged, out_weight, block, 1, [early[1]], 60
    )
    second = (wide(second) + wide(third)).astype(BF16)
    parts, second = lax.optimization_barrier((parts, second))
    bit = 2
    while bit < tensor_size:
        part = (wide(parts[0]) + wide(parts[1])).astype(BF16)
        part, next_door = lax.optimization_barrier((part, next_door))
        parts = [part, across(part, bit)]
        bit *= 2
    arrived = [across(second, 2), across(next_door, 1)]
    for ahead in range(4, tensor_size, 2):
        (near,) = stream_terms(tensor_at, tagged, out_weight, block, ahead)
        (far,) = stream_terms(tensor_at, tagged, out_weight, block, ahead + 1)
        arrived.append(across((wide(near) + wide(across(far, 1))).astype(BF16), ahead))

    deltas = expand(blocks, parts, expand_factors, limits, batch_at)
    deltas, late_tagged = lax.optimization_barrier((deltas, tagged))
    (own,) = stream_terms(tensor_at, late_tagged, out_weight, block, 0, (), 60)
    so_far = partial_total([own, deltas[0], arrived[0], *arrived[2:]], 0)
    terms = [partial_total([so_far, arrived[1]], 8 << 20)]
    terms += [to_chip(home, -shift) for shift, home in enumerate(deltas[1:], 1)]
    return total(rows, block, terms)


def solution(mesh):
    placed = (
        P(("groups", "batch"), "tensor", None),
        P(("groups", "batch"), None, None, None),
        P(("groups", "batch"), None, None, None),
        P(("groups", "batch"), None, None),
        P(("groups", "batch"), None, None),
        P(("groups", "batch")),
        P("tensor", None),
        P("batch", "tensor", None),
        P("batch", None, "tensor"),
        P("batch"),
        P(("groups", "batch")),
        P(("groups", "batch")),
    )

    def placed_local(*arrays):
        return local(mesh.shape["tensor"], mesh.shape["batch"], *arrays)

    return jax.shard_map(
        placed_local,
        mesh=mesh,
        in_specs=placed,
        out_specs=P(("groups", "batch"), "tensor"),
        check_vma=False,
    )
```

```python
import functools

import jax
import jax.numpy as jnp
from jax import lax
from jax.experimental import pallas as pl
from jax.experimental.pallas import tpu as pltpu
from jax.sharding import PartitionSpec as P

HQ = 32
KVH = 4
LANES = 128
EARLY = (3,)
EARLY_CUTS = 4
VMEM = pltpu.VMEM
GRANT = 56 << 20
F32, BF16 = jnp.float32, jnp.bfloat16


def permuted(array, axis, size, partner):
    return lax.ppermute(array, axis, [(i, partner(i)) for i in range(size)])


def in_hbm(*arrays):
    return [pltpu.with_memory_space_constraint(array, pltpu.HBM) for array in arrays]


def lane_of(shape):
    return lax.broadcasted_iota(jnp.int32, shape, len(shape) - 1)


def attend_kernel(parts, rank_width, count, group_at, early_at, *refs):
    given, (out_weight, tagged, *early, limits) = refs[:9], refs[9 : 9 + 3 + count]
    scratch = refs[9 + 3 + count :]
    held, (spread_out, small_sems, key_sems, value_sems, early_sems) = scratch[:9], scratch[9:]
    key_cache, value_cache = given[:2]
    keys, values, queries, new_key, new_value, lengths, row_adapter, adapter_list, ranks = held
    rows, heads, width = queries.shape
    positions = key_cache.shape[2]
    group = group_at[0]
    some = rows // parts

    def cache_copies(part):
        at = pl.ds(part * some, some)
        return (
            pltpu.make_async_copy(key_cache.at[at, group], keys.at[at], key_sems.at[part]),
            pltpu.make_async_copy(value_cache.at[at, group], values.at[at], value_sems.at[part]),
        )

    small = [
        pltpu.make_async_copy(given[i], held[i], small_sems.at[i - 2]) for i in range(2, 9)
    ]
    for copy in small:
        copy.start()
    for part in range(parts):
        for copy in cache_copies(part):
            copy.start()
    early_copies = []
    for which, out in enumerate(early):
        rows_each, block = out.shape[0] // EARLY_CUTS, out.shape[1]
        start = pl.multiple_of((early_at[0] ^ EARLY[which]) * block, block)
        for cut in range(EARLY_CUTS):
            at = pl.ds(cut * rows_each, rows_each)
            early_copies.append(
                pltpu.make_async_copy(
                    out_weight.at[at, pl.ds(start, block)],
                    out.at[at],
                    early_sems.at[which * EARLY_CUTS + cut],
                )
            )
    for copy in early_copies:
        copy.start()
    for copy in small:
        copy.wait()
    at_row = lax.broadcasted_iota(jnp.int32, (rows, LANES), 0)
    tag = jnp.zeros((rows, LANES), jnp.int32)
    for row in range(rows):
        tag = jnp.where(at_row == row, adapter_list[row_adapter[row]], tag)
    tag = tag.astype(F32).astype(BF16)
    slot = lax.broadcasted_iota(jnp.int32, limits.shape, 0) * (LANES // rank_width)
    slot = slot + lane_of(limits.shape) // rank_width
    limit = jnp.zeros(limits.shape, jnp.int32)
    for held_at in range(ranks.shape[0]):
        limit = jnp.where(slot == held_at, ranks[held_at], limit)
    limits[...] = limit

    group_row = lax.broadcasted_iota(jnp.int32, new_key.shape, 1) == group
    fresh_key = jnp.sum(
        jnp.where(group_row, new_key[...].astype(F32), F32(0.0)), axis=1, keepdims=True
    )
    fresh_value = jnp.sum(
        jnp.where(group_row, new_value[...].astype(F32), F32(0.0)), axis=1, keepdims=True
    )
    score_scale = width ** (-0.5)
    fresh = jnp.sum(queries[...].astype(F32) * fresh_key, axis=-1, keepdims=True) * score_scale
    for part in range(parts):
        at = slice(part * some, (part + 1) * some)
        key_copy, value_copy = cache_copies(part)
        key_copy.wait()
        scores = (
            lax.dot_general(
                queries[at], keys[at], (((2,), (2,)), ((0,), (0,))), preferred_element_type=F32
            )
            * score_scale
        )
        length = jnp.stack(
            [
                jnp.full((heads, positions), lengths[row], jnp.int32)
                for row in range(part * some, (part + 1) * some)
            ]
        )
        valid = lane_of(scores.shape) < length
        masked = jnp.where(valid, scores, F32(-1e30))
        highest = jnp.maximum(jnp.max(masked, axis=-1, keepdims=True), fresh[at])
        cached_exp = jnp.where(valid, jnp.exp(masked - highest), F32(0.0))
        fresh_exp = jnp.exp(fresh[at] - highest)
        totals = jnp.sum(cached_exp, axis=-1, keepdims=True) + fresh_exp
        cached_w = (cached_exp / totals).astype(BF16)
        fresh_w = (fresh_exp / totals).astype(BF16).astype(F32)
        value_copy.wait()
        attended = lax.dot_general(
            cached_w, values[at], (((2,), (1,)), ((0,), (0,))), preferred_element_type=F32
        )
        attended = attended + fresh_w * fresh_value[at]
        spread_out[pl.ds(part * some * heads, some * heads)] = attended.reshape(
            some * heads, width
        )
    tagged[:, heads * width :] = tag
    for head in range(heads):
        tagged[:, head * width : (head + 1) * width] = spread_out[
            pl.ds(head, rows, stride=heads)
        ].astype(BF16)
    for copy in early_copies:
        copy.wait()


def attend(
    early_at,
    block,
    out_weight,
    queries,
    key_cache,
    value_cache,
    new_key,
    new_value,
    lengths,
    adapter_list,
    row_adapter,
    adapter_rank,
    rank_width,
):
    rows, heads, width = queries.shape
    positions = key_cache.shape[2]
    per_group = HQ // KVH
    group_at = (lax.axis_index("tensor") * heads // per_group).reshape(1).astype(jnp.int32)
    full = -(-heads // 8) * 8
    if full != heads:
        queries = jnp.pad(queries, ((0, 0), (0, full - heads), (0, 0)))
    parts = 2
    smem = pl.BlockSpec(memory_space=pltpu.SMEM)
    away = pl.BlockSpec(memory_space=pl.ANY)
    tagged, *early, limits = pl.pallas_call(
        functools.partial(attend_kernel, parts, rank_width, len(EARLY)),
        out_shape=[
            jax.ShapeDtypeStruct((rows, full * width + LANES), BF16),
            *[VMEM((out_weight.shape[0], block), BF16) for _ in EARLY],
            jax.ShapeDtypeStruct((8, LANES), jnp.int32),
        ],
        in_specs=[smem, smem] + [away] * 10,
        out_specs=[pl.BlockSpec(memory_space=VMEM)] * (2 + len(EARLY)),
        scratch_shapes=[
            VMEM((rows, positions, width), BF16),
            VMEM((rows, positions, width), BF16),
            VMEM(queries.shape, BF16),
            VMEM(new_key.shape, BF16),
            VMEM(new_value.shape, BF16),
            pltpu.SMEM(lengths.shape, jnp.int32),
            pltpu.SMEM(row_adapter.shape, jnp.int32),
            pltpu.SMEM(adapter_list.shape, jnp.int32),
            pltpu.SMEM(adapter_rank.shape, jnp.int32),
            VMEM((rows * full, width), F32),
            pltpu.SemaphoreType.DMA((7,)),
            pltpu.SemaphoreType.DMA((parts,)),
            pltpu.SemaphoreType.DMA((parts,)),
            pltpu.SemaphoreType.DMA((len(EARLY) * EARLY_CUTS,)),
        ],
        compiler_params=pltpu.CompilerParams(vmem_limit_bytes=8 << 20),
        cost_estimate=pl.CostEstimate(
            flops=4 * rows * heads * positions * width,
            bytes_accessed=4 * rows * positions * width,
            transcendentals=rows * heads * positions,
        ),
        name="attention",
    )(
        group_at,
        early_at,
        *in_hbm(
            key_cache,
            value_cache,
            queries,
            new_key,
            new_value,
            lengths,
            row_adapter,
            adapter_list,
            adapter_rank,
            out_weight,
        ),
    )
    if full != heads:
        tagged = jnp.concatenate([tagged[:, : heads * width], tagged[:, full * width :]], axis=1)
    return tagged, early, limits


def put_stacked(out, start, term):
    rows = term.shape[0]
    for column in range(0, term.shape[1], LANES):
        at = (start + column) // LANES * rows
        out[at : at + rows] = term[:, column : column + LANES].astype(out.dtype)


def base_kernel(apart, piece, tensor_at, tagged, weight, *outs):
    width = weight.shape[0]
    for ahead, out in zip(apart, outs):
        block = out.shape[0] // tagged.shape[0] * LANES
        for at in range(0, block, piece):
            start = at
            if weight.shape[1] > block:
                start = pl.multiple_of((tensor_at[0] ^ ahead) * block + at, piece)
            term = jnp.dot(
                tagged[:, :width], weight[:, pl.ds(start, piece)], preferred_element_type=F32
            )
            put_stacked(out, at, term)


def base_terms(tensor_at, tagged, weight, block, apart, cost):
    rows = tagged.shape[0]
    width = weight.shape[0]
    whole = pl.BlockSpec(memory_space=VMEM)
    return pl.pallas_call(
        functools.partial(base_kernel, apart, min(block, 512)),
        out_shape=[
            jax.ShapeDtypeStruct((block // LANES * rows, LANES), BF16 if ahead else F32)
            for ahead in apart
        ],
        in_specs=[pl.BlockSpec(memory_space=pltpu.SMEM), whole, whole],
        out_specs=[whole] * len(apart),
        compiler_params=pltpu.CompilerParams(vmem_limit_bytes=6 << 20),
        cost_estimate=pl.CostEstimate(
            flops=cost * rows * width * block * len(apart),
            bytes_accessed=2 * width * block * len(apart),
            transcendentals=0,
        ),
        name="base_terms",
    )(tensor_at, tagged, weight)


def stream_kernel(ahead, deep, tensor_at, tagged, out_weight, *refs):
    *near, out, held, sums, sems = refs
    _, deep_rows, block = held.shape
    width = out_weight.shape[0]
    count = width // deep_rows
    column = pl.ds(pl.multiple_of((tensor_at[0] ^ ahead) * block, block), block)

    def copy(at):
        return pltpu.make_async_copy(
            out_weight.at[pl.ds(at * deep_rows, deep_rows), column],
            held.at[at % deep],
            sems.at[at % deep],
        )

    for at in range(min(deep, count)):
        copy(at).start()
    piece = min(block, 512)
    if near:
        early, early_out = near
        for start in range(0, block, piece):
            columns = slice(start, start + piece)
            term = jnp.dot(tagged[:, :width], early[:, columns], preferred_element_type=F32)
            put_stacked(early_out, start, term)
    for at in range(count):
        copy(at).wait()
        inputs = slice(at * deep_rows, (at + 1) * deep_rows)
        for start in range(0, block, piece):
            columns = slice(start, start + piece)
            term = jnp.dot(
                tagged[:, inputs], held[at % deep, :, columns], preferred_element_type=F32
            )
            if at:
                term = term + sums[:, columns]
            if at < count - 1:
                sums[:, columns] = term
            else:
                put_stacked(out, start, term)
        if at + deep < count:
            copy(at + deep).start()


def stream_terms(tensor_at, tagged, out_weight, block, ahead, early=(), cost=2):
    rows = tagged.shape[0]
    width = out_weight.shape[0]
    deep, deep_rows = 4, min(width, 256)
    whole = pl.BlockSpec(memory_space=VMEM)
    count = 1 + len(early)
    return pl.pallas_call(
        functools.partial(stream_kernel, ahead, deep),
        out_shape=[jax.ShapeDtypeStruct((block // LANES * rows, LANES), BF16 if ahead else F32)]
        * count,
        in_specs=[pl.BlockSpec(memory_space=pltpu.SMEM), whole, pl.BlockSpec(memory_space=pl.ANY)]
        + [whole] * len(early),
        out_specs=[whole] * count,
        scratch_shapes=[
            VMEM((deep, deep_rows, block), BF16),
            VMEM((rows, block), F32),
            pltpu.SemaphoreType.DMA((deep,)),
        ],
        compiler_params=pltpu.CompilerParams(vmem_limit_bytes=12 << 20),
        cost_estimate=pl.CostEstimate(
            flops=cost * rows * width * block * count,
            bytes_accessed=2 * width * block * count,
            transcendentals=0,
        ),
        name="base_terms",
    )(tensor_at, tagged, *in_hbm(out_weight), *early)


def slots_of(tags, batch_at, pool, tile, per):
    lane = lane_of(tags.shape)
    ids = tags.astype(F32).astype(jnp.int32)
    mine = tile * per + lane // (LANES // per)
    held = tile * per // pool
    return ids - (batch_at[0] ^ held) * pool + held * pool, mine


def shrink_kernel(batch_at, *refs):
    blocks, factors, out = refs[:-3], refs[-3:-1], refs[-1]
    pool, rank_width, width = factors[0].shape
    everyone = jnp.concatenate([block[...] for block in blocks], axis=0)
    per = LANES // rank_width
    lane = lane_of((everyone.shape[0], LANES))
    kept = jnp.zeros(lane.shape, F32)
    for held, weights in enumerate(factors):
        terms = lax.dot_general(
            everyone[:, :width],
            weights[...].reshape(pool * rank_width, width),
            (((1,), (1,)), ((), ())),
            preferred_element_type=F32,
        )
        for tile in range(pool // per):
            slot, mine = slots_of(everyone[:, width:], batch_at, pool, held * pool // per + tile, per)
            kept = kept + jnp.where(
                slot == mine, terms[:, tile * LANES : (tile + 1) * LANES], F32(0.0)
            )
    both = kept + pltpu.roll(kept, rank_width, 1)
    half = both.shape[0] // 2
    packed = jnp.where(lane[:half] < rank_width, both[:half], both[half:])
    out[...] = packed.astype(out.dtype)


def shrink_part(blocks, factors, batch_at):
    pool, rank_width, width = factors[0].shape
    rows = len(blocks) * blocks[0].shape[0]
    smem = pl.BlockSpec(memory_space=pltpu.SMEM)
    whole = pl.BlockSpec(memory_space=VMEM)
    return pl.pallas_call(
        shrink_kernel,
        out_shape=jax.ShapeDtypeStruct((rows // 2, LANES), BF16),
        in_specs=[smem] + [whole] * (len(blocks) + 2),
        out_specs=whole,
        compiler_params=pltpu.CompilerParams(vmem_limit_bytes=8 << 20),
        cost_estimate=pl.CostEstimate(
            flops=4 * rows * width * pool * rank_width,
            bytes_accessed=2 * width * (rows + 2 * pool * rank_width),
            transcendentals=0,
        ),
        name="shrink",
    )(batch_at, *blocks, *factors)


def expand_kernel(count, sums, rank_width, batch_at, *refs):
    limits, refs = refs[:2], refs[2:]
    tags, parts = refs[:count], refs[count : count + sums]
    factors, outs = refs[count + sums : count + sums + 2], refs[count + sums + 2 :]
    tags = jnp.concatenate([tag[...] for tag in tags], axis=0)
    total = parts[0][...].astype(F32)
    for part in parts[1:]:
        total = total + part[...].astype(F32)
    total = total.astype(BF16).astype(F32)
    other = pltpu.roll(total, rank_width, 1)
    low = lane_of(total.shape) < rank_width
    shrink = jnp.concatenate(
        [jnp.where(low, total, other), jnp.where(low, other, total)], axis=0
    )
    per = LANES // rank_width
    inputs, block = factors[0].shape
    pool = inputs // rank_width
    tiles = []
    for tile in range(2 * pool // per):
        slot, mine = slots_of(tags, batch_at, pool, tile, per)
        held, at = divmod(tile * per, pool)
        limit = limits[held][at // per : at // per + 1]
        keep = (slot == mine) & (lane_of(tags.shape) % rank_width < limit)
        tiles.append(jnp.where(keep, shrink, F32(0.0)).astype(BF16))
    half = len(tiles) // 2
    spreads = [jnp.concatenate(tiles[:half], axis=1), jnp.concatenate(tiles[half:], axis=1)]
    rows = tags.shape[0] // count
    piece = min(block, 512)
    for at in range(0, block, piece):
        delta = sum(
            jnp.dot(spread, each[:, at : at + piece], preferred_element_type=F32)
            for spread, each in zip(spreads, factors)
        )
        for which, out in enumerate(outs):
            put_stacked(out, at, delta[which * rows : (which + 1) * rows])


def expand(blocks, parts, factors, limits, batch_at):
    pool, rank_width, block = factors[0].shape
    rows, tagged_width = blocks[0].shape
    count = len(blocks)
    stack = rows * block // LANES
    tag = pl.BlockSpec((rows, LANES), lambda i: (0, tagged_width // LANES - 1))
    full = pl.BlockSpec((pool * rank_width, block), lambda i: (0, 0))
    part = pl.BlockSpec(parts[0].shape, lambda i: (0, 0))
    return pl.pallas_call(
        functools.partial(expand_kernel, count, len(parts), rank_width),
        grid=(1,),
        out_shape=[jax.ShapeDtypeStruct((stack, LANES), BF16) for _ in blocks],
        in_specs=[pl.BlockSpec(memory_space=pltpu.SMEM)]
        + [pl.BlockSpec(each.shape, lambda i: (0, 0)) for each in limits]
        + [tag] * count
        + [part] * len(parts)
        + [full] * 2,
        out_specs=[pl.BlockSpec((stack, LANES), lambda i: (0, 0)) for _ in blocks],
        compiler_params=pltpu.CompilerParams(vmem_limit_bytes=16 << 20),
        cost_estimate=pl.CostEstimate(
            flops=4 * rows * count * pool * rank_width * block,
            bytes_accessed=2 * pool * rank_width * block,
            transcendentals=0,
        ),
        name="expand",
    )(batch_at, *limits, *blocks, *parts, *[each.reshape(pool * rank_width, block) for each in factors])


def total_kernel(*refs):
    terms, out = refs[:-1], refs[-1]
    rows = out.shape[0]
    for column in range(0, out.shape[1], LANES):
        at = slice(column // LANES * rows, (column // LANES + 1) * rows)
        total = terms[0][at].astype(F32)
        for term in terms[1:]:
            total = total + term[at].astype(F32)
        out[:, column : column + LANES] = total.astype(out.dtype)


def total(rows, block, terms):
    whole = pl.BlockSpec(memory_space=VMEM)
    return pl.pallas_call(
        total_kernel,
        out_shape=jax.ShapeDtypeStruct((rows, block), BF16),
        in_specs=[whole] * len(terms),
        out_specs=whole,
        compiler_params=pltpu.CompilerParams(vmem_limit_bytes=8 << 20),
        cost_estimate=pl.CostEstimate(
            flops=rows * block * len(terms),
            bytes_accessed=2 * rows * block * (1 + len(terms)),
            transcendentals=0,
        ),
        name="total",
    )(*terms)


def partial_kernel(*refs):
    terms, out = refs[:-1], refs[-1]
    total = terms[0][...].astype(F32)
    for term in terms[1:]:
        total = total + term[...].astype(F32)
    out[...] = total


def partial_total(terms, weight):
    whole = pl.BlockSpec(memory_space=VMEM)
    return pl.pallas_call(
        partial_kernel,
        out_shape=jax.ShapeDtypeStruct(terms[0].shape, F32),
        in_specs=[whole] * len(terms),
        out_specs=whole,
        compiler_params=pltpu.CompilerParams(vmem_limit_bytes=8 << 20),
        cost_estimate=pl.CostEstimate(
            flops=weight,
            bytes_accessed=4 * terms[0].size * len(terms),
            transcendentals=0,
        ),
        name="partial_total",
    )(*terms)


def local(
    tensor_size,
    batch_size,
    queries,
    key_cache,
    value_cache,
    new_key,
    new_value,
    lengths,
    out_weight,
    shrink_weight,
    expand_weight,
    adapter_rank,
    adapter_list,
    row_adapter,
):
    rows = queries.shape[0]
    block = expand_weight.shape[2]
    chips = batch_size // 2
    batch_at = lax.axis_index("batch").reshape(1).astype(jnp.int32)
    tensor_at = lax.axis_index("tensor").reshape(1).astype(jnp.int32)

    def to_sibling(array):
        return permuted(array, "batch", batch_size, lambda i: i ^ 1)

    def to_chip(array, shift):
        return permuted(array, "batch", batch_size, lambda i: (i + 2 * shift) % batch_size)

    def across(array, bit):
        return permuted(array, "tensor", tensor_size, lambda i: i ^ bit)

    def wide(array):
        return array.astype(F32)

    stack = block // LANES * rows
    tagged, early, limits = attend(
        tensor_at,
        block,
        out_weight,
        queries,
        key_cache,
        value_cache,
        new_key,
        new_value,
        lengths,
        adapter_list,
        row_adapter,
        adapter_rank,
        shrink_weight.shape[2],
    )
    limits = [limits, to_sibling(limits)]
    shrink_weight = jnp.swapaxes(shrink_weight, 1, 2)
    shrink_factors = [shrink_weight, to_sibling(shrink_weight)]
    expand_factors = [expand_weight, to_sibling(expand_weight)]
    visiting = [to_chip(tagged, shift) for shift in range(1, chips)]
    (third,) = base_terms(tensor_at, tagged, early[0], block, [3], 60)
    visiting, limits = lax.optimization_barrier((visiting, limits))
    blocks = [tagged] + visiting
    third = across(third, 1)

    part = shrink_part(blocks, shrink_factors, batch_at)
    parts = [part, across(part, 1)]
    part, later_tagged = lax.optimization_barrier((part, tagged))
    (second,) = stream_terms(tensor_at, later_tagged, out_weight, block, 2, (), 60)
    second = (wide(second) + wide(third)).astype(BF16)
    parts, second, later_tagged = lax.optimization_barrier((parts, second, later_tagged))
    (next_door,) = stream_terms(tensor_at, later_tagged, out_weight, block, 1, (), 60)
    bit = 2
    while bit < tensor_size:
        part = (wide(parts[0]) + wide(parts[1])).astype(BF16)
        parts = [part, across(part, bit)]
        bit *= 2
    arrived = [across(second, 2), across(next_door, 1)]
    for ahead in range(4, tensor_size, 2):
        (near,) = stream_terms(tensor_at, tagged, out_weight, block, ahead)
        (far,) = stream_terms(tensor_at, tagged, out_weight, block, ahead + 1)
        arrived.append(across((wide(near) + wide(across(far, 1))).astype(BF16), ahead))

    deltas = expand(blocks, parts, expand_factors, limits, batch_at)
    deltas, late_tagged = lax.optimization_barrier((deltas, tagged))
    (own,) = stream_terms(tensor_at, late_tagged, out_weight, block, 0, (), 60)
    so_far = partial_total([own, deltas[0], arrived[0], *arrived[2:]], 1000)
    terms = [partial_total([so_far, arrived[1]], 1000)]
    terms += [to_chip(home, -shift) for shift, home in enumerate(deltas[1:], 1)]
    return total(rows, block, terms)


def solution(mesh):
    placed = (
        P(("groups", "batch"), "tensor", None),
        P(("groups", "batch"), None, None, None),
        P(("groups", "batch"), None, None, None),
        P(("groups", "batch"), None, None),
        P(("groups", "batch"), None, None),
        P(("groups", "batch")),
        P("tensor", None),
        P("batch", "tensor", None),
        P("batch", None, "tensor"),
        P("batch"),
        P(("groups", "batch")),
        P(("groups", "batch")),
    )

    def placed_local(*arrays):
        return local(mesh.shape["tensor"], mesh.shape["batch"], *arrays)

    return jax.shard_map(
        placed_local,
        mesh=mesh,
        in_specs=placed,
        out_specs=P(("groups", "batch"), "tensor"),
        check_vma=False,
    )
```

```python
import functools

import jax
import jax.numpy as jnp
from jax import lax
from jax.experimental import pallas as pl
from jax.experimental.pallas import tpu as pltpu
from jax.sharding import PartitionSpec as P

HQ = 32
KVH = 4
LANES = 128
VMEM = pltpu.VMEM
GRANT = 56 << 20
F32, BF16 = jnp.float32, jnp.bfloat16


def permuted(array, axis, size, partner):
    return lax.ppermute(array, axis, [(i, partner(i)) for i in range(size)])


def in_hbm(*arrays):
    return [pltpu.with_memory_space_constraint(array, pltpu.HBM) for array in arrays]


def lane_of(shape):
    return lax.broadcasted_iota(jnp.int32, shape, len(shape) - 1)


def attend_kernel(parts, rank_width, group_at, early_at, *refs):
    given, (out_weight, tagged, early, limits, *scratch) = refs[:9], refs[9:]
    held, (spread_out, small_sems, key_sems, value_sems, early_sem) = scratch[:9], scratch[9:]
    key_cache, value_cache = given[:2]
    keys, values, queries, new_key, new_value, lengths, row_adapter, adapter_list, ranks = held
    rows, heads, width = queries.shape
    positions = key_cache.shape[2]
    group = group_at[0]
    some = rows // parts

    def cache_copies(part):
        at = pl.ds(part * some, some)
        return (
            pltpu.make_async_copy(key_cache.at[at, group], keys.at[at], key_sems.at[part]),
            pltpu.make_async_copy(value_cache.at[at, group], values.at[at], value_sems.at[part]),
        )

    small = [
        pltpu.make_async_copy(given[i], held[i], small_sems.at[i - 2]) for i in range(2, 9)
    ]
    for copy in small:
        copy.start()
    for part in range(parts):
        for copy in cache_copies(part):
            copy.start()
    block = early.shape[1]
    start = pl.multiple_of(early_at[0] * block, block)
    early_copy = pltpu.make_async_copy(out_weight.at[:, pl.ds(start, block)], early, early_sem)
    early_copy.start()
    for copy in small:
        copy.wait()
    at_row = lax.broadcasted_iota(jnp.int32, (rows, LANES), 0)
    tag = jnp.zeros((rows, LANES), jnp.int32)
    for row in range(rows):
        tag = jnp.where(at_row == row, adapter_list[row_adapter[row]], tag)
    tag = tag.astype(F32).astype(BF16)
    slot = lax.broadcasted_iota(jnp.int32, limits.shape, 0) * (LANES // rank_width)
    slot = slot + lane_of(limits.shape) // rank_width
    limit = jnp.zeros(limits.shape, jnp.int32)
    for held_at in range(ranks.shape[0]):
        limit = jnp.where(slot == held_at, ranks[held_at], limit)
    limits[...] = limit

    group_row = lax.broadcasted_iota(jnp.int32, new_key.shape, 1) == group
    fresh_key = jnp.sum(
        jnp.where(group_row, new_key[...].astype(F32), F32(0.0)), axis=1, keepdims=True
    )
    fresh_value = jnp.sum(
        jnp.where(group_row, new_value[...].astype(F32), F32(0.0)), axis=1, keepdims=True
    )
    score_scale = width ** (-0.5)
    fresh = jnp.sum(queries[...].astype(F32) * fresh_key, axis=-1, keepdims=True) * score_scale
    for part in range(parts):
        at = slice(part * some, (part + 1) * some)
        key_copy, value_copy = cache_copies(part)
        key_copy.wait()
        scores = (
            lax.dot_general(
                queries[at], keys[at], (((2,), (2,)), ((0,), (0,))), preferred_element_type=F32
            )
            * score_scale
        )
        length = jnp.stack(
            [
                jnp.full((heads, positions), lengths[row], jnp.int32)
                for row in range(part * some, (part + 1) * some)
            ]
        )
        valid = lane_of(scores.shape) < length
        masked = jnp.where(valid, scores, F32(-1e30))
        highest = jnp.maximum(jnp.max(masked, axis=-1, keepdims=True), fresh[at])
        cached_exp = jnp.where(valid, jnp.exp(masked - highest), F32(0.0))
        fresh_exp = jnp.exp(fresh[at] - highest)
        totals = jnp.sum(cached_exp, axis=-1, keepdims=True) + fresh_exp
        cached_w = (cached_exp / totals).astype(BF16)
        fresh_w = (fresh_exp / totals).astype(BF16).astype(F32)
        value_copy.wait()
        attended = lax.dot_general(
            cached_w, values[at], (((2,), (1,)), ((0,), (0,))), preferred_element_type=F32
        )
        attended = attended + fresh_w * fresh_value[at]
        spread_out[pl.ds(part * some * heads, some * heads)] = attended.reshape(
            some * heads, width
        )
    tagged[:, heads * width :] = tag
    for head in range(heads):
        tagged[:, head * width : (head + 1) * width] = spread_out[
            pl.ds(head, rows, stride=heads)
        ].astype(BF16)
    early_copy.wait()


def attend(
    early_at,
    block,
    out_weight,
    queries,
    key_cache,
    value_cache,
    new_key,
    new_value,
    lengths,
    adapter_list,
    row_adapter,
    adapter_rank,
    rank_width,
):
    rows, heads, width = queries.shape
    positions = key_cache.shape[2]
    per_group = HQ // KVH
    group_at = (lax.axis_index("tensor") * heads // per_group).reshape(1).astype(jnp.int32)
    full = -(-heads // 8) * 8
    if full != heads:
        queries = jnp.pad(queries, ((0, 0), (0, full - heads), (0, 0)))
    parts = 2
    smem = pl.BlockSpec(memory_space=pltpu.SMEM)
    away = pl.BlockSpec(memory_space=pl.ANY)
    tagged, early, limits = pl.pallas_call(
        functools.partial(attend_kernel, parts, rank_width),
        out_shape=[
            jax.ShapeDtypeStruct((rows, full * width + LANES), BF16),
            VMEM((out_weight.shape[0], block), BF16),
            jax.ShapeDtypeStruct((8, LANES), jnp.int32),
        ],
        in_specs=[smem, smem] + [away] * 10,
        out_specs=[pl.BlockSpec(memory_space=VMEM)] * 3,
        scratch_shapes=[
            VMEM((rows, positions, width), BF16),
            VMEM((rows, positions, width), BF16),
            VMEM(queries.shape, BF16),
            VMEM(new_key.shape, BF16),
            VMEM(new_value.shape, BF16),
            pltpu.SMEM(lengths.shape, jnp.int32),
            pltpu.SMEM(row_adapter.shape, jnp.int32),
            pltpu.SMEM(adapter_list.shape, jnp.int32),
            pltpu.SMEM(adapter_rank.shape, jnp.int32),
            VMEM((rows * full, width), F32),
            pltpu.SemaphoreType.DMA((7,)),
            pltpu.SemaphoreType.DMA((parts,)),
            pltpu.SemaphoreType.DMA((parts,)),
            pltpu.SemaphoreType.DMA,
        ],
        compiler_params=pltpu.CompilerParams(vmem_limit_bytes=8 << 20),
        cost_estimate=pl.CostEstimate(
            flops=3 * 10**9,
            bytes_accessed=4 * rows * positions * width,
            transcendentals=rows * heads * positions,
        ),
        name="attention",
    )(
        group_at,
        early_at,
        *in_hbm(
            key_cache,
            value_cache,
            queries,
            new_key,
            new_value,
            lengths,
            row_adapter,
            adapter_list,
            adapter_rank,
            out_weight,
        ),
    )
    if full != heads:
        tagged = jnp.concatenate([tagged[:, : heads * width], tagged[:, full * width :]], axis=1)
    return tagged, early, limits


def put_stacked(out, start, term):
    rows = term.shape[0]
    for column in range(0, term.shape[1], LANES):
        at = (start + column) // LANES * rows
        out[at : at + rows] = term[:, column : column + LANES].astype(out.dtype)


def base_kernel(apart, piece, tensor_at, tagged, weight, *outs):
    width = weight.shape[0]
    for ahead, out in zip(apart, outs):
        block = out.shape[0] // tagged.shape[0] * LANES
        for at in range(0, block, piece):
            start = at
            if weight.shape[1] > block:
                start = pl.multiple_of((tensor_at[0] ^ ahead) * block + at, piece)
            term = jnp.dot(
                tagged[:, :width], weight[:, pl.ds(start, piece)], preferred_element_type=F32
            )
            put_stacked(out, at, term)


def base_terms(tensor_at, tagged, weight, block, apart, cost):
    rows = tagged.shape[0]
    width = weight.shape[0]
    whole = pl.BlockSpec(memory_space=VMEM)
    return pl.pallas_call(
        functools.partial(base_kernel, apart, min(block, 512)),
        out_shape=[
            jax.ShapeDtypeStruct((block // LANES * rows, LANES), BF16 if ahead else F32)
            for ahead in apart
        ],
        in_specs=[pl.BlockSpec(memory_space=pltpu.SMEM), whole, whole],
        out_specs=[whole] * len(apart),
        compiler_params=pltpu.CompilerParams(vmem_limit_bytes=24 << 20),
        cost_estimate=pl.CostEstimate(
            flops=cost * rows * width * block * len(apart),
            bytes_accessed=2 * width * block * len(apart),
            transcendentals=0,
        ),
        name="base_terms",
    )(tensor_at, tagged, weight)


def slots_of(tags, batch_at, pool, tile, per):
    lane = lane_of(tags.shape)
    ids = tags.astype(F32).astype(jnp.int32)
    mine = tile * per + lane // (LANES // per)
    held = tile * per // pool
    return ids - (batch_at[0] ^ held) * pool + held * pool, mine


def shrink_kernel(batch_at, *refs):
    blocks, factors, out = refs[:-3], refs[-3:-1], refs[-1]
    pool, rank_width, width = factors[0].shape
    everyone = jnp.concatenate([block[...] for block in blocks], axis=0)
    per = LANES // rank_width
    lane = lane_of((everyone.shape[0], LANES))
    kept = jnp.zeros(lane.shape, F32)
    for held, weights in enumerate(factors):
        terms = lax.dot_general(
            everyone[:, :width],
            weights[...].reshape(pool * rank_width, width),
            (((1,), (1,)), ((), ())),
            preferred_element_type=F32,
        )
        for tile in range(pool // per):
            slot, mine = slots_of(everyone[:, width:], batch_at, pool, held * pool // per + tile, per)
            kept = kept + jnp.where(
                slot == mine, terms[:, tile * LANES : (tile + 1) * LANES], F32(0.0)
            )
    both = kept + pltpu.roll(kept, rank_width, 1)
    half = both.shape[0] // 2
    packed = jnp.where(lane[:half] < rank_width, both[:half], both[half:])
    out[...] = packed.astype(out.dtype)


def shrink_part(blocks, factors, batch_at):
    pool, rank_width, width = factors[0].shape
    rows = len(blocks) * blocks[0].shape[0]
    smem = pl.BlockSpec(memory_space=pltpu.SMEM)
    whole = pl.BlockSpec(memory_space=VMEM)
    return pl.pallas_call(
        shrink_kernel,
        out_shape=jax.ShapeDtypeStruct((rows // 2, LANES), BF16),
        in_specs=[smem] + [whole] * (len(blocks) + 2),
        out_specs=whole,
        compiler_params=pltpu.CompilerParams(vmem_limit_bytes=8 << 20),
        cost_estimate=pl.CostEstimate(
            flops=4 * rows * width * pool * rank_width,
            bytes_accessed=2 * width * (rows + 2 * pool * rank_width),
            transcendentals=0,
        ),
        name="shrink",
    )(batch_at, *blocks, *factors)


def expand_kernel(count, sums, rank_width, batch_at, *refs):
    limits, refs = refs[:2], refs[2:]
    tags, parts = refs[:count], refs[count : count + sums]
    factors, outs = refs[count + sums : count + sums + 2], refs[count + sums + 2 :]
    tags = jnp.concatenate([tag[...] for tag in tags], axis=0)
    total = parts[0][...].astype(F32)
    for part in parts[1:]:
        total = total + part[...].astype(F32)
    total = total.astype(BF16).astype(F32)
    other = pltpu.roll(total, rank_width, 1)
    low = lane_of(total.shape) < rank_width
    shrink = jnp.concatenate(
        [jnp.where(low, total, other), jnp.where(low, other, total)], axis=0
    )
    per = LANES // rank_width
    inputs, block = factors[0].shape
    pool = inputs // rank_width
    tiles = []
    for tile in range(2 * pool // per):
        slot, mine = slots_of(tags, batch_at, pool, tile, per)
        held, at = divmod(tile * per, pool)
        limit = limits[held][at // per : at // per + 1]
        keep = (slot == mine) & (lane_of(tags.shape) % rank_width < limit)
        tiles.append(jnp.where(keep, shrink, F32(0.0)).astype(BF16))
    half = len(tiles) // 2
    spreads = [jnp.concatenate(tiles[:half], axis=1), jnp.concatenate(tiles[half:], axis=1)]
    rows = tags.shape[0] // count
    piece = min(block, 512)
    for at in range(0, block, piece):
        delta = sum(
            jnp.dot(spread, each[:, at : at + piece], preferred_element_type=F32)
            for spread, each in zip(spreads, factors)
        )
        for which, out in enumerate(outs):
            put_stacked(out, at, delta[which * rows : (which + 1) * rows])


def expand(blocks, parts, factors, limits, batch_at):
    pool, rank_width, block = factors[0].shape
    rows, tagged_width = blocks[0].shape
    count = len(blocks)
    stack = rows * block // LANES
    tag = pl.BlockSpec((rows, LANES), lambda i: (0, tagged_width // LANES - 1))
    full = pl.BlockSpec((pool * rank_width, block), lambda i: (0, 0))
    part = pl.BlockSpec(parts[0].shape, lambda i: (0, 0))
    return pl.pallas_call(
        functools.partial(expand_kernel, count, len(parts), rank_width),
        grid=(1,),
        out_shape=[jax.ShapeDtypeStruct((stack, LANES), BF16) for _ in blocks],
        in_specs=[pl.BlockSpec(memory_space=pltpu.SMEM)]
        + [pl.BlockSpec(each.shape, lambda i: (0, 0)) for each in limits]
        + [tag] * count
        + [part] * len(parts)
        + [full] * 2,
        out_specs=[pl.BlockSpec((stack, LANES), lambda i: (0, 0)) for _ in blocks],
        compiler_params=pltpu.CompilerParams(vmem_limit_bytes=16 << 20),
        cost_estimate=pl.CostEstimate(
            flops=4 * rows * count * pool * rank_width * block,
            bytes_accessed=2 * pool * rank_width * block,
            transcendentals=0,
        ),
        name="expand",
    )(batch_at, *limits, *blocks, *parts, *[each.reshape(pool * rank_width, block) for each in factors])


def total_kernel(*refs):
    terms, out = refs[:-1], refs[-1]
    rows = out.shape[0]
    for column in range(0, out.shape[1], LANES):
        at = slice(column // LANES * rows, (column // LANES + 1) * rows)
        total = terms[0][at].astype(F32)
        for term in terms[1:]:
            total = total + term[at].astype(F32)
        out[:, column : column + LANES] = total.astype(out.dtype)


def total(rows, block, terms):
    whole = pl.BlockSpec(memory_space=VMEM)
    return pl.pallas_call(
        total_kernel,
        out_shape=jax.ShapeDtypeStruct((rows, block), BF16),
        in_specs=[whole] * len(terms),
        out_specs=whole,
        compiler_params=pltpu.CompilerParams(vmem_limit_bytes=8 << 20),
        cost_estimate=pl.CostEstimate(
            flops=rows * block * len(terms),
            bytes_accessed=2 * rows * block * (1 + len(terms)),
            transcendentals=0,
        ),
        name="total",
    )(*terms)


def partial_kernel(*refs):
    terms, out = refs[:-1], refs[-1]
    total = terms[0][...].astype(F32)
    for term in terms[1:]:
        total = total + term[...].astype(F32)
    out[...] = total


def partial_total(terms, weight):
    whole = pl.BlockSpec(memory_space=VMEM)
    return pl.pallas_call(
        partial_kernel,
        out_shape=jax.ShapeDtypeStruct(terms[0].shape, F32),
        in_specs=[whole] * len(terms),
        out_specs=whole,
        compiler_params=pltpu.CompilerParams(vmem_limit_bytes=8 << 20),
        cost_estimate=pl.CostEstimate(
            flops=terms[0].size * len(terms),
            bytes_accessed=4 * terms[0].size + weight,
            transcendentals=0,
        ),
        name="partial_total",
    )(*terms)


def local(
    tensor_size,
    batch_size,
    queries,
    key_cache,
    value_cache,
    new_key,
    new_value,
    lengths,
    out_weight,
    shrink_weight,
    expand_weight,
    adapter_rank,
    adapter_list,
    row_adapter,
):
    rows = queries.shape[0]
    block = expand_weight.shape[2]
    chips = batch_size // 2
    batch_at = lax.axis_index("batch").reshape(1).astype(jnp.int32)
    tensor_at = lax.axis_index("tensor").reshape(1).astype(jnp.int32)

    def to_sibling(array):
        return permuted(array, "batch", batch_size, lambda i: i ^ 1)

    def to_chip(array, shift):
        return permuted(array, "batch", batch_size, lambda i: (i + 2 * shift) % batch_size)

    def across(array, bit):
        return permuted(array, "tensor", tensor_size, lambda i: i ^ bit)

    def wide(array):
        return array.astype(F32)

    stack = block // LANES * rows
    tagged, early, limits = attend(
        tensor_at ^ 3,
        block,
        out_weight,
        queries,
        key_cache,
        value_cache,
        new_key,
        new_value,
        lengths,
        adapter_list,
        row_adapter,
        adapter_rank,
        shrink_weight.shape[2],
    )
    limits = [limits, to_sibling(limits)]
    shrink_weight = jnp.swapaxes(shrink_weight, 1, 2)
    shrink_factors = [shrink_weight, to_sibling(shrink_weight)]
    expand_factors = [expand_weight, to_sibling(expand_weight)]
    visiting = [to_chip(tagged, shift) for shift in range(1, chips)]
    weight = out_weight
    (third,) = base_terms(tensor_at, tagged, early, block, [3], 20)
    visiting, limits = lax.optimization_barrier((visiting, limits))
    blocks = [tagged] + visiting
    third = across(third, 1)

    part = shrink_part(blocks, shrink_factors, batch_at)
    parts = [part, across(part, 1)]
    part, later_tagged = lax.optimization_barrier((part, tagged))
    second, next_door = base_terms(tensor_at, later_tagged, weight, block, [2, 1], 20)
    second = (wide(second) + wide(third)).astype(BF16)
    parts, second = lax.optimization_barrier((parts, second))
    bit = 2
    while bit < tensor_size:
        part = (wide(parts[0]) + wide(parts[1])).astype(BF16)
        part, next_door = lax.optimization_barrier((part, next_door))
        parts = [part, across(part, bit)]
        bit *= 2
    arrived = [across(second, 2), across(next_door, 1)]
    for ahead in range(4, tensor_size, 2):
        near, far = base_terms(tensor_at, tagged, weight, block, [ahead, ahead + 1], 20)
        arrived.append(across((wide(near) + wide(across(far, 1))).astype(BF16), ahead))

    deltas = expand(blocks, parts, expand_factors, limits, batch_at)
    deltas, late_tagged = lax.optimization_barrier((deltas, tagged))
    (own,) = base_terms(tensor_at, late_tagged, weight, block, [0], 20)
    so_far = partial_total([own, deltas[0], arrived[0], *arrived[2:]], 0)
    terms = [partial_total([so_far, arrived[1]], 8 << 20)]
    terms += [to_chip(home, -shift) for shift, home in enumerate(deltas[1:], 1)]
    return total(rows, block, terms)


def solution(mesh):
    placed = (
        P(("groups", "batch"), "tensor", None),
        P(("groups", "batch"), None, None, None),
        P(("groups", "batch"), None, None, None),
        P(("groups", "batch"), None, None),
        P(("groups", "batch"), None, None),
        P(("groups", "batch")),
        P("tensor", None),
        P("batch", "tensor", None),
        P("batch", None, "tensor"),
        P("batch"),
        P(("groups", "batch")),
        P(("groups", "batch")),
    )

    def placed_local(*arrays):
        return local(mesh.shape["tensor"], mesh.shape["batch"], *arrays)

    return jax.shard_map(
        placed_local,
        mesh=mesh,
        in_specs=placed,
        out_specs=P(("groups", "batch"), "tensor"),
        check_vma=False,
    )
```

```python
import functools

import jax
import jax.numpy as jnp
from jax import lax
from jax.experimental import pallas as pl
from jax.experimental.pallas import tpu as pltpu
from jax.sharding import PartitionSpec as P

HQ = 32
KVH = 4
LANES = 128
VMEM = pltpu.VMEM
GRANT = 56 << 20
F32, BF16 = jnp.float32, jnp.bfloat16


def permuted(array, axis, size, partner):
    return lax.ppermute(array, axis, [(i, partner(i)) for i in range(size)])


def in_hbm(*arrays):
    return [pltpu.with_memory_space_constraint(array, pltpu.HBM) for array in arrays]


def lane_of(shape):
    return lax.broadcasted_iota(jnp.int32, shape, len(shape) - 1)


def attend_kernel(parts, rank_width, group_at, early_at, *refs):
    given, (out_weight, tagged, early, limits, *scratch) = refs[:9], refs[9:]
    held, (spread_out, small_sems, key_sems, value_sems, early_sem) = scratch[:9], scratch[9:]
    key_cache, value_cache = given[:2]
    keys, values, queries, new_key, new_value, lengths, row_adapter, adapter_list, ranks = held
    rows, heads, width = queries.shape
    positions = key_cache.shape[2]
    group = group_at[0]
    some = rows // parts

    def cache_copies(part):
        at = pl.ds(part * some, some)
        return (
            pltpu.make_async_copy(key_cache.at[at, group], keys.at[at], key_sems.at[part]),
            pltpu.make_async_copy(value_cache.at[at, group], values.at[at], value_sems.at[part]),
        )

    small = [
        pltpu.make_async_copy(given[i], held[i], small_sems.at[i - 2]) for i in range(2, 9)
    ]
    for copy in small:
        copy.start()
    for part in range(parts):
        for copy in cache_copies(part):
            copy.start()
    block = early.shape[1]
    start = pl.multiple_of(early_at[0] * block, block)
    early_copy = pltpu.make_async_copy(out_weight.at[:, pl.ds(start, block)], early, early_sem)
    early_copy.start()
    for copy in small:
        copy.wait()
    at_row = lax.broadcasted_iota(jnp.int32, (rows, LANES), 0)
    tag = jnp.zeros((rows, LANES), jnp.int32)
    for row in range(rows):
        tag = jnp.where(at_row == row, adapter_list[row_adapter[row]], tag)
    tag = tag.astype(F32).astype(BF16)
    slot = lax.broadcasted_iota(jnp.int32, limits.shape, 0) * (LANES // rank_width)
    slot = slot + lane_of(limits.shape) // rank_width
    limit = jnp.zeros(limits.shape, jnp.int32)
    for held_at in range(ranks.shape[0]):
        limit = jnp.where(slot == held_at, ranks[held_at], limit)
    limits[...] = limit

    group_row = lax.broadcasted_iota(jnp.int32, new_key.shape, 1) == group
    fresh_key = jnp.sum(
        jnp.where(group_row, new_key[...].astype(F32), F32(0.0)), axis=1, keepdims=True
    )
    fresh_value = jnp.sum(
        jnp.where(group_row, new_value[...].astype(F32), F32(0.0)), axis=1, keepdims=True
    )
    score_scale = width ** (-0.5)
    fresh = jnp.sum(queries[...].astype(F32) * fresh_key, axis=-1, keepdims=True) * score_scale
    for part in range(parts):
        at = slice(part * some, (part + 1) * some)
        key_copy, value_copy = cache_copies(part)
        key_copy.wait()
        scores = (
            lax.dot_general(
                queries[at], keys[at], (((2,), (2,)), ((0,), (0,))), preferred_element_type=F32
            )
            * score_scale
        )
        length = jnp.stack(
            [
                jnp.full((heads, positions), lengths[row], jnp.int32)
                for row in range(part * some, (part + 1) * some)
            ]
        )
        valid = lane_of(scores.shape) < length
        masked = jnp.where(valid, scores, F32(-1e30))
        highest = jnp.maximum(jnp.max(masked, axis=-1, keepdims=True), fresh[at])
        cached_exp = jnp.where(valid, jnp.exp(masked - highest), F32(0.0))
        fresh_exp = jnp.exp(fresh[at] - highest)
        totals = jnp.sum(cached_exp, axis=-1, keepdims=True) + fresh_exp
        cached_w = (cached_exp / totals).astype(BF16)
        fresh_w = (fresh_exp / totals).astype(BF16).astype(F32)
        value_copy.wait()
        attended = lax.dot_general(
            cached_w, values[at], (((2,), (1,)), ((0,), (0,))), preferred_element_type=F32
        )
        attended = attended + fresh_w * fresh_value[at]
        spread_out[pl.ds(part * some * heads, some * heads)] = attended.reshape(
            some * heads, width
        )
    tagged[:, heads * width :] = tag
    for head in range(heads):
        tagged[:, head * width : (head + 1) * width] = spread_out[
            pl.ds(head, rows, stride=heads)
        ].astype(BF16)
    early_copy.wait()


def attend(
    early_at,
    block,
    out_weight,
    queries,
    key_cache,
    value_cache,
    new_key,
    new_value,
    lengths,
    adapter_list,
    row_adapter,
    adapter_rank,
    rank_width,
):
    rows, heads, width = queries.shape
    positions = key_cache.shape[2]
    per_group = HQ // KVH
    group_at = (lax.axis_index("tensor") * heads // per_group).reshape(1).astype(jnp.int32)
    full = -(-heads // 8) * 8
    if full != heads:
        queries = jnp.pad(queries, ((0, 0), (0, full - heads), (0, 0)))
    parts = 2
    smem = pl.BlockSpec(memory_space=pltpu.SMEM)
    away = pl.BlockSpec(memory_space=pl.ANY)
    tagged, early, limits = pl.pallas_call(
        functools.partial(attend_kernel, parts, rank_width),
        out_shape=[
            jax.ShapeDtypeStruct((rows, full * width + LANES), BF16),
            VMEM((out_weight.shape[0], block), BF16),
            jax.ShapeDtypeStruct((8, LANES), jnp.int32),
        ],
        in_specs=[smem, smem] + [away] * 10,
        out_specs=[pl.BlockSpec(memory_space=VMEM)] * 3,
        scratch_shapes=[
            VMEM((rows, positions, width), BF16),
            VMEM((rows, positions, width), BF16),
            VMEM(queries.shape, BF16),
            VMEM(new_key.shape, BF16),
            VMEM(new_value.shape, BF16),
            pltpu.SMEM(lengths.shape, jnp.int32),
            pltpu.SMEM(row_adapter.shape, jnp.int32),
            pltpu.SMEM(adapter_list.shape, jnp.int32),
            pltpu.SMEM(adapter_rank.shape, jnp.int32),
            VMEM((rows * full, width), F32),
            pltpu.SemaphoreType.DMA((7,)),
            pltpu.SemaphoreType.DMA((parts,)),
            pltpu.SemaphoreType.DMA((parts,)),
            pltpu.SemaphoreType.DMA,
        ],
        compiler_params=pltpu.CompilerParams(vmem_limit_bytes=8 << 20),
        cost_estimate=pl.CostEstimate(
            flops=4 * rows * heads * positions * width,
            bytes_accessed=4 * rows * positions * width,
            transcendentals=rows * heads * positions,
        ),
        name="attention",
    )(
        group_at,
        early_at,
        *in_hbm(
            key_cache,
            value_cache,
            queries,
            new_key,
            new_value,
            lengths,
            row_adapter,
            adapter_list,
            adapter_rank,
            out_weight,
        ),
    )
    if full != heads:
        tagged = jnp.concatenate([tagged[:, : heads * width], tagged[:, full * width :]], axis=1)
    return tagged, early, limits


def put_stacked(out, start, term, first=0, others=()):
    rows = term.shape[0]
    for column in range(0, term.shape[1], LANES):
        at = first + (start + column) // LANES * rows
        part = term[:, column : column + LANES]
        for other in others:
            part = part + other[at : at + rows].astype(F32)
        out[at : at + rows] = part.astype(out.dtype)


def base_kernel(ahead, deep, arriving, tensor_at, tagged, out_weight, *refs):
    arrived, (*near, out, held, sums, sems) = refs[:arriving], refs[arriving:]
    _, deep_rows, block = held.shape
    width = out_weight.shape[0]
    count = width // deep_rows
    column = pl.ds(pl.multiple_of((tensor_at[0] ^ ahead) * block, block), block)

    def copy(at):
        return pltpu.make_async_copy(
            out_weight.at[pl.ds(at * deep_rows, deep_rows), column],
            held.at[at % deep],
            sems.at[at % deep],
        )

    for at in range(min(deep, count)):
        copy(at).start()
    piece = min(block, 512)
    if near:
        early, early_out = near
        for start in range(0, block, piece):
            columns = slice(start, start + piece)
            term = jnp.dot(tagged[:, :width], early[:, columns], preferred_element_type=F32)
            put_stacked(early_out, start, term)
    for at in range(count):
        copy(at).wait()
        inputs = slice(at * deep_rows, (at + 1) * deep_rows)
        for start in range(0, block, piece):
            columns = slice(start, start + piece)
            term = jnp.dot(
                tagged[:, inputs], held[at % deep, :, columns], preferred_element_type=F32
            )
            if at:
                term = term + sums[:, columns]
            if at < count - 1:
                sums[:, columns] = term
            else:
                put_stacked(out, start, term, 0, arrived)
        if at + deep < count:
            copy(at + deep).start()


def base_block(tensor_at, tagged, out_weight, block, ahead, early=(), arrived=(), cost=2):
    rows = tagged.shape[0]
    width = out_weight.shape[0]
    deep, deep_rows = 4, min(width, 256)
    whole = pl.BlockSpec(memory_space=VMEM)
    count = 1 + len(early)
    return pl.pallas_call(
        functools.partial(base_kernel, ahead, deep, len(arrived)),
        out_shape=[jax.ShapeDtypeStruct((block // LANES * rows, LANES), BF16 if ahead else F32)]
        * count,
        in_specs=[pl.BlockSpec(memory_space=pltpu.SMEM), whole, pl.BlockSpec(memory_space=pl.ANY)]
        + [whole] * (len(arrived) + len(early)),
        out_specs=[whole] * count,
        scratch_shapes=[
            VMEM((deep, deep_rows, block), BF16),
            VMEM((rows, block), F32),
            pltpu.SemaphoreType.DMA((deep,)),
        ],
        compiler_params=pltpu.CompilerParams(vmem_limit_bytes=12 << 20),
        cost_estimate=pl.CostEstimate(
            flops=cost * rows * width * block * count,
            bytes_accessed=2 * width * block * (2 if arrived else count),
            transcendentals=0,
        ),
        name="base_terms",
    )(tensor_at, tagged, *in_hbm(out_weight), *arrived, *early)


def slots_of(tags, batch_at, pool, tile, per):
    lane = lane_of(tags.shape)
    ids = tags.astype(F32).astype(jnp.int32)
    mine = tile * per + lane // (LANES // per)
    held = tile * per // pool
    return ids - (batch_at[0] ^ held) * pool + held * pool, mine


def shrink_kernel(batch_at, *refs):
    blocks, factors, out = refs[:-3], refs[-3:-1], refs[-1]
    pool, rank_width, width = factors[0].shape
    everyone = jnp.concatenate([block[...] for block in blocks], axis=0)
    per = LANES // rank_width
    lane = lane_of((everyone.shape[0], LANES))
    kept = jnp.zeros(lane.shape, F32)
    for held, weights in enumerate(factors):
        terms = lax.dot_general(
            everyone[:, :width],
            weights[...].reshape(pool * rank_width, width),
            (((1,), (1,)), ((), ())),
            preferred_element_type=F32,
        )
        for tile in range(pool // per):
            slot, mine = slots_of(everyone[:, width:], batch_at, pool, held * pool // per + tile, per)
            kept = kept + jnp.where(
                slot == mine, terms[:, tile * LANES : (tile + 1) * LANES], F32(0.0)
            )
    both = kept + pltpu.roll(kept, rank_width, 1)
    half = both.shape[0] // 2
    packed = jnp.where(lane[:half] < rank_width, both[:half], both[half:])
    out[...] = packed.astype(out.dtype)


def shrink_part(blocks, factors, batch_at):
    pool, rank_width, width = factors[0].shape
    rows = len(blocks) * blocks[0].shape[0]
    smem = pl.BlockSpec(memory_space=pltpu.SMEM)
    whole = pl.BlockSpec(memory_space=VMEM)
    return pl.pallas_call(
        shrink_kernel,
        out_shape=jax.ShapeDtypeStruct((rows // 2, LANES), BF16),
        in_specs=[smem] + [whole] * (len(blocks) + 2),
        out_specs=whole,
        compiler_params=pltpu.CompilerParams(vmem_limit_bytes=8 << 20),
        cost_estimate=pl.CostEstimate(
            flops=4 * rows * width * pool * rank_width,
            bytes_accessed=2 * width * (rows + 2 * pool * rank_width),
            transcendentals=0,
        ),
        name="shrink",
    )(batch_at, *blocks, *factors)


def expand_kernel(count, sums, rank_width, batch_at, *refs):
    limits, refs = refs[:2], refs[2:]
    tags, parts = refs[:count], refs[count : count + sums]
    factors, outs = refs[count + sums : count + sums + 2], refs[count + sums + 2 :]
    tags = jnp.concatenate([tag[...] for tag in tags], axis=0)
    total = parts[0][...].astype(F32)
    for part in parts[1:]:
        total = total + part[...].astype(F32)
    total = total.astype(BF16).astype(F32)
    other = pltpu.roll(total, rank_width, 1)
    low = lane_of(total.shape) < rank_width
    shrink = jnp.concatenate(
        [jnp.where(low, total, other), jnp.where(low, other, total)], axis=0
    )
    per = LANES // rank_width
    inputs, block = factors[0].shape
    pool = inputs // rank_width
    tiles = []
    for tile in range(2 * pool // per):
        slot, mine = slots_of(tags, batch_at, pool, tile, per)
        held, at = divmod(tile * per, pool)
        limit = limits[held][at // per : at // per + 1]
        keep = (slot == mine) & (lane_of(tags.shape) % rank_width < limit)
        tiles.append(jnp.where(keep, shrink, F32(0.0)).astype(BF16))
    half = len(tiles) // 2
    spreads = [jnp.concatenate(tiles[:half], axis=1), jnp.concatenate(tiles[half:], axis=1)]
    rows = tags.shape[0] // count
    piece = min(block, 512)
    for at in range(0, block, piece):
        delta = sum(
            jnp.dot(spread, each[:, at : at + piece], preferred_element_type=F32)
            for spread, each in zip(spreads, factors)
        )
        for which, out in enumerate(outs):
            put_stacked(out, at, delta[which * rows : (which + 1) * rows])


def expand(blocks, parts, factors, limits, batch_at):
    pool, rank_width, block = factors[0].shape
    rows, tagged_width = blocks[0].shape
    count = len(blocks)
    stack = rows * block // LANES
    tag = pl.BlockSpec((rows, LANES), lambda i: (0, tagged_width // LANES - 1))
    full = pl.BlockSpec((pool * rank_width, block), lambda i: (0, 0))
    part = pl.BlockSpec(parts[0].shape, lambda i: (0, 0))
    return pl.pallas_call(
        functools.partial(expand_kernel, count, len(parts), rank_width),
        grid=(1,),
        out_shape=[jax.ShapeDtypeStruct((stack, LANES), BF16) for _ in blocks],
        in_specs=[pl.BlockSpec(memory_space=pltpu.SMEM)]
        + [pl.BlockSpec(each.shape, lambda i: (0, 0)) for each in limits]
        + [tag] * count
        + [part] * len(parts)
        + [full] * 2,
        out_specs=[pl.BlockSpec((stack, LANES), lambda i: (0, 0)) for _ in blocks],
        compiler_params=pltpu.CompilerParams(vmem_limit_bytes=16 << 20),
        cost_estimate=pl.CostEstimate(
            flops=4 * rows * count * pool * rank_width * block,
            bytes_accessed=2 * pool * rank_width * block,
            transcendentals=0,
        ),
        name="expand",
    )(batch_at, *limits, *blocks, *parts, *[each.reshape(pool * rank_width, block) for each in factors])


def total_kernel(*refs):
    terms, out = refs[:-1], refs[-1]
    rows = out.shape[0]
    for column in range(0, out.shape[1], LANES):
        at = slice(column // LANES * rows, (column // LANES + 1) * rows)
        total = terms[0][at].astype(F32)
        for term in terms[1:]:
            total = total + term[at].astype(F32)
        out[:, column : column + LANES] = total.astype(out.dtype)


def total(rows, block, terms):
    whole = pl.BlockSpec(memory_space=VMEM)
    return pl.pallas_call(
        total_kernel,
        out_shape=jax.ShapeDtypeStruct((rows, block), BF16),
        in_specs=[whole] * len(terms),
        out_specs=whole,
        compiler_params=pltpu.CompilerParams(vmem_limit_bytes=8 << 20),
        cost_estimate=pl.CostEstimate(
            flops=rows * block * len(terms),
            bytes_accessed=2 * rows * block * (1 + len(terms)),
            transcendentals=0,
        ),
        name="total",
    )(*terms)


def partial_kernel(*refs):
    terms, out = refs[:-1], refs[-1]
    total = terms[0][...].astype(F32)
    for term in terms[1:]:
        total = total + term[...].astype(F32)
    out[...] = total


def partial_total(terms, weight):
    whole = pl.BlockSpec(memory_space=VMEM)
    return pl.pallas_call(
        partial_kernel,
        out_shape=jax.ShapeDtypeStruct(terms[0].shape, F32),
        in_specs=[whole] * len(terms),
        out_specs=whole,
        compiler_params=pltpu.CompilerParams(vmem_limit_bytes=8 << 20),
        cost_estimate=pl.CostEstimate(
            flops=terms[0].size * len(terms),
            bytes_accessed=4 * terms[0].size + weight,
            transcendentals=0,
        ),
        name="partial_total",
    )(*terms)


def local(
    tensor_size,
    batch_size,
    queries,
    key_cache,
    value_cache,
    new_key,
    new_value,
    lengths,
    out_weight,
    shrink_weight,
    expand_weight,
    adapter_rank,
    adapter_list,
    row_adapter,
):
    rows = queries.shape[0]
    block = expand_weight.shape[2]
    chips = batch_size // 2
    batch_at = lax.axis_index("batch").reshape(1).astype(jnp.int32)
    tensor_at = lax.axis_index("tensor").reshape(1).astype(jnp.int32)

    def to_sibling(array):
        return permuted(array, "batch", batch_size, lambda i: i ^ 1)

    def to_chip(array, shift):
        return permuted(array, "batch", batch_size, lambda i: (i + 2 * shift) % batch_size)

    def across(array, bit):
        return permuted(array, "tensor", tensor_size, lambda i: i ^ bit)

    def wide(array):
        return array.astype(F32)

    stack = block // LANES * rows
    tagged, early, limits = attend(
        tensor_at ^ 3,
        block,
        out_weight,
        queries,
        key_cache,
        value_cache,
        new_key,
        new_value,
        lengths,
        adapter_list,
        row_adapter,
        adapter_rank,
        shrink_weight.shape[2],
    )
    limits = [limits, to_sibling(limits)]
    shrink_weight = jnp.swapaxes(shrink_weight, 1, 2)
    shrink_factors = [shrink_weight, to_sibling(shrink_weight)]
    expand_factors = [expand_weight, to_sibling(expand_weight)]
    visiting = [to_chip(tagged, shift) for shift in range(1, chips)]
    third, next_door = base_block(
        tensor_at, tagged, out_weight, block, 1, [early], (), 30
    )
    visiting, next_door, limits = lax.optimization_barrier((visiting, next_door, limits))
    blocks = [tagged] + visiting
    third = across(third, 1)

    part = shrink_part(blocks, shrink_factors, batch_at)
    parts = [part, across(part, 1)]
    part, later_tagged = lax.optimization_barrier((part, tagged))
    (second,) = base_block(tensor_at, later_tagged, out_weight, block, 2, (), (), 120)
    second = (wide(second) + wide(third)).astype(BF16)
    parts, second = lax.optimization_barrier((parts, second))
    bit = 2
    while bit < tensor_size:
        part = (wide(parts[0]) + wide(parts[1])).astype(BF16)
        part, next_door = lax.optimization_barrier((part, next_door))
        parts = [part, across(part, bit)]
        bit *= 2
    arrived = [across(second, 2), across(next_door, 1)]
    for ahead in range(4, tensor_size, 2):
        (near,) = base_block(tensor_at, tagged, out_weight, block, ahead)
        (far,) = base_block(tensor_at, tagged, out_weight, block, ahead + 1)
        arrived.append(across((wide(near) + wide(across(far, 1))).astype(BF16), ahead))

    deltas = expand(blocks, parts, expand_factors, limits, batch_at)
    deltas, late_tagged = lax.optimization_barrier((deltas, tagged))
    (own,) = base_block(tensor_at, late_tagged, out_weight, block, 0, (), (), 60)
    so_far = partial_total([own, deltas[0], arrived[0], *arrived[2:]], 0)
    terms = [partial_total([so_far, arrived[1]], 8 << 20)]
    terms += [to_chip(home, -shift) for shift, home in enumerate(deltas[1:], 1)]
    return total(rows, block, terms)


def solution(mesh):
    placed = (
        P(("groups", "batch"), "tensor", None),
        P(("groups", "batch"), None, None, None),
        P(("groups", "batch"), None, None, None),
        P(("groups", "batch"), None, None),
        P(("groups", "batch"), None, None),
        P(("groups", "batch")),
        P("tensor", None),
        P("batch", "tensor", None),
        P("batch", None, "tensor"),
        P("batch"),
        P(("groups", "batch")),
        P(("groups", "batch")),
    )

    def placed_local(*arrays):
        return local(mesh.shape["tensor"], mesh.shape["batch"], *arrays)

    return jax.shard_map(
        placed_local,
        mesh=mesh,
        in_specs=placed,
        out_specs=P(("groups", "batch"), "tensor"),
        check_vma=False,
    )
```

```python
import functools

import jax
import jax.numpy as jnp
from jax import lax
from jax.experimental import pallas as pl
from jax.experimental.pallas import tpu as pltpu
from jax.sharding import PartitionSpec as P

HQ = 32
KVH = 4
LANES = 128
VMEM = pltpu.VMEM
GRANT = 56 << 20
F32, BF16 = jnp.float32, jnp.bfloat16


def permuted(array, axis, size, partner):
    return lax.ppermute(array, axis, [(i, partner(i)) for i in range(size)])


def in_hbm(*arrays):
    return [pltpu.with_memory_space_constraint(array, pltpu.HBM) for array in arrays]


def lane_of(shape):
    return lax.broadcasted_iota(jnp.int32, shape, len(shape) - 1)


def attend_kernel(parts, rank_width, group_at, early_at, *refs):
    given, (out_weight, tagged, early, limits, *scratch) = refs[:9], refs[9:]
    held, (spread_out, small_sems, key_sems, value_sems, early_sem) = scratch[:9], scratch[9:]
    key_cache, value_cache = given[:2]
    keys, values, queries, new_key, new_value, lengths, row_adapter, adapter_list, ranks = held
    rows, heads, width = queries.shape
    positions = key_cache.shape[2]
    group = group_at[0]
    some = rows // parts

    def cache_copies(part):
        at = pl.ds(part * some, some)
        return (
            pltpu.make_async_copy(key_cache.at[at, group], keys.at[at], key_sems.at[part]),
            pltpu.make_async_copy(value_cache.at[at, group], values.at[at], value_sems.at[part]),
        )

    small = [
        pltpu.make_async_copy(given[i], held[i], small_sems.at[i - 2]) for i in range(2, 9)
    ]
    for copy in small:
        copy.start()
    for part in range(parts):
        for copy in cache_copies(part):
            copy.start()
    block = early.shape[1]
    start = pl.multiple_of(early_at[0] * block, block)
    early_copy = pltpu.make_async_copy(out_weight.at[:, pl.ds(start, block)], early, early_sem)
    early_copy.start()
    for copy in small:
        copy.wait()
    at_row = lax.broadcasted_iota(jnp.int32, (rows, LANES), 0)
    tag = jnp.zeros((rows, LANES), jnp.int32)
    for row in range(rows):
        tag = jnp.where(at_row == row, adapter_list[row_adapter[row]], tag)
    tag = tag.astype(F32).astype(BF16)
    slot = lax.broadcasted_iota(jnp.int32, limits.shape, 0) * (LANES // rank_width)
    slot = slot + lane_of(limits.shape) // rank_width
    limit = jnp.zeros(limits.shape, jnp.int32)
    for held_at in range(ranks.shape[0]):
        limit = jnp.where(slot == held_at, ranks[held_at], limit)
    limits[...] = limit

    group_row = lax.broadcasted_iota(jnp.int32, new_key.shape, 1) == group
    fresh_key = jnp.sum(
        jnp.where(group_row, new_key[...].astype(F32), F32(0.0)), axis=1, keepdims=True
    )
    fresh_value = jnp.sum(
        jnp.where(group_row, new_value[...].astype(F32), F32(0.0)), axis=1, keepdims=True
    )
    score_scale = width ** (-0.5)
    fresh = jnp.sum(queries[...].astype(F32) * fresh_key, axis=-1, keepdims=True) * score_scale
    for part in range(parts):
        at = slice(part * some, (part + 1) * some)
        key_copy, value_copy = cache_copies(part)
        key_copy.wait()
        scores = (
            lax.dot_general(
                queries[at], keys[at], (((2,), (2,)), ((0,), (0,))), preferred_element_type=F32
            )
            * score_scale
        )
        length = jnp.stack(
            [
                jnp.full((heads, positions), lengths[row], jnp.int32)
                for row in range(part * some, (part + 1) * some)
            ]
        )
        valid = lane_of(scores.shape) < length
        masked = jnp.where(valid, scores, F32(-1e30))
        highest = jnp.maximum(jnp.max(masked, axis=-1, keepdims=True), fresh[at])
        cached_exp = jnp.where(valid, jnp.exp(masked - highest), F32(0.0))
        fresh_exp = jnp.exp(fresh[at] - highest)
        totals = jnp.sum(cached_exp, axis=-1, keepdims=True) + fresh_exp
        cached_w = (cached_exp / totals).astype(BF16)
        fresh_w = (fresh_exp / totals).astype(BF16).astype(F32)
        value_copy.wait()
        attended = lax.dot_general(
            cached_w, values[at], (((2,), (1,)), ((0,), (0,))), preferred_element_type=F32
        )
        attended = attended + fresh_w * fresh_value[at]
        spread_out[pl.ds(part * some * heads, some * heads)] = attended.reshape(
            some * heads, width
        )
    tagged[:, heads * width :] = tag
    for head in range(heads):
        tagged[:, head * width : (head + 1) * width] = spread_out[
            pl.ds(head, rows, stride=heads)
        ].astype(BF16)
    early_copy.wait()


def attend(
    early_at,
    block,
    out_weight,
    queries,
    key_cache,
    value_cache,
    new_key,
    new_value,
    lengths,
    adapter_list,
    row_adapter,
    adapter_rank,
    rank_width,
):
    rows, heads, width = queries.shape
    positions = key_cache.shape[2]
    per_group = HQ // KVH
    group_at = (lax.axis_index("tensor") * heads // per_group).reshape(1).astype(jnp.int32)
    full = -(-heads // 8) * 8
    if full != heads:
        queries = jnp.pad(queries, ((0, 0), (0, full - heads), (0, 0)))
    parts = 2
    smem = pl.BlockSpec(memory_space=pltpu.SMEM)
    away = pl.BlockSpec(memory_space=pl.ANY)
    tagged, early, limits = pl.pallas_call(
        functools.partial(attend_kernel, parts, rank_width),
        out_shape=[
            jax.ShapeDtypeStruct((rows, full * width + LANES), BF16),
            VMEM((out_weight.shape[0], block), BF16),
            jax.ShapeDtypeStruct((8, LANES), jnp.int32),
        ],
        in_specs=[smem, smem] + [away] * 10,
        out_specs=[pl.BlockSpec(memory_space=VMEM)] * 3,
        scratch_shapes=[
            VMEM((rows, positions, width), BF16),
            VMEM((rows, positions, width), BF16),
            VMEM(queries.shape, BF16),
            VMEM(new_key.shape, BF16),
            VMEM(new_value.shape, BF16),
            pltpu.SMEM(lengths.shape, jnp.int32),
            pltpu.SMEM(row_adapter.shape, jnp.int32),
            pltpu.SMEM(adapter_list.shape, jnp.int32),
            pltpu.SMEM(adapter_rank.shape, jnp.int32),
            VMEM((rows * full, width), F32),
            pltpu.SemaphoreType.DMA((7,)),
            pltpu.SemaphoreType.DMA((parts,)),
            pltpu.SemaphoreType.DMA((parts,)),
            pltpu.SemaphoreType.DMA,
        ],
        compiler_params=pltpu.CompilerParams(vmem_limit_bytes=8 << 20),
        cost_estimate=pl.CostEstimate(
            flops=4 * rows * heads * positions * width,
            bytes_accessed=4 * rows * positions * width,
            transcendentals=rows * heads * positions,
        ),
        name="attention",
    )(
        group_at,
        early_at,
        *in_hbm(
            key_cache,
            value_cache,
            queries,
            new_key,
            new_value,
            lengths,
            row_adapter,
            adapter_list,
            adapter_rank,
            out_weight,
        ),
    )
    if full != heads:
        tagged = jnp.concatenate([tagged[:, : heads * width], tagged[:, full * width :]], axis=1)
    return tagged, early, limits


def put_stacked(out, start, term, first=0, others=()):
    rows = term.shape[0]
    for column in range(0, term.shape[1], LANES):
        at = first + (start + column) // LANES * rows
        part = term[:, column : column + LANES]
        for other in others:
            part = part + other[at : at + rows].astype(F32)
        out[at : at + rows] = part.astype(out.dtype)


def base_kernel(ahead, deep, arriving, tensor_at, tagged, out_weight, *refs):
    arrived, (*near, out, held, sums, sems) = refs[:arriving], refs[arriving:]
    _, deep_rows, block = held.shape
    width = out_weight.shape[0]
    count = width // deep_rows
    column = pl.ds(pl.multiple_of((tensor_at[0] ^ ahead) * block, block), block)

    def copy(at):
        return pltpu.make_async_copy(
            out_weight.at[pl.ds(at * deep_rows, deep_rows), column],
            held.at[at % deep],
            sems.at[at % deep],
        )

    for at in range(min(deep, count)):
        copy(at).start()
    piece = min(block, 512)
    if near:
        early, early_out = near
        for start in range(0, block, piece):
            columns = slice(start, start + piece)
            term = jnp.dot(tagged[:, :width], early[:, columns], preferred_element_type=F32)
            put_stacked(early_out, start, term)
    for at in range(count):
        copy(at).wait()
        inputs = slice(at * deep_rows, (at + 1) * deep_rows)
        for start in range(0, block, piece):
            columns = slice(start, start + piece)
            term = jnp.dot(
                tagged[:, inputs], held[at % deep, :, columns], preferred_element_type=F32
            )
            if at:
                term = term + sums[:, columns]
            if at < count - 1:
                sums[:, columns] = term
            else:
                put_stacked(out, start, term, 0, arrived)
        if at + deep < count:
            copy(at + deep).start()


def base_block(tensor_at, tagged, out_weight, block, ahead, early=(), arrived=(), cost=2):
    rows = tagged.shape[0]
    width = out_weight.shape[0]
    deep, deep_rows = 4, min(width, 256)
    whole = pl.BlockSpec(memory_space=VMEM)
    count = 1 + len(early)
    return pl.pallas_call(
        functools.partial(base_kernel, ahead, deep, len(arrived)),
        out_shape=[jax.ShapeDtypeStruct((block // LANES * rows, LANES), BF16 if ahead else F32)]
        * count,
        in_specs=[pl.BlockSpec(memory_space=pltpu.SMEM), whole, pl.BlockSpec(memory_space=pl.ANY)]
        + [whole] * (len(arrived) + len(early)),
        out_specs=[whole] * count,
        scratch_shapes=[
            VMEM((deep, deep_rows, block), BF16),
            VMEM((rows, block), F32),
            pltpu.SemaphoreType.DMA((deep,)),
        ],
        compiler_params=pltpu.CompilerParams(vmem_limit_bytes=12 << 20),
        cost_estimate=pl.CostEstimate(
            flops=cost * rows * width * block * count,
            bytes_accessed=2 * width * block * (2 if arrived else count),
            transcendentals=0,
        ),
        name="base_terms",
    )(tensor_at, tagged, *in_hbm(out_weight), *arrived, *early)


def slots_of(tags, batch_at, pool, tile, per):
    lane = lane_of(tags.shape)
    ids = tags.astype(F32).astype(jnp.int32)
    mine = tile * per + lane // (LANES // per)
    held = tile * per // pool
    return ids - (batch_at[0] ^ held) * pool + held * pool, mine


def shrink_kernel(batch_at, *refs):
    blocks, factors, out = refs[:-3], refs[-3:-1], refs[-1]
    pool, rank_width, width = factors[0].shape
    everyone = jnp.concatenate([block[...] for block in blocks], axis=0)
    per = LANES // rank_width
    lane = lane_of((everyone.shape[0], LANES))
    kept = jnp.zeros(lane.shape, F32)
    for held, weights in enumerate(factors):
        terms = lax.dot_general(
            everyone[:, :width],
            weights[...].reshape(pool * rank_width, width),
            (((1,), (1,)), ((), ())),
            preferred_element_type=F32,
        )
        for tile in range(pool // per):
            slot, mine = slots_of(everyone[:, width:], batch_at, pool, held * pool // per + tile, per)
            kept = kept + jnp.where(
                slot == mine, terms[:, tile * LANES : (tile + 1) * LANES], F32(0.0)
            )
    both = kept + pltpu.roll(kept, rank_width, 1)
    half = both.shape[0] // 2
    packed = jnp.where(lane[:half] < rank_width, both[:half], both[half:])
    out[...] = packed.astype(out.dtype)


def shrink_part(blocks, factors, batch_at):
    pool, rank_width, width = factors[0].shape
    rows = len(blocks) * blocks[0].shape[0]
    smem = pl.BlockSpec(memory_space=pltpu.SMEM)
    whole = pl.BlockSpec(memory_space=VMEM)
    return pl.pallas_call(
        shrink_kernel,
        out_shape=jax.ShapeDtypeStruct((rows // 2, LANES), BF16),
        in_specs=[smem] + [whole] * (len(blocks) + 2),
        out_specs=whole,
        compiler_params=pltpu.CompilerParams(vmem_limit_bytes=8 << 20),
        cost_estimate=pl.CostEstimate(
            flops=4 * rows * width * pool * rank_width,
            bytes_accessed=2 * width * (rows + 2 * pool * rank_width),
            transcendentals=0,
        ),
        name="shrink",
    )(batch_at, *blocks, *factors)


def expand_kernel(count, sums, rank_width, batch_at, *refs):
    limits, refs = refs[:2], refs[2:]
    tags, parts = refs[:count], refs[count : count + sums]
    factors, outs = refs[count + sums : count + sums + 2], refs[count + sums + 2 :]
    tags = jnp.concatenate([tag[...] for tag in tags], axis=0)
    total = parts[0][...].astype(F32)
    for part in parts[1:]:
        total = total + part[...].astype(F32)
    total = total.astype(BF16).astype(F32)
    other = pltpu.roll(total, rank_width, 1)
    low = lane_of(total.shape) < rank_width
    shrink = jnp.concatenate(
        [jnp.where(low, total, other), jnp.where(low, other, total)], axis=0
    )
    per = LANES // rank_width
    inputs, block = factors[0].shape
    pool = inputs // rank_width
    tiles = []
    for tile in range(2 * pool // per):
        slot, mine = slots_of(tags, batch_at, pool, tile, per)
        held, at = divmod(tile * per, pool)
        limit = limits[held][at // per : at // per + 1]
        keep = (slot == mine) & (lane_of(tags.shape) % rank_width < limit)
        tiles.append(jnp.where(keep, shrink, F32(0.0)).astype(BF16))
    half = len(tiles) // 2
    spreads = [jnp.concatenate(tiles[:half], axis=1), jnp.concatenate(tiles[half:], axis=1)]
    rows = tags.shape[0] // count
    piece = min(block, 512)
    for at in range(0, block, piece):
        delta = sum(
            jnp.dot(spread, each[:, at : at + piece], preferred_element_type=F32)
            for spread, each in zip(spreads, factors)
        )
        for which, out in enumerate(outs):
            put_stacked(out, at, delta[which * rows : (which + 1) * rows])


def expand(blocks, parts, factors, limits, batch_at):
    pool, rank_width, block = factors[0].shape
    rows, tagged_width = blocks[0].shape
    count = len(blocks)
    stack = rows * block // LANES
    tag = pl.BlockSpec((rows, LANES), lambda i: (0, tagged_width // LANES - 1))
    full = pl.BlockSpec((pool * rank_width, block), lambda i: (0, 0))
    part = pl.BlockSpec(parts[0].shape, lambda i: (0, 0))
    return pl.pallas_call(
        functools.partial(expand_kernel, count, len(parts), rank_width),
        grid=(1,),
        out_shape=[jax.ShapeDtypeStruct((stack, LANES), BF16) for _ in blocks],
        in_specs=[pl.BlockSpec(memory_space=pltpu.SMEM)]
        + [pl.BlockSpec(each.shape, lambda i: (0, 0)) for each in limits]
        + [tag] * count
        + [part] * len(parts)
        + [full] * 2,
        out_specs=[pl.BlockSpec((stack, LANES), lambda i: (0, 0)) for _ in blocks],
        compiler_params=pltpu.CompilerParams(vmem_limit_bytes=16 << 20),
        cost_estimate=pl.CostEstimate(
            flops=4 * rows * count * pool * rank_width * block,
            bytes_accessed=2 * pool * rank_width * block,
            transcendentals=0,
        ),
        name="expand",
    )(batch_at, *limits, *blocks, *parts, *[each.reshape(pool * rank_width, block) for each in factors])


def total_kernel(*refs):
    terms, out = refs[:-1], refs[-1]
    rows = out.shape[0]
    for column in range(0, out.shape[1], LANES):
        at = slice(column // LANES * rows, (column // LANES + 1) * rows)
        total = terms[0][at].astype(F32)
        for term in terms[1:]:
            total = total + term[at].astype(F32)
        out[:, column : column + LANES] = total.astype(out.dtype)


def total(rows, block, terms):
    whole = pl.BlockSpec(memory_space=VMEM)
    return pl.pallas_call(
        total_kernel,
        out_shape=jax.ShapeDtypeStruct((rows, block), BF16),
        in_specs=[whole] * len(terms),
        out_specs=whole,
        compiler_params=pltpu.CompilerParams(vmem_limit_bytes=8 << 20),
        cost_estimate=pl.CostEstimate(
            flops=rows * block * len(terms),
            bytes_accessed=2 * rows * block * (1 + len(terms)),
            transcendentals=0,
        ),
        name="total",
    )(*terms)


def partial_kernel(*refs):
    terms, out = refs[:-1], refs[-1]
    total = terms[0][...].astype(F32)
    for term in terms[1:]:
        total = total + term[...].astype(F32)
    out[...] = total


def partial_total(terms, weight):
    whole = pl.BlockSpec(memory_space=VMEM)
    return pl.pallas_call(
        partial_kernel,
        out_shape=jax.ShapeDtypeStruct(terms[0].shape, F32),
        in_specs=[whole] * len(terms),
        out_specs=whole,
        compiler_params=pltpu.CompilerParams(vmem_limit_bytes=8 << 20),
        cost_estimate=pl.CostEstimate(
            flops=terms[0].size * len(terms),
            bytes_accessed=4 * terms[0].size + weight,
            transcendentals=0,
        ),
        name="partial_total",
    )(*terms)


def local(
    tensor_size,
    batch_size,
    queries,
    key_cache,
    value_cache,
    new_key,
    new_value,
    lengths,
    out_weight,
    shrink_weight,
    expand_weight,
    adapter_rank,
    adapter_list,
    row_adapter,
):
    rows = queries.shape[0]
    block = expand_weight.shape[2]
    chips = batch_size // 2
    batch_at = lax.axis_index("batch").reshape(1).astype(jnp.int32)
    tensor_at = lax.axis_index("tensor").reshape(1).astype(jnp.int32)

    def to_sibling(array):
        return permuted(array, "batch", batch_size, lambda i: i ^ 1)

    def to_chip(array, shift):
        return permuted(array, "batch", batch_size, lambda i: (i + 2 * shift) % batch_size)

    def across(array, bit):
        return permuted(array, "tensor", tensor_size, lambda i: i ^ bit)

    def wide(array):
        return array.astype(F32)

    stack = block // LANES * rows
    tagged, early, limits = attend(
        tensor_at ^ 3,
        block,
        out_weight,
        queries,
        key_cache,
        value_cache,
        new_key,
        new_value,
        lengths,
        adapter_list,
        row_adapter,
        adapter_rank,
        shrink_weight.shape[2],
    )
    limits = [limits, to_sibling(limits)]
    shrink_weight = jnp.swapaxes(shrink_weight, 1, 2)
    shrink_factors = [shrink_weight, to_sibling(shrink_weight)]
    expand_factors = [expand_weight, to_sibling(expand_weight)]
    visiting = [to_chip(tagged, shift) for shift in range(1, chips)]
    third, next_door = base_block(
        tensor_at, tagged, out_weight, block, 1, [early], (), 2
    )
    visiting, next_door, limits = lax.optimization_barrier((visiting, next_door, limits))
    blocks = [tagged] + visiting
    third = across(third, 1)

    part = shrink_part(blocks, shrink_factors, batch_at)
    parts = [part, across(part, 1)]
    part, later_tagged = lax.optimization_barrier((part, tagged))
    (second,) = base_block(tensor_at, later_tagged, out_weight, block, 2, (), (), 60)
    second = (wide(second) + wide(third)).astype(BF16)
    parts, second = lax.optimization_barrier((parts, second))
    bit = 2
    while bit < tensor_size:
        part = (wide(parts[0]) + wide(parts[1])).astype(BF16)
        part, next_door = lax.optimization_barrier((part, next_door))
        parts = [part, across(part, bit)]
        bit *= 2
    arrived = [across(second, 2), across(next_door, 1)]
    for ahead in range(4, tensor_size, 2):
        (near,) = base_block(tensor_at, tagged, out_weight, block, ahead)
        (far,) = base_block(tensor_at, tagged, out_weight, block, ahead + 1)
        arrived.append(across((wide(near) + wide(across(far, 1))).astype(BF16), ahead))

    deltas = expand(blocks, parts, expand_factors, limits, batch_at)
    deltas, late_tagged = lax.optimization_barrier((deltas, tagged))
    (own,) = base_block(tensor_at, late_tagged, out_weight, block, 0, (), (), 2)
    so_far = partial_total([own, deltas[0], arrived[0], *arrived[2:]], 0)
    terms = [partial_total([so_far, arrived[1]], 8 << 20)]
    terms += [to_chip(home, -shift) for shift, home in enumerate(deltas[1:], 1)]
    return total(rows, block, terms)


def solution(mesh):
    placed = (
        P(("groups", "batch"), "tensor", None),
        P(("groups", "batch"), None, None, None),
        P(("groups", "batch"), None, None, None),
        P(("groups", "batch"), None, None),
        P(("groups", "batch"), None, None),
        P(("groups", "batch")),
        P("tensor", None),
        P("batch", "tensor", None),
        P("batch", None, "tensor"),
        P("batch"),
        P(("groups", "batch")),
        P(("groups", "batch")),
    )

    def placed_local(*arrays):
        return local(mesh.shape["tensor"], mesh.shape["batch"], *arrays)

    return jax.shard_map(
        placed_local,
        mesh=mesh,
        in_specs=placed,
        out_specs=P(("groups", "batch"), "tensor"),
        check_vma=False,
    )
```

```python
import functools

import jax
import jax.numpy as jnp
from jax import lax
from jax.experimental import pallas as pl
from jax.experimental.pallas import tpu as pltpu
from jax.sharding import PartitionSpec as P

HQ = 32
KVH = 4
LANES = 128
VMEM = pltpu.VMEM
GRANT = 56 << 20
F32, BF16 = jnp.float32, jnp.bfloat16


def permuted(array, axis, size, partner):
    return lax.ppermute(array, axis, [(i, partner(i)) for i in range(size)])


def in_hbm(*arrays):
    return [pltpu.with_memory_space_constraint(array, pltpu.HBM) for array in arrays]


def lane_of(shape):
    return lax.broadcasted_iota(jnp.int32, shape, len(shape) - 1)


def attend_kernel(parts, rank_width, group_at, early_at, *refs):
    given, (out_weight, tagged, early, limits, *scratch) = refs[:9], refs[9:]
    held, (spread_out, small_sems, key_sems, value_sems, early_sem) = scratch[:9], scratch[9:]
    key_cache, value_cache = given[:2]
    keys, values, queries, new_key, new_value, lengths, row_adapter, adapter_list, ranks = held
    rows, heads, width = queries.shape
    positions = key_cache.shape[2]
    group = group_at[0]
    some = rows // parts

    def cache_copies(part):
        at = pl.ds(part * some, some)
        return (
            pltpu.make_async_copy(key_cache.at[at, group], keys.at[at], key_sems.at[part]),
            pltpu.make_async_copy(value_cache.at[at, group], values.at[at], value_sems.at[part]),
        )

    small = [
        pltpu.make_async_copy(given[i], held[i], small_sems.at[i - 2]) for i in range(2, 9)
    ]
    for copy in small:
        copy.start()
    for part in range(parts):
        for copy in cache_copies(part):
            copy.start()
    block = early.shape[1]
    start = pl.multiple_of(early_at[0] * block, block)
    early_copy = pltpu.make_async_copy(out_weight.at[:, pl.ds(start, block)], early, early_sem)
    early_copy.start()
    for copy in small:
        copy.wait()
    at_row = lax.broadcasted_iota(jnp.int32, (rows, LANES), 0)
    tag = jnp.zeros((rows, LANES), jnp.int32)
    for row in range(rows):
        tag = jnp.where(at_row == row, adapter_list[row_adapter[row]], tag)
    tag = tag.astype(F32).astype(BF16)
    slot = lax.broadcasted_iota(jnp.int32, limits.shape, 0) * (LANES // rank_width)
    slot = slot + lane_of(limits.shape) // rank_width
    limit = jnp.zeros(limits.shape, jnp.int32)
    for held_at in range(ranks.shape[0]):
        limit = jnp.where(slot == held_at, ranks[held_at], limit)
    limits[...] = limit

    group_row = lax.broadcasted_iota(jnp.int32, new_key.shape, 1) == group
    fresh_key = jnp.sum(
        jnp.where(group_row, new_key[...].astype(F32), F32(0.0)), axis=1, keepdims=True
    )
    fresh_value = jnp.sum(
        jnp.where(group_row, new_value[...].astype(F32), F32(0.0)), axis=1, keepdims=True
    )
    score_scale = width ** (-0.5)
    fresh = jnp.sum(queries[...].astype(F32) * fresh_key, axis=-1, keepdims=True) * score_scale
    for part in range(parts):
        at = slice(part * some, (part + 1) * some)
        key_copy, value_copy = cache_copies(part)
        key_copy.wait()
        scores = (
            lax.dot_general(
                queries[at], keys[at], (((2,), (2,)), ((0,), (0,))), preferred_element_type=F32
            )
            * score_scale
        )
        length = jnp.stack(
            [
                jnp.full((heads, positions), lengths[row], jnp.int32)
                for row in range(part * some, (part + 1) * some)
            ]
        )
        valid = lane_of(scores.shape) < length
        masked = jnp.where(valid, scores, F32(-1e30))
        highest = jnp.maximum(jnp.max(masked, axis=-1, keepdims=True), fresh[at])
        cached_exp = jnp.where(valid, jnp.exp(masked - highest), F32(0.0))
        fresh_exp = jnp.exp(fresh[at] - highest)
        totals = jnp.sum(cached_exp, axis=-1, keepdims=True) + fresh_exp
        cached_w = (cached_exp / totals).astype(BF16)
        fresh_w = (fresh_exp / totals).astype(BF16).astype(F32)
        value_copy.wait()
        attended = lax.dot_general(
            cached_w, values[at], (((2,), (1,)), ((0,), (0,))), preferred_element_type=F32
        )
        attended = attended + fresh_w * fresh_value[at]
        spread_out[pl.ds(part * some * heads, some * heads)] = attended.reshape(
            some * heads, width
        )
    tagged[:, heads * width :] = tag
    for head in range(heads):
        tagged[:, head * width : (head + 1) * width] = spread_out[
            pl.ds(head, rows, stride=heads)
        ].astype(BF16)
    early_copy.wait()


def attend(
    early_at,
    block,
    out_weight,
    queries,
    key_cache,
    value_cache,
    new_key,
    new_value,
    lengths,
    adapter_list,
    row_adapter,
    adapter_rank,
    rank_width,
):
    rows, heads, width = queries.shape
    positions = key_cache.shape[2]
    per_group = HQ // KVH
    group_at = (lax.axis_index("tensor") * heads // per_group).reshape(1).astype(jnp.int32)
    full = -(-heads // 8) * 8
    if full != heads:
        queries = jnp.pad(queries, ((0, 0), (0, full - heads), (0, 0)))
    parts = 2
    smem = pl.BlockSpec(memory_space=pltpu.SMEM)
    away = pl.BlockSpec(memory_space=pl.ANY)
    tagged, early, limits = pl.pallas_call(
        functools.partial(attend_kernel, parts, rank_width),
        out_shape=[
            jax.ShapeDtypeStruct((rows, full * width + LANES), BF16),
            VMEM((out_weight.shape[0], block), BF16),
            jax.ShapeDtypeStruct((8, LANES), jnp.int32),
        ],
        in_specs=[smem, smem] + [away] * 10,
        out_specs=[pl.BlockSpec(memory_space=VMEM)] * 3,
        scratch_shapes=[
            VMEM((rows, positions, width), BF16),
            VMEM((rows, positions, width), BF16),
            VMEM(queries.shape, BF16),
            VMEM(new_key.shape, BF16),
            VMEM(new_value.shape, BF16),
            pltpu.SMEM(lengths.shape, jnp.int32),
            pltpu.SMEM(row_adapter.shape, jnp.int32),
            pltpu.SMEM(adapter_list.shape, jnp.int32),
            pltpu.SMEM(adapter_rank.shape, jnp.int32),
            VMEM((rows * full, width), F32),
            pltpu.SemaphoreType.DMA((7,)),
            pltpu.SemaphoreType.DMA((parts,)),
            pltpu.SemaphoreType.DMA((parts,)),
            pltpu.SemaphoreType.DMA,
        ],
        compiler_params=pltpu.CompilerParams(vmem_limit_bytes=8 << 20),
        cost_estimate=pl.CostEstimate(
            flops=4 * rows * heads * positions * width,
            bytes_accessed=4 * rows * positions * width,
            transcendentals=rows * heads * positions,
        ),
        name="attention",
    )(
        group_at,
        early_at,
        *in_hbm(
            key_cache,
            value_cache,
            queries,
            new_key,
            new_value,
            lengths,
            row_adapter,
            adapter_list,
            adapter_rank,
            out_weight,
        ),
    )
    if full != heads:
        tagged = jnp.concatenate([tagged[:, : heads * width], tagged[:, full * width :]], axis=1)
    return tagged, early, limits


def put_stacked(out, start, term, first=0, others=()):
    rows = term.shape[0]
    for column in range(0, term.shape[1], LANES):
        at = first + (start + column) // LANES * rows
        part = term[:, column : column + LANES]
        for other in others:
            part = part + other[at : at + rows].astype(F32)
        out[at : at + rows] = part.astype(out.dtype)


def base_kernel(ahead, deep, arriving, tensor_at, tagged, out_weight, *refs):
    arrived, (*near, out, held, sums, sems) = refs[:arriving], refs[arriving:]
    _, deep_rows, block = held.shape
    width = out_weight.shape[0]
    count = width // deep_rows
    column = pl.ds(pl.multiple_of((tensor_at[0] ^ ahead) * block, block), block)

    def copy(at):
        return pltpu.make_async_copy(
            out_weight.at[pl.ds(at * deep_rows, deep_rows), column],
            held.at[at % deep],
            sems.at[at % deep],
        )

    for at in range(min(deep, count)):
        copy(at).start()
    piece = min(block, 512)
    if near:
        early, early_out = near
        for start in range(0, block, piece):
            columns = slice(start, start + piece)
            term = jnp.dot(tagged[:, :width], early[:, columns], preferred_element_type=F32)
            put_stacked(early_out, start, term)
    for at in range(count):
        copy(at).wait()
        inputs = slice(at * deep_rows, (at + 1) * deep_rows)
        for start in range(0, block, piece):
            columns = slice(start, start + piece)
            term = jnp.dot(
                tagged[:, inputs], held[at % deep, :, columns], preferred_element_type=F32
            )
            if at:
                term = term + sums[:, columns]
            if at < count - 1:
                sums[:, columns] = term
            else:
                put_stacked(out, start, term, 0, arrived)
        if at + deep < count:
            copy(at + deep).start()


def base_block(tensor_at, tagged, out_weight, block, ahead, early=(), arrived=(), cost=2):
    rows = tagged.shape[0]
    width = out_weight.shape[0]
    deep, deep_rows = 4, min(width, 256)
    whole = pl.BlockSpec(memory_space=VMEM)
    count = 1 + len(early)
    return pl.pallas_call(
        functools.partial(base_kernel, ahead, deep, len(arrived)),
        out_shape=[jax.ShapeDtypeStruct((block // LANES * rows, LANES), BF16 if ahead else F32)]
        * count,
        in_specs=[pl.BlockSpec(memory_space=pltpu.SMEM), whole, pl.BlockSpec(memory_space=pl.ANY)]
        + [whole] * (len(arrived) + len(early)),
        out_specs=[whole] * count,
        scratch_shapes=[
            VMEM((deep, deep_rows, block), BF16),
            VMEM((rows, block), F32),
            pltpu.SemaphoreType.DMA((deep,)),
        ],
        compiler_params=pltpu.CompilerParams(vmem_limit_bytes=12 << 20),
        cost_estimate=pl.CostEstimate(
            flops=cost * rows * width * block * count,
            bytes_accessed=2 * width * block * (2 if arrived else count),
            transcendentals=0,
        ),
        name="base_terms",
    )(tensor_at, tagged, *in_hbm(out_weight), *arrived, *early)


def slots_of(tags, batch_at, pool, tile, per):
    lane = lane_of(tags.shape)
    ids = tags.astype(F32).astype(jnp.int32)
    mine = tile * per + lane // (LANES // per)
    held = tile * per // pool
    return ids - (batch_at[0] ^ held) * pool + held * pool, mine


def shrink_kernel(batch_at, *refs):
    blocks, factors, out = refs[:-3], refs[-3:-1], refs[-1]
    pool, rank_width, width = factors[0].shape
    everyone = jnp.concatenate([block[...] for block in blocks], axis=0)
    per = LANES // rank_width
    lane = lane_of((everyone.shape[0], LANES))
    kept = jnp.zeros(lane.shape, F32)
    for held, weights in enumerate(factors):
        terms = lax.dot_general(
            everyone[:, :width],
            weights[...].reshape(pool * rank_width, width),
            (((1,), (1,)), ((), ())),
            preferred_element_type=F32,
        )
        for tile in range(pool // per):
            slot, mine = slots_of(everyone[:, width:], batch_at, pool, held * pool // per + tile, per)
            kept = kept + jnp.where(
                slot == mine, terms[:, tile * LANES : (tile + 1) * LANES], F32(0.0)
            )
    both = kept + pltpu.roll(kept, rank_width, 1)
    half = both.shape[0] // 2
    packed = jnp.where(lane[:half] < rank_width, both[:half], both[half:])
    out[...] = packed.astype(out.dtype)


def shrink_part(blocks, factors, batch_at):
    pool, rank_width, width = factors[0].shape
    rows = len(blocks) * blocks[0].shape[0]
    smem = pl.BlockSpec(memory_space=pltpu.SMEM)
    whole = pl.BlockSpec(memory_space=VMEM)
    return pl.pallas_call(
        shrink_kernel,
        out_shape=jax.ShapeDtypeStruct((rows // 2, LANES), BF16),
        in_specs=[smem] + [whole] * (len(blocks) + 2),
        out_specs=whole,
        compiler_params=pltpu.CompilerParams(vmem_limit_bytes=8 << 20),
        cost_estimate=pl.CostEstimate(
            flops=4 * rows * width * pool * rank_width,
            bytes_accessed=2 * width * (rows + 2 * pool * rank_width),
            transcendentals=0,
        ),
        name="shrink",
    )(batch_at, *blocks, *factors)


def expand_kernel(count, sums, rank_width, batch_at, *refs):
    limits, refs = refs[:2], refs[2:]
    tags, parts = refs[:count], refs[count : count + sums]
    factors, outs = refs[count + sums : count + sums + 2], refs[count + sums + 2 :]
    tags = jnp.concatenate([tag[...] for tag in tags], axis=0)
    total = parts[0][...].astype(F32)
    for part in parts[1:]:
        total = total + part[...].astype(F32)
    total = total.astype(BF16).astype(F32)
    other = pltpu.roll(total, rank_width, 1)
    low = lane_of(total.shape) < rank_width
    shrink = jnp.concatenate(
        [jnp.where(low, total, other), jnp.where(low, other, total)], axis=0
    )
    per = LANES // rank_width
    inputs, block = factors[0].shape
    pool = inputs // rank_width
    tiles = []
    for tile in range(2 * pool // per):
        slot, mine = slots_of(tags, batch_at, pool, tile, per)
        held, at = divmod(tile * per, pool)
        limit = limits[held][at // per : at // per + 1]
        keep = (slot == mine) & (lane_of(tags.shape) % rank_width < limit)
        tiles.append(jnp.where(keep, shrink, F32(0.0)).astype(BF16))
    half = len(tiles) // 2
    spreads = [jnp.concatenate(tiles[:half], axis=1), jnp.concatenate(tiles[half:], axis=1)]
    rows = tags.shape[0] // count
    piece = min(block, 512)
    for at in range(0, block, piece):
        delta = sum(
            jnp.dot(spread, each[:, at : at + piece], preferred_element_type=F32)
            for spread, each in zip(spreads, factors)
        )
        for which, out in enumerate(outs):
            put_stacked(out, at, delta[which * rows : (which + 1) * rows])


def expand(blocks, parts, factors, limits, batch_at):
    pool, rank_width, block = factors[0].shape
    rows, tagged_width = blocks[0].shape
    count = len(blocks)
    stack = rows * block // LANES
    tag = pl.BlockSpec((rows, LANES), lambda i: (0, tagged_width // LANES - 1))
    full = pl.BlockSpec((pool * rank_width, block), lambda i: (0, 0))
    part = pl.BlockSpec(parts[0].shape, lambda i: (0, 0))
    return pl.pallas_call(
        functools.partial(expand_kernel, count, len(parts), rank_width),
        grid=(1,),
        out_shape=[jax.ShapeDtypeStruct((stack, LANES), BF16) for _ in blocks],
        in_specs=[pl.BlockSpec(memory_space=pltpu.SMEM)]
        + [pl.BlockSpec(each.shape, lambda i: (0, 0)) for each in limits]
        + [tag] * count
        + [part] * len(parts)
        + [full] * 2,
        out_specs=[pl.BlockSpec((stack, LANES), lambda i: (0, 0)) for _ in blocks],
        compiler_params=pltpu.CompilerParams(vmem_limit_bytes=16 << 20),
        cost_estimate=pl.CostEstimate(
            flops=4 * rows * count * pool * rank_width * block,
            bytes_accessed=2 * pool * rank_width * block,
            transcendentals=0,
        ),
        name="expand",
    )(batch_at, *limits, *blocks, *parts, *[each.reshape(pool * rank_width, block) for each in factors])


def total_kernel(*refs):
    terms, out = refs[:-1], refs[-1]
    rows = out.shape[0]
    for column in range(0, out.shape[1], LANES):
        at = slice(column // LANES * rows, (column // LANES + 1) * rows)
        total = terms[0][at].astype(F32)
        for term in terms[1:]:
            total = total + term[at].astype(F32)
        out[:, column : column + LANES] = total.astype(out.dtype)


def total(rows, block, terms):
    whole = pl.BlockSpec(memory_space=VMEM)
    return pl.pallas_call(
        total_kernel,
        out_shape=jax.ShapeDtypeStruct((rows, block), BF16),
        in_specs=[whole] * len(terms),
        out_specs=whole,
        compiler_params=pltpu.CompilerParams(vmem_limit_bytes=8 << 20),
        cost_estimate=pl.CostEstimate(
            flops=rows * block * len(terms),
            bytes_accessed=2 * rows * block * (1 + len(terms)),
            transcendentals=0,
        ),
        name="total",
    )(*terms)


def partial_kernel(*refs):
    terms, out = refs[:-1], refs[-1]
    total = terms[0][...].astype(F32)
    for term in terms[1:]:
        total = total + term[...].astype(F32)
    out[...] = total


def partial_total(terms, weight):
    whole = pl.BlockSpec(memory_space=VMEM)
    return pl.pallas_call(
        partial_kernel,
        out_shape=jax.ShapeDtypeStruct(terms[0].shape, F32),
        in_specs=[whole] * len(terms),
        out_specs=whole,
        compiler_params=pltpu.CompilerParams(vmem_limit_bytes=8 << 20),
        cost_estimate=pl.CostEstimate(
            flops=terms[0].size * len(terms),
            bytes_accessed=4 * terms[0].size + weight,
            transcendentals=0,
        ),
        name="partial_total",
    )(*terms)


def local(
    tensor_size,
    batch_size,
    queries,
    key_cache,
    value_cache,
    new_key,
    new_value,
    lengths,
    out_weight,
    shrink_weight,
    expand_weight,
    adapter_rank,
    adapter_list,
    row_adapter,
):
    rows = queries.shape[0]
    block = expand_weight.shape[2]
    chips = batch_size // 2
    batch_at = lax.axis_index("batch").reshape(1).astype(jnp.int32)
    tensor_at = lax.axis_index("tensor").reshape(1).astype(jnp.int32)

    def to_sibling(array):
        return permuted(array, "batch", batch_size, lambda i: i ^ 1)

    def to_chip(array, shift):
        return permuted(array, "batch", batch_size, lambda i: (i + 2 * shift) % batch_size)

    def across(array, bit):
        return permuted(array, "tensor", tensor_size, lambda i: i ^ bit)

    def wide(array):
        return array.astype(F32)

    stack = block // LANES * rows
    tagged, early, limits = attend(
        tensor_at ^ 3,
        block,
        out_weight,
        queries,
        key_cache,
        value_cache,
        new_key,
        new_value,
        lengths,
        adapter_list,
        row_adapter,
        adapter_rank,
        shrink_weight.shape[2],
    )
    limits = [limits, to_sibling(limits)]
    shrink_weight = jnp.swapaxes(shrink_weight, 1, 2)
    shrink_factors = [shrink_weight, to_sibling(shrink_weight)]
    expand_factors = [expand_weight, to_sibling(expand_weight)]
    visiting = [to_chip(tagged, shift) for shift in range(1, chips)]
    third, next_door = base_block(
        tensor_at, tagged, out_weight, block, 1, [early], (), 2
    )
    visiting, next_door, limits = lax.optimization_barrier((visiting, next_door, limits))
    blocks = [tagged] + visiting
    third = across(third, 1)

    part = shrink_part(blocks, shrink_factors, batch_at)
    parts = [part, across(part, 1)]
    part, later_tagged, next_door = lax.optimization_barrier((part, tagged, next_door))
    next_door = across(next_door, 1)
    (second,) = base_block(tensor_at, later_tagged, out_weight, block, 2, (), (), 30)
    second = (wide(second) + wide(third)).astype(BF16)
    parts, second = lax.optimization_barrier((parts, second))
    bit = 2
    while bit < tensor_size:
        part = (wide(parts[0]) + wide(parts[1])).astype(BF16)
        parts = [part, across(part, bit)]
        bit *= 2
    arrived = [across(second, 2)]
    for ahead in range(4, tensor_size, 2):
        (near,) = base_block(tensor_at, tagged, out_weight, block, ahead)
        (far,) = base_block(tensor_at, tagged, out_weight, block, ahead + 1)
        arrived.append(across((wide(near) + wide(across(far, 1))).astype(BF16), ahead))

    parts, next_door = lax.optimization_barrier((parts, next_door))
    deltas = expand(blocks, parts, expand_factors, limits, batch_at)
    deltas, late_tagged = lax.optimization_barrier((deltas, tagged))
    (own,) = base_block(tensor_at, late_tagged, out_weight, block, 0, (), (), 2)
    terms = [partial_total([own, deltas[0], next_door, *arrived], 8 << 20)]
    terms += [to_chip(home, -shift) for shift, home in enumerate(deltas[1:], 1)]
    return total(rows, block, terms)


def solution(mesh):
    placed = (
        P(("groups", "batch"), "tensor", None),
        P(("groups", "batch"), None, None, None),
        P(("groups", "batch"), None, None, None),
        P(("groups", "batch"), None, None),
        P(("groups", "batch"), None, None),
        P(("groups", "batch")),
        P("tensor", None),
        P("batch", "tensor", None),
        P("batch", None, "tensor"),
        P("batch"),
        P(("groups", "batch")),
        P(("groups", "batch")),
    )

    def placed_local(*arrays):
        return local(mesh.shape["tensor"], mesh.shape["batch"], *arrays)

    return jax.shard_map(
        placed_local,
        mesh=mesh,
        in_specs=placed,
        out_specs=P(("groups", "batch"), "tensor"),
        check_vma=False,
    )
```

```python
import functools

import jax
import jax.numpy as jnp
from jax import lax
from jax.experimental import pallas as pl
from jax.experimental.pallas import tpu as pltpu
from jax.sharding import PartitionSpec as P

HQ = 32
KVH = 4
LANES = 128
VMEM = pltpu.VMEM
GRANT = 56 << 20
F32, BF16 = jnp.float32, jnp.bfloat16


def permuted(array, axis, size, partner):
    return lax.ppermute(array, axis, [(i, partner(i)) for i in range(size)])


def in_hbm(*arrays):
    return [pltpu.with_memory_space_constraint(array, pltpu.HBM) for array in arrays]


def lane_of(shape):
    return lax.broadcasted_iota(jnp.int32, shape, len(shape) - 1)


def attend_kernel(parts, rank_width, group_at, early_at, *refs):
    given, (out_weight, tagged, early, limits, *scratch) = refs[:9], refs[9:]
    held, (spread_out, small_sems, key_sems, value_sems, early_sem) = scratch[:9], scratch[9:]
    key_cache, value_cache = given[:2]
    keys, values, queries, new_key, new_value, lengths, row_adapter, adapter_list, ranks = held
    rows, heads, width = queries.shape
    positions = key_cache.shape[2]
    group = group_at[0]
    some = rows // parts

    def cache_copies(part):
        at = pl.ds(part * some, some)
        return (
            pltpu.make_async_copy(key_cache.at[at, group], keys.at[at], key_sems.at[part]),
            pltpu.make_async_copy(value_cache.at[at, group], values.at[at], value_sems.at[part]),
        )

    small = [
        pltpu.make_async_copy(given[i], held[i], small_sems.at[i - 2]) for i in range(2, 9)
    ]
    for copy in small:
        copy.start()
    for part in range(parts):
        for copy in cache_copies(part):
            copy.start()
    block = early.shape[1]
    start = pl.multiple_of(early_at[0] * block, block)
    early_copy = pltpu.make_async_copy(out_weight.at[:, pl.ds(start, block)], early, early_sem)
    early_copy.start(priority=1)
    for copy in small:
        copy.wait()
    at_row = lax.broadcasted_iota(jnp.int32, (rows, LANES), 0)
    tag = jnp.zeros((rows, LANES), jnp.int32)
    for row in range(rows):
        tag = jnp.where(at_row == row, adapter_list[row_adapter[row]], tag)
    tag = tag.astype(F32).astype(BF16)
    slot = lax.broadcasted_iota(jnp.int32, limits.shape, 0) * (LANES // rank_width)
    slot = slot + lane_of(limits.shape) // rank_width
    limit = jnp.zeros(limits.shape, jnp.int32)
    for held_at in range(ranks.shape[0]):
        limit = jnp.where(slot == held_at, ranks[held_at], limit)
    limits[...] = limit

    group_row = lax.broadcasted_iota(jnp.int32, new_key.shape, 1) == group
    fresh_key = jnp.sum(
        jnp.where(group_row, new_key[...].astype(F32), F32(0.0)), axis=1, keepdims=True
    )
    fresh_value = jnp.sum(
        jnp.where(group_row, new_value[...].astype(F32), F32(0.0)), axis=1, keepdims=True
    )
    score_scale = width ** (-0.5)
    fresh = jnp.sum(queries[...].astype(F32) * fresh_key, axis=-1, keepdims=True) * score_scale
    for part in range(parts):
        at = slice(part * some, (part + 1) * some)
        key_copy, value_copy = cache_copies(part)
        key_copy.wait()
        scores = (
            lax.dot_general(
                queries[at], keys[at], (((2,), (2,)), ((0,), (0,))), preferred_element_type=F32
            )
            * score_scale
        )
        length = jnp.stack(
            [
                jnp.full((heads, positions), lengths[row], jnp.int32)
                for row in range(part * some, (part + 1) * some)
            ]
        )
        valid = lane_of(scores.shape) < length
        masked = jnp.where(valid, scores, F32(-1e30))
        highest = jnp.maximum(jnp.max(masked, axis=-1, keepdims=True), fresh[at])
        cached_exp = jnp.where(valid, jnp.exp(masked - highest), F32(0.0))
        fresh_exp = jnp.exp(fresh[at] - highest)
        totals = jnp.sum(cached_exp, axis=-1, keepdims=True) + fresh_exp
        cached_w = (cached_exp / totals).astype(BF16)
        fresh_w = (fresh_exp / totals).astype(BF16).astype(F32)
        value_copy.wait()
        attended = lax.dot_general(
            cached_w, values[at], (((2,), (1,)), ((0,), (0,))), preferred_element_type=F32
        )
        attended = attended + fresh_w * fresh_value[at]
        spread_out[pl.ds(part * some * heads, some * heads)] = attended.reshape(
            some * heads, width
        )
    tagged[:, heads * width :] = tag
    for head in range(heads):
        tagged[:, head * width : (head + 1) * width] = spread_out[
            pl.ds(head, rows, stride=heads)
        ].astype(BF16)
    early_copy.wait()


def attend(
    early_at,
    block,
    out_weight,
    queries,
    key_cache,
    value_cache,
    new_key,
    new_value,
    lengths,
    adapter_list,
    row_adapter,
    adapter_rank,
    rank_width,
):
    rows, heads, width = queries.shape
    positions = key_cache.shape[2]
    per_group = HQ // KVH
    group_at = (lax.axis_index("tensor") * heads // per_group).reshape(1).astype(jnp.int32)
    full = -(-heads // 8) * 8
    if full != heads:
        queries = jnp.pad(queries, ((0, 0), (0, full - heads), (0, 0)))
    parts = 2
    smem = pl.BlockSpec(memory_space=pltpu.SMEM)
    away = pl.BlockSpec(memory_space=pl.ANY)
    tagged, early, limits = pl.pallas_call(
        functools.partial(attend_kernel, parts, rank_width),
        out_shape=[
            jax.ShapeDtypeStruct((rows, full * width + LANES), BF16),
            VMEM((out_weight.shape[0], block), BF16),
            jax.ShapeDtypeStruct((8, LANES), jnp.int32),
        ],
        in_specs=[smem, smem] + [away] * 10,
        out_specs=[pl.BlockSpec(memory_space=VMEM)] * 3,
        scratch_shapes=[
            VMEM((rows, positions, width), BF16),
            VMEM((rows, positions, width), BF16),
            VMEM(queries.shape, BF16),
            VMEM(new_key.shape, BF16),
            VMEM(new_value.shape, BF16),
            pltpu.SMEM(lengths.shape, jnp.int32),
            pltpu.SMEM(row_adapter.shape, jnp.int32),
            pltpu.SMEM(adapter_list.shape, jnp.int32),
            pltpu.SMEM(adapter_rank.shape, jnp.int32),
            VMEM((rows * full, width), F32),
            pltpu.SemaphoreType.DMA((7,)),
            pltpu.SemaphoreType.DMA((parts,)),
            pltpu.SemaphoreType.DMA((parts,)),
            pltpu.SemaphoreType.DMA,
        ],
        compiler_params=pltpu.CompilerParams(vmem_limit_bytes=8 << 20),
        cost_estimate=pl.CostEstimate(
            flops=4 * rows * heads * positions * width,
            bytes_accessed=4 * rows * positions * width,
            transcendentals=rows * heads * positions,
        ),
        name="attention",
    )(
        group_at,
        early_at,
        *in_hbm(
            key_cache,
            value_cache,
            queries,
            new_key,
            new_value,
            lengths,
            row_adapter,
            adapter_list,
            adapter_rank,
            out_weight,
        ),
    )
    if full != heads:
        tagged = jnp.concatenate([tagged[:, : heads * width], tagged[:, full * width :]], axis=1)
    return tagged, early, limits


def put_stacked(out, start, term, first=0, others=()):
    rows = term.shape[0]
    for column in range(0, term.shape[1], LANES):
        at = first + (start + column) // LANES * rows
        part = term[:, column : column + LANES]
        for other in others:
            part = part + other[at : at + rows].astype(F32)
        out[at : at + rows] = part.astype(out.dtype)


def base_kernel(ahead, deep, arriving, tensor_at, tagged, out_weight, *refs):
    arrived, (*near, out, held, sums, sems) = refs[:arriving], refs[arriving:]
    _, deep_rows, block = held.shape
    width = out_weight.shape[0]
    count = width // deep_rows
    column = pl.ds(pl.multiple_of((tensor_at[0] ^ ahead) * block, block), block)

    def copy(at):
        return pltpu.make_async_copy(
            out_weight.at[pl.ds(at * deep_rows, deep_rows), column],
            held.at[at % deep],
            sems.at[at % deep],
        )

    for at in range(min(deep, count)):
        copy(at).start(priority=at % 2)
    piece = min(block, 512)
    if near:
        early, early_out = near
        for start in range(0, block, piece):
            columns = slice(start, start + piece)
            term = jnp.dot(tagged[:, :width], early[:, columns], preferred_element_type=F32)
            put_stacked(early_out, start, term)
    for at in range(count):
        copy(at).wait()
        inputs = slice(at * deep_rows, (at + 1) * deep_rows)
        for start in range(0, block, piece):
            columns = slice(start, start + piece)
            term = jnp.dot(
                tagged[:, inputs], held[at % deep, :, columns], preferred_element_type=F32
            )
            if at:
                term = term + sums[:, columns]
            if at < count - 1:
                sums[:, columns] = term
            else:
                put_stacked(out, start, term, 0, arrived)
        if at + deep < count:
            copy(at + deep).start(priority=at % 2)


def base_block(tensor_at, tagged, out_weight, block, ahead, early=(), arrived=()):
    rows = tagged.shape[0]
    width = out_weight.shape[0]
    deep, deep_rows = 4, min(width, 256)
    whole = pl.BlockSpec(memory_space=VMEM)
    count = 1 + len(early)
    return pl.pallas_call(
        functools.partial(base_kernel, ahead, deep, len(arrived)),
        out_shape=[jax.ShapeDtypeStruct((block // LANES * rows, LANES), BF16 if ahead else F32)]
        * count,
        in_specs=[pl.BlockSpec(memory_space=pltpu.SMEM), whole, pl.BlockSpec(memory_space=pl.ANY)]
        + [whole] * (len(arrived) + len(early)),
        out_specs=[whole] * count,
        scratch_shapes=[
            VMEM((deep, deep_rows, block), BF16),
            VMEM((rows, block), F32),
            pltpu.SemaphoreType.DMA((deep,)),
        ],
        compiler_params=pltpu.CompilerParams(vmem_limit_bytes=12 << 20),
        cost_estimate=pl.CostEstimate(
            flops=2 * rows * width * block * count,
            bytes_accessed=2 * width * block * (2 if arrived else count),
            transcendentals=0,
        ),
        name="base_terms",
    )(tensor_at, tagged, *in_hbm(out_weight), *arrived, *early)


def slots_of(tags, batch_at, pool, tile, per):
    lane = lane_of(tags.shape)
    ids = tags.astype(F32).astype(jnp.int32)
    mine = tile * per + lane // (LANES // per)
    held = tile * per // pool
    return ids - (batch_at[0] ^ held) * pool + held * pool, mine


def shrink_kernel(batch_at, *refs):
    blocks, factors, out = refs[:-3], refs[-3:-1], refs[-1]
    pool, rank_width, width = factors[0].shape
    everyone = jnp.concatenate([block[...] for block in blocks], axis=0)
    per = LANES // rank_width
    lane = lane_of((everyone.shape[0], LANES))
    kept = jnp.zeros(lane.shape, F32)
    for held, weights in enumerate(factors):
        terms = lax.dot_general(
            everyone[:, :width],
            weights[...].reshape(pool * rank_width, width),
            (((1,), (1,)), ((), ())),
            preferred_element_type=F32,
        )
        for tile in range(pool // per):
            slot, mine = slots_of(everyone[:, width:], batch_at, pool, held * pool // per + tile, per)
            kept = kept + jnp.where(
                slot == mine, terms[:, tile * LANES : (tile + 1) * LANES], F32(0.0)
            )
    both = kept + pltpu.roll(kept, rank_width, 1)
    half = both.shape[0] // 2
    packed = jnp.where(lane[:half] < rank_width, both[:half], both[half:])
    out[...] = packed.astype(out.dtype)


def shrink_part(blocks, factors, batch_at):
    pool, rank_width, width = factors[0].shape
    rows = len(blocks) * blocks[0].shape[0]
    smem = pl.BlockSpec(memory_space=pltpu.SMEM)
    whole = pl.BlockSpec(memory_space=VMEM)
    return pl.pallas_call(
        shrink_kernel,
        out_shape=jax.ShapeDtypeStruct((rows // 2, LANES), BF16),
        in_specs=[smem] + [whole] * (len(blocks) + 2),
        out_specs=whole,
        compiler_params=pltpu.CompilerParams(vmem_limit_bytes=8 << 20),
        cost_estimate=pl.CostEstimate(
            flops=4 * rows * width * pool * rank_width,
            bytes_accessed=2 * width * (rows + 2 * pool * rank_width),
            transcendentals=0,
        ),
        name="shrink",
    )(batch_at, *blocks, *factors)


def expand_kernel(count, sums, rank_width, batch_at, *refs):
    limits, refs = refs[:2], refs[2:]
    tags, parts = refs[:count], refs[count : count + sums]
    factors, outs = refs[count + sums : count + sums + 2], refs[count + sums + 2 :]
    tags = jnp.concatenate([tag[...] for tag in tags], axis=0)
    total = parts[0][...].astype(F32)
    for part in parts[1:]:
        total = total + part[...].astype(F32)
    total = total.astype(BF16).astype(F32)
    other = pltpu.roll(total, rank_width, 1)
    low = lane_of(total.shape) < rank_width
    shrink = jnp.concatenate(
        [jnp.where(low, total, other), jnp.where(low, other, total)], axis=0
    )
    per = LANES // rank_width
    inputs, block = factors[0].shape
    pool = inputs // rank_width
    tiles = []
    for tile in range(2 * pool // per):
        slot, mine = slots_of(tags, batch_at, pool, tile, per)
        held, at = divmod(tile * per, pool)
        limit = limits[held][at // per : at // per + 1]
        keep = (slot == mine) & (lane_of(tags.shape) % rank_width < limit)
        tiles.append(jnp.where(keep, shrink, F32(0.0)).astype(BF16))
    half = len(tiles) // 2
    spreads = [jnp.concatenate(tiles[:half], axis=1), jnp.concatenate(tiles[half:], axis=1)]
    rows = tags.shape[0] // count
    piece = min(block, 512)
    for at in range(0, block, piece):
        delta = sum(
            jnp.dot(spread, each[:, at : at + piece], preferred_element_type=F32)
            for spread, each in zip(spreads, factors)
        )
        for which, out in enumerate(outs):
            put_stacked(out, at, delta[which * rows : (which + 1) * rows])


def expand(blocks, parts, factors, limits, batch_at):
    pool, rank_width, block = factors[0].shape
    rows, tagged_width = blocks[0].shape
    count = len(blocks)
    stack = rows * block // LANES
    tag = pl.BlockSpec((rows, LANES), lambda i: (0, tagged_width // LANES - 1))
    full = pl.BlockSpec((pool * rank_width, block), lambda i: (0, 0))
    part = pl.BlockSpec(parts[0].shape, lambda i: (0, 0))
    return pl.pallas_call(
        functools.partial(expand_kernel, count, len(parts), rank_width),
        grid=(1,),
        out_shape=[jax.ShapeDtypeStruct((stack, LANES), BF16) for _ in blocks],
        in_specs=[pl.BlockSpec(memory_space=pltpu.SMEM)]
        + [pl.BlockSpec(each.shape, lambda i: (0, 0)) for each in limits]
        + [tag] * count
        + [part] * len(parts)
        + [full] * 2,
        out_specs=[pl.BlockSpec((stack, LANES), lambda i: (0, 0)) for _ in blocks],
        compiler_params=pltpu.CompilerParams(vmem_limit_bytes=16 << 20),
        cost_estimate=pl.CostEstimate(
            flops=4 * rows * count * pool * rank_width * block,
            bytes_accessed=2 * pool * rank_width * block,
            transcendentals=0,
        ),
        name="expand",
    )(batch_at, *limits, *blocks, *parts, *[each.reshape(pool * rank_width, block) for each in factors])


def total_kernel(*refs):
    terms, out = refs[:-1], refs[-1]
    rows = out.shape[0]
    for column in range(0, out.shape[1], LANES):
        at = slice(column // LANES * rows, (column // LANES + 1) * rows)
        total = terms[0][at].astype(F32)
        for term in terms[1:]:
            total = total + term[at].astype(F32)
        out[:, column : column + LANES] = total.astype(out.dtype)


def total(rows, block, terms):
    whole = pl.BlockSpec(memory_space=VMEM)
    return pl.pallas_call(
        total_kernel,
        out_shape=jax.ShapeDtypeStruct((rows, block), BF16),
        in_specs=[whole] * len(terms),
        out_specs=whole,
        compiler_params=pltpu.CompilerParams(vmem_limit_bytes=8 << 20),
        cost_estimate=pl.CostEstimate(
            flops=rows * block * len(terms),
            bytes_accessed=2 * rows * block * (1 + len(terms)),
            transcendentals=0,
        ),
        name="total",
    )(*terms)


def partial_kernel(*refs):
    terms, out = refs[:-1], refs[-1]
    total = terms[0][...].astype(F32)
    for term in terms[1:]:
        total = total + term[...].astype(F32)
    out[...] = total


def partial_total(terms, weight):
    whole = pl.BlockSpec(memory_space=VMEM)
    return pl.pallas_call(
        partial_kernel,
        out_shape=jax.ShapeDtypeStruct(terms[0].shape, F32),
        in_specs=[whole] * len(terms),
        out_specs=whole,
        compiler_params=pltpu.CompilerParams(vmem_limit_bytes=8 << 20),
        cost_estimate=pl.CostEstimate(
            flops=terms[0].size * len(terms),
            bytes_accessed=4 * terms[0].size + weight,
            transcendentals=0,
        ),
        name="partial_total",
    )(*terms)


def local(
    tensor_size,
    batch_size,
    queries,
    key_cache,
    value_cache,
    new_key,
    new_value,
    lengths,
    out_weight,
    shrink_weight,
    expand_weight,
    adapter_rank,
    adapter_list,
    row_adapter,
):
    rows = queries.shape[0]
    block = expand_weight.shape[2]
    chips = batch_size // 2
    batch_at = lax.axis_index("batch").reshape(1).astype(jnp.int32)
    tensor_at = lax.axis_index("tensor").reshape(1).astype(jnp.int32)

    def to_sibling(array):
        return permuted(array, "batch", batch_size, lambda i: i ^ 1)

    def to_chip(array, shift):
        return permuted(array, "batch", batch_size, lambda i: (i + 2 * shift) % batch_size)

    def across(array, bit):
        return permuted(array, "tensor", tensor_size, lambda i: i ^ bit)

    def wide(array):
        return array.astype(F32)

    stack = block // LANES * rows
    tagged, early, limits = attend(
        tensor_at ^ 3,
        block,
        out_weight,
        queries,
        key_cache,
        value_cache,
        new_key,
        new_value,
        lengths,
        adapter_list,
        row_adapter,
        adapter_rank,
        shrink_weight.shape[2],
    )
    limits = [limits, to_sibling(limits)]
    shrink_weight = jnp.swapaxes(shrink_weight, 1, 2)
    shrink_factors = [shrink_weight, to_sibling(shrink_weight)]
    expand_factors = [expand_weight, to_sibling(expand_weight)]
    visiting = [to_chip(tagged, shift) for shift in range(1, chips)]
    third, next_door = base_block(tensor_at, tagged, out_weight, block, 1, [early])
    visiting, third, next_door, limits = lax.optimization_barrier(
        (visiting, third, next_door, limits)
    )
    blocks = [tagged] + visiting
    third = across(third, 1)

    part = shrink_part(blocks, shrink_factors, batch_at)
    parts = [part, across(part, 1)]
    part, later_tagged = lax.optimization_barrier((part, tagged))
    (second,) = base_block(tensor_at, later_tagged, out_weight, block, 2)
    second = (wide(second) + wide(third)).astype(BF16)
    parts, second = lax.optimization_barrier((parts, second))
    bit = 2
    while bit < tensor_size:
        part = (wide(parts[0]) + wide(parts[1])).astype(BF16)
        part, next_door = lax.optimization_barrier((part, next_door))
        parts = [part, across(part, bit)]
        bit *= 2
    arrived = [across(second, 2), across(next_door, 1)]
    for ahead in range(4, tensor_size, 2):
        (near,) = base_block(tensor_at, tagged, out_weight, block, ahead)
        (far,) = base_block(tensor_at, tagged, out_weight, block, ahead + 1)
        arrived.append(across((wide(near) + wide(across(far, 1))).astype(BF16), ahead))

    deltas = expand(blocks, parts, expand_factors, limits, batch_at)
    deltas, late_tagged = lax.optimization_barrier((deltas, tagged))
    (own,) = base_block(tensor_at, late_tagged, out_weight, block, 0)
    so_far = partial_total([own, deltas[0], arrived[0], *arrived[2:]], 0)
    terms = [partial_total([so_far, arrived[1]], 8 << 20)]
    terms += [to_chip(home, -shift) for shift, home in enumerate(deltas[1:], 1)]
    return total(rows, block, terms)


def solution(mesh):
    placed = (
        P(("groups", "batch"), "tensor", None),
        P(("groups", "batch"), None, None, None),
        P(("groups", "batch"), None, None, None),
        P(("groups", "batch"), None, None),
        P(("groups", "batch"), None, None),
        P(("groups", "batch")),
        P("tensor", None),
        P("batch", "tensor", None),
        P("batch", None, "tensor"),
        P("batch"),
        P(("groups", "batch")),
        P(("groups", "batch")),
    )

    def placed_local(*arrays):
        return local(mesh.shape["tensor"], mesh.shape["batch"], *arrays)

    return jax.shard_map(
        placed_local,
        mesh=mesh,
        in_specs=placed,
        out_specs=P(("groups", "batch"), "tensor"),
        check_vma=False,
    )
```

```python
import functools

import jax
import jax.numpy as jnp
from jax import lax
from jax.experimental import pallas as pl
from jax.experimental.pallas import tpu as pltpu
from jax.sharding import PartitionSpec as P

HQ = 32
KVH = 4
LANES = 128
VMEM = pltpu.VMEM
GRANT = 56 << 20
F32, BF16 = jnp.float32, jnp.bfloat16


def permuted(array, axis, size, partner):
    return lax.ppermute(array, axis, [(i, partner(i)) for i in range(size)])


def in_hbm(*arrays):
    return [pltpu.with_memory_space_constraint(array, pltpu.HBM) for array in arrays]


def lane_of(shape):
    return lax.broadcasted_iota(jnp.int32, shape, len(shape) - 1)


def attend_kernel(parts, rank_width, group_at, early_at, *refs):
    given, (out_weight, tagged, early, limits, *scratch) = refs[:9], refs[9:]
    held, (spread_out, small_sems, key_sems, value_sems, early_sem) = scratch[:9], scratch[9:]
    key_cache, value_cache = given[:2]
    keys, values, queries, new_key, new_value, lengths, row_adapter, adapter_list, ranks = held
    rows, heads, width = queries.shape
    positions = key_cache.shape[2]
    group = group_at[0]
    some = rows // parts

    def cache_copies(part):
        at = pl.ds(part * some, some)
        return (
            pltpu.make_async_copy(key_cache.at[at, group], keys.at[at], key_sems.at[part]),
            pltpu.make_async_copy(value_cache.at[at, group], values.at[at], value_sems.at[part]),
        )

    small = [
        pltpu.make_async_copy(given[i], held[i], small_sems.at[i - 2]) for i in range(2, 9)
    ]
    for copy in small:
        copy.start()
    for part in range(parts):
        for copy in cache_copies(part):
            copy.start()
    block = early.shape[1]
    start = pl.multiple_of(early_at[0] * block, block)
    early_copy = pltpu.make_async_copy(out_weight.at[:, pl.ds(start, block)], early, early_sem)
    early_copy.start()
    for copy in small:
        copy.wait()
    at_row = lax.broadcasted_iota(jnp.int32, (rows, LANES), 0)
    tag = jnp.zeros((rows, LANES), jnp.int32)
    for row in range(rows):
        tag = jnp.where(at_row == row, adapter_list[row_adapter[row]], tag)
    tag = tag.astype(F32).astype(BF16)
    slot = lax.broadcasted_iota(jnp.int32, limits.shape, 0) * (LANES // rank_width)
    slot = slot + lane_of(limits.shape) // rank_width
    limit = jnp.zeros(limits.shape, jnp.int32)
    for held_at in range(ranks.shape[0]):
        limit = jnp.where(slot == held_at, ranks[held_at], limit)
    limits[...] = limit

    group_row = lax.broadcasted_iota(jnp.int32, new_key.shape, 1) == group
    fresh_key = jnp.sum(
        jnp.where(group_row, new_key[...].astype(F32), F32(0.0)), axis=1, keepdims=True
    )
    fresh_value = jnp.sum(
        jnp.where(group_row, new_value[...].astype(F32), F32(0.0)), axis=1, keepdims=True
    )
    score_scale = width ** (-0.5)
    fresh = jnp.sum(queries[...].astype(F32) * fresh_key, axis=-1, keepdims=True) * score_scale
    for part in range(parts):
        at = slice(part * some, (part + 1) * some)
        key_copy, value_copy = cache_copies(part)
        key_copy.wait()
        scores = (
            lax.dot_general(
                queries[at], keys[at], (((2,), (2,)), ((0,), (0,))), preferred_element_type=F32
            )
            * score_scale
        )
        length = jnp.stack(
            [
                jnp.full((heads, positions), lengths[row], jnp.int32)
                for row in range(part * some, (part + 1) * some)
            ]
        )
        valid = lane_of(scores.shape) < length
        masked = jnp.where(valid, scores, F32(-1e30))
        highest = jnp.maximum(jnp.max(masked, axis=-1, keepdims=True), fresh[at])
        cached_exp = jnp.where(valid, jnp.exp(masked - highest), F32(0.0))
        fresh_exp = jnp.exp(fresh[at] - highest)
        totals = jnp.sum(cached_exp, axis=-1, keepdims=True) + fresh_exp
        cached_w = (cached_exp / totals).astype(BF16)
        fresh_w = (fresh_exp / totals).astype(BF16).astype(F32)
        value_copy.wait()
        attended = lax.dot_general(
            cached_w, values[at], (((2,), (1,)), ((0,), (0,))), preferred_element_type=F32
        )
        attended = attended + fresh_w * fresh_value[at]
        spread_out[pl.ds(part * some * heads, some * heads)] = attended.reshape(
            some * heads, width
        )
    tagged[:, heads * width :] = tag
    for head in range(heads):
        tagged[:, head * width : (head + 1) * width] = spread_out[
            pl.ds(head, rows, stride=heads)
        ].astype(BF16)
    early_copy.wait()


def attend(
    early_at,
    block,
    out_weight,
    queries,
    key_cache,
    value_cache,
    new_key,
    new_value,
    lengths,
    adapter_list,
    row_adapter,
    adapter_rank,
    rank_width,
):
    rows, heads, width = queries.shape
    positions = key_cache.shape[2]
    per_group = HQ // KVH
    group_at = (lax.axis_index("tensor") * heads // per_group).reshape(1).astype(jnp.int32)
    full = -(-heads // 8) * 8
    if full != heads:
        queries = jnp.pad(queries, ((0, 0), (0, full - heads), (0, 0)))
    parts = 2
    smem = pl.BlockSpec(memory_space=pltpu.SMEM)
    away = pl.BlockSpec(memory_space=pl.ANY)
    tagged, early, limits = pl.pallas_call(
        functools.partial(attend_kernel, parts, rank_width),
        out_shape=[
            jax.ShapeDtypeStruct((rows, full * width + LANES), BF16),
            VMEM((out_weight.shape[0], block), BF16),
            jax.ShapeDtypeStruct((8, LANES), jnp.int32),
        ],
        in_specs=[smem, smem] + [away] * 10,
        out_specs=[pl.BlockSpec(memory_space=VMEM)] * 3,
        scratch_shapes=[
            VMEM((rows, positions, width), BF16),
            VMEM((rows, positions, width), BF16),
            VMEM(queries.shape, BF16),
            VMEM(new_key.shape, BF16),
            VMEM(new_value.shape, BF16),
            pltpu.SMEM(lengths.shape, jnp.int32),
            pltpu.SMEM(row_adapter.shape, jnp.int32),
            pltpu.SMEM(adapter_list.shape, jnp.int32),
            pltpu.SMEM(adapter_rank.shape, jnp.int32),
            VMEM((rows * full, width), F32),
            pltpu.SemaphoreType.DMA((7,)),
            pltpu.SemaphoreType.DMA((parts,)),
            pltpu.SemaphoreType.DMA((parts,)),
            pltpu.SemaphoreType.DMA,
        ],
        compiler_params=pltpu.CompilerParams(vmem_limit_bytes=8 << 20),
        cost_estimate=pl.CostEstimate(
            flops=4 * rows * heads * positions * width,
            bytes_accessed=4 * rows * positions * width,
            transcendentals=rows * heads * positions,
        ),
        name="attention",
    )(
        group_at,
        early_at,
        *in_hbm(
            key_cache,
            value_cache,
            queries,
            new_key,
            new_value,
            lengths,
            row_adapter,
            adapter_list,
            adapter_rank,
            out_weight,
        ),
    )
    if full != heads:
        tagged = jnp.concatenate([tagged[:, : heads * width], tagged[:, full * width :]], axis=1)
    return tagged, early, limits


def put_stacked(out, start, term, first=0, others=()):
    rows = term.shape[0]
    for column in range(0, term.shape[1], LANES):
        at = first + (start + column) // LANES * rows
        part = term[:, column : column + LANES]
        for other in others:
            part = part + other[at : at + rows].astype(F32)
        out[at : at + rows] = part.astype(out.dtype)


def base_kernel(ahead, deep, arriving, tensor_at, tagged, out_weight, *refs):
    arrived, (*near, out, held, sums, sems) = refs[:arriving], refs[arriving:]
    _, deep_rows, block = held.shape
    width = out_weight.shape[0]
    count = width // deep_rows
    column = pl.ds(pl.multiple_of((tensor_at[0] ^ ahead) * block, block), block)

    def copy(at):
        return pltpu.make_async_copy(
            out_weight.at[pl.ds(at * deep_rows, deep_rows), column],
            held.at[at % deep],
            sems.at[at % deep],
        )

    for at in range(min(deep, count)):
        copy(at).start()
    piece = min(block, 512)
    if near:
        early, early_out = near
        for start in range(0, block, piece):
            columns = slice(start, start + piece)
            term = jnp.dot(tagged[:, :width], early[:, columns], preferred_element_type=F32)
            put_stacked(early_out, start, term)
    for at in range(count):
        copy(at).wait()
        inputs = slice(at * deep_rows, (at + 1) * deep_rows)
        for start in range(0, block, piece):
            columns = slice(start, start + piece)
            term = jnp.dot(
                tagged[:, inputs], held[at % deep, :, columns], preferred_element_type=F32
            )
            if at:
                term = term + sums[:, columns]
            if at < count - 1:
                sums[:, columns] = term
            else:
                put_stacked(out, start, term, 0, arrived)
        if at + deep < count:
            copy(at + deep).start()


def base_block(tensor_at, tagged, out_weight, block, ahead, early=(), arrived=()):
    rows = tagged.shape[0]
    width = out_weight.shape[0]
    deep, deep_rows = 4, min(width, 256)
    whole = pl.BlockSpec(memory_space=VMEM)
    count = 1 + len(early)
    return pl.pallas_call(
        functools.partial(base_kernel, ahead, deep, len(arrived)),
        out_shape=[jax.ShapeDtypeStruct((block // LANES * rows, LANES), BF16 if ahead else F32)]
        * count,
        in_specs=[pl.BlockSpec(memory_space=pltpu.SMEM), whole, pl.BlockSpec(memory_space=pl.ANY)]
        + [whole] * (len(arrived) + len(early)),
        out_specs=[whole] * count,
        scratch_shapes=[
            VMEM((deep, deep_rows, block), BF16),
            VMEM((rows, block), F32),
            pltpu.SemaphoreType.DMA((deep,)),
        ],
        compiler_params=pltpu.CompilerParams(vmem_limit_bytes=12 << 20),
        cost_estimate=pl.CostEstimate(
            flops=2 * rows * width * block * count,
            bytes_accessed=2 * width * block * (2 if arrived else count),
            transcendentals=0,
        ),
        name="base_terms",
    )(tensor_at, tagged, *in_hbm(out_weight), *arrived, *early)


def slots_of(tags, batch_at, pool, tile, per):
    lane = lane_of(tags.shape)
    ids = tags.astype(F32).astype(jnp.int32)
    mine = tile * per + lane // (LANES // per)
    held = tile * per // pool
    return ids - (batch_at[0] ^ held) * pool + held * pool, mine


def shrink_kernel(batch_at, *refs):
    blocks, factors, out = refs[:-3], refs[-3:-1], refs[-1]
    pool, rank_width, width = factors[0].shape
    everyone = jnp.concatenate([block[...] for block in blocks], axis=0)
    per = LANES // rank_width
    lane = lane_of((everyone.shape[0], LANES))
    kept = jnp.zeros(lane.shape, F32)
    for held, weights in enumerate(factors):
        terms = lax.dot_general(
            everyone[:, :width],
            weights[...].reshape(pool * rank_width, width),
            (((1,), (1,)), ((), ())),
            preferred_element_type=F32,
        )
        for tile in range(pool // per):
            slot, mine = slots_of(everyone[:, width:], batch_at, pool, held * pool // per + tile, per)
            kept = kept + jnp.where(
                slot == mine, terms[:, tile * LANES : (tile + 1) * LANES], F32(0.0)
            )
    both = kept + pltpu.roll(kept, rank_width, 1)
    half = both.shape[0] // 2
    packed = jnp.where(lane[:half] < rank_width, both[:half], both[half:])
    out[...] = packed.astype(out.dtype)


def shrink_part(blocks, factors, batch_at):
    pool, rank_width, width = factors[0].shape
    rows = len(blocks) * blocks[0].shape[0]
    smem = pl.BlockSpec(memory_space=pltpu.SMEM)
    whole = pl.BlockSpec(memory_space=VMEM)
    return pl.pallas_call(
        shrink_kernel,
        out_shape=jax.ShapeDtypeStruct((rows // 2, LANES), BF16),
        in_specs=[smem] + [whole] * (len(blocks) + 2),
        out_specs=whole,
        compiler_params=pltpu.CompilerParams(vmem_limit_bytes=8 << 20),
        cost_estimate=pl.CostEstimate(
            flops=4 * rows * width * pool * rank_width,
            bytes_accessed=2 * width * (rows + 2 * pool * rank_width),
            transcendentals=0,
        ),
        name="shrink",
    )(batch_at, *blocks, *factors)


def expand_kernel(count, sums, rank_width, batch_at, *refs):
    limits, refs = refs[:2], refs[2:]
    tags, parts = refs[:count], refs[count : count + sums]
    factors, outs = refs[count + sums : count + sums + 2], refs[count + sums + 2 :]
    tags = jnp.concatenate([tag[...] for tag in tags], axis=0)
    total = parts[0][...].astype(F32)
    for part in parts[1:]:
        total = total + part[...].astype(F32)
    total = total.astype(BF16).astype(F32)
    other = pltpu.roll(total, rank_width, 1)
    low = lane_of(total.shape) < rank_width
    shrink = jnp.concatenate(
        [jnp.where(low, total, other), jnp.where(low, other, total)], axis=0
    )
    per = LANES // rank_width
    inputs, block = factors[0].shape
    pool = inputs // rank_width
    tiles = []
    for tile in range(2 * pool // per):
        slot, mine = slots_of(tags, batch_at, pool, tile, per)
        held, at = divmod(tile * per, pool)
        limit = limits[held][at // per : at // per + 1]
        keep = (slot == mine) & (lane_of(tags.shape) % rank_width < limit)
        tiles.append(jnp.where(keep, shrink, F32(0.0)).astype(BF16))
    half = len(tiles) // 2
    spreads = [jnp.concatenate(tiles[:half], axis=1), jnp.concatenate(tiles[half:], axis=1)]
    rows = tags.shape[0] // count
    piece = min(block, 512)
    for at in range(0, block, piece):
        delta = sum(
            jnp.dot(spread, each[:, at : at + piece], preferred_element_type=F32)
            for spread, each in zip(spreads, factors)
        )
        for which, out in enumerate(outs):
            put_stacked(out, at, delta[which * rows : (which + 1) * rows])


def expand(blocks, parts, factors, limits, batch_at):
    pool, rank_width, block = factors[0].shape
    rows, tagged_width = blocks[0].shape
    count = len(blocks)
    stack = rows * block // LANES
    tag = pl.BlockSpec((rows, LANES), lambda i: (0, tagged_width // LANES - 1))
    full = pl.BlockSpec((pool * rank_width, block), lambda i: (0, 0))
    part = pl.BlockSpec(parts[0].shape, lambda i: (0, 0))
    return pl.pallas_call(
        functools.partial(expand_kernel, count, len(parts), rank_width),
        grid=(1,),
        out_shape=[jax.ShapeDtypeStruct((stack, LANES), BF16) for _ in blocks],
        in_specs=[pl.BlockSpec(memory_space=pltpu.SMEM)]
        + [pl.BlockSpec(each.shape, lambda i: (0, 0)) for each in limits]
        + [tag] * count
        + [part] * len(parts)
        + [full] * 2,
        out_specs=[pl.BlockSpec((stack, LANES), lambda i: (0, 0)) for _ in blocks],
        compiler_params=pltpu.CompilerParams(vmem_limit_bytes=16 << 20),
        cost_estimate=pl.CostEstimate(
            flops=4 * rows * count * pool * rank_width * block,
            bytes_accessed=2 * pool * rank_width * block,
            transcendentals=0,
        ),
        name="expand",
    )(batch_at, *limits, *blocks, *parts, *[each.reshape(pool * rank_width, block) for each in factors])


def total_kernel(*refs):
    terms, out = refs[:-1], refs[-1]
    rows = out.shape[0]
    for column in range(0, out.shape[1], LANES):
        at = slice(column // LANES * rows, (column // LANES + 1) * rows)
        total = terms[0][at].astype(F32)
        for term in terms[1:]:
            total = total + term[at].astype(F32)
        out[:, column : column + LANES] = total.astype(out.dtype)


def total(rows, block, terms):
    whole = pl.BlockSpec(memory_space=VMEM)
    return pl.pallas_call(
        total_kernel,
        out_shape=jax.ShapeDtypeStruct((rows, block), BF16),
        in_specs=[whole] * len(terms),
        out_specs=whole,
        compiler_params=pltpu.CompilerParams(vmem_limit_bytes=8 << 20),
        cost_estimate=pl.CostEstimate(
            flops=rows * block * len(terms),
            bytes_accessed=2 * rows * block * (1 + len(terms)),
            transcendentals=0,
        ),
        name="total",
    )(*terms)


def partial_kernel(*refs):
    terms, out = refs[:-1], refs[-1]
    total = terms[0][...].astype(F32)
    for term in terms[1:]:
        total = total + term[...].astype(F32)
    out[...] = total


def partial_total(terms, weight):
    whole = pl.BlockSpec(memory_space=VMEM)
    return pl.pallas_call(
        partial_kernel,
        out_shape=jax.ShapeDtypeStruct(terms[0].shape, F32),
        in_specs=[whole] * len(terms),
        out_specs=whole,
        compiler_params=pltpu.CompilerParams(vmem_limit_bytes=8 << 20),
        cost_estimate=pl.CostEstimate(
            flops=terms[0].size * len(terms),
            bytes_accessed=4 * terms[0].size + weight,
            transcendentals=0,
        ),
        name="partial_total",
    )(*terms)


def local(
    tensor_size,
    batch_size,
    queries,
    key_cache,
    value_cache,
    new_key,
    new_value,
    lengths,
    out_weight,
    shrink_weight,
    expand_weight,
    adapter_rank,
    adapter_list,
    row_adapter,
):
    rows = queries.shape[0]
    block = expand_weight.shape[2]
    chips = batch_size // 2
    batch_at = lax.axis_index("batch").reshape(1).astype(jnp.int32)
    tensor_at = lax.axis_index("tensor").reshape(1).astype(jnp.int32)

    def to_sibling(array):
        return permuted(array, "batch", batch_size, lambda i: i ^ 1)

    def to_chip(array, shift):
        return permuted(array, "batch", batch_size, lambda i: (i + 2 * shift) % batch_size)

    def across(array, bit):
        return permuted(array, "tensor", tensor_size, lambda i: i ^ bit)

    def wide(array):
        return array.astype(F32)

    stack = block // LANES * rows
    tagged, early, limits = attend(
        tensor_at ^ 3,
        block,
        out_weight,
        queries,
        key_cache,
        value_cache,
        new_key,
        new_value,
        lengths,
        adapter_list,
        row_adapter,
        adapter_rank,
        shrink_weight.shape[2],
    )
    limits = [limits, to_sibling(limits)]
    shrink_weight = jnp.swapaxes(shrink_weight, 1, 2)
    shrink_factors = [shrink_weight, to_sibling(shrink_weight)]
    expand_factors = [expand_weight, to_sibling(expand_weight)]
    visiting = [to_chip(tagged, shift) for shift in range(1, chips)]
    third, next_door = base_block(tensor_at, tagged, out_weight, block, 1, [early])
    visiting, third, next_door, limits = lax.optimization_barrier(
        (visiting, third, next_door, limits)
    )
    blocks = [tagged] + visiting
    third = across(third, 1)

    part = shrink_part(blocks, shrink_factors, batch_at)
    bit = tensor_size // 2
    parts = [part, across(part, bit)]
    part, later_tagged = lax.optimization_barrier((part, tagged))
    (second,) = base_block(tensor_at, later_tagged, out_weight, block, 2)
    second = (wide(second) + wide(third)).astype(BF16)
    parts, second = lax.optimization_barrier((parts, second))
    while bit > 1:
        bit //= 2
        part = (wide(parts[0]) + wide(parts[1])).astype(BF16)
        part, next_door = lax.optimization_barrier((part, next_door))
        parts = [part, across(part, bit)]
    arrived = [across(second, 2), across(next_door, 1)]
    for ahead in range(4, tensor_size, 2):
        (near,) = base_block(tensor_at, tagged, out_weight, block, ahead)
        (far,) = base_block(tensor_at, tagged, out_weight, block, ahead + 1)
        arrived.append(across((wide(near) + wide(across(far, 1))).astype(BF16), ahead))

    deltas = expand(blocks, parts, expand_factors, limits, batch_at)
    deltas, late_tagged = lax.optimization_barrier((deltas, tagged))
    (own,) = base_block(tensor_at, late_tagged, out_weight, block, 0)
    so_far = partial_total([own, deltas[0], arrived[0], *arrived[2:]], 0)
    terms = [partial_total([so_far, arrived[1]], 8 << 20)]
    terms += [to_chip(home, -shift) for shift, home in enumerate(deltas[1:], 1)]
    return total(rows, block, terms)


def solution(mesh):
    placed = (
        P(("groups", "batch"), "tensor", None),
        P(("groups", "batch"), None, None, None),
        P(("groups", "batch"), None, None, None),
        P(("groups", "batch"), None, None),
        P(("groups", "batch"), None, None),
        P(("groups", "batch")),
        P("tensor", None),
        P("batch", "tensor", None),
        P("batch", None, "tensor"),
        P("batch"),
        P(("groups", "batch")),
        P(("groups", "batch")),
    )

    def placed_local(*arrays):
        return local(mesh.shape["tensor"], mesh.shape["batch"], *arrays)

    return jax.shard_map(
        placed_local,
        mesh=mesh,
        in_specs=placed,
        out_specs=P(("groups", "batch"), "tensor"),
        check_vma=False,
    )
```

```python
import functools

import jax
import jax.numpy as jnp
from jax import lax
from jax.experimental import pallas as pl
from jax.experimental.pallas import tpu as pltpu
from jax.sharding import PartitionSpec as P

HQ = 32
KVH = 4
LANES = 128
VMEM = pltpu.VMEM
GRANT = 56 << 20
F32, BF16 = jnp.float32, jnp.bfloat16


def permuted(array, axis, size, partner):
    return lax.ppermute(array, axis, [(i, partner(i)) for i in range(size)])


def in_hbm(*arrays):
    return [pltpu.with_memory_space_constraint(array, pltpu.HBM) for array in arrays]


def lane_of(shape):
    return lax.broadcasted_iota(jnp.int32, shape, len(shape) - 1)


def attend_kernel(parts, rank_width, group_at, early_at, *refs):
    given, (out_weight, tagged, early, limits, *scratch) = refs[:9], refs[9:]
    held, (spread_out, small_sems, key_sems, value_sems, early_sem) = scratch[:9], scratch[9:]
    key_cache, value_cache = given[:2]
    keys, values, queries, new_key, new_value, lengths, row_adapter, adapter_list, ranks = held
    rows, heads, width = queries.shape
    positions = key_cache.shape[2]
    group = group_at[0]
    some = rows // parts

    def cache_copies(part):
        at = pl.ds(part * some, some)
        return (
            pltpu.make_async_copy(key_cache.at[at, group], keys.at[at], key_sems.at[part]),
            pltpu.make_async_copy(value_cache.at[at, group], values.at[at], value_sems.at[part]),
        )

    small = [
        pltpu.make_async_copy(given[i], held[i], small_sems.at[i - 2]) for i in range(2, 9)
    ]
    for part in range(parts):
        for copy in cache_copies(part):
            copy.start()
    for copy in small:
        copy.start()
    block = early.shape[1]
    start = pl.multiple_of(early_at[0] * block, block)
    early_copy = pltpu.make_async_copy(out_weight.at[:, pl.ds(start, block)], early, early_sem)
    early_copy.start()
    for copy in small:
        copy.wait()
    at_row = lax.broadcasted_iota(jnp.int32, (rows, LANES), 0)
    tag = jnp.zeros((rows, LANES), jnp.int32)
    for row in range(rows):
        tag = jnp.where(at_row == row, adapter_list[row_adapter[row]], tag)
    tag = tag.astype(F32).astype(BF16)
    slot = lax.broadcasted_iota(jnp.int32, limits.shape, 0) * (LANES // rank_width)
    slot = slot + lane_of(limits.shape) // rank_width
    limit = jnp.zeros(limits.shape, jnp.int32)
    for held_at in range(ranks.shape[0]):
        limit = jnp.where(slot == held_at, ranks[held_at], limit)
    limits[...] = limit

    group_row = lax.broadcasted_iota(jnp.int32, new_key.shape, 1) == group
    fresh_key = jnp.sum(
        jnp.where(group_row, new_key[...].astype(F32), F32(0.0)), axis=1, keepdims=True
    )
    fresh_value = jnp.sum(
        jnp.where(group_row, new_value[...].astype(F32), F32(0.0)), axis=1, keepdims=True
    )
    score_scale = width ** (-0.5)
    fresh = jnp.sum(queries[...].astype(F32) * fresh_key, axis=-1, keepdims=True) * score_scale
    for part in range(parts):
        at = slice(part * some, (part + 1) * some)
        key_copy, value_copy = cache_copies(part)
        key_copy.wait()
        scores = (
            lax.dot_general(
                queries[at], keys[at], (((2,), (2,)), ((0,), (0,))), preferred_element_type=F32
            )
            * score_scale
        )
        length = jnp.stack(
            [
                jnp.full((heads, positions), lengths[row], jnp.int32)
                for row in range(part * some, (part + 1) * some)
            ]
        )
        valid = lane_of(scores.shape) < length
        masked = jnp.where(valid, scores, F32(-1e30))
        highest = jnp.maximum(jnp.max(masked, axis=-1, keepdims=True), fresh[at])
        cached_exp = jnp.where(valid, jnp.exp(masked - highest), F32(0.0))
        fresh_exp = jnp.exp(fresh[at] - highest)
        totals = jnp.sum(cached_exp, axis=-1, keepdims=True) + fresh_exp
        cached_w = (cached_exp / totals).astype(BF16)
        fresh_w = (fresh_exp / totals).astype(BF16).astype(F32)
        value_copy.wait()
        attended = lax.dot_general(
            cached_w, values[at], (((2,), (1,)), ((0,), (0,))), preferred_element_type=F32
        )
        attended = attended + fresh_w * fresh_value[at]
        spread_out[pl.ds(part * some * heads, some * heads)] = attended.reshape(
            some * heads, width
        )
    tagged[:, heads * width :] = tag
    for head in range(heads):
        tagged[:, head * width : (head + 1) * width] = spread_out[
            pl.ds(head, rows, stride=heads)
        ].astype(BF16)
    early_copy.wait()


def attend(
    early_at,
    block,
    out_weight,
    queries,
    key_cache,
    value_cache,
    new_key,
    new_value,
    lengths,
    adapter_list,
    row_adapter,
    adapter_rank,
    rank_width,
):
    rows, heads, width = queries.shape
    positions = key_cache.shape[2]
    per_group = HQ // KVH
    group_at = (lax.axis_index("tensor") * heads // per_group).reshape(1).astype(jnp.int32)
    full = -(-heads // 8) * 8
    if full != heads:
        queries = jnp.pad(queries, ((0, 0), (0, full - heads), (0, 0)))
    parts = 1
    smem = pl.BlockSpec(memory_space=pltpu.SMEM)
    away = pl.BlockSpec(memory_space=pl.ANY)
    tagged, early, limits = pl.pallas_call(
        functools.partial(attend_kernel, parts, rank_width),
        out_shape=[
            jax.ShapeDtypeStruct((rows, full * width + LANES), BF16),
            VMEM((out_weight.shape[0], block), BF16),
            jax.ShapeDtypeStruct((8, LANES), jnp.int32),
        ],
        in_specs=[smem, smem] + [away] * 10,
        out_specs=[pl.BlockSpec(memory_space=VMEM)] * 3,
        scratch_shapes=[
            VMEM((rows, positions, width), BF16),
            VMEM((rows, positions, width), BF16),
            VMEM(queries.shape, BF16),
            VMEM(new_key.shape, BF16),
            VMEM(new_value.shape, BF16),
            pltpu.SMEM(lengths.shape, jnp.int32),
            pltpu.SMEM(row_adapter.shape, jnp.int32),
            pltpu.SMEM(adapter_list.shape, jnp.int32),
            pltpu.SMEM(adapter_rank.shape, jnp.int32),
            VMEM((rows * full, width), F32),
            pltpu.SemaphoreType.DMA((7,)),
            pltpu.SemaphoreType.DMA((parts,)),
            pltpu.SemaphoreType.DMA((parts,)),
            pltpu.SemaphoreType.DMA,
        ],
        compiler_params=pltpu.CompilerParams(vmem_limit_bytes=8 << 20),
        cost_estimate=pl.CostEstimate(
            flops=4 * rows * heads * positions * width,
            bytes_accessed=4 * rows * positions * width,
            transcendentals=rows * heads * positions,
        ),
        name="attention",
    )(
        group_at,
        early_at,
        *in_hbm(
            key_cache,
            value_cache,
            queries,
            new_key,
            new_value,
            lengths,
            row_adapter,
            adapter_list,
            adapter_rank,
            out_weight,
        ),
    )
    if full != heads:
        tagged = jnp.concatenate([tagged[:, : heads * width], tagged[:, full * width :]], axis=1)
    return tagged, early, limits


def put_stacked(out, start, term, first=0, others=()):
    rows = term.shape[0]
    for column in range(0, term.shape[1], LANES):
        at = first + (start + column) // LANES * rows
        part = term[:, column : column + LANES]
        for other in others:
            part = part + other[at : at + rows].astype(F32)
        out[at : at + rows] = part.astype(out.dtype)


def base_kernel(ahead, deep, arriving, tensor_at, tagged, out_weight, *refs):
    arrived, (*near, out, held, sums, sems) = refs[:arriving], refs[arriving:]
    _, deep_rows, block = held.shape
    width = out_weight.shape[0]
    count = width // deep_rows
    column = pl.ds(pl.multiple_of((tensor_at[0] ^ ahead) * block, block), block)

    def copy(at):
        return pltpu.make_async_copy(
            out_weight.at[pl.ds(at * deep_rows, deep_rows), column],
            held.at[at % deep],
            sems.at[at % deep],
        )

    for at in range(min(deep, count)):
        copy(at).start()
    piece = min(block, 512)
    if near:
        early, early_out = near
        for start in range(0, block, piece):
            columns = slice(start, start + piece)
            term = jnp.dot(tagged[:, :width], early[:, columns], preferred_element_type=F32)
            put_stacked(early_out, start, term)
    for at in range(count):
        copy(at).wait()
        inputs = slice(at * deep_rows, (at + 1) * deep_rows)
        for start in range(0, block, piece):
            columns = slice(start, start + piece)
            term = jnp.dot(
                tagged[:, inputs], held[at % deep, :, columns], preferred_element_type=F32
            )
            if at:
                term = term + sums[:, columns]
            if at < count - 1:
                sums[:, columns] = term
            else:
                put_stacked(out, start, term, 0, arrived)
        if at + deep < count:
            copy(at + deep).start()


def base_block(tensor_at, tagged, out_weight, block, ahead, early=(), arrived=()):
    rows = tagged.shape[0]
    width = out_weight.shape[0]
    deep, deep_rows = 4, min(width, 256)
    whole = pl.BlockSpec(memory_space=VMEM)
    count = 1 + len(early)
    return pl.pallas_call(
        functools.partial(base_kernel, ahead, deep, len(arrived)),
        out_shape=[jax.ShapeDtypeStruct((block // LANES * rows, LANES), BF16 if ahead else F32)]
        * count,
        in_specs=[pl.BlockSpec(memory_space=pltpu.SMEM), whole, pl.BlockSpec(memory_space=pl.ANY)]
        + [whole] * (len(arrived) + len(early)),
        out_specs=[whole] * count,
        scratch_shapes=[
            VMEM((deep, deep_rows, block), BF16),
            VMEM((rows, block), F32),
            pltpu.SemaphoreType.DMA((deep,)),
        ],
        compiler_params=pltpu.CompilerParams(vmem_limit_bytes=12 << 20),
        cost_estimate=pl.CostEstimate(
            flops=2 * rows * width * block * count,
            bytes_accessed=2 * width * block * (2 if arrived else count),
            transcendentals=0,
        ),
        name="base_terms",
    )(tensor_at, tagged, *in_hbm(out_weight), *arrived, *early)


def slots_of(tags, batch_at, pool, tile, per):
    lane = lane_of(tags.shape)
    ids = tags.astype(F32).astype(jnp.int32)
    mine = tile * per + lane // (LANES // per)
    held = tile * per // pool
    return ids - (batch_at[0] ^ held) * pool + held * pool, mine


def shrink_kernel(batch_at, *refs):
    blocks, factors, out = refs[:-3], refs[-3:-1], refs[-1]
    pool, rank_width, width = factors[0].shape
    everyone = jnp.concatenate([block[...] for block in blocks], axis=0)
    per = LANES // rank_width
    lane = lane_of((everyone.shape[0], LANES))
    kept = jnp.zeros(lane.shape, F32)
    for held, weights in enumerate(factors):
        terms = lax.dot_general(
            everyone[:, :width],
            weights[...].reshape(pool * rank_width, width),
            (((1,), (1,)), ((), ())),
            preferred_element_type=F32,
        )
        for tile in range(pool // per):
            slot, mine = slots_of(everyone[:, width:], batch_at, pool, held * pool // per + tile, per)
            kept = kept + jnp.where(
                slot == mine, terms[:, tile * LANES : (tile + 1) * LANES], F32(0.0)
            )
    both = kept + pltpu.roll(kept, rank_width, 1)
    half = both.shape[0] // 2
    packed = jnp.where(lane[:half] < rank_width, both[:half], both[half:])
    out[...] = packed.astype(out.dtype)


def shrink_part(blocks, factors, batch_at):
    pool, rank_width, width = factors[0].shape
    rows = len(blocks) * blocks[0].shape[0]
    smem = pl.BlockSpec(memory_space=pltpu.SMEM)
    whole = pl.BlockSpec(memory_space=VMEM)
    return pl.pallas_call(
        shrink_kernel,
        out_shape=jax.ShapeDtypeStruct((rows // 2, LANES), BF16),
        in_specs=[smem] + [whole] * (len(blocks) + 2),
        out_specs=whole,
        compiler_params=pltpu.CompilerParams(vmem_limit_bytes=8 << 20),
        cost_estimate=pl.CostEstimate(
            flops=4 * rows * width * pool * rank_width,
            bytes_accessed=2 * width * (rows + 2 * pool * rank_width),
            transcendentals=0,
        ),
        name="shrink",
    )(batch_at, *blocks, *factors)


def expand_kernel(count, sums, rank_width, batch_at, *refs):
    limits, refs = refs[:2], refs[2:]
    tags, parts = refs[:count], refs[count : count + sums]
    factors, outs = refs[count + sums : count + sums + 2], refs[count + sums + 2 :]
    tags = jnp.concatenate([tag[...] for tag in tags], axis=0)
    total = parts[0][...].astype(F32)
    for part in parts[1:]:
        total = total + part[...].astype(F32)
    total = total.astype(BF16).astype(F32)
    other = pltpu.roll(total, rank_width, 1)
    low = lane_of(total.shape) < rank_width
    shrink = jnp.concatenate(
        [jnp.where(low, total, other), jnp.where(low, other, total)], axis=0
    )
    per = LANES // rank_width
    inputs, block = factors[0].shape
    pool = inputs // rank_width
    tiles = []
    for tile in range(2 * pool // per):
        slot, mine = slots_of(tags, batch_at, pool, tile, per)
        held, at = divmod(tile * per, pool)
        limit = limits[held][at // per : at // per + 1]
        keep = (slot == mine) & (lane_of(tags.shape) % rank_width < limit)
        tiles.append(jnp.where(keep, shrink, F32(0.0)).astype(BF16))
    half = len(tiles) // 2
    spreads = [jnp.concatenate(tiles[:half], axis=1), jnp.concatenate(tiles[half:], axis=1)]
    rows = tags.shape[0] // count
    piece = min(block, 512)
    for at in range(0, block, piece):
        delta = sum(
            jnp.dot(spread, each[:, at : at + piece], preferred_element_type=F32)
            for spread, each in zip(spreads, factors)
        )
        for which, out in enumerate(outs):
            put_stacked(out, at, delta[which * rows : (which + 1) * rows])


def expand(blocks, parts, factors, limits, batch_at):
    pool, rank_width, block = factors[0].shape
    rows, tagged_width = blocks[0].shape
    count = len(blocks)
    stack = rows * block // LANES
    tag = pl.BlockSpec((rows, LANES), lambda i: (0, tagged_width // LANES - 1))
    full = pl.BlockSpec((pool * rank_width, block), lambda i: (0, 0))
    part = pl.BlockSpec(parts[0].shape, lambda i: (0, 0))
    return pl.pallas_call(
        functools.partial(expand_kernel, count, len(parts), rank_width),
        grid=(1,),
        out_shape=[jax.ShapeDtypeStruct((stack, LANES), BF16) for _ in blocks],
        in_specs=[pl.BlockSpec(memory_space=pltpu.SMEM)]
        + [pl.BlockSpec(each.shape, lambda i: (0, 0)) for each in limits]
        + [tag] * count
        + [part] * len(parts)
        + [full] * 2,
        out_specs=[pl.BlockSpec((stack, LANES), lambda i: (0, 0)) for _ in blocks],
        compiler_params=pltpu.CompilerParams(vmem_limit_bytes=16 << 20),
        cost_estimate=pl.CostEstimate(
            flops=4 * rows * count * pool * rank_width * block,
            bytes_accessed=2 * pool * rank_width * block,
            transcendentals=0,
        ),
        name="expand",
    )(batch_at, *limits, *blocks, *parts, *[each.reshape(pool * rank_width, block) for each in factors])


def total_kernel(*refs):
    terms, out = refs[:-1], refs[-1]
    rows = out.shape[0]
    for column in range(0, out.shape[1], LANES):
        at = slice(column // LANES * rows, (column // LANES + 1) * rows)
        total = terms[0][at].astype(F32)
        for term in terms[1:]:
            total = total + term[at].astype(F32)
        out[:, column : column + LANES] = total.astype(out.dtype)


def total(rows, block, terms):
    whole = pl.BlockSpec(memory_space=VMEM)
    return pl.pallas_call(
        total_kernel,
        out_shape=jax.ShapeDtypeStruct((rows, block), BF16),
        in_specs=[whole] * len(terms),
        out_specs=whole,
        compiler_params=pltpu.CompilerParams(vmem_limit_bytes=8 << 20),
        cost_estimate=pl.CostEstimate(
            flops=rows * block * len(terms),
            bytes_accessed=2 * rows * block * (1 + len(terms)),
            transcendentals=0,
        ),
        name="total",
    )(*terms)


def partial_kernel(*refs):
    terms, out = refs[:-1], refs[-1]
    total = terms[0][...].astype(F32)
    for term in terms[1:]:
        total = total + term[...].astype(F32)
    out[...] = total


def partial_total(terms, weight):
    whole = pl.BlockSpec(memory_space=VMEM)
    return pl.pallas_call(
        partial_kernel,
        out_shape=jax.ShapeDtypeStruct(terms[0].shape, F32),
        in_specs=[whole] * len(terms),
        out_specs=whole,
        compiler_params=pltpu.CompilerParams(vmem_limit_bytes=8 << 20),
        cost_estimate=pl.CostEstimate(
            flops=terms[0].size * len(terms),
            bytes_accessed=4 * terms[0].size + weight,
            transcendentals=0,
        ),
        name="partial_total",
    )(*terms)


def local(
    tensor_size,
    batch_size,
    queries,
    key_cache,
    value_cache,
    new_key,
    new_value,
    lengths,
    out_weight,
    shrink_weight,
    expand_weight,
    adapter_rank,
    adapter_list,
    row_adapter,
):
    rows = queries.shape[0]
    block = expand_weight.shape[2]
    chips = batch_size // 2
    batch_at = lax.axis_index("batch").reshape(1).astype(jnp.int32)
    tensor_at = lax.axis_index("tensor").reshape(1).astype(jnp.int32)

    def to_sibling(array):
        return permuted(array, "batch", batch_size, lambda i: i ^ 1)

    def to_chip(array, shift):
        return permuted(array, "batch", batch_size, lambda i: (i + 2 * shift) % batch_size)

    def across(array, bit):
        return permuted(array, "tensor", tensor_size, lambda i: i ^ bit)

    def wide(array):
        return array.astype(F32)

    stack = block // LANES * rows
    tagged, early, limits = attend(
        tensor_at ^ 3,
        block,
        out_weight,
        queries,
        key_cache,
        value_cache,
        new_key,
        new_value,
        lengths,
        adapter_list,
        row_adapter,
        adapter_rank,
        shrink_weight.shape[2],
    )
    limits = [limits, to_sibling(limits)]
    shrink_weight = jnp.swapaxes(shrink_weight, 1, 2)
    shrink_factors = [shrink_weight, to_sibling(shrink_weight)]
    expand_factors = [expand_weight, to_sibling(expand_weight)]
    visiting = [to_chip(tagged, shift) for shift in range(1, chips)]
    third, next_door = base_block(tensor_at, tagged, out_weight, block, 1, [early])
    visiting, third, next_door, limits = lax.optimization_barrier(
        (visiting, third, next_door, limits)
    )
    blocks = [tagged] + visiting
    third = across(third, 1)

    part = shrink_part(blocks, shrink_factors, batch_at)
    parts = [part, across(part, 1)]
    part, later_tagged = lax.optimization_barrier((part, tagged))
    (second,) = base_block(tensor_at, later_tagged, out_weight, block, 2)
    second = (wide(second) + wide(third)).astype(BF16)
    parts, second = lax.optimization_barrier((parts, second))
    bit = 2
    while bit < tensor_size:
        part = (wide(parts[0]) + wide(parts[1])).astype(BF16)
        part, next_door = lax.optimization_barrier((part, next_door))
        parts = [part, across(part, bit)]
        bit *= 2
    arrived = [across(second, 2), across(next_door, 1)]
    for ahead in range(4, tensor_size, 2):
        (near,) = base_block(tensor_at, tagged, out_weight, block, ahead)
        (far,) = base_block(tensor_at, tagged, out_weight, block, ahead + 1)
        arrived.append(across((wide(near) + wide(across(far, 1))).astype(BF16), ahead))

    deltas = expand(blocks, parts, expand_factors, limits, batch_at)
    deltas, late_tagged = lax.optimization_barrier((deltas, tagged))
    (own,) = base_block(tensor_at, late_tagged, out_weight, block, 0)
    so_far = partial_total([own, deltas[0], arrived[0], *arrived[2:]], 0)
    terms = [partial_total([so_far, arrived[1]], 8 << 20)]
    terms += [to_chip(home, -shift) for shift, home in enumerate(deltas[1:], 1)]
    return total(rows, block, terms)


def solution(mesh):
    placed = (
        P(("groups", "batch"), "tensor", None),
        P(("groups", "batch"), None, None, None),
        P(("groups", "batch"), None, None, None),
        P(("groups", "batch"), None, None),
        P(("groups", "batch"), None, None),
        P(("groups", "batch")),
        P("tensor", None),
        P("batch", "tensor", None),
        P("batch", None, "tensor"),
        P("batch"),
        P(("groups", "batch")),
        P(("groups", "batch")),
    )

    def placed_local(*arrays):
        return local(mesh.shape["tensor"], mesh.shape["batch"], *arrays)

    return jax.shard_map(
        placed_local,
        mesh=mesh,
        in_specs=placed,
        out_specs=P(("groups", "batch"), "tensor"),
        check_vma=False,
    )
```

```python
import functools

import jax
import jax.numpy as jnp
from jax import lax
from jax.experimental import pallas as pl
from jax.experimental.pallas import tpu as pltpu
from jax.sharding import PartitionSpec as P

HQ = 32
KVH = 4
LANES = 128
VMEM = pltpu.VMEM
GRANT = 56 << 20
F32, BF16 = jnp.float32, jnp.bfloat16


def permuted(array, axis, size, partner):
    return lax.ppermute(array, axis, [(i, partner(i)) for i in range(size)])


def in_hbm(*arrays):
    return [pltpu.with_memory_space_constraint(array, pltpu.HBM) for array in arrays]


def lane_of(shape):
    return lax.broadcasted_iota(jnp.int32, shape, len(shape) - 1)


def attend_kernel(parts, rank_width, group_at, early_at, *refs):
    given, (out_weight, tagged, early, limits, *scratch) = refs[:9], refs[9:]
    held, (spread_out, small_sems, key_sems, value_sems, early_sem) = scratch[:9], scratch[9:]
    key_cache, value_cache = given[:2]
    keys, values, queries, new_key, new_value, lengths, row_adapter, adapter_list, ranks = held
    rows, heads, width = queries.shape
    positions = key_cache.shape[2]
    group = group_at[0]
    some = rows // parts

    def cache_copies(part):
        at = pl.ds(part * some, some)
        return (
            pltpu.make_async_copy(key_cache.at[at, group], keys.at[at], key_sems.at[part]),
            pltpu.make_async_copy(value_cache.at[at, group], values.at[at], value_sems.at[part]),
        )

    small = [
        pltpu.make_async_copy(given[i], held[i], small_sems.at[i - 2]) for i in range(2, 9)
    ]
    for part in range(parts):
        for copy in cache_copies(part):
            copy.start()
    for copy in small:
        copy.start()
    block = early.shape[1]
    start = pl.multiple_of(early_at[0] * block, block)
    early_copy = pltpu.make_async_copy(out_weight.at[:, pl.ds(start, block)], early, early_sem)
    early_copy.start()
    for copy in small:
        copy.wait()
    at_row = lax.broadcasted_iota(jnp.int32, (rows, LANES), 0)
    tag = jnp.zeros((rows, LANES), jnp.int32)
    for row in range(rows):
        tag = jnp.where(at_row == row, adapter_list[row_adapter[row]], tag)
    tag = tag.astype(F32).astype(BF16)
    slot = lax.broadcasted_iota(jnp.int32, limits.shape, 0) * (LANES // rank_width)
    slot = slot + lane_of(limits.shape) // rank_width
    limit = jnp.zeros(limits.shape, jnp.int32)
    for held_at in range(ranks.shape[0]):
        limit = jnp.where(slot == held_at, ranks[held_at], limit)
    limits[...] = limit

    group_row = lax.broadcasted_iota(jnp.int32, new_key.shape, 1) == group
    fresh_key = jnp.sum(
        jnp.where(group_row, new_key[...].astype(F32), F32(0.0)), axis=1, keepdims=True
    )
    fresh_value = jnp.sum(
        jnp.where(group_row, new_value[...].astype(F32), F32(0.0)), axis=1, keepdims=True
    )
    score_scale = width ** (-0.5)
    fresh = jnp.sum(queries[...].astype(F32) * fresh_key, axis=-1, keepdims=True) * score_scale
    for part in range(parts):
        at = slice(part * some, (part + 1) * some)
        key_copy, value_copy = cache_copies(part)
        key_copy.wait()
        scores = (
            lax.dot_general(
                queries[at], keys[at], (((2,), (2,)), ((0,), (0,))), preferred_element_type=F32
            )
            * score_scale
        )
        length = jnp.stack(
            [
                jnp.full((heads, positions), lengths[row], jnp.int32)
                for row in range(part * some, (part + 1) * some)
            ]
        )
        valid = lane_of(scores.shape) < length
        masked = jnp.where(valid, scores, F32(-1e30))
        highest = jnp.maximum(jnp.max(masked, axis=-1, keepdims=True), fresh[at])
        cached_exp = jnp.where(valid, jnp.exp(masked - highest), F32(0.0))
        fresh_exp = jnp.exp(fresh[at] - highest)
        totals = jnp.sum(cached_exp, axis=-1, keepdims=True) + fresh_exp
        cached_w = (cached_exp / totals).astype(BF16)
        fresh_w = (fresh_exp / totals).astype(BF16).astype(F32)
        value_copy.wait()
        attended = lax.dot_general(
            cached_w, values[at], (((2,), (1,)), ((0,), (0,))), preferred_element_type=F32
        )
        attended = attended + fresh_w * fresh_value[at]
        spread_out[pl.ds(part * some * heads, some * heads)] = attended.reshape(
            some * heads, width
        )
    tagged[:, heads * width :] = tag
    for head in range(heads):
        tagged[:, head * width : (head + 1) * width] = spread_out[
            pl.ds(head, rows, stride=heads)
        ].astype(BF16)
    early_copy.wait()


def attend(
    early_at,
    block,
    out_weight,
    queries,
    key_cache,
    value_cache,
    new_key,
    new_value,
    lengths,
    adapter_list,
    row_adapter,
    adapter_rank,
    rank_width,
):
    rows, heads, width = queries.shape
    positions = key_cache.shape[2]
    per_group = HQ // KVH
    group_at = (lax.axis_index("tensor") * heads // per_group).reshape(1).astype(jnp.int32)
    full = -(-heads // 8) * 8
    if full != heads:
        queries = jnp.pad(queries, ((0, 0), (0, full - heads), (0, 0)))
    parts = 1
    smem = pl.BlockSpec(memory_space=pltpu.SMEM)
    away = pl.BlockSpec(memory_space=pl.ANY)
    tagged, early, limits = pl.pallas_call(
        functools.partial(attend_kernel, parts, rank_width),
        out_shape=[
            jax.ShapeDtypeStruct((rows, full * width + LANES), BF16),
            VMEM((out_weight.shape[0], block), BF16),
            jax.ShapeDtypeStruct((8, LANES), jnp.int32),
        ],
        in_specs=[smem, smem] + [away] * 10,
        out_specs=[pl.BlockSpec(memory_space=VMEM)] * 3,
        scratch_shapes=[
            VMEM((rows, positions, width), BF16),
            VMEM((rows, positions, width), BF16),
            VMEM(queries.shape, BF16),
            VMEM(new_key.shape, BF16),
            VMEM(new_value.shape, BF16),
            pltpu.SMEM(lengths.shape, jnp.int32),
            pltpu.SMEM(row_adapter.shape, jnp.int32),
            pltpu.SMEM(adapter_list.shape, jnp.int32),
            pltpu.SMEM(adapter_rank.shape, jnp.int32),
            VMEM((rows * full, width), F32),
            pltpu.SemaphoreType.DMA((7,)),
            pltpu.SemaphoreType.DMA((parts,)),
            pltpu.SemaphoreType.DMA((parts,)),
            pltpu.SemaphoreType.DMA,
        ],
        compiler_params=pltpu.CompilerParams(vmem_limit_bytes=8 << 20),
        cost_estimate=pl.CostEstimate(
            flops=4 * rows * heads * positions * width,
            bytes_accessed=4 * rows * positions * width,
            transcendentals=rows * heads * positions,
        ),
        name="attention",
    )(
        group_at,
        early_at,
        *in_hbm(
            key_cache,
            value_cache,
            queries,
            new_key,
            new_value,
            lengths,
            row_adapter,
            adapter_list,
            adapter_rank,
            out_weight,
        ),
    )
    if full != heads:
        tagged = jnp.concatenate([tagged[:, : heads * width], tagged[:, full * width :]], axis=1)
    return tagged, early, limits


def put_stacked(out, start, term, first=0, others=()):
    rows = term.shape[0]
    for column in range(0, term.shape[1], LANES):
        at = first + (start + column) // LANES * rows
        part = term[:, column : column + LANES]
        for other in others:
            part = part + other[at : at + rows].astype(F32)
        out[at : at + rows] = part.astype(out.dtype)


def base_kernel(ahead, deep, arriving, tensor_at, tagged, out_weight, *refs):
    arrived, (*near, out, held, sums, sems) = refs[:arriving], refs[arriving:]
    _, deep_rows, block = held.shape
    width = out_weight.shape[0]
    count = width // deep_rows
    column = pl.ds(pl.multiple_of((tensor_at[0] ^ ahead) * block, block), block)

    def copy(at):
        return pltpu.make_async_copy(
            out_weight.at[pl.ds(at * deep_rows, deep_rows), column],
            held.at[at % deep],
            sems.at[at % deep],
        )

    for at in range(min(deep, count)):
        copy(at).start()
    piece = min(block, 512)
    if near:
        early, early_out = near
        for start in range(0, block, piece):
            columns = slice(start, start + piece)
            term = jnp.dot(tagged[:, :width], early[:, columns], preferred_element_type=F32)
            put_stacked(early_out, start, term)
    for at in range(count):
        copy(at).wait()
        inputs = slice(at * deep_rows, (at + 1) * deep_rows)
        for start in range(0, block, piece):
            columns = slice(start, start + piece)
            term = jnp.dot(
                tagged[:, inputs], held[at % deep, :, columns], preferred_element_type=F32
            )
            if at:
                term = term + sums[:, columns]
            if at < count - 1:
                sums[:, columns] = term
            else:
                put_stacked(out, start, term, 0, arrived)
        if at + deep < count:
            copy(at + deep).start()


def base_block(tensor_at, tagged, out_weight, block, ahead, early=(), arrived=()):
    rows = tagged.shape[0]
    width = out_weight.shape[0]
    deep, deep_rows = 4, min(width, 256)
    whole = pl.BlockSpec(memory_space=VMEM)
    count = 1 + len(early)
    return pl.pallas_call(
        functools.partial(base_kernel, ahead, deep, len(arrived)),
        out_shape=[jax.ShapeDtypeStruct((block // LANES * rows, LANES), BF16 if ahead else F32)]
        * count,
        in_specs=[pl.BlockSpec(memory_space=pltpu.SMEM), whole, pl.BlockSpec(memory_space=pl.ANY)]
        + [whole] * (len(arrived) + len(early)),
        out_specs=[whole] * count,
        scratch_shapes=[
            VMEM((deep, deep_rows, block), BF16),
            VMEM((rows, block), F32),
            pltpu.SemaphoreType.DMA((deep,)),
        ],
        compiler_params=pltpu.CompilerParams(vmem_limit_bytes=12 << 20),
        cost_estimate=pl.CostEstimate(
            flops=2 * rows * width * block * count,
            bytes_accessed=2 * width * block * (2 if arrived else count),
            transcendentals=0,
        ),
        name="base_terms",
    )(tensor_at, tagged, *in_hbm(out_weight), *arrived, *early)


def slots_of(tags, batch_at, pool, tile, per):
    lane = lane_of(tags.shape)
    ids = tags.astype(F32).astype(jnp.int32)
    mine = tile * per + lane // (LANES // per)
    held = tile * per // pool
    return ids - (batch_at[0] ^ held) * pool + held * pool, mine


def shrink_kernel(batch_at, *refs):
    blocks, factors, out = refs[:-3], refs[-3:-1], refs[-1]
    pool, rank_width, width = factors[0].shape
    everyone = jnp.concatenate([block[...] for block in blocks], axis=0)
    per = LANES // rank_width
    lane = lane_of((everyone.shape[0], LANES))
    kept = jnp.zeros(lane.shape, F32)
    for held, weights in enumerate(factors):
        terms = lax.dot_general(
            everyone[:, :width],
            weights[...].reshape(pool * rank_width, width),
            (((1,), (1,)), ((), ())),
            preferred_element_type=F32,
        )
        for tile in range(pool // per):
            slot, mine = slots_of(everyone[:, width:], batch_at, pool, held * pool // per + tile, per)
            kept = kept + jnp.where(
                slot == mine, terms[:, tile * LANES : (tile + 1) * LANES], F32(0.0)
            )
    both = kept + pltpu.roll(kept, rank_width, 1)
    half = both.shape[0] // 2
    packed = jnp.where(lane[:half] < rank_width, both[:half], both[half:])
    out[...] = packed.astype(out.dtype)


def shrink_part(blocks, factors, batch_at):
    pool, rank_width, width = factors[0].shape
    rows = len(blocks) * blocks[0].shape[0]
    smem = pl.BlockSpec(memory_space=pltpu.SMEM)
    whole = pl.BlockSpec(memory_space=VMEM)
    return pl.pallas_call(
        shrink_kernel,
        out_shape=jax.ShapeDtypeStruct((rows // 2, LANES), BF16),
        in_specs=[smem] + [whole] * (len(blocks) + 2),
        out_specs=whole,
        compiler_params=pltpu.CompilerParams(vmem_limit_bytes=8 << 20),
        cost_estimate=pl.CostEstimate(
            flops=4 * rows * width * pool * rank_width,
            bytes_accessed=2 * width * (rows + 2 * pool * rank_width),
            transcendentals=0,
        ),
        name="shrink",
    )(batch_at, *blocks, *factors)


def expand_kernel(count, sums, rank_width, batch_at, *refs):
    limits, refs = refs[:2], refs[2:]
    tags, parts = refs[:count], refs[count : count + sums]
    factors, outs = refs[count + sums : count + sums + 2], refs[count + sums + 2 :]
    tags = jnp.concatenate([tag[...] for tag in tags], axis=0)
    total = parts[0][...].astype(F32)
    for part in parts[1:]:
        total = total + part[...].astype(F32)
    total = total.astype(BF16).astype(F32)
    other = pltpu.roll(total, rank_width, 1)
    low = lane_of(total.shape) < rank_width
    shrink = jnp.concatenate(
        [jnp.where(low, total, other), jnp.where(low, other, total)], axis=0
    )
    per = LANES // rank_width
    inputs, block = factors[0].shape
    pool = inputs // rank_width
    tiles = []
    for tile in range(2 * pool // per):
        slot, mine = slots_of(tags, batch_at, pool, tile, per)
        held, at = divmod(tile * per, pool)
        limit = limits[held][at // per : at // per + 1]
        keep = (slot == mine) & (lane_of(tags.shape) % rank_width < limit)
        tiles.append(jnp.where(keep, shrink, F32(0.0)).astype(BF16))
    half = len(tiles) // 2
    spreads = [jnp.concatenate(tiles[:half], axis=1), jnp.concatenate(tiles[half:], axis=1)]
    rows = tags.shape[0] // count
    piece = min(block, 512)
    for at in range(0, block, piece):
        delta = sum(
            jnp.dot(spread, each[:, at : at + piece], preferred_element_type=F32)
            for spread, each in zip(spreads, factors)
        )
        for which, out in enumerate(outs):
            put_stacked(out, at, delta[which * rows : (which + 1) * rows])


def expand(blocks, parts, factors, limits, batch_at):
    pool, rank_width, block = factors[0].shape
    rows, tagged_width = blocks[0].shape
    count = len(blocks)
    stack = rows * block // LANES
    tag = pl.BlockSpec((rows, LANES), lambda i: (0, tagged_width // LANES - 1))
    full = pl.BlockSpec((pool * rank_width, block), lambda i: (0, 0))
    part = pl.BlockSpec(parts[0].shape, lambda i: (0, 0))
    return pl.pallas_call(
        functools.partial(expand_kernel, count, len(parts), rank_width),
        grid=(1,),
        out_shape=[jax.ShapeDtypeStruct((stack, LANES), BF16) for _ in blocks],
        in_specs=[pl.BlockSpec(memory_space=pltpu.SMEM)]
        + [pl.BlockSpec(each.shape, lambda i: (0, 0)) for each in limits]
        + [tag] * count
        + [part] * len(parts)
        + [full] * 2,
        out_specs=[pl.BlockSpec((stack, LANES), lambda i: (0, 0)) for _ in blocks],
        compiler_params=pltpu.CompilerParams(vmem_limit_bytes=16 << 20),
        cost_estimate=pl.CostEstimate(
            flops=4 * rows * count * pool * rank_width * block,
            bytes_accessed=2 * pool * rank_width * block,
            transcendentals=0,
        ),
        name="expand",
    )(batch_at, *limits, *blocks, *parts, *[each.reshape(pool * rank_width, block) for each in factors])


def total_kernel(*refs):
    terms, out = refs[:-1], refs[-1]
    rows = out.shape[0]
    for column in range(0, out.shape[1], LANES):
        at = slice(column // LANES * rows, (column // LANES + 1) * rows)
        total = terms[0][at].astype(F32)
        for term in terms[1:]:
            total = total + term[at].astype(F32)
        out[:, column : column + LANES] = total.astype(out.dtype)


def total(rows, block, terms):
    whole = pl.BlockSpec(memory_space=VMEM)
    return pl.pallas_call(
        total_kernel,
        out_shape=jax.ShapeDtypeStruct((rows, block), BF16),
        in_specs=[whole] * len(terms),
        out_specs=whole,
        compiler_params=pltpu.CompilerParams(vmem_limit_bytes=8 << 20),
        cost_estimate=pl.CostEstimate(
            flops=rows * block * len(terms),
            bytes_accessed=2 * rows * block * (1 + len(terms)),
            transcendentals=0,
        ),
        name="total",
    )(*terms)


def partial_kernel(*refs):
    terms, out = refs[:-1], refs[-1]
    total = terms[0][...].astype(F32)
    for term in terms[1:]:
        total = total + term[...].astype(F32)
    out[...] = total


def partial_total(terms, weight):
    whole = pl.BlockSpec(memory_space=VMEM)
    return pl.pallas_call(
        partial_kernel,
        out_shape=jax.ShapeDtypeStruct(terms[0].shape, F32),
        in_specs=[whole] * len(terms),
        out_specs=whole,
        compiler_params=pltpu.CompilerParams(vmem_limit_bytes=8 << 20),
        cost_estimate=pl.CostEstimate(
            flops=terms[0].size * len(terms),
            bytes_accessed=4 * terms[0].size + weight,
            transcendentals=0,
        ),
        name="partial_total",
    )(*terms)


def local(
    tensor_size,
    batch_size,
    queries,
    key_cache,
    value_cache,
    new_key,
    new_value,
    lengths,
    out_weight,
    shrink_weight,
    expand_weight,
    adapter_rank,
    adapter_list,
    row_adapter,
):
    rows = queries.shape[0]
    block = expand_weight.shape[2]
    chips = batch_size // 2
    batch_at = lax.axis_index("batch").reshape(1).astype(jnp.int32)
    tensor_at = lax.axis_index("tensor").reshape(1).astype(jnp.int32)

    def to_sibling(array):
        return permuted(array, "batch", batch_size, lambda i: i ^ 1)

    def to_chip(array, shift):
        return permuted(array, "batch", batch_size, lambda i: (i + 2 * shift) % batch_size)

    def across(array, bit):
        return permuted(array, "tensor", tensor_size, lambda i: i ^ bit)

    def wide(array):
        return array.astype(F32)

    stack = block // LANES * rows
    tagged, early, limits = attend(
        tensor_at ^ 3,
        block,
        out_weight,
        queries,
        key_cache,
        value_cache,
        new_key,
        new_value,
        lengths,
        adapter_list,
        row_adapter,
        adapter_rank,
        shrink_weight.shape[2],
    )
    limits = [limits, to_sibling(limits)]
    shrink_weight = jnp.swapaxes(shrink_weight, 1, 2)
    shrink_factors = [shrink_weight, to_sibling(shrink_weight)]
    expand_factors = [expand_weight, to_sibling(expand_weight)]
    visiting = [to_chip(tagged, shift) for shift in range(1, chips)]
    third, next_door = base_block(tensor_at, tagged, out_weight, block, 1, [early])
    visiting, third, next_door, limits = lax.optimization_barrier(
        (visiting, third, next_door, limits)
    )
    blocks = [tagged] + visiting
    third = across(third, 1)

    part = shrink_part(blocks, shrink_factors, batch_at)
    parts = [part] + [across(part, ahead) for ahead in range(1, tensor_size)]
    part, later_tagged = lax.optimization_barrier((part, tagged))
    (second,) = base_block(tensor_at, later_tagged, out_weight, block, 2)
    second = (wide(second) + wide(third)).astype(BF16)
    parts[1], second, next_door = lax.optimization_barrier((parts[1], second, next_door))
    arrived = [across(second, 2), across(next_door, 1)]
    for ahead in range(4, tensor_size, 2):
        (near,) = base_block(tensor_at, tagged, out_weight, block, ahead)
        (far,) = base_block(tensor_at, tagged, out_weight, block, ahead + 1)
        arrived.append(across((wide(near) + wide(across(far, 1))).astype(BF16), ahead))

    deltas = expand(blocks, parts, expand_factors, limits, batch_at)
    deltas, late_tagged = lax.optimization_barrier((deltas, tagged))
    (own,) = base_block(tensor_at, late_tagged, out_weight, block, 0)
    so_far = partial_total([own, deltas[0], arrived[0], *arrived[2:]], 0)
    terms = [partial_total([so_far, arrived[1]], 8 << 20)]
    terms += [to_chip(home, -shift) for shift, home in enumerate(deltas[1:], 1)]
    return total(rows, block, terms)


def solution(mesh):
    placed = (
        P(("groups", "batch"), "tensor", None),
        P(("groups", "batch"), None, None, None),
        P(("groups", "batch"), None, None, None),
        P(("groups", "batch"), None, None),
        P(("groups", "batch"), None, None),
        P(("groups", "batch")),
        P("tensor", None),
        P("batch", "tensor", None),
        P("batch", None, "tensor"),
        P("batch"),
        P(("groups", "batch")),
        P(("groups", "batch")),
    )

    def placed_local(*arrays):
        return local(mesh.shape["tensor"], mesh.shape["batch"], *arrays)

    return jax.shard_map(
        placed_local,
        mesh=mesh,
        in_specs=placed,
        out_specs=P(("groups", "batch"), "tensor"),
        check_vma=False,
    )
```

```python
import functools

import jax
import jax.numpy as jnp
from jax import lax
from jax.experimental import pallas as pl
from jax.experimental.pallas import tpu as pltpu
from jax.sharding import PartitionSpec as P

HQ = 32
KVH = 4
LANES = 128
VMEM = pltpu.VMEM
GRANT = 56 << 20
F32, BF16 = jnp.float32, jnp.bfloat16


def permuted(array, axis, size, partner):
    return lax.ppermute(array, axis, [(i, partner(i)) for i in range(size)])


def in_hbm(*arrays):
    return [pltpu.with_memory_space_constraint(array, pltpu.HBM) for array in arrays]


def lane_of(shape):
    return lax.broadcasted_iota(jnp.int32, shape, len(shape) - 1)


def attend_kernel(parts, rank_width, group_at, early_at, *refs):
    given, (out_weight, tagged, early, limits, *scratch) = refs[:9], refs[9:]
    held, (spread_out, small_sems, key_sems, value_sems, early_sem) = scratch[:9], scratch[9:]
    key_cache, value_cache = given[:2]
    keys, values, queries, new_key, new_value, lengths, row_adapter, adapter_list, ranks = held
    rows, heads, width = queries.shape
    positions = key_cache.shape[2]
    group = group_at[0]
    some = rows // parts

    def cache_copies(part):
        at = pl.ds(part * some, some)
        return (
            pltpu.make_async_copy(key_cache.at[at, group], keys.at[at], key_sems.at[part]),
            pltpu.make_async_copy(value_cache.at[at, group], values.at[at], value_sems.at[part]),
        )

    small = [
        pltpu.make_async_copy(given[i], held[i], small_sems.at[i - 2]) for i in range(2, 9)
    ]
    for part in range(parts):
        for copy in cache_copies(part):
            copy.start()
    for copy in small:
        copy.start()
    block = early.shape[1]
    start = pl.multiple_of(early_at[0] * block, block)
    early_copy = pltpu.make_async_copy(out_weight.at[:, pl.ds(start, block)], early, early_sem)
    early_copy.start()
    for copy in small:
        copy.wait()
    at_row = lax.broadcasted_iota(jnp.int32, (rows, LANES), 0)
    tag = jnp.zeros((rows, LANES), jnp.int32)
    for row in range(rows):
        tag = jnp.where(at_row == row, adapter_list[row_adapter[row]], tag)
    tag = tag.astype(F32).astype(BF16)
    slot = lax.broadcasted_iota(jnp.int32, limits.shape, 0) * (LANES // rank_width)
    slot = slot + lane_of(limits.shape) // rank_width
    limit = jnp.zeros(limits.shape, jnp.int32)
    for held_at in range(ranks.shape[0]):
        limit = jnp.where(slot == held_at, ranks[held_at], limit)
    limits[...] = limit

    group_row = lax.broadcasted_iota(jnp.int32, new_key.shape, 1) == group
    fresh_key = jnp.sum(
        jnp.where(group_row, new_key[...].astype(F32), F32(0.0)), axis=1, keepdims=True
    )
    fresh_value = jnp.sum(
        jnp.where(group_row, new_value[...].astype(F32), F32(0.0)), axis=1, keepdims=True
    )
    score_scale = width ** (-0.5)
    fresh = jnp.sum(queries[...].astype(F32) * fresh_key, axis=-1, keepdims=True) * score_scale
    for part in range(parts):
        at = slice(part * some, (part + 1) * some)
        key_copy, value_copy = cache_copies(part)
        key_copy.wait()
        scores = (
            lax.dot_general(
                queries[at], keys[at], (((2,), (2,)), ((0,), (0,))), preferred_element_type=F32
            )
            * score_scale
        )
        length = jnp.stack(
            [
                jnp.full((heads, positions), lengths[row], jnp.int32)
                for row in range(part * some, (part + 1) * some)
            ]
        )
        valid = lane_of(scores.shape) < length
        masked = jnp.where(valid, scores, F32(-1e30))
        highest = jnp.maximum(jnp.max(masked, axis=-1, keepdims=True), fresh[at])
        cached_exp = jnp.where(valid, jnp.exp(masked - highest), F32(0.0))
        fresh_exp = jnp.exp(fresh[at] - highest)
        totals = jnp.sum(cached_exp, axis=-1, keepdims=True) + fresh_exp
        cached_w = (cached_exp / totals).astype(BF16)
        fresh_w = (fresh_exp / totals).astype(BF16).astype(F32)
        value_copy.wait()
        attended = lax.dot_general(
            cached_w, values[at], (((2,), (1,)), ((0,), (0,))), preferred_element_type=F32
        )
        attended = attended + fresh_w * fresh_value[at]
        spread_out[pl.ds(part * some * heads, some * heads)] = attended.reshape(
            some * heads, width
        )
    tagged[:, heads * width :] = tag
    for head in range(heads):
        tagged[:, head * width : (head + 1) * width] = spread_out[
            pl.ds(head, rows, stride=heads)
        ].astype(BF16)
    early_copy.wait()


def attend(
    early_at,
    block,
    out_weight,
    queries,
    key_cache,
    value_cache,
    new_key,
    new_value,
    lengths,
    adapter_list,
    row_adapter,
    adapter_rank,
    rank_width,
):
    rows, heads, width = queries.shape
    positions = key_cache.shape[2]
    per_group = HQ // KVH
    group_at = (lax.axis_index("tensor") * heads // per_group).reshape(1).astype(jnp.int32)
    full = -(-heads // 8) * 8
    if full != heads:
        queries = jnp.pad(queries, ((0, 0), (0, full - heads), (0, 0)))
    parts = 1
    smem = pl.BlockSpec(memory_space=pltpu.SMEM)
    away = pl.BlockSpec(memory_space=pl.ANY)
    tagged, early, limits = pl.pallas_call(
        functools.partial(attend_kernel, parts, rank_width),
        out_shape=[
            jax.ShapeDtypeStruct((rows, full * width + LANES), BF16),
            VMEM((out_weight.shape[0], block), BF16),
            jax.ShapeDtypeStruct((8, LANES), jnp.int32),
        ],
        in_specs=[smem, smem] + [away] * 10,
        out_specs=[pl.BlockSpec(memory_space=VMEM)] * 3,
        scratch_shapes=[
            VMEM((rows, positions, width), BF16),
            VMEM((rows, positions, width), BF16),
            VMEM(queries.shape, BF16),
            VMEM(new_key.shape, BF16),
            VMEM(new_value.shape, BF16),
            pltpu.SMEM(lengths.shape, jnp.int32),
            pltpu.SMEM(row_adapter.shape, jnp.int32),
            pltpu.SMEM(adapter_list.shape, jnp.int32),
            pltpu.SMEM(adapter_rank.shape, jnp.int32),
            VMEM((rows * full, width), F32),
            pltpu.SemaphoreType.DMA((7,)),
            pltpu.SemaphoreType.DMA((parts,)),
            pltpu.SemaphoreType.DMA((parts,)),
            pltpu.SemaphoreType.DMA,
        ],
        compiler_params=pltpu.CompilerParams(vmem_limit_bytes=8 << 20),
        cost_estimate=pl.CostEstimate(
            flops=4 * rows * heads * positions * width,
            bytes_accessed=4 * rows * positions * width,
            transcendentals=rows * heads * positions,
        ),
        name="attention",
    )(
        group_at,
        early_at,
        *in_hbm(
            key_cache,
            value_cache,
            queries,
            new_key,
            new_value,
            lengths,
            row_adapter,
            adapter_list,
            adapter_rank,
            out_weight,
        ),
    )
    if full != heads:
        tagged = jnp.concatenate([tagged[:, : heads * width], tagged[:, full * width :]], axis=1)
    return tagged, early, limits


def put_stacked(out, start, term, first=0, others=()):
    rows = term.shape[0]
    for column in range(0, term.shape[1], LANES):
        at = first + (start + column) // LANES * rows
        part = term[:, column : column + LANES]
        for other in others:
            part = part + other[at : at + rows].astype(F32)
        out[at : at + rows] = part.astype(out.dtype)


def base_kernel(ahead, deep, arriving, tensor_at, tagged, out_weight, *refs):
    arrived, (*near, out, held, sums, sems) = refs[:arriving], refs[arriving:]
    _, deep_rows, block = held.shape
    width = out_weight.shape[0]
    count = width // deep_rows
    column = pl.ds(pl.multiple_of((tensor_at[0] ^ ahead) * block, block), block)

    def copy(at):
        return pltpu.make_async_copy(
            out_weight.at[pl.ds(at * deep_rows, deep_rows), column],
            held.at[at % deep],
            sems.at[at % deep],
        )

    for at in range(min(deep, count)):
        copy(at).start()
    piece = min(block, 512)
    if near:
        early, early_out = near
        for start in range(0, block, piece):
            columns = slice(start, start + piece)
            term = jnp.dot(tagged[:, :width], early[:, columns], preferred_element_type=F32)
            put_stacked(early_out, start, term)
    for at in range(count):
        copy(at).wait()
        inputs = slice(at * deep_rows, (at + 1) * deep_rows)
        for start in range(0, block, piece):
            columns = slice(start, start + piece)
            term = jnp.dot(
                tagged[:, inputs], held[at % deep, :, columns], preferred_element_type=F32
            )
            if at:
                term = term + sums[:, columns]
            if at < count - 1:
                sums[:, columns] = term
            else:
                put_stacked(out, start, term, 0, arrived)
        if at + deep < count:
            copy(at + deep).start()


def base_block(tensor_at, tagged, out_weight, block, ahead, early=(), arrived=()):
    rows = tagged.shape[0]
    width = out_weight.shape[0]
    deep, deep_rows = 8, min(width, 128)
    whole = pl.BlockSpec(memory_space=VMEM)
    count = 1 + len(early)
    return pl.pallas_call(
        functools.partial(base_kernel, ahead, deep, len(arrived)),
        out_shape=[jax.ShapeDtypeStruct((block // LANES * rows, LANES), BF16 if ahead else F32)]
        * count,
        in_specs=[pl.BlockSpec(memory_space=pltpu.SMEM), whole, pl.BlockSpec(memory_space=pl.ANY)]
        + [whole] * (len(arrived) + len(early)),
        out_specs=[whole] * count,
        scratch_shapes=[
            VMEM((deep, deep_rows, block), BF16),
            VMEM((rows, block), F32),
            pltpu.SemaphoreType.DMA((deep,)),
        ],
        compiler_params=pltpu.CompilerParams(vmem_limit_bytes=12 << 20),
        cost_estimate=pl.CostEstimate(
            flops=2 * rows * width * block * count,
            bytes_accessed=2 * width * block * (2 if arrived else count),
            transcendentals=0,
        ),
        name="base_terms",
    )(tensor_at, tagged, *in_hbm(out_weight), *arrived, *early)


def slots_of(tags, batch_at, pool, tile, per):
    lane = lane_of(tags.shape)
    ids = tags.astype(F32).astype(jnp.int32)
    mine = tile * per + lane // (LANES // per)
    held = tile * per // pool
    return ids - (batch_at[0] ^ held) * pool + held * pool, mine


def shrink_kernel(batch_at, *refs):
    blocks, factors, out = refs[:-3], refs[-3:-1], refs[-1]
    pool, rank_width, width = factors[0].shape
    everyone = jnp.concatenate([block[...] for block in blocks], axis=0)
    per = LANES // rank_width
    lane = lane_of((everyone.shape[0], LANES))
    kept = jnp.zeros(lane.shape, F32)
    for held, weights in enumerate(factors):
        terms = lax.dot_general(
            everyone[:, :width],
            weights[...].reshape(pool * rank_width, width),
            (((1,), (1,)), ((), ())),
            preferred_element_type=F32,
        )
        for tile in range(pool // per):
            slot, mine = slots_of(everyone[:, width:], batch_at, pool, held * pool // per + tile, per)
            kept = kept + jnp.where(
                slot == mine, terms[:, tile * LANES : (tile + 1) * LANES], F32(0.0)
            )
    both = kept + pltpu.roll(kept, rank_width, 1)
    half = both.shape[0] // 2
    packed = jnp.where(lane[:half] < rank_width, both[:half], both[half:])
    out[...] = packed.astype(out.dtype)


def shrink_part(blocks, factors, batch_at):
    pool, rank_width, width = factors[0].shape
    rows = len(blocks) * blocks[0].shape[0]
    smem = pl.BlockSpec(memory_space=pltpu.SMEM)
    whole = pl.BlockSpec(memory_space=VMEM)
    return pl.pallas_call(
        shrink_kernel,
        out_shape=jax.ShapeDtypeStruct((rows // 2, LANES), BF16),
        in_specs=[smem] + [whole] * (len(blocks) + 2),
        out_specs=whole,
        compiler_params=pltpu.CompilerParams(vmem_limit_bytes=8 << 20),
        cost_estimate=pl.CostEstimate(
            flops=4 * rows * width * pool * rank_width,
            bytes_accessed=2 * width * (rows + 2 * pool * rank_width),
            transcendentals=0,
        ),
        name="shrink",
    )(batch_at, *blocks, *factors)


def expand_kernel(count, sums, rank_width, batch_at, *refs):
    limits, refs = refs[:2], refs[2:]
    tags, parts = refs[:count], refs[count : count + sums]
    factors, outs = refs[count + sums : count + sums + 2], refs[count + sums + 2 :]
    tags = jnp.concatenate([tag[...] for tag in tags], axis=0)
    total = parts[0][...].astype(F32)
    for part in parts[1:]:
        total = total + part[...].astype(F32)
    total = total.astype(BF16).astype(F32)
    other = pltpu.roll(total, rank_width, 1)
    low = lane_of(total.shape) < rank_width
    shrink = jnp.concatenate(
        [jnp.where(low, total, other), jnp.where(low, other, total)], axis=0
    )
    per = LANES // rank_width
    inputs, block = factors[0].shape
    pool = inputs // rank_width
    tiles = []
    for tile in range(2 * pool // per):
        slot, mine = slots_of(tags, batch_at, pool, tile, per)
        held, at = divmod(tile * per, pool)
        limit = limits[held][at // per : at // per + 1]
        keep = (slot == mine) & (lane_of(tags.shape) % rank_width < limit)
        tiles.append(jnp.where(keep, shrink, F32(0.0)).astype(BF16))
    half = len(tiles) // 2
    spreads = [jnp.concatenate(tiles[:half], axis=1), jnp.concatenate(tiles[half:], axis=1)]
    rows = tags.shape[0] // count
    piece = min(block, 512)
    for at in range(0, block, piece):
        delta = sum(
            jnp.dot(spread, each[:, at : at + piece], preferred_element_type=F32)
            for spread, each in zip(spreads, factors)
        )
        for which, out in enumerate(outs):
            put_stacked(out, at, delta[which * rows : (which + 1) * rows])


def expand(blocks, parts, factors, limits, batch_at):
    pool, rank_width, block = factors[0].shape
    rows, tagged_width = blocks[0].shape
    count = len(blocks)
    stack = rows * block // LANES
    tag = pl.BlockSpec((rows, LANES), lambda i: (0, tagged_width // LANES - 1))
    full = pl.BlockSpec((pool * rank_width, block), lambda i: (0, 0))
    part = pl.BlockSpec(parts[0].shape, lambda i: (0, 0))
    return pl.pallas_call(
        functools.partial(expand_kernel, count, len(parts), rank_width),
        grid=(1,),
        out_shape=[jax.ShapeDtypeStruct((stack, LANES), BF16) for _ in blocks],
        in_specs=[pl.BlockSpec(memory_space=pltpu.SMEM)]
        + [pl.BlockSpec(each.shape, lambda i: (0, 0)) for each in limits]
        + [tag] * count
        + [part] * len(parts)
        + [full] * 2,
        out_specs=[pl.BlockSpec((stack, LANES), lambda i: (0, 0)) for _ in blocks],
        compiler_params=pltpu.CompilerParams(vmem_limit_bytes=16 << 20),
        cost_estimate=pl.CostEstimate(
            flops=4 * rows * count * pool * rank_width * block,
            bytes_accessed=2 * pool * rank_width * block,
            transcendentals=0,
        ),
        name="expand",
    )(batch_at, *limits, *blocks, *parts, *[each.reshape(pool * rank_width, block) for each in factors])


def total_kernel(*refs):
    terms, out = refs[:-1], refs[-1]
    rows = out.shape[0]
    for column in range(0, out.shape[1], LANES):
        at = slice(column // LANES * rows, (column // LANES + 1) * rows)
        total = terms[0][at].astype(F32)
        for term in terms[1:]:
            total = total + term[at].astype(F32)
        out[:, column : column + LANES] = total.astype(out.dtype)


def total(rows, block, terms):
    whole = pl.BlockSpec(memory_space=VMEM)
    return pl.pallas_call(
        total_kernel,
        out_shape=jax.ShapeDtypeStruct((rows, block), BF16),
        in_specs=[whole] * len(terms),
        out_specs=whole,
        compiler_params=pltpu.CompilerParams(vmem_limit_bytes=8 << 20),
        cost_estimate=pl.CostEstimate(
            flops=rows * block * len(terms),
            bytes_accessed=2 * rows * block * (1 + len(terms)),
            transcendentals=0,
        ),
        name="total",
    )(*terms)


def partial_kernel(*refs):
    terms, out = refs[:-1], refs[-1]
    total = terms[0][...].astype(F32)
    for term in terms[1:]:
        total = total + term[...].astype(F32)
    out[...] = total


def partial_total(terms, weight):
    whole = pl.BlockSpec(memory_space=VMEM)
    return pl.pallas_call(
        partial_kernel,
        out_shape=jax.ShapeDtypeStruct(terms[0].shape, F32),
        in_specs=[whole] * len(terms),
        out_specs=whole,
        compiler_params=pltpu.CompilerParams(vmem_limit_bytes=8 << 20),
        cost_estimate=pl.CostEstimate(
            flops=terms[0].size * len(terms),
            bytes_accessed=4 * terms[0].size + weight,
            transcendentals=0,
        ),
        name="partial_total",
    )(*terms)


def local(
    tensor_size,
    batch_size,
    queries,
    key_cache,
    value_cache,
    new_key,
    new_value,
    lengths,
    out_weight,
    shrink_weight,
    expand_weight,
    adapter_rank,
    adapter_list,
    row_adapter,
):
    rows = queries.shape[0]
    block = expand_weight.shape[2]
    chips = batch_size // 2
    batch_at = lax.axis_index("batch").reshape(1).astype(jnp.int32)
    tensor_at = lax.axis_index("tensor").reshape(1).astype(jnp.int32)

    def to_sibling(array):
        return permuted(array, "batch", batch_size, lambda i: i ^ 1)

    def to_chip(array, shift):
        return permuted(array, "batch", batch_size, lambda i: (i + 2 * shift) % batch_size)

    def across(array, bit):
        return permuted(array, "tensor", tensor_size, lambda i: i ^ bit)

    def wide(array):
        return array.astype(F32)

    stack = block // LANES * rows
    tagged, early, limits = attend(
        tensor_at ^ 3,
        block,
        out_weight,
        queries,
        key_cache,
        value_cache,
        new_key,
        new_value,
        lengths,
        adapter_list,
        row_adapter,
        adapter_rank,
        shrink_weight.shape[2],
    )
    limits = [limits, to_sibling(limits)]
    shrink_weight = jnp.swapaxes(shrink_weight, 1, 2)
    shrink_factors = [shrink_weight, to_sibling(shrink_weight)]
    expand_factors = [expand_weight, to_sibling(expand_weight)]
    visiting = [to_chip(tagged, shift) for shift in range(1, chips)]
    third, next_door = base_block(tensor_at, tagged, out_weight, block, 1, [early])
    visiting, third, next_door, limits = lax.optimization_barrier(
        (visiting, third, next_door, limits)
    )
    blocks = [tagged] + visiting
    third = across(third, 1)

    part = shrink_part(blocks, shrink_factors, batch_at)
    parts = [part, across(part, 1)]
    part, later_tagged = lax.optimization_barrier((part, tagged))
    (second,) = base_block(tensor_at, later_tagged, out_weight, block, 2)
    second = (wide(second) + wide(third)).astype(BF16)
    parts, second = lax.optimization_barrier((parts, second))
    bit = 2
    while bit < tensor_size:
        part = (wide(parts[0]) + wide(parts[1])).astype(BF16)
        part, next_door = lax.optimization_barrier((part, next_door))
        parts = [part, across(part, bit)]
        bit *= 2
    arrived = [across(second, 2), across(next_door, 1)]
    for ahead in range(4, tensor_size, 2):
        (near,) = base_block(tensor_at, tagged, out_weight, block, ahead)
        (far,) = base_block(tensor_at, tagged, out_weight, block, ahead + 1)
        arrived.append(across((wide(near) + wide(across(far, 1))).astype(BF16), ahead))

    deltas = expand(blocks, parts, expand_factors, limits, batch_at)
    deltas, late_tagged = lax.optimization_barrier((deltas, tagged))
    (own,) = base_block(tensor_at, late_tagged, out_weight, block, 0)
    so_far = partial_total([own, deltas[0], arrived[0], *arrived[2:]], 0)
    terms = [partial_total([so_far, arrived[1]], 8 << 20)]
    terms += [to_chip(home, -shift) for shift, home in enumerate(deltas[1:], 1)]
    return total(rows, block, terms)


def solution(mesh):
    placed = (
        P(("groups", "batch"), "tensor", None),
        P(("groups", "batch"), None, None, None),
        P(("groups", "batch"), None, None, None),
        P(("groups", "batch"), None, None),
        P(("groups", "batch"), None, None),
        P(("groups", "batch")),
        P("tensor", None),
        P("batch", "tensor", None),
        P("batch", None, "tensor"),
        P("batch"),
        P(("groups", "batch")),
        P(("groups", "batch")),
    )

    def placed_local(*arrays):
        return local(mesh.shape["tensor"], mesh.shape["batch"], *arrays)

    return jax.shard_map(
        placed_local,
        mesh=mesh,
        in_specs=placed,
        out_specs=P(("groups", "batch"), "tensor"),
        check_vma=False,
    )
```
